32 devices in a mesh: member: 2 (over y), tile: 8 (over z, x), comp: 2 (over core).
Axes of the slice: x: 2, y: 2, z: 4, core: 2. Of those that a mesh axis runs over, the one named last changes fastest.
Arguments:
- sky_warmth_deviation: float32 [72, 1024, 128], P(None, ('member', 'tile', 'comp')), parts along dimension 1, may hold values from -6 to 6
- random_forcing_pattern: float32 [4, 1024, 128], P(None, ('member', 'tile', 'comp')), parts along dimension 1, may hold values from -6 to 6
- vertical_shape_curve: float32 [72], replicated, may hold values from 0.2 to 1
- sky_felt_skin_warmth: float32 [1024, 128], P(('member', 'tile', 'comp')), parts along dimension 0, may hold values from -6 to 6
- exchange_rate_factor: float32 [512, 128], P(('tile', 'comp')), may hold values from 0.05 to 0.5
- sky_diffusive_solve: float32 [72, 72], replicated, may hold values from -1 to 1
- crossing_share_matrix: bfloat16 [4, 128, 128], replicated, may hold values from -0.5 to 0.5
- owning_patch_number: int32 [512, 4], P(('tile', 'comp')), may hold values from 0 to 7, all different within a row; in each aligned block of 32 rows (0 to 31, 32 to 63, ...) at most 32 rows name the same one
- local_latitude_number: int32 [512, 4], P(('tile', 'comp')), may hold values from 0 to 15
- marine_warmth_deviation: float32 [62, 512, 128], P(None, ('member', 'tile', 'comp')), parts along dimension 1, may hold values from -6 to 6
- marine_brine_deviation: float32 [62, 512, 128], P(None, ('member', 'tile', 'comp')), parts along dimension 1, may hold values from -6 to 6
- wet_cell_indicator: int32 [256, 128], P(('tile', 'comp')), may hold values 0 or 1
- marine_diffusive_solve: float32 [62, 62], replicated, may hold values from -1 to 1
Outputs:
- atm_out: float32 [72, 1024, 128], P(None, ('member', 'tile', 'comp')), parts along dimension 1
- final_marine_warmth: float32 [62, 512, 128], P(None, ('member', 'tile', 'comp')), parts along dimension 1
- final_brine_level: float32 [62, 512, 128], P(None, ('member', 'tile', 'comp')), parts along dimension 1
The draws below stay inside these ranges and needn't reach their ends.
There are 2 independent parts, one for each index of `member`. The reference program is written for one: setup_inputs(seed, part) draws one part's arguments, and reference() takes and returns one part's arrays. A program takes and returns all parts, laid end to end along the dimension named above; an argument that names none is the same for every part. Nothing has to cross between parts.
Inputs may be any that keep to these rules, and one draw needn't show every extreme that they name: `owning_patch_number`: each row names 4 different tiles; in the 32 rows of one device no tile is named by more than 32 rows, a bound that some block reaches.
All inputs are finite; a program needn't handle non-finite values. No bound on the sum of `wet_cell_indicator` on one device may be relied on, other than what follows from the above.
Results may differ from the reference program's by a relative error of at most 0.0003.
Values sent between devices are 32-bit elements; how exact they have to be, the bound alone decides.
No kernel may reach another device: no remote copies, remote signals or barrier semaphores. Data moves between devices by JAX's collectives and lax.ppermute only.
A program may use at most 64 MiB of HBM per device.

```python
import math
import jax
import jax.numpy as jnp
import numpy as np
from jax import lax

SKY_LAYERS = 72
SEA_LAYERS = 62
SKY_PART_LONGS = 128
SEA_PART_LONGS = 128
AR = 32
OR = 16
NSA = 4
TOPK = 4
CAP = 32
SKY_LATITUDES = 512
SEA_LATITUDES = 256
N_TILE = 8
N_COMP = 2


def mixing_matrix(key, levels):
    diag_key, off_key = jax.random.split(key)
    diagonal = jax.random.uniform(diag_key, (levels,), jnp.float32, 0.55, 0.85)
    off_part = jax.random.normal(off_key, (levels, levels), jnp.float32) * (0.35 / levels ** 0.5)
    off_part = jnp.clip(off_part, -0.9, 0.9)
    same = jnp.arange(levels)[:, None] == jnp.arange(levels)[None, :]
    return jnp.where(same, diagonal[:, None] + 0.0 * off_part, off_part)


def draw_sky_diffusive_solve(key, part):
    key = jax.random.fold_in(key, 11)
    return mixing_matrix(key, SKY_LAYERS)


def draw_marine_diffusive_solve(key, part):
    key = jax.random.fold_in(key, 23)
    return mixing_matrix(key, SEA_LAYERS)


def plant(result, rng, smallest, largest):
    extent = result.shape
    index_at = [jax.random.randint(jax.random.fold_in(rng, axis), (), 0, extent[axis]) for axis in range(len(extent))]
    result = result.at[tuple(index_at)].set(smallest)
    longest = extent.index(max(extent))
    index_at[longest] = (index_at[longest] + 1) % extent[longest]
    return result.at[tuple(index_at)].set(largest)


def block_scale(own_key, shape, cuts, low, largest):
    loudness, own = 1.0, jax.random.fold_in(own_key, 6)
    for axis_at, parts in cuts:
        heights = jnp.exp(jax.random.uniform(jax.random.fold_in(own, axis_at), (parts,), jnp.float32, low / len(cuts), largest / len(cuts)))
        loudness = loudness * jnp.repeat(heights, shape[axis_at] // parts).reshape([-1 if axis == axis_at else 1 for axis in range(len(shape))])
    return loudness


def deal_out(rng, own, number, rows, count, top, reach, lean):
    sequence = jax.random.permutation(rng, count)
    packed, usual = portions_of(count, rows * top, reach, lean, True), portions_of(count, rows * top, reach, lean, False)
    places = jnp.arange(count)

    def named(sizes, turn):
        used = int((sizes > 0).sum())
        fixed = max(1, used // 4)
        passed = fixed + (places - fixed + turn * (used - fixed)) % max(1, count - fixed)
        return jnp.zeros((count,), jnp.int32).at[sequence[jnp.where(places < fixed, places, passed)]].set(jnp.asarray(sizes, jnp.int32))

    sizes = jnp.where(number % 4 == 0, named(packed, number // 4), named(usual, number - number // 4 - 1))
    mixed = jax.random.permutation(jax.random.fold_in(own, 3), count)
    giver, taker = mixed[0:count // 2 * 2:2], mixed[1:count // 2 * 2:2]
    slack = jnp.minimum(sizes[giver] - 1, reach - sizes[taker]) // 2
    slack = jnp.where((giver == sequence[0]) | (taker == sequence[0]) | (sizes[taker] == 0), 0, jnp.maximum(slack, 0))
    passed = jax.random.randint(jax.random.fold_in(own, 4), (count // 2,), 0, 1 << 20) % (slack + 1)
    sizes = sizes.at[giver].add(-passed).at[taker].add(passed)
    members = jnp.searchsorted(jnp.cumsum(sizes), jnp.arange(rows * top), side="right").astype(jnp.int32)
    table = members.reshape(top, rows).T
    table = table[jax.random.permutation(jax.random.fold_in(own, 1), rows)]
    turn = jax.random.randint(jax.random.fold_in(own, 2), (rows, 1), 0, top)
    return jnp.take_along_axis(table, (jnp.arange(top)[None, :] + turn) % top, axis=1)


def portions_of(number_of, total, bound, slope, full):
    portions = [(1 << 20) // math.isqrt(rank ** slope) + 1 for rank in range(1, number_of + 1)]
    largest = bound if full else min(bound, max(-(-total // number_of), total * portions[0] // sum(portions)))
    least = 1 if total - largest >= number_of - 1 else 0
    holding, spare = [largest] + [least] * (number_of - 1), total - largest - least * (number_of - 1)
    while spare > 0:
        free = [i for i in range(1, number_of) if holding[i] < largest] or [i for i in range(1, number_of) if holding[i] < bound]
        mass, remaining = sum([portions[i] for i in free]), spare
        for i in free:
            addition = min(bound - holding[i], max(1, remaining * portions[i] // mass), spare)
            holding[i] = holding[i] + addition
            spare = spare - addition
    return np.array(holding)


def scatter_about(own_key, dims, deviation, reach, cuts=(), kind=jnp.bfloat16):
    gain = block_scale(own_key, dims, cuts, -0.22, 0.18) if cuts else 1.0
    entries = jax.random.normal(own_key, dims, jnp.float32) * deviation * gain
    return jnp.minimum(jnp.maximum(entries, -reach), reach).astype(kind)


def setup_inputs(seed: int = 0, part: int = 0) -> dict:
    arg_keys = jax.random.split(jax.random.key(seed), 14)
    part_splits = jax.random.split(jax.random.fold_in(arg_keys[13], part), 14)
    sky_warmth_deviation = scatter_about(part_splits[0], (SKY_LAYERS, SKY_LATITUDES, SKY_PART_LONGS), 1.0, 6.0, ((1, 16),), jnp.float32)
    random_forcing_pattern = scatter_about(part_splits[1], (NSA, SKY_LATITUDES, SKY_PART_LONGS), 1.0, 6.0, ((1, 16),), jnp.float32)
    vertical_shape_curve = jnp.clip(jax.random.uniform(arg_keys[2], (SKY_LAYERS,), jnp.float32, 0.2, 1.0), 0.2, 1.0)
    sky_felt_skin_warmth = scatter_about(part_splits[3], (SKY_LATITUDES, SKY_PART_LONGS), 1.0, 6.0, ((0, 16),), jnp.float32)
    exchange_rate_factor = jnp.clip(jnp.exp(math.log(0.5) - 2.3025851 * jax.random.uniform(arg_keys[4], (SKY_LATITUDES, SKY_PART_LONGS), jnp.float32) ** block_scale(arg_keys[4], (SKY_LATITUDES, SKY_PART_LONGS), ((0, 16),), -0.2, 0.2)), 0.05, 0.5)
    sky_diffusive_solve = draw_sky_diffusive_solve(jax.random.fold_in(arg_keys[13], 71), part)
    crossing_share_matrix = scatter_about(arg_keys[6], (TOPK, SKY_PART_LONGS, SEA_PART_LONGS), SKY_PART_LONGS ** -0.5, 0.5)
    owning_patch_number_keys = jax.random.split(jax.random.fold_in(arg_keys[7], 1), SKY_LATITUDES // AR)
    owning_patch_number_turns = jax.random.permutation(jax.random.fold_in(arg_keys[7], 3), SKY_LATITUDES // AR)
    owning_patch_number = jax.vmap(lambda own, number: deal_out(jax.random.fold_in(arg_keys[7], 2), own, number, AR, N_TILE, TOPK, CAP, 2))(owning_patch_number_keys, owning_patch_number_turns).reshape((SKY_LATITUDES, TOPK))
    local_latitude_number = plant(jax.random.randint(arg_keys[8], (SKY_LATITUDES, TOPK), 0, OR), jax.random.fold_in(arg_keys[8], 1), 0, OR - 1).astype(jnp.int32)
    marine_warmth_deviation = scatter_about(part_splits[9], (SEA_LAYERS, SEA_LATITUDES, SEA_PART_LONGS), 1.0, 6.0, ((1, 16),), jnp.float32)
    marine_brine_deviation = scatter_about(part_splits[10], (SEA_LAYERS, SEA_LATITUDES, SEA_PART_LONGS), 1.0, 6.0, ((1, 16),), jnp.float32)
    wet_cell_indicator = plant((jax.random.randint(arg_keys[11], (SEA_LATITUDES, SEA_PART_LONGS), 0, 4) < 3).astype(jnp.int32), jax.random.fold_in(arg_keys[11], 1), 0, 1)
    marine_diffusive_solve = draw_marine_diffusive_solve(jax.random.fold_in(arg_keys[13], 71), part)
    return {"sky_warmth_deviation": sky_warmth_deviation, "random_forcing_pattern": random_forcing_pattern, "vertical_shape_curve": vertical_shape_curve, "sky_felt_skin_warmth": sky_felt_skin_warmth, "exchange_rate_factor": exchange_rate_factor, "sky_diffusive_solve": sky_diffusive_solve, "crossing_share_matrix": crossing_share_matrix, "owning_patch_number": owning_patch_number, "local_latitude_number": local_latitude_number, "marine_warmth_deviation": marine_warmth_deviation, "marine_brine_deviation": marine_brine_deviation, "wet_cell_indicator": wet_cell_indicator, "marine_diffusive_solve": marine_diffusive_solve}


atm_diffusion = 0.2
ocean_diffusion = 0.2


def advance_air_column(bordered_arrays, forcing, surface, coefficient, vmix, vertical_shape_curve):
    center = bordered_arrays[:, 1:-1, :]
    laplace = bordered_arrays[:, 2:, :] + bordered_arrays[:, :-2, :] + jnp.roll(center, 1, 2) + jnp.roll(center, -1, 2) - 4.0 * center
    interface_heat_flux = coefficient * (center[-1] - surface)
    updated = center + atm_diffusion * laplace + vertical_shape_curve[:, None, None] * forcing[None]
    updated = jnp.concatenate([updated[:-1], (updated[-1] - interface_heat_flux)[None]], 0)
    mixed = jnp.einsum("kl,lrx->krx", vmix, updated, precision=lax.Precision.HIGHEST)
    return mixed, interface_heat_flux


def marine_refresh(bordered_arrays, temp, salt, wet_indicator_real, thermal_energy, vmix):
    levels = temp.shape[0]
    center = bordered_arrays[:, 1:-1, :]
    summed = bordered_arrays[:, 2:, :] + bordered_arrays[:, :-2, :] + jnp.roll(center, 1, 2) + jnp.roll(center, -1, 2)
    count = summed[2 * levels]
    laplace_t = wet_indicator_real * (summed[:levels] - temp * count)
    laplace_s = wet_indicator_real * (summed[levels:2 * levels] - salt * count)
    temp_pre = temp + ocean_diffusion * laplace_t
    temp_pre = jnp.concatenate([(temp_pre[0] + wet_indicator_real * thermal_energy)[None], temp_pre[1:]], 0)
    salt_pre = salt + ocean_diffusion * laplace_s
    mixed_t = jnp.einsum("kl,lrx->krx", vmix, temp_pre, precision=lax.Precision.HIGHEST)
    mixed_s = jnp.einsum("kl,lrx->krx", vmix, salt_pre, precision=lax.Precision.HIGHEST)
    temp_new = wet_indicator_real * mixed_t + (1.0 - wet_indicator_real) * temp
    salt_new = wet_indicator_real * mixed_s + (1.0 - wet_indicator_real) * salt
    return temp_new, salt_new


def reference(sky_warmth_deviation, random_forcing_pattern, vertical_shape_curve, sky_felt_skin_warmth, exchange_rate_factor, sky_diffusive_solve, crossing_share_matrix, owning_patch_number, local_latitude_number, marine_warmth_deviation, marine_brine_deviation, wet_cell_indicator, marine_diffusive_solve):
    joint_condition = sky_warmth_deviation
    grand_total = jnp.zeros(sky_felt_skin_warmth.shape, jnp.float32)
    for advance_window in range(NSA):
        bordered_arrays = jnp.pad(joint_condition, ((0, 0), (1, 1), (0, 0)))
        joint_condition, interface_heat_flux = advance_air_column(bordered_arrays, random_forcing_pattern[advance_window], sky_felt_skin_warmth, exchange_rate_factor, sky_diffusive_solve, vertical_shape_curve)
        grand_total = grand_total + interface_heat_flux
    flux_mean = (grand_total / NSA).astype(jnp.bfloat16)
    pieces = []
    for index in range(TOPK):
        pieces.append(jnp.dot(flux_mean, crossing_share_matrix[index], preferred_element_type=jnp.float32))
    projected = jnp.stack(pieces, 1)
    comp_of_row = ((jnp.arange(SKY_LATITUDES) // AR) % N_COMP).astype(jnp.int32)
    target = (owning_patch_number * N_COMP + comp_of_row[:, None]) * OR + local_latitude_number
    thermal_energy = jax.ops.segment_sum(projected.reshape(-1, SEA_PART_LONGS), target.reshape(-1), num_segments=SEA_LATITUDES)
    wet_indicator_real = wet_cell_indicator.astype(jnp.float32)
    piled_arrays = jnp.concatenate([wet_indicator_real[None] * marine_warmth_deviation, wet_indicator_real[None] * marine_brine_deviation, wet_indicator_real[None]], 0)
    bordered_arrays = jnp.pad(piled_arrays, ((0, 0), (1, 1), (0, 0)))
    final_marine_warmth, final_brine_level = marine_refresh(bordered_arrays, marine_warmth_deviation, marine_brine_deviation, wet_indicator_real, thermal_energy, marine_diffusive_solve)
    return joint_condition, final_marine_warmth, final_brine_level
```

```python
import functools

import jax
import jax.numpy as jnp
from jax import lax
from jax.experimental import pallas as pl
from jax.experimental.pallas import tpu as pltpu
from jax.sharding import PartitionSpec as P

atm_diffusion = 0.2
ocean_diffusion = 0.2
HALO = 4
EXACT = lax.Precision.HIGHEST
VMEM = pl.BlockSpec(memory_space=pltpu.VMEM)
f32, bf16 = jnp.float32, jnp.bfloat16


def up_to(n, m):
    return -(-n // m) * m


def call(kernel, out_shape, *args, scratch=(), in_specs=None, flops=0, moved=0):
    return pl.pallas_call(
        kernel,
        out_shape=out_shape,
        in_specs=in_specs or [VMEM] * len(args),
        out_specs=jax.tree.map(lambda _: VMEM, out_shape),
        scratch_shapes=list(scratch),
        compiler_params=pltpu.CompilerParams(vmem_limit_bytes=24 * 2**20),
        cost_estimate=pl.CostEstimate(flops=flops, bytes_accessed=moved, transcendentals=0),
    )(*args)


def pack_kernel(sizes, sky, forcing, surface, rate, warmth, brine, wet, up, down):
    levels, rows, steps, sea_levels, sea_rows, stride, sea_stride = sizes
    width = sky.shape[1]
    m = wet[...].astype(f32)
    for out, first, sea_row in ((up, 0, 0), (down, rows - HALO, sea_rows - 1)):
        for j in range(HALO):
            row = first + j
            out[j * stride : j * stride + levels, :] = sky[pl.ds(row, levels, stride=rows), :]
            base = j * stride + levels
            tail = [forcing[s * rows + row : s * rows + row + 1, :] for s in range(steps)]
            tail += [surface[row : row + 1, :], rate[row : row + 1, :], jnp.ones((1, width), f32)]
            tail += [jnp.zeros((stride - levels - len(tail), width), f32)]
            out[base : (j + 1) * stride, :] = jnp.concatenate(tail, 0)
        base = HALO * stride
        edge = m[sea_row : sea_row + 1]
        out[base : base + sea_levels, :] = warmth[pl.ds(sea_row, sea_levels, stride=sea_rows), :] * edge
        base += sea_stride
        out[base : base + sea_levels, :] = brine[pl.ds(sea_row, sea_levels, stride=sea_rows), :] * edge
        base += sea_stride
        out[base : base + 8, :] = jnp.concatenate([edge, jnp.zeros((7, width), f32)], 0)


def split(x):
    high = x.astype(bf16)
    return high, (x - high.astype(f32)).astype(bf16)


def three_terms(w, depth):
    high = w.astype(bf16).astype(f32)
    low = w - high
    return (high + pltpu.roll(high, depth, 1) + pltpu.roll(low, 2 * depth, 1)).astype(bf16)


def local_kernel(sizes, vmix, curve, sea_mix, sky, rows_of_mix, source_rows, weights, sea_weights, sea_first, own):
    levels, rows, steps, sea_levels, sea_rows, stride, sea_stride = sizes
    width = sky.shape[1]
    depth = up_to(levels + 2 * steps, 16)
    v = vmix[...]
    dot = functools.partial(jnp.dot, precision=EXACT, preferred_element_type=f32)
    powers = [v]
    for _ in range(steps - 1):
        powers.append(dot(v, powers[-1]))
    last = (lax.broadcasted_iota(jnp.int32, (levels, width), 0) == levels - 1).astype(f32)
    for s in range(1, steps):
        rows_of_mix[(s - 1) * levels : s * levels, :] = lax.dot_general(
            powers[s - 1], last, (((0,), (0,)), ((), ())), precision=EXACT, preferred_element_type=f32
        )
    by_curve = jnp.broadcast_to(curve[...], (width, levels))
    of_curve = [
        lax.dot_general(p, by_curve, (((1,), (1,)), ((), ())), precision=EXACT, preferred_element_type=f32)
        for p in powers
    ]
    of_last = [jnp.broadcast_to(p[:, levels - 1 : levels], (levels, width)) for p in powers]
    found = [of_curve[i][levels - 1 :] for i in range(steps - 1)]
    found += [of_last[i][levels - 1 :] for i in range(steps - 1)]
    found += [jnp.zeros((8 - len(found), width), f32)]
    source_rows[...] = jnp.concatenate(found, 0)
    lane = lax.broadcasted_iota(jnp.int32, (levels, width), 1)
    wide = jnp.concatenate(
        [powers[-1] * atm_diffusion**steps, jnp.zeros((levels, width - levels), f32)], 1
    )
    for j in range(steps):
        factor = atm_diffusion ** (steps - 1 - j)
        wide = jnp.where(lane == levels + j, of_curve[steps - 1 - j] * factor, wide)
        wide = jnp.where(lane == levels + steps + j, of_last[steps - 1 - j] * -factor, wide)
    wide = jnp.concatenate([wide, jnp.zeros((levels, width), f32)], 1)
    wide = jnp.concatenate([wide, jnp.zeros((weights.shape[0] - levels, 2 * width), f32)], 0)
    weights[...] = three_terms(wide, depth)
    sea = sea_mix[...]
    sea = jnp.concatenate([sea, jnp.zeros((sea_levels, 2 * width - sea_levels), f32)], 1)
    sea = jnp.concatenate([sea, jnp.zeros((sea_stride - sea_levels, 2 * width), f32)], 0)
    sea_weights[...] = three_terms(sea, sea_stride)
    sea_first[...] = jnp.broadcast_to(sea[:, 0:1], sea_first.shape)
    sums = [jnp.zeros((rows, width), f32) for _ in range(steps - 1)]
    for l in range(levels):
        x = sky[l * rows : (l + 1) * rows, :]
        for s in range(steps - 1):
            sums[s] = sums[s] + rows_of_mix[s * levels + l : s * levels + l + 1, :] * x
    for s in range(steps - 1):
        own[s * rows : (s + 1) * rows, :] = sums[s]


def cross(x):
    n, w = x.shape
    return (
        x + pltpu.roll(x, 1, 0) + pltpu.roll(x, n - 1, 0) + pltpu.roll(x, 1, 1) + pltpu.roll(x, w - 1, 1)
    )


def masked(x, rows, inside):
    return jnp.concatenate([x[:rows], x[rows:] * inside], 0)


def flux_kernel(
    sizes, sky, forcing, surface, rate, rows_of_mix, source_rows, own, owners, locals_, below, above,
    sent, fluxes, halo
):
    levels, rows, steps, sea_levels, sea_rows, stride, sea_stride = sizes
    width = sky.shape[1]
    halo[: HALO * stride, :] = below[: HALO * stride, :]
    halo[HALO * stride :, :] = above[: HALO * stride, :]

    def edge(l):
        return halo[pl.ds(l, 2 * HALO, stride=stride), :]

    inside = edge(levels + steps + 2)
    sums = [jnp.zeros((2 * HALO, width), f32) for _ in range(steps - 1)]
    for l in range(levels):
        x = edge(l)
        for s in range(steps - 1):
            sums[s] = sums[s] + rows_of_mix[s * levels + l : s * levels + l + 1, :] * x
    tops = [jnp.concatenate([sky[...], edge(levels - 1)], 0)]
    tops += [jnp.concatenate([own[s * rows : (s + 1) * rows, :], sums[s]], 0) for s in range(steps - 1)]
    surf = jnp.concatenate([surface[...], edge(levels + steps)], 0)
    coef = jnp.concatenate([rate[...], edge(levels + steps + 1)], 0)
    force = [
        jnp.concatenate([forcing[s * rows : (s + 1) * rows, :], edge(levels + s)], 0) for s in range(steps)
    ]

    flux = []
    for s in range(steps):
        state = tops[s]
        for i in range(s):
            m = s - 1 - i
            state = masked(cross(state) * atm_diffusion, rows, inside)
            state = state + source_rows[m : m + 1, :] * force[i]
            state = state - source_rows[steps - 1 + m : steps + m, :] * flux[i]
        flux.append(coef * (state - surf))
        fluxes[s * (rows + 2 * HALO) : (s + 1) * (rows + 2 * HALO), :] = flux[s]
    total = flux[0][:rows]
    for s in range(1, steps):
        total = total + flux[s][:rows]
    mean = (total / steps).astype(bf16).astype(f32)
    times = width // rows
    owner = owners[...].astype(f32)
    row = locals_[...].astype(f32)
    table = jnp.concatenate(
        [jnp.concatenate([owner] * times, 1), jnp.concatenate([row] * times, 1)], 0
    )
    per = mean.shape[0] + table.shape[0]
    for t in range(sent.shape[0] // per):
        sent[t * per : t * per + rows, :] = mean
        sent[t * per + rows : (t + 1) * per, :] = table


def sky_kernel(sizes, sky, forcing, fluxes, weights, below, above, out, halo, spread):
    levels, rows, steps, sea_levels, sea_rows, stride, sea_stride = sizes
    width = sky.shape[1]
    depth = up_to(levels + 2 * steps, 16)
    halo[: HALO * stride, :] = below[: HALO * stride, :]
    halo[HALO * stride :, :] = above[: HALO * stride, :]

    def edge(l):
        return halo[pl.ds(l, 2 * HALO, stride=stride), :]

    inside = edge(levels + steps + 2)

    def times(x, n):
        for i in range(n):
            x = cross(x)
            if i < n - 1:
                x = masked(x, rows, inside)
        return x[:rows]

    @pl.loop(0, levels // 4)
    def _(q):
        for i in range(4):
            l = q * 4 + i
            at = pl.multiple_of(l * rows, 8)
            x = jnp.concatenate([sky[pl.ds(at, rows), :], edge(l)], 0)
            spread[pl.ds(at, rows), :] = times(x, steps)

    for j in range(steps):
        x = jnp.concatenate([forcing[j * rows : (j + 1) * rows, :], edge(levels + j)], 0)
        spread[(levels + j) * rows : (levels + j + 1) * rows, :] = times(x, steps - 1 - j)
        x = fluxes[j * (rows + 2 * HALO) : (j + 1) * (rows + 2 * HALO), :]
        spread[(levels + steps + j) * rows : (levels + steps + j + 1) * rows, :] = times(
            x, steps - 1 - j
        )

    w = weights[:, : 3 * depth]
    for r in range(0, rows, 2):
        x = jnp.concatenate([spread[pl.ds(r + i, depth, stride=rows), :] for i in range(2)], 1)
        high, low = split(x)
        y = jnp.dot(w, jnp.concatenate([high, low, high], 0), preferred_element_type=f32)
        for i in range(2):
            out[pl.ds(r + i, levels, stride=rows), :] = y[:levels, i * width : (i + 1) * width]


def sea_kernel(sizes, warmth, brine, wet, weights, below, above, warm_out, brine_out, edges, spread):
    levels, rows, steps, sea_levels, sea_rows, stride, sea_stride = sizes
    width = warmth.shape[1]
    base = HALO * stride
    m = wet[...].astype(f32)
    at = lax.broadcasted_iota(jnp.int32, (sea_rows, width), 0)

    def around(x, top, bottom):
        north = jnp.where(at == 0, top, pltpu.roll(x, 1, 0))
        south = jnp.where(at == sea_rows - 1, bottom, pltpu.roll(x, sea_rows - 1, 0))
        return north + south + pltpu.roll(x, 1, 1) + pltpu.roll(x, width - 1, 1)

    mark = base + 2 * sea_stride
    count = around(m, above[mark : mark + 1, :], below[mark : mark + 1, :])
    for f, field in enumerate((warmth, brine)):
        first = base + f * sea_stride
        for l in range(sea_levels):
            x = field[l * sea_rows : (l + 1) * sea_rows, :]
            near = around(m * x, above[first + l : first + l + 1, :], below[first + l : first + l + 1, :])
            spread[f, l * sea_rows : (l + 1) * sea_rows, :] = x + ocean_diffusion * (m * (near - x * count))
        if sea_stride > sea_levels:
            spread[f, sea_levels * sea_rows :, :] = jnp.zeros(((sea_stride - sea_levels) * sea_rows, width), f32)

    w = weights[:, : 3 * sea_stride]
    for r in range(sea_rows):
        x = jnp.concatenate([spread[f, pl.ds(r, sea_stride, stride=sea_rows), :] for f in range(2)], 1)
        high, low = split(x)
        y = jnp.dot(w, jnp.concatenate([high, low, high], 0), preferred_element_type=f32)
        wet_row = m[r : r + 1]
        for f, (field, out) in enumerate(((warmth, warm_out), (brine, brine_out))):
            old = field[pl.ds(r, sea_levels, stride=sea_rows), :]
            new = y[:sea_levels, f * width : (f + 1) * width]
            out[pl.ds(r, sea_levels, stride=sea_rows), :] = wet_row * new + (1.0 - wet_row) * old


def heat_kernel(sizes, topk, got, mine, shares, wet, sea_first, before, after):
    levels, rows, steps, sea_levels, sea_rows, stride, sea_stride = sizes
    width = before.shape[1]
    per = rows + 2 * topk
    group = width // rows
    me = mine[0].astype(f32)
    part = lax.broadcasted_iota(jnp.int32, (1, width), 1) // rows
    to = lax.broadcasted_iota(jnp.int32, (sea_rows, width), 0).astype(f32)
    picked = jnp.zeros((topk * sea_rows, width), f32)
    for g in range(got.shape[0] // (per * group)):
        at = [(g * group + i) * per for i in range(group)]
        mean = jnp.concatenate([got[a : a + rows, :] for a in at], 0).astype(bf16)
        table = got[at[0] + rows : at[0] + per, :]
        for i in range(1, group):
            table = jnp.where(part == i, got[at[i] + rows : at[i] + per, :], table)
        hot = []
        for k in range(topk):
            row = jnp.where(table[k : k + 1] == me, table[topk + k : topk + k + 1], -1.0)
            hot.append(jnp.where(to == row, 1.0, 0.0))
        hot = jnp.concatenate(hot, 0).astype(bf16)
        picked = picked + jnp.dot(hot, mean, preferred_element_type=f32)
    side = jnp.concatenate([picked[k * sea_rows : (k + 1) * sea_rows] for k in range(topk)], 1)
    first = side.astype(bf16).astype(f32)
    second = (side - first).astype(bf16).astype(f32)
    third = side - first - second
    parts = jnp.concatenate([first, second, third], 0).astype(bf16)
    y = jnp.dot(parts, shares[...], preferred_element_type=f32)
    heat = y[:sea_rows] + y[sea_rows : 2 * sea_rows] + y[2 * sea_rows :]
    heat = wet[...].astype(f32) * heat
    for l in range(sea_levels):
        after[l * sea_rows : (l + 1) * sea_rows, :] = (
            before[l * sea_rows : (l + 1) * sea_rows, :] + sea_first[l : l + 1, :] * heat
        )


def body(sky, forcing, curve, surface, rate, vmix, shares, owners, locals_, warmth, brine, wet, sea_mix):
    levels, rows, width = sky.shape
    steps = forcing.shape[0]
    sea_levels, sea_rows, _ = warmth.shape
    topk = owners.shape[1]
    stride = up_to(levels + steps + 3, 8)
    sea_stride = up_to(sea_levels, 16)
    sizes = (levels, rows, steps, sea_levels, sea_rows, stride, sea_stride)
    tiles = lax.axis_size("tile")
    sky2, forcing2 = sky.reshape(-1, width), forcing.reshape(-1, width)
    warmth2, brine2 = warmth.reshape(-1, width), brine.reshape(-1, width)
    flat = lambda n, kind=f32: jax.ShapeDtypeStruct((n, width), kind)

    length = HALO * stride + 2 * sea_stride + 8
    up, down = call(
        functools.partial(pack_kernel, sizes), [flat(length)] * 2,
        sky2, forcing2, surface, rate, warmth2, brine2, wet, moved=4 << 20,
    )
    count = lax.axis_size(("tile", "comp"))
    above = lax.ppermute(down, ("tile", "comp"), [(i, i + 1) for i in range(count - 1)])
    below = lax.ppermute(up, ("tile", "comp"), [(i + 1, i) for i in range(count - 1)])

    mix_rows = up_to(levels, 16)
    rows_of_mix, source_rows, weights, sea_weights, sea_first, own = call(
        functools.partial(local_kernel, sizes),
        [
            flat((steps - 1) * levels), flat(8), jax.ShapeDtypeStruct((mix_rows, 2 * width), bf16),
            jax.ShapeDtypeStruct((sea_stride, 2 * width), bf16), flat(sea_stride), flat((steps - 1) * rows),
        ],
        vmix, curve[None], sea_mix, sky2, flops=1 << 30, moved=4 << 20,
    )

    per = rows + 2 * topk
    sent, fluxes = call(
        functools.partial(flux_kernel, sizes), [flat(tiles * per), flat(steps * (rows + 2 * HALO))],
        sky[-1], forcing2, surface, rate, rows_of_mix, source_rows, own, owners.T, locals_.T, below, above,
        scratch=[pltpu.VMEM((2 * HALO * stride, width), f32)], moved=2 << 20,
    )
    got = lax.all_to_all(sent.reshape(tiles, per, width), "tile", split_axis=0, concat_axis=0, tiled=True)
    got = got.reshape(-1, width)

    sky_out = call(
        functools.partial(sky_kernel, sizes), flat(levels * rows),
        sky2, forcing2, fluxes, weights, below, above,
        scratch=[
            pltpu.VMEM((2 * HALO * stride, width), f32),
            pltpu.VMEM((up_to(levels + 2 * steps, 16) * rows, width), f32),
        ],
        flops=4 << 30, moved=8 << 20,
    )
    warm, salt = call(
        functools.partial(sea_kernel, sizes), [flat(sea_levels * sea_rows)] * 2,
        warmth2, brine2, wet, sea_weights, below, above,
        scratch=[pltpu.VMEM((8, width), f32), pltpu.VMEM((2, sea_stride * sea_rows, width), f32)],
        flops=2 << 30, moved=4 << 20,
    )
    mine = lax.axis_index("tile").astype(jnp.int32)[None]
    warm = call(
        functools.partial(heat_kernel, sizes, topk), flat(sea_levels * sea_rows),
        got, mine, shares.reshape(-1, width), wet, sea_first, warm,
        in_specs=[VMEM, pl.BlockSpec(memory_space=pltpu.SMEM)] + [VMEM] * 4, moved=2 << 20,
    )
    return sky_out.reshape(sky.shape), warm.reshape(warmth.shape), salt.reshape(brine.shape)


def solution(mesh):
    both = P(None, ("member", "tile", "comp"), None)
    one = P(("tile", "comp"), None)
    return jax.shard_map(
        body,
        mesh=mesh,
        in_specs=(
            both, both, P(), P(("member", "tile", "comp"), None), one, P(), P(), one, one, both, both, one, P(),
        ),
        out_specs=(both, both, both),
        check_vma=False,
    )
```

```python
import functools

import jax
import jax.numpy as jnp
from jax import lax
from jax.experimental import pallas as pl
from jax.experimental.pallas import tpu as pltpu
from jax.sharding import PartitionSpec as P

atm_diffusion = 0.2
ocean_diffusion = 0.2
HALO = 4
EXACT = lax.Precision.HIGHEST
VMEM = pl.BlockSpec(memory_space=pltpu.VMEM)
f32, bf16 = jnp.float32, jnp.bfloat16


def up_to(n, m):
    return -(-n // m) * m


def call(kernel, out_shape, *args, scratch=(), in_specs=None, flops=0, moved=0, grant=24):
    return pl.pallas_call(
        kernel,
        out_shape=out_shape,
        in_specs=in_specs or [VMEM] * len(args),
        out_specs=jax.tree.map(lambda _: VMEM, out_shape),
        scratch_shapes=list(scratch),
        compiler_params=pltpu.CompilerParams(vmem_limit_bytes=grant * 2**20),
        cost_estimate=pl.CostEstimate(flops=flops, bytes_accessed=moved, transcendentals=0),
    )(*args)


def pack_kernel(sizes, sky, forcing, surface, rate, warmth, brine, wet, up, down):
    levels, rows, steps, sea_levels, sea_rows, stride, sea_stride = sizes
    width = sky.shape[1]
    m = wet[...].astype(f32)
    for out, first, sea_row in ((up, 0, 0), (down, rows - HALO, sea_rows - 1)):
        for j in range(HALO):
            row = first + j
            out[j * stride : j * stride + levels, :] = sky[pl.ds(row, levels, stride=rows), :]
            base = j * stride + levels
            tail = [forcing[s * rows + row : s * rows + row + 1, :] for s in range(steps)]
            tail += [surface[row : row + 1, :], rate[row : row + 1, :], jnp.ones((1, width), f32)]
            tail += [jnp.zeros((stride - levels - len(tail), width), f32)]
            out[base : (j + 1) * stride, :] = jnp.concatenate(tail, 0)
        base = HALO * stride
        edge = m[sea_row : sea_row + 1]
        out[base : base + sea_levels, :] = warmth[pl.ds(sea_row, sea_levels, stride=sea_rows), :] * edge
        base += sea_stride
        out[base : base + sea_levels, :] = brine[pl.ds(sea_row, sea_levels, stride=sea_rows), :] * edge
        base += sea_stride
        out[base : base + 8, :] = jnp.concatenate([edge, jnp.zeros((7, width), f32)], 0)


def split(x):
    high = x.astype(bf16)
    return high, (x - high.astype(f32)).astype(bf16)


def three_terms(w, depth):
    high = w.astype(bf16).astype(f32)
    low = w - high
    return (high + pltpu.roll(high, depth, 1) + pltpu.roll(low, 2 * depth, 1)).astype(bf16)


def local_kernel(sizes, vmix, curve, sea_mix, sky, rows_of_mix, source_rows, weights, sea_weights, sea_first, own):
    levels, rows, steps, sea_levels, sea_rows, stride, sea_stride = sizes
    width = sky.shape[1]
    depth = up_to(levels + 2 * steps, 16)
    v = vmix[...]
    dot = functools.partial(jnp.dot, precision=EXACT, preferred_element_type=f32)
    powers = [v]
    for _ in range(steps - 1):
        powers.append(dot(v, powers[-1]))
    last = (lax.broadcasted_iota(jnp.int32, (levels, width), 0) == levels - 1).astype(f32)
    for s in range(1, steps):
        rows_of_mix[(s - 1) * levels : s * levels, :] = lax.dot_general(
            powers[s - 1], last, (((0,), (0,)), ((), ())), precision=EXACT, preferred_element_type=f32
        )
    by_curve = jnp.broadcast_to(curve[...], (width, levels))
    of_curve = [
        lax.dot_general(p, by_curve, (((1,), (1,)), ((), ())), precision=EXACT, preferred_element_type=f32)
        for p in powers
    ]
    of_last = [jnp.broadcast_to(p[:, levels - 1 : levels], (levels, width)) for p in powers]
    found = [of_curve[i][levels - 1 :] for i in range(steps - 1)]
    found += [of_last[i][levels - 1 :] for i in range(steps - 1)]
    found += [jnp.zeros((8 - len(found), width), f32)]
    source_rows[...] = jnp.concatenate(found, 0)
    lane = lax.broadcasted_iota(jnp.int32, (levels, width), 1)
    wide = jnp.concatenate(
        [powers[-1] * atm_diffusion**steps, jnp.zeros((levels, width - levels), f32)], 1
    )
    for j in range(steps):
        factor = atm_diffusion ** (steps - 1 - j)
        wide = jnp.where(lane == levels + j, of_curve[steps - 1 - j] * factor, wide)
        wide = jnp.where(lane == levels + steps + j, of_last[steps - 1 - j] * -factor, wide)
    wide = jnp.concatenate([wide, jnp.zeros((levels, width), f32)], 1)
    wide = jnp.concatenate([wide, jnp.zeros((weights.shape[0] - levels, 2 * width), f32)], 0)
    weights[...] = three_terms(wide, depth)
    sea = sea_mix[...]
    sea = jnp.concatenate([sea, jnp.zeros((sea_levels, 2 * width - sea_levels), f32)], 1)
    sea = jnp.concatenate([sea, jnp.zeros((sea_stride - sea_levels, 2 * width), f32)], 0)
    sea_weights[...] = three_terms(sea, sea_stride)
    sea_first[...] = jnp.broadcast_to(sea[:, 0:1], sea_first.shape)
    sums = [jnp.zeros((rows, width), f32) for _ in range(steps - 1)]
    for l in range(levels):
        x = sky[l * rows : (l + 1) * rows, :]
        for s in range(steps - 1):
            sums[s] = sums[s] + rows_of_mix[s * levels + l : s * levels + l + 1, :] * x
    for s in range(steps - 1):
        own[s * rows : (s + 1) * rows, :] = sums[s]


def cross(x):
    n, w = x.shape
    return (
        x + pltpu.roll(x, 1, 0) + pltpu.roll(x, n - 1, 0) + pltpu.roll(x, 1, 1) + pltpu.roll(x, w - 1, 1)
    )


def masked(x, rows, inside):
    return jnp.concatenate([x[:rows], x[rows:] * inside], 0)


def flux_kernel(
    sizes, sky, forcing, surface, rate, rows_of_mix, source_rows, own, owners, locals_, below, above,
    sent, fluxes, halo
):
    levels, rows, steps, sea_levels, sea_rows, stride, sea_stride = sizes
    width = sky.shape[1]
    halo[: HALO * stride, :] = below[: HALO * stride, :]
    halo[HALO * stride :, :] = above[: HALO * stride, :]

    def edge(l):
        return halo[pl.ds(l, 2 * HALO, stride=stride), :]

    inside = edge(levels + steps + 2)
    sums = [jnp.zeros((2 * HALO, width), f32) for _ in range(steps - 1)]
    for l in range(levels):
        x = edge(l)
        for s in range(steps - 1):
            sums[s] = sums[s] + rows_of_mix[s * levels + l : s * levels + l + 1, :] * x
    tops = [jnp.concatenate([sky[...], edge(levels - 1)], 0)]
    tops += [jnp.concatenate([own[s * rows : (s + 1) * rows, :], sums[s]], 0) for s in range(steps - 1)]
    surf = jnp.concatenate([surface[...], edge(levels + steps)], 0)
    coef = jnp.concatenate([rate[...], edge(levels + steps + 1)], 0)
    force = [
        jnp.concatenate([forcing[s * rows : (s + 1) * rows, :], edge(levels + s)], 0) for s in range(steps)
    ]

    flux = []
    for s in range(steps):
        state = tops[s]
        for i in range(s):
            m = s - 1 - i
            state = masked(cross(state) * atm_diffusion, rows, inside)
            state = state + source_rows[m : m + 1, :] * force[i]
            state = state - source_rows[steps - 1 + m : steps + m, :] * flux[i]
        flux.append(coef * (state - surf))
        fluxes[s * (rows + 2 * HALO) : (s + 1) * (rows + 2 * HALO), :] = flux[s]
    total = flux[0][:rows]
    for s in range(1, steps):
        total = total + flux[s][:rows]
    mean = (total / steps).astype(bf16).astype(f32)
    times = width // rows
    owner = owners[...].astype(f32)
    row = locals_[...].astype(f32)
    table = jnp.concatenate(
        [jnp.concatenate([owner] * times, 1), jnp.concatenate([row] * times, 1)], 0
    )
    sent[:rows, :] = mean
    sent[rows:, :] = table


def sky_kernel(sizes, sky, forcing, fluxes, weights, below, above, out, halo, spread):
    levels, rows, steps, sea_levels, sea_rows, stride, sea_stride = sizes
    width = sky.shape[1]
    depth = up_to(levels + 2 * steps, 16)
    halo[: HALO * stride, :] = below[: HALO * stride, :]
    halo[HALO * stride :, :] = above[: HALO * stride, :]

    def edge(l):
        return halo[pl.ds(l, 2 * HALO, stride=stride), :]

    inside = edge(levels + steps + 2)

    def times(x, n):
        for i in range(n):
            x = cross(x)
            if i < n - 1:
                x = masked(x, rows, inside)
        return x[:rows]

    @pl.loop(0, levels // 4)
    def _(q):
        for i in range(4):
            l = q * 4 + i
            at = pl.multiple_of(l * rows, 8)
            x = jnp.concatenate([sky[pl.ds(at, rows), :], edge(l)], 0)
            spread[pl.ds(at, rows), :] = times(x, steps)

    for j in range(steps):
        x = jnp.concatenate([forcing[j * rows : (j + 1) * rows, :], edge(levels + j)], 0)
        spread[(levels + j) * rows : (levels + j + 1) * rows, :] = times(x, steps - 1 - j)
        x = fluxes[j * (rows + 2 * HALO) : (j + 1) * (rows + 2 * HALO), :]
        spread[(levels + steps + j) * rows : (levels + steps + j + 1) * rows, :] = times(
            x, steps - 1 - j
        )

    w = weights[:, : 3 * depth]
    for r in range(0, rows, 2):
        x = jnp.concatenate([spread[pl.ds(r + i, depth, stride=rows), :] for i in range(2)], 1)
        high, low = split(x)
        y = jnp.dot(w, jnp.concatenate([high, low, high], 0), preferred_element_type=f32)
        for i in range(2):
            out[pl.ds(r + i, levels, stride=rows), :] = y[:levels, i * width : (i + 1) * width]


def sea_kernel(sizes, warmth, brine, wet, weights, below, above, warm_out, brine_out, edges, spread):
    levels, rows, steps, sea_levels, sea_rows, stride, sea_stride = sizes
    width = warmth.shape[1]
    base = HALO * stride
    m = wet[...].astype(f32)
    at = lax.broadcasted_iota(jnp.int32, (sea_rows, width), 0)

    def around(x, top, bottom):
        north = jnp.where(at == 0, top, pltpu.roll(x, 1, 0))
        south = jnp.where(at == sea_rows - 1, bottom, pltpu.roll(x, sea_rows - 1, 0))
        return north + south + pltpu.roll(x, 1, 1) + pltpu.roll(x, width - 1, 1)

    mark = base + 2 * sea_stride
    count = around(m, above[mark : mark + 1, :], below[mark : mark + 1, :])
    for f, field in enumerate((warmth, brine)):
        first = base + f * sea_stride
        for l in range(sea_levels):
            x = field[l * sea_rows : (l + 1) * sea_rows, :]
            near = around(m * x, above[first + l : first + l + 1, :], below[first + l : first + l + 1, :])
            spread[f, l * sea_rows : (l + 1) * sea_rows, :] = x + ocean_diffusion * (m * (near - x * count))
        if sea_stride > sea_levels:
            spread[f, sea_levels * sea_rows :, :] = jnp.zeros(((sea_stride - sea_levels) * sea_rows, width), f32)

    w = weights[:, : 3 * sea_stride]
    for r in range(sea_rows):
        x = jnp.concatenate([spread[f, pl.ds(r, sea_stride, stride=sea_rows), :] for f in range(2)], 1)
        high, low = split(x)
        y = jnp.dot(w, jnp.concatenate([high, low, high], 0), preferred_element_type=f32)
        wet_row = m[r : r + 1]
        for f, (field, out) in enumerate(((warmth, warm_out), (brine, brine_out))):
            old = field[pl.ds(r, sea_levels, stride=sea_rows), :]
            new = y[:sea_levels, f * width : (f + 1) * width]
            out[pl.ds(r, sea_levels, stride=sea_rows), :] = wet_row * new + (1.0 - wet_row) * old


def heat_kernel(sizes, topk, got, mine, shares, wet, sea_first, before, after):
    levels, rows, steps, sea_levels, sea_rows, stride, sea_stride = sizes
    width = before.shape[1]
    per = rows + 2 * topk
    group = width // rows
    me = mine[0].astype(f32)
    part = lax.broadcasted_iota(jnp.int32, (1, width), 1) // rows
    to = lax.broadcasted_iota(jnp.int32, (sea_rows, width), 0).astype(f32)
    picked = jnp.zeros((topk * sea_rows, width), f32)
    for g in range(got.shape[0] // (per * group)):
        at = [(g * group + i) * per for i in range(group)]
        mean = jnp.concatenate([got[a : a + rows, :] for a in at], 0).astype(bf16)
        table = got[at[0] + rows : at[0] + per, :]
        for i in range(1, group):
            table = jnp.where(part == i, got[at[i] + rows : at[i] + per, :], table)
        hot = []
        for k in range(topk):
            row = jnp.where(table[k : k + 1] == me, table[topk + k : topk + k + 1], -1.0)
            hot.append(jnp.where(to == row, 1.0, 0.0))
        hot = jnp.concatenate(hot, 0).astype(bf16)
        picked = picked + jnp.dot(hot, mean, preferred_element_type=f32)
    side = jnp.concatenate([picked[k * sea_rows : (k + 1) * sea_rows] for k in range(topk)], 1)
    first = side.astype(bf16).astype(f32)
    second = (side - first).astype(bf16).astype(f32)
    third = side - first - second
    parts = jnp.concatenate([first, second, third], 0).astype(bf16)
    y = jnp.dot(parts, shares[...], preferred_element_type=f32)
    heat = y[:sea_rows] + y[sea_rows : 2 * sea_rows] + y[2 * sea_rows :]
    heat = wet[...].astype(f32) * heat
    for l in range(sea_levels):
        after[l * sea_rows : (l + 1) * sea_rows, :] = (
            before[l * sea_rows : (l + 1) * sea_rows, :] + sea_first[l : l + 1, :] * heat
        )


def body(sky, forcing, curve, surface, rate, vmix, shares, owners, locals_, warmth, brine, wet, sea_mix):
    levels, rows, width = sky.shape
    steps = forcing.shape[0]
    sea_levels, sea_rows, _ = warmth.shape
    topk = owners.shape[1]
    stride = up_to(levels + steps + 3, 8)
    sea_stride = up_to(sea_levels, 16)
    sizes = (levels, rows, steps, sea_levels, sea_rows, stride, sea_stride)
    sky2, forcing2 = sky.reshape(-1, width), forcing.reshape(-1, width)
    warmth2, brine2 = warmth.reshape(-1, width), brine.reshape(-1, width)
    flat = lambda n, kind=f32: jax.ShapeDtypeStruct((n, width), kind)

    length = HALO * stride + 2 * sea_stride + 8
    up, down = call(
        functools.partial(pack_kernel, sizes), [flat(length)] * 2,
        sky2, forcing2, surface, rate, warmth2, brine2, wet, moved=4 << 20, grant=60,
    )
    count = lax.axis_size(("tile", "comp"))
    above = lax.ppermute(down, ("tile", "comp"), [(i, i + 1) for i in range(count - 1)])
    below = lax.ppermute(up, ("tile", "comp"), [(i + 1, i) for i in range(count - 1)])

    mix_rows = up_to(levels, 16)
    rows_of_mix, source_rows, weights, sea_weights, sea_first, own = call(
        functools.partial(local_kernel, sizes),
        [
            flat((steps - 1) * levels), flat(8), jax.ShapeDtypeStruct((mix_rows, 2 * width), bf16),
            jax.ShapeDtypeStruct((sea_stride, 2 * width), bf16), flat(sea_stride), flat((steps - 1) * rows),
        ],
        vmix, curve[None], sea_mix, sky2, flops=1 << 30, moved=4 << 20,
    )

    per = rows + 2 * topk
    sent, fluxes = call(
        functools.partial(flux_kernel, sizes), [flat(per), flat(steps * (rows + 2 * HALO))],
        sky[-1], forcing2, surface, rate, rows_of_mix, source_rows, own, owners.T, locals_.T, below, above,
        scratch=[pltpu.VMEM((2 * HALO * stride, width), f32)], moved=2 << 20,
    )
    got = lax.all_gather(sent, "tile", axis=0, tiled=True)

    sky_out = call(
        functools.partial(sky_kernel, sizes), flat(levels * rows),
        sky2, forcing2, fluxes, weights, below, above,
        scratch=[
            pltpu.VMEM((2 * HALO * stride, width), f32),
            pltpu.VMEM((up_to(levels + 2 * steps, 16) * rows, width), f32),
        ],
        flops=4 << 30, moved=8 << 20,
    )
    warm, salt = call(
        functools.partial(sea_kernel, sizes), [flat(sea_levels * sea_rows)] * 2,
        warmth2, brine2, wet, sea_weights, below, above,
        scratch=[pltpu.VMEM((8, width), f32), pltpu.VMEM((2, sea_stride * sea_rows, width), f32)],
        flops=2 << 30, moved=4 << 20,
    )
    mine = lax.axis_index("tile").astype(jnp.int32)[None]
    warm = call(
        functools.partial(heat_kernel, sizes, topk), flat(sea_levels * sea_rows),
        got, mine, shares.reshape(-1, width), wet, sea_first, warm,
        in_specs=[VMEM, pl.BlockSpec(memory_space=pltpu.SMEM)] + [VMEM] * 4, moved=2 << 20,
    )
    return sky_out.reshape(sky.shape), warm.reshape(warmth.shape), salt.reshape(brine.shape)


def solution(mesh):
    both = P(None, ("member", "tile", "comp"), None)
    one = P(("tile", "comp"), None)
    return jax.shard_map(
        body,
        mesh=mesh,
        in_specs=(
            both, both, P(), P(("member", "tile", "comp"), None), one, P(), P(), one, one, both, both, one, P(),
        ),
        out_specs=(both, both, both),
        check_vma=False,
    )
```

```python
import functools

import jax
import jax.numpy as jnp
from jax import lax
from jax.experimental import pallas as pl
from jax.experimental.pallas import tpu as pltpu
from jax.sharding import PartitionSpec as P

atm_diffusion = 0.2
ocean_diffusion = 0.2
HALO = 4
EXACT = lax.Precision.HIGHEST
VMEM = pl.BlockSpec(memory_space=pltpu.VMEM)
f32, bf16 = jnp.float32, jnp.bfloat16


def up_to(n, m):
    return -(-n // m) * m


def call(kernel, out_shape, *args, scratch=(), in_specs=None, flops=0, moved=0, grant=24):
    return pl.pallas_call(
        kernel,
        out_shape=out_shape,
        in_specs=in_specs or [VMEM] * len(args),
        out_specs=jax.tree.map(lambda _: VMEM, out_shape),
        scratch_shapes=list(scratch),
        compiler_params=pltpu.CompilerParams(vmem_limit_bytes=grant * 2**20),
        cost_estimate=pl.CostEstimate(flops=flops, bytes_accessed=moved, transcendentals=0),
    )(*args)


def pack_kernel(sizes, sky, forcing, surface, rate, warmth, brine, wet, up, down):
    levels, rows, steps, sea_levels, sea_rows, stride, sea_stride = sizes
    width = sky.shape[1]
    m = wet[...].astype(f32)
    for out, first, sea_row in ((up, 0, 0), (down, rows - HALO, sea_rows - 1)):
        for j in range(HALO):
            row = first + j
            out[j * stride : j * stride + levels, :] = sky[pl.ds(row, levels, stride=rows), :]
            base = j * stride + levels
            tail = [forcing[s * rows + row : s * rows + row + 1, :] for s in range(steps)]
            tail += [surface[row : row + 1, :], rate[row : row + 1, :], jnp.ones((1, width), f32)]
            tail += [jnp.zeros((stride - levels - len(tail), width), f32)]
            out[base : (j + 1) * stride, :] = jnp.concatenate(tail, 0)
        base = HALO * stride
        edge = m[sea_row : sea_row + 1]
        out[base : base + sea_levels, :] = warmth[pl.ds(sea_row, sea_levels, stride=sea_rows), :] * edge
        base += sea_stride
        out[base : base + sea_levels, :] = brine[pl.ds(sea_row, sea_levels, stride=sea_rows), :] * edge
        base += sea_stride
        out[base : base + 8, :] = jnp.concatenate([edge, jnp.zeros((7, width), f32)], 0)


def split(x):
    high = x.astype(bf16)
    return high, (x - high.astype(f32)).astype(bf16)


def three_terms(w, depth):
    high = w.astype(bf16).astype(f32)
    low = w - high
    return (high + pltpu.roll(high, depth, 1) + pltpu.roll(low, 2 * depth, 1)).astype(bf16)


def row_of(ref, first, count, step, size):
    x = ref[pl.ds(first, count, stride=step), :]
    if count < size:
        x = jnp.concatenate([x, jnp.zeros((size - count, x.shape[1]), f32)], 0)
    return x


def beside(x):
    return pltpu.roll(x, 1, 1) + pltpu.roll(x, x.shape[1] - 1, 1)


def stencil(x):
    return [x[i - 1] + x[i] + x[i + 1] + beside(x[i]) for i in range(1, len(x) - 1)]


def product(weights, x):
    high, low = split(x)
    return jnp.dot(weights, jnp.concatenate([high, low, high], 0), preferred_element_type=f32)


def local_kernel(
    sizes, vmix, curve, sea_mix, sky, warmth, brine, wet,
    rows_of_mix, source_rows, weights, source_weights, sea_weights, sea_first, own, middle, warm_out, brine_out,
    spread, sea_spread,
):
    levels, rows, steps, sea_levels, sea_rows, stride, sea_stride = sizes
    width = sky.shape[1]
    depth = up_to(levels + 2 * steps, 16)
    v = vmix[...]
    dot = functools.partial(jnp.dot, precision=EXACT, preferred_element_type=f32)
    powers = [v]
    for _ in range(steps - 1):
        powers.append(dot(v, powers[-1]))
    last = (lax.broadcasted_iota(jnp.int32, (levels, width), 0) == levels - 1).astype(f32)
    for s in range(1, steps):
        rows_of_mix[(s - 1) * levels : s * levels, :] = lax.dot_general(
            powers[s - 1], last, (((0,), (0,)), ((), ())), precision=EXACT, preferred_element_type=f32
        )
    by_curve = jnp.broadcast_to(curve[...], (width, levels))
    of_curve = [
        lax.dot_general(p, by_curve, (((1,), (1,)), ((), ())), precision=EXACT, preferred_element_type=f32)
        for p in powers
    ]
    of_last = [jnp.broadcast_to(p[:, levels - 1 : levels], (levels, width)) for p in powers]
    found = [of_curve[i][levels - 1 :] for i in range(steps - 1)]
    found += [of_last[i][levels - 1 :] for i in range(steps - 1)]
    found += [jnp.zeros((8 - len(found), width), f32)]
    source_rows[...] = jnp.concatenate(found, 0)
    lane = lax.broadcasted_iota(jnp.int32, (levels, width), 1)
    wide = jnp.concatenate(
        [powers[-1] * atm_diffusion**steps, jnp.zeros((levels, width - levels), f32)], 1
    )
    sources = jnp.zeros((levels, width), f32)
    for j in range(steps):
        factor = atm_diffusion ** (steps - 1 - j)
        for at, value in ((j, of_curve[steps - 1 - j] * factor), (steps + j, of_last[steps - 1 - j] * -factor)):
            wide = jnp.where(lane == levels + at, value, wide)
            sources = jnp.where(lane == at, value, sources)
    more = jnp.zeros((weights.shape[0] - levels, width), f32)
    wide = jnp.concatenate([wide, more], 0)
    wide = jnp.concatenate([wide, jnp.zeros_like(wide)], 1)
    weights[...] = three_terms(wide, depth)
    source_weights[...] = three_terms(jnp.concatenate([sources, more], 0), 16)
    sea = sea_mix[...]
    sea = jnp.concatenate([sea, jnp.zeros((sea_levels, 2 * width - sea_levels), f32)], 1)
    sea = jnp.concatenate([sea, jnp.zeros((sea_stride - sea_levels, 2 * width), f32)], 0)
    sea_weights[...] = three_terms(sea, sea_stride)
    sea_first[...] = jnp.broadcast_to(sea[:, 0:1], sea_first.shape)
    sums = [jnp.zeros((rows, width), f32) for _ in range(steps - 1)]
    for l in range(levels):
        x = sky[l * rows : (l + 1) * rows, :]
        for s in range(steps - 1):
            sums[s] = sums[s] + rows_of_mix[s * levels + l : s * levels + l + 1, :] * x
    for s in range(steps - 1):
        own[s * rows : (s + 1) * rows, :] = sums[s]

    inner = rows - 2 * HALO

    @pl.loop(0, levels // 8)
    def _(c):
        x = [sky[pl.ds(c * 8 * rows + r, 8, stride=rows), :] for r in range(rows)]
        for _ in range(steps):
            x = stencil(x)
        for r in range(inner):
            spread[pl.ds(pl.multiple_of(r * depth + c * 8, 8), 8), :] = x[r]

    if depth > levels:
        for r in range(inner):
            spread[r * depth + levels : (r + 1) * depth, :] = jnp.zeros((depth - levels, width), f32)
    w = weights[:, : 3 * depth]
    for r in range(0, inner, 2):
        x = jnp.concatenate([spread[(r + i) * depth : (r + i + 1) * depth, :] for i in range(2)], 1)
        y = product(w, x)
        for i in range(2):
            middle[(r + i) * levels : (r + i + 1) * levels, :] = y[:levels, i * width : (i + 1) * width]

    m = wet[...].astype(f32)
    mark = [m[r : r + 1] for r in range(sea_rows)]
    edge = jnp.zeros((1, width), f32)

    def near(x):
        x = [jnp.zeros_like(x[0])] + x + [jnp.zeros_like(x[0])]
        return [x[i - 1] + x[i + 1] + beside(x[i]) for i in range(1, len(x) - 1)]

    around = (
        jnp.concatenate([edge, m[:-1]], 0) + jnp.concatenate([m[1:], edge], 0) + beside(m)
    ) * ocean_diffusion
    share = [around[r : r + 1] for r in range(sea_rows)]
    for f, field in enumerate((warmth, brine)):
        for c in range(sea_stride // 8):
            count = min(8, sea_levels - c * 8)
            x = [row_of(field, c * 8 * sea_rows + r, count, sea_rows, 8) for r in range(sea_rows)]
            y = near([mark[r] * x[r] for r in range(sea_rows)])
            for r in range(sea_rows):
                at = r * sea_stride + c * 8
                sea_spread[f, at : at + 8, :] = x[r] + mark[r] * (ocean_diffusion * y[r] - x[r] * share[r])
    w = sea_weights[:, : 3 * sea_stride]
    for r in range(sea_rows):
        x = jnp.concatenate([sea_spread[f, r * sea_stride : (r + 1) * sea_stride, :] for f in range(2)], 1)
        y = product(w, x)
        for f, (field, out) in enumerate(((warmth, warm_out), (brine, brine_out))):
            old = field[pl.ds(r, sea_levels, stride=sea_rows), :]
            new = y[:sea_levels, f * width : (f + 1) * width]
            out[pl.ds(r, sea_levels, stride=sea_rows), :] = mark[r] * new + (1.0 - mark[r]) * old


def cross(x):
    n, w = x.shape
    return (
        x + pltpu.roll(x, 1, 0) + pltpu.roll(x, n - 1, 0) + pltpu.roll(x, 1, 1) + pltpu.roll(x, w - 1, 1)
    )


def masked(x, rows, inside):
    return jnp.concatenate([x[:rows], x[rows:] * inside], 0)


def flux_kernel(
    sizes, sky, forcing, surface, rate, rows_of_mix, source_rows, own, owners, locals_, below, above,
    sent, fluxes, halo
):
    levels, rows, steps, sea_levels, sea_rows, stride, sea_stride = sizes
    width = sky.shape[1]
    halo[: HALO * stride, :] = below[: HALO * stride, :]
    halo[HALO * stride :, :] = above[: HALO * stride, :]

    def edge(l):
        return halo[pl.ds(l, 2 * HALO, stride=stride), :]

    inside = edge(levels + steps + 2)
    sums = [jnp.zeros((2 * HALO, width), f32) for _ in range(steps - 1)]
    for l in range(levels):
        x = edge(l)
        for s in range(steps - 1):
            sums[s] = sums[s] + rows_of_mix[s * levels + l : s * levels + l + 1, :] * x
    tops = [jnp.concatenate([sky[...], edge(levels - 1)], 0)]
    tops += [jnp.concatenate([own[s * rows : (s + 1) * rows, :], sums[s]], 0) for s in range(steps - 1)]
    surf = jnp.concatenate([surface[...], edge(levels + steps)], 0)
    coef = jnp.concatenate([rate[...], edge(levels + steps + 1)], 0)
    force = [
        jnp.concatenate([forcing[s * rows : (s + 1) * rows, :], edge(levels + s)], 0) for s in range(steps)
    ]

    flux = []
    for s in range(steps):
        state = tops[s]
        for i in range(s):
            m = s - 1 - i
            state = masked(cross(state) * atm_diffusion, rows, inside)
            state = state + source_rows[m : m + 1, :] * force[i]
            state = state - source_rows[steps - 1 + m : steps + m, :] * flux[i]
        flux.append(coef * (state - surf))
        reach = rows + 2 * HALO
        fluxes[pl.ds(s, reach, stride=2 * steps), :] = force[s]
        fluxes[pl.ds(steps + s, reach, stride=2 * steps), :] = flux[s]
    total = flux[0][:rows]
    for s in range(1, steps):
        total = total + flux[s][:rows]
    mean = (total / steps).astype(bf16).astype(f32)
    times = width // rows
    owner = owners[...].astype(f32)
    row = locals_[...].astype(f32)
    table = jnp.concatenate(
        [jnp.concatenate([owner] * times, 1), jnp.concatenate([row] * times, 1)], 0
    )
    per = mean.shape[0] + table.shape[0]
    for t in range(sent.shape[0] // per):
        sent[t * per : t * per + rows, :] = mean
        sent[t * per + rows : (t + 1) * per, :] = table


def rest_kernel(
    sizes, sky, fluxes, weights, source_weights, middle, warmth, brine, wet, sea_weights, warm, salt, below, above,
    out, warm_out, brine_out, spread, sources
):
    levels, rows, steps, sea_levels, sea_rows, stride, sea_stride = sizes
    width = sky.shape[1]
    depth = up_to(levels + 2 * steps, 16)
    flag = levels + steps + 2
    inside_above, inside_below = above[flag : flag + 1, :], below[flag : flag + 1, :]

    reach = rows + 2 * HALO
    x = [fluxes[(r % reach) * 2 * steps : (r % reach + 1) * 2 * steps, :] for r in range(1 - steps, rows + steps - 1)]
    field = lax.broadcasted_iota(jnp.int32, (2 * steps, width), 0) % steps
    for n in range(1, steps):
        y = stencil(x)
        x = [jnp.where(field < steps - n, y[i], x[i + 1]) for i in range(len(y))]
        for i in range(steps - 1 - n):
            x[i] = x[i] * inside_above
            x[-1 - i] = x[-1 - i] * inside_below
    for r in range(rows):
        sources[r * 16 : (r + 1) * 16, :] = jnp.concatenate([x[r], jnp.zeros((16 - 2 * steps, width), f32)], 0)

    @pl.loop(0, levels // 8)
    def _(c):
        def own(r):
            return sky[pl.ds(c * 8 * rows + r, 8, stride=rows), :]

        def other(ref, j):
            return ref[pl.ds(pl.multiple_of(j * stride + c * 8, 8), 8), :]

        top = [other(above, j) for j in range(HALO)] + [own(r) for r in range(2 * HALO)]
        low = [own(rows - 2 * HALO + r) for r in range(2 * HALO)] + [other(below, j) for j in range(HALO)]
        for n in range(steps):
            top, low = stencil(top), stencil(low)
            for i in range(steps - 1 - n):
                top[i] = top[i] * inside_above
                low[-1 - i] = low[-1 - i] * inside_below
        for i, value in enumerate(top + low):
            spread[pl.ds(pl.multiple_of(i * depth + c * 8, 8), 8), :] = value

    w = weights[:, : 3 * depth]
    for i in range(0, 2 * HALO, 2):
        at = [q if q < HALO else rows - 2 * HALO + q for q in (i, i + 1)]
        x = jnp.concatenate(
            [
                jnp.concatenate([spread[(i + q) * depth : i * depth + q * depth + levels, :],
                                 sources[at[q] * 16 : at[q] * 16 + depth - levels, :]], 0)
                for q in range(2)
            ],
            1,
        )
        y = product(w, x)
        for q in range(2):
            out[pl.ds(at[q], levels, stride=rows), :] = y[:levels, q * width : (q + 1) * width]
    w = source_weights[:, :48]
    for r in range(HALO, rows - HALO, 2):
        y = product(w, jnp.concatenate([sources[(r + q) * 16 : (r + q + 1) * 16, :] for q in range(2)], 1))
        for q in range(2):
            at = (r + q - HALO) * levels
            out[pl.ds(r + q, levels, stride=rows), :] = (
                middle[at : at + levels, :] + y[:levels, q * width : (q + 1) * width]
            )

    warm_out[...] = warm[...]
    brine_out[...] = salt[...]
    m = wet[...].astype(f32)
    base = HALO * stride
    w = sea_weights[:, : 3 * sea_stride]
    for r, other in ((0, above), (sea_rows - 1, below)):
        mark = m[r : r + 1]
        far = other[base + 2 * sea_stride : base + 2 * sea_stride + 1, :]
        x = []
        for f, field in enumerate((warmth, brine)):
            at = base + f * sea_stride
            step = other[at : at + sea_levels, :] - field[pl.ds(r, sea_levels, stride=sea_rows), :] * far
            step = ocean_diffusion * (mark * step)
            x.append(jnp.concatenate([step, jnp.zeros((sea_stride - sea_levels, width), f32)], 0))
        y = product(w, jnp.concatenate(x, 1))
        for f, to in enumerate((warm_out, brine_out)):
            rows_at = pl.ds(r, sea_levels, stride=sea_rows)
            to[rows_at, :] = to[rows_at, :] + mark * y[:sea_levels, f * width : (f + 1) * width]


def heat_kernel(sizes, topk, got, mine, shares, wet, sea_first, before, after):
    levels, rows, steps, sea_levels, sea_rows, stride, sea_stride = sizes
    width = before.shape[1]
    per = rows + 2 * topk
    group = width // rows
    me = mine[0].astype(f32)
    part = lax.broadcasted_iota(jnp.int32, (1, width), 1) // rows
    to = lax.broadcasted_iota(jnp.int32, (sea_rows, width), 0).astype(f32)
    picked = jnp.zeros((topk * sea_rows, width), f32)
    for g in range(got.shape[0] // (per * group)):
        at = [(g * group + i) * per for i in range(group)]
        mean = jnp.concatenate([got[a : a + rows, :] for a in at], 0).astype(bf16)
        table = got[at[0] + rows : at[0] + per, :]
        for i in range(1, group):
            table = jnp.where(part == i, got[at[i] + rows : at[i] + per, :], table)
        hot = []
        for k in range(topk):
            row = jnp.where(table[k : k + 1] == me, table[topk + k : topk + k + 1], -1.0)
            hot.append(jnp.where(to == row, 1.0, 0.0))
        hot = jnp.concatenate(hot, 0).astype(bf16)
        picked = picked + jnp.dot(hot, mean, preferred_element_type=f32)
    side = jnp.concatenate([picked[k * sea_rows : (k + 1) * sea_rows] for k in range(topk)], 1)
    first = side.astype(bf16).astype(f32)
    second = (side - first).astype(bf16).astype(f32)
    third = side - first - second
    parts = jnp.concatenate([first, second, third], 0).astype(bf16)
    y = jnp.dot(parts, shares[...], preferred_element_type=f32)
    heat = y[:sea_rows] + y[sea_rows : 2 * sea_rows] + y[2 * sea_rows :]
    heat = wet[...].astype(f32) * heat
    for l in range(sea_levels):
        after[l * sea_rows : (l + 1) * sea_rows, :] = (
            before[l * sea_rows : (l + 1) * sea_rows, :] + sea_first[l : l + 1, :] * heat
        )


def body(sky, forcing, curve, surface, rate, vmix, shares, owners, locals_, warmth, brine, wet, sea_mix):
    levels, rows, width = sky.shape
    steps = forcing.shape[0]
    sea_levels, sea_rows, _ = warmth.shape
    topk = owners.shape[1]
    stride = up_to(levels + steps + 3, 8)
    sea_stride = up_to(sea_levels, 16)
    sizes = (levels, rows, steps, sea_levels, sea_rows, stride, sea_stride)
    sky2, forcing2 = sky.reshape(-1, width), forcing.reshape(-1, width)
    warmth2, brine2 = warmth.reshape(-1, width), brine.reshape(-1, width)
    flat = lambda n, kind=f32: jax.ShapeDtypeStruct((n, width), kind)

    length = HALO * stride + 2 * sea_stride + 8
    up, down = call(
        functools.partial(pack_kernel, sizes), [flat(length)] * 2,
        sky2, forcing2, surface, rate, warmth2, brine2, wet, moved=4 << 20, grant=60,
    )
    count = lax.axis_size(("tile", "comp"))
    above = lax.ppermute(down, ("tile", "comp"), [(i, i + 1) for i in range(count - 1)])
    below = lax.ppermute(up, ("tile", "comp"), [(i + 1, i) for i in range(count - 1)])

    depth = up_to(levels + 2 * steps, 16)
    inner = rows - 2 * HALO
    mix_rows = up_to(levels, 16)
    sea_flat = flat(sea_levels * sea_rows)
    (rows_of_mix, source_rows, weights, source_weights, sea_weights, sea_first, own, middle, warm, salt) = call(
        functools.partial(local_kernel, sizes),
        [
            flat((steps - 1) * levels), flat(8), jax.ShapeDtypeStruct((mix_rows, 2 * width), bf16),
            flat(mix_rows, bf16), jax.ShapeDtypeStruct((sea_stride, 2 * width), bf16), flat(sea_stride),
            flat((steps - 1) * rows), flat(inner * levels), sea_flat, sea_flat,
        ],
        vmix, curve[None], sea_mix, sky2, warmth2, brine2, wet,
        scratch=[pltpu.VMEM((inner * depth, width), f32), pltpu.VMEM((2, sea_rows * sea_stride, width), f32)],
        flops=4 << 30, moved=8 << 20,
    )

    per = rows + 2 * topk
    tiles = lax.axis_size("tile")
    sent, fluxes = call(
        functools.partial(flux_kernel, sizes), [flat(tiles * per), flat(2 * steps * (rows + 2 * HALO))],
        sky[-1], forcing2, surface, rate, rows_of_mix, source_rows, own, owners.T, locals_.T, below, above,
        scratch=[pltpu.VMEM((2 * HALO * stride, width), f32)], moved=2 << 20,
    )
    got = lax.all_to_all(sent.reshape(tiles, per, width), "tile", split_axis=0, concat_axis=0, tiled=True)
    got = got.reshape(-1, width)

    sky_out, warm, salt = call(
        functools.partial(rest_kernel, sizes), [flat(levels * rows), sea_flat, sea_flat],
        sky2, fluxes, weights, source_weights, middle, warmth2, brine2, wet, sea_weights, warm, salt, below, above,
        scratch=[pltpu.VMEM((2 * HALO * depth, width), f32), pltpu.VMEM((rows * 16, width), f32)],
        flops=2 << 30, moved=8 << 20,
    )
    mine = lax.axis_index("tile").astype(jnp.int32)[None]
    warm = call(
        functools.partial(heat_kernel, sizes, topk), flat(sea_levels * sea_rows),
        got, mine, shares.reshape(-1, width), wet, sea_first, warm,
        in_specs=[VMEM, pl.BlockSpec(memory_space=pltpu.SMEM)] + [VMEM] * 4, moved=2 << 20,
    )
    return sky_out.reshape(sky.shape), warm.reshape(warmth.shape), salt.reshape(brine.shape)


def solution(mesh):
    both = P(None, ("member", "tile", "comp"), None)
    one = P(("tile", "comp"), None)
    return jax.shard_map(
        body,
        mesh=mesh,
        in_specs=(
            both, both, P(), P(("member", "tile", "comp"), None), one, P(), P(), one, one, both, both, one, P(),
        ),
        out_specs=(both, both, both),
        check_vma=False,
    )
```

```python
import functools

import jax
import jax.numpy as jnp
from jax import lax
from jax.experimental import pallas as pl
from jax.experimental.pallas import tpu as pltpu
from jax.sharding import PartitionSpec as P

atm_diffusion = 0.2
ocean_diffusion = 0.2
HALO = 4
EXACT = lax.Precision.HIGHEST
VMEM = pl.BlockSpec(memory_space=pltpu.VMEM)
HBM = pl.BlockSpec(memory_space=pltpu.HBM)
f32, bf16 = jnp.float32, jnp.bfloat16


def up_to(n, m):
    return -(-n // m) * m


def call(kernel, out_shape, *args, scratch=(), in_specs=None, out_specs=None, flops=0, moved=0):
    return pl.pallas_call(
        kernel,
        out_shape=out_shape,
        in_specs=in_specs or [VMEM] * len(args),
        out_specs=out_specs or jax.tree.map(lambda _: VMEM, out_shape),
        scratch_shapes=list(scratch),
        compiler_params=pltpu.CompilerParams(vmem_limit_bytes=24 * 2**20),
        cost_estimate=pl.CostEstimate(flops=flops, bytes_accessed=moved, transcendentals=0),
    )(*args)


def copies(pairs, done):
    return [pltpu.make_async_copy(src, dst, done.at[i]) for i, (src, dst) in enumerate(pairs)]


def pack_kernel(
    sizes, sky, forcing, surface, rate, warmth, brine, wet, up, down,
    ends, force, sea, flat, marks, done
):
    levels, rows, steps, sea_levels, sea_rows, stride, sea_stride = sizes
    width = sky.shape[2]
    low = rows - 8
    moves = copies(
        [
            (sky.at[:, 0:8, :], ends.at[0]), (sky.at[:, low:rows, :], ends.at[1]), (forcing, force),
            (surface, flat.at[0]), (rate, flat.at[1]), (warmth, sea.at[0]), (brine, sea.at[1]), (wet, marks),
        ],
        done,
    )
    for move in moves:
        move.start()
    for move in moves:
        move.wait()
    m = marks[...].astype(f32)
    for which, out, first, sea_row in ((0, up, 0, 0), (1, down, rows - HALO, sea_rows - 1)):
        end = ends.at[which].reshape(levels * 8, width)
        for j in range(HALO):
            row = first + j
            out[j * stride : j * stride + levels, :] = end[pl.ds(row - which * low, levels, stride=8), :]
            base = j * stride + levels
            tail = [force[s, row : row + 1, :] for s in range(steps)]
            tail += [flat[0, row : row + 1, :], flat[1, row : row + 1, :], jnp.ones((1, width), f32)]
            tail += [jnp.zeros((stride - levels - len(tail), width), f32)]
            out[base : (j + 1) * stride, :] = jnp.concatenate(tail, 0)
        base = HALO * stride
        edge = m[sea_row : sea_row + 1]
        for f in range(2):
            out[base : base + sea_levels, :] = sea[f, pl.ds(sea_row, sea_levels, stride=sea_rows), :] * edge
            base += sea_stride
        out[base : base + 8, :] = jnp.concatenate([edge, jnp.zeros((7, width), f32)], 0)


def split(x):
    high = x.astype(bf16)
    return high, (x - high.astype(f32)).astype(bf16)


def three_terms(w, depth):
    high = w.astype(bf16).astype(f32)
    low = w - high
    return (high + pltpu.roll(high, depth, 1) + pltpu.roll(low, 2 * depth, 1)).astype(bf16)


def row_of(ref, first, count, step, size):
    x = ref[pl.ds(first, count, stride=step), :]
    if count < size:
        x = jnp.concatenate([x, jnp.zeros((size - count, x.shape[1]), f32)], 0)
    return x


def beside(x):
    return pltpu.roll(x, 1, 1) + pltpu.roll(x, x.shape[1] - 1, 1)


def stencil(x):
    return [x[i - 1] + x[i] + x[i + 1] + beside(x[i]) for i in range(1, len(x) - 1)]


def product(weights, x):
    high, low = split(x)
    return jnp.dot(weights, jnp.concatenate([high, low, high], 0), preferred_element_type=f32)


def local_kernel(
    sizes, vmix, curve, sea_mix, sky, warmth, brine, wet,
    rows_of_mix, source_rows, own, *others
):
    kept, found, (spread, sea_spread, done) = others[:8], others[8:16], others[16:]
    weights, source_weights, sea_weights, sea_first, middle, warm_out, brine_out, sea_ends = found
    moves = copies(list(zip(found, kept)), done)
    levels, rows, steps, sea_levels, sea_rows, stride, sea_stride = sizes
    width = sky.shape[1]
    depth = up_to(levels + 2 * steps, 16)
    v = vmix[...]
    dot = functools.partial(jnp.dot, precision=EXACT, preferred_element_type=f32)
    powers = [v]
    for _ in range(steps - 1):
        powers.append(dot(v, powers[-1]))
    last = (lax.broadcasted_iota(jnp.int32, (levels, width), 0) == levels - 1).astype(f32)
    for s in range(1, steps):
        rows_of_mix[(s - 1) * levels : s * levels, :] = lax.dot_general(
            powers[s - 1], last, (((0,), (0,)), ((), ())), precision=EXACT, preferred_element_type=f32
        )
    by_curve = jnp.broadcast_to(curve[...], (width, levels))
    of_curve = [
        lax.dot_general(p, by_curve, (((1,), (1,)), ((), ())), precision=EXACT, preferred_element_type=f32)
        for p in powers
    ]
    of_last = [jnp.broadcast_to(p[:, levels - 1 : levels], (levels, width)) for p in powers]
    found = [of_curve[i][levels - 1 :] for i in range(steps - 1)]
    found += [of_last[i][levels - 1 :] for i in range(steps - 1)]
    found += [jnp.zeros((8 - len(found), width), f32)]
    source_rows[...] = jnp.concatenate(found, 0)
    lane = lax.broadcasted_iota(jnp.int32, (levels, width), 1)
    wide = jnp.concatenate(
        [powers[-1] * atm_diffusion**steps, jnp.zeros((levels, width - levels), f32)], 1
    )
    sources = jnp.zeros((levels, width), f32)
    for j in range(steps):
        factor = atm_diffusion ** (steps - 1 - j)
        for at, value in ((j, of_curve[steps - 1 - j] * factor), (steps + j, of_last[steps - 1 - j] * -factor)):
            wide = jnp.where(lane == levels + at, value, wide)
            sources = jnp.where(lane == at, value, sources)
    more = jnp.zeros((weights.shape[0] - levels, width), f32)
    wide = jnp.concatenate([wide, more], 0)
    wide = jnp.concatenate([wide, jnp.zeros_like(wide)], 1)
    weights[...] = three_terms(wide, depth)
    source_weights[...] = three_terms(jnp.concatenate([sources, more], 0), 16)
    sea = sea_mix[...]
    sea = jnp.concatenate([sea, jnp.zeros((sea_levels, 2 * width - sea_levels), f32)], 1)
    sea = jnp.concatenate([sea, jnp.zeros((sea_stride - sea_levels, 2 * width), f32)], 0)
    sea_weights[...] = three_terms(sea, sea_stride)
    sea_first[...] = jnp.broadcast_to(sea[:, 0:1], sea_first.shape)
    for move in moves[:4]:
        move.start()
    sums = [jnp.zeros((rows, width), f32) for _ in range(steps - 1)]
    for l in range(levels):
        x = sky[l * rows : (l + 1) * rows, :]
        for s in range(steps - 1):
            sums[s] = sums[s] + rows_of_mix[s * levels + l : s * levels + l + 1, :] * x
    for s in range(steps - 1):
        own[s * rows : (s + 1) * rows, :] = sums[s]

    inner = rows - 2 * HALO

    @pl.loop(0, levels // 8)
    def _(c):
        x = [sky[pl.ds(c * 8 * rows + r, 8, stride=rows), :] for r in range(rows)]
        for _ in range(steps):
            x = stencil(x)
        for r in range(inner):
            spread[pl.ds(pl.multiple_of(r * depth + c * 8, 8), 8), :] = x[r]

    if depth > levels:
        for r in range(inner):
            spread[r * depth + levels : (r + 1) * depth, :] = jnp.zeros((depth - levels, width), f32)
    w = weights[:, : 3 * depth]
    for r in range(0, inner, 2):
        x = jnp.concatenate([spread[(r + i) * depth : (r + i + 1) * depth, :] for i in range(2)], 1)
        y = product(w, x)
        for i in range(2):
            middle[(r + i) * levels : (r + i + 1) * levels, :] = y[:levels, i * width : (i + 1) * width]
    moves[4].start()

    m = wet[...].astype(f32)
    mark = [m[r : r + 1] for r in range(sea_rows)]
    edge = jnp.zeros((1, width), f32)

    def near(x):
        x = [jnp.zeros_like(x[0])] + x + [jnp.zeros_like(x[0])]
        return [x[i - 1] + x[i + 1] + beside(x[i]) for i in range(1, len(x) - 1)]

    around = (
        jnp.concatenate([edge, m[:-1]], 0) + jnp.concatenate([m[1:], edge], 0) + beside(m)
    ) * ocean_diffusion
    share = [around[r : r + 1] for r in range(sea_rows)]
    for f, field in enumerate((warmth, brine)):
        for c in range(sea_stride // 8):
            count = min(8, sea_levels - c * 8)
            x = [row_of(field, c * 8 * sea_rows + r, count, sea_rows, 8) for r in range(sea_rows)]
            y = near([mark[r] * x[r] for r in range(sea_rows)])
            for r in range(sea_rows):
                at = r * sea_stride + c * 8
                sea_spread[f, at : at + 8, :] = x[r] + mark[r] * (ocean_diffusion * y[r] - x[r] * share[r])
    w = sea_weights[:, : 3 * sea_stride]
    for r in range(sea_rows):
        x = jnp.concatenate([sea_spread[f, r * sea_stride : (r + 1) * sea_stride, :] for f in range(2)], 1)
        y = product(w, x)
        for f, (field, out) in enumerate(((warmth, warm_out), (brine, brine_out))):
            old = field[pl.ds(r, sea_levels, stride=sea_rows), :]
            new = y[:sea_levels, f * width : (f + 1) * width]
            out[pl.ds(r, sea_levels, stride=sea_rows), :] = mark[r] * new + (1.0 - mark[r]) * old
            if r in (0, sea_rows - 1):
                at = (2 * f + (r > 0)) * sea_stride
                sea_ends[at : at + sea_levels, :] = old
    for move in moves[5:]:
        move.start()
    for move in moves:
        move.wait()


def cross(x):
    n, w = x.shape
    return (
        x + pltpu.roll(x, 1, 0) + pltpu.roll(x, n - 1, 0) + pltpu.roll(x, 1, 1) + pltpu.roll(x, w - 1, 1)
    )


def masked(x, rows, inside):
    return jnp.concatenate([x[:rows], x[rows:] * inside], 0)


def flux_kernel(
    sizes, sky, forcing, surface, rate, rows_of_mix, source_rows, own, owners, locals_, below, above,
    sent, kept, fluxes, halo, done
):
    levels, rows, steps, sea_levels, sea_rows, stride, sea_stride = sizes
    width = sky.shape[1]
    halo[: HALO * stride, :] = below[: HALO * stride, :]
    halo[HALO * stride :, :] = above[: HALO * stride, :]

    def edge(l):
        return halo[pl.ds(l, 2 * HALO, stride=stride), :]

    inside = edge(levels + steps + 2)
    sums = [jnp.zeros((2 * HALO, width), f32) for _ in range(steps - 1)]
    for l in range(levels):
        x = edge(l)
        for s in range(steps - 1):
            sums[s] = sums[s] + rows_of_mix[s * levels + l : s * levels + l + 1, :] * x
    tops = [jnp.concatenate([sky[...], edge(levels - 1)], 0)]
    tops += [jnp.concatenate([own[s * rows : (s + 1) * rows, :], sums[s]], 0) for s in range(steps - 1)]
    surf = jnp.concatenate([surface[...], edge(levels + steps)], 0)
    coef = jnp.concatenate([rate[...], edge(levels + steps + 1)], 0)
    force = [
        jnp.concatenate([forcing[s * rows : (s + 1) * rows, :], edge(levels + s)], 0) for s in range(steps)
    ]

    flux = []
    for s in range(steps):
        state = tops[s]
        for i in range(s):
            m = s - 1 - i
            state = masked(cross(state) * atm_diffusion, rows, inside)
            state = state + source_rows[m : m + 1, :] * force[i]
            state = state - source_rows[steps - 1 + m : steps + m, :] * flux[i]
        flux.append(coef * (state - surf))
        reach = rows + 2 * HALO
        fluxes[pl.ds(s, reach, stride=2 * steps), :] = force[s]
        fluxes[pl.ds(steps + s, reach, stride=2 * steps), :] = flux[s]
    move = pltpu.make_async_copy(fluxes, kept, done)
    move.start()
    total = flux[0][:rows]
    for s in range(1, steps):
        total = total + flux[s][:rows]
    mean = (total / steps).astype(bf16).astype(f32)
    times = width // rows
    owner = owners[...].astype(f32)
    row = locals_[...].astype(f32)
    table = jnp.concatenate(
        [jnp.concatenate([owner] * times, 1), jnp.concatenate([row] * times, 1)], 0
    )
    per = mean.shape[0] + table.shape[0]
    for t in range(sent.shape[0] // per):
        sent[t * per : t * per + rows, :] = mean
        sent[t * per + rows : (t + 1) * per, :] = table
    move.wait()


def rest_kernel(
    sizes, sky, fluxes_in, weights_in, source_weights_in, sea_weights_in, middle_in, warm_in, salt_in, sea_ends_in,
    wet, below, above, out, brine_out, warm_out,
    ends, fluxes, weights, source_weights, sea_weights, middle, salt, sea_ends, spread, sources, result, done
):
    levels, rows, steps, sea_levels, sea_rows, stride, sea_stride = sizes
    width = sky.shape[2]
    depth = up_to(levels + 2 * steps, 16)
    moves = copies(
        [
            (fluxes_in, fluxes), (sky.at[:, 0:8, :], ends.at[0]), (sky.at[:, rows - 8 : rows, :], ends.at[1]),
            (sea_weights_in, sea_weights), (sea_ends_in, sea_ends), (salt_in, salt), (warm_in, warm_out),
            (weights_in, weights), (source_weights_in, source_weights), (middle_in, middle),
        ],
        done,
    )
    count = len(moves)
    for move in moves:
        move.start()
    flag = levels + steps + 2
    inside_above, inside_below = above[flag : flag + 1, :], below[flag : flag + 1, :]

    moves[0].wait()
    reach = rows + 2 * HALO
    x = [fluxes[(r % reach) * 2 * steps : (r % reach + 1) * 2 * steps, :] for r in range(1 - steps, rows + steps - 1)]
    field = lax.broadcasted_iota(jnp.int32, (2 * steps, width), 0) % steps
    for n in range(1, steps):
        y = stencil(x)
        x = [jnp.where(field < steps - n, y[i], x[i + 1]) for i in range(len(y))]
        for i in range(steps - 1 - n):
            x[i] = x[i] * inside_above
            x[-1 - i] = x[-1 - i] * inside_below
    for r in range(rows):
        sources[r * 16 : (r + 1) * 16, :] = jnp.concatenate([x[r], jnp.zeros((16 - 2 * steps, width), f32)], 0)

    for move in moves[3:7]:
        move.wait()
    m = wet[...].astype(f32)
    base = HALO * stride
    w = sea_weights[:, : 3 * sea_stride]
    for e, (r, other) in enumerate(((0, above), (sea_rows - 1, below))):
        mark = m[r : r + 1]
        far = other[base + 2 * sea_stride : base + 2 * sea_stride + 1, :]
        x = []
        for f in range(2):
            at = base + f * sea_stride
            mine = (2 * f + e) * sea_stride
            step = other[at : at + sea_levels, :] - sea_ends[mine : mine + sea_levels, :] * far
            step = ocean_diffusion * (mark * step)
            x.append(jnp.concatenate([step, jnp.zeros((sea_stride - sea_levels, width), f32)], 0))
        y = product(w, jnp.concatenate(x, 1))
        for f, to in enumerate((warm_out, salt)):
            rows_at = pl.ds(r, sea_levels, stride=sea_rows)
            to[rows_at, :] = to[rows_at, :] + mark * y[:sea_levels, f * width : (f + 1) * width]
    leave = [pltpu.make_async_copy(salt, brine_out, done.at[count])]
    leave[0].start()

    moves[1].wait()
    moves[2].wait()
    first, final = (ends.at[i].reshape(levels * 8, width) for i in range(2))

    @pl.loop(0, levels // 8)
    def _(c):
        def own(ref, r):
            return ref[pl.ds(c * 64 + r, 8, stride=8), :]

        def other(ref, j):
            return ref[pl.ds(pl.multiple_of(j * stride + c * 8, 8), 8), :]

        top = [other(above, j) for j in range(HALO)] + [own(first, r) for r in range(2 * HALO)]
        low = [own(final, r) for r in range(2 * HALO)] + [other(below, j) for j in range(HALO)]
        for n in range(steps):
            top, low = stencil(top), stencil(low)
            for i in range(steps - 1 - n):
                top[i] = top[i] * inside_above
                low[-1 - i] = low[-1 - i] * inside_below
        for i, value in enumerate(top + low):
            spread[pl.ds(pl.multiple_of(i * depth + c * 8, 8), 8), :] = value

    for move in moves[7:]:
        move.wait()
    w = weights[:, : 3 * depth]
    v = source_weights[:, :48]
    for g in range(rows // 8):
        to = result.at[g].reshape(levels * 8, width)
        for r in range(g * 8, g * 8 + 8, 2):
            x = [sources[(r + q) * 16 : (r + q + 1) * 16, :] for q in range(2)]
            if HALO <= r < rows - HALO:
                y = product(v, jnp.concatenate(x, 1))
                for q in range(2):
                    at = (r + q - HALO) * levels
                    to[pl.ds((r + q) % 8, levels, stride=8), :] = (
                        middle[at : at + levels, :] + y[:levels, q * width : (q + 1) * width]
                    )
            else:
                i = r if r < HALO else r - rows + 2 * HALO
                x = [
                    jnp.concatenate(
                        [spread[(i + q) * depth : (i + q) * depth + levels, :], x[q][: depth - levels]], 0
                    )
                    for q in range(2)
                ]
                y = product(w, jnp.concatenate(x, 1))
                for q in range(2):
                    to[pl.ds((r + q) % 8, levels, stride=8), :] = y[:levels, q * width : (q + 1) * width]
        leave.append(pltpu.make_async_copy(result.at[g], out.at[:, g], done.at[count + 1 + g]))
        leave[-1].start()
    for move in leave:
        move.wait()


def heat_kernel(sizes, topk, got, mine, shares, wet, sea_first, before, after):
    levels, rows, steps, sea_levels, sea_rows, stride, sea_stride = sizes
    width = before.shape[1]
    per = rows + 2 * topk
    group = width // rows
    me = mine[0].astype(f32)
    part = lax.broadcasted_iota(jnp.int32, (1, width), 1) // rows
    to = lax.broadcasted_iota(jnp.int32, (sea_rows, width), 0).astype(f32)
    picked = jnp.zeros((topk * sea_rows, width), f32)
    for g in range(got.shape[0] // (per * group)):
        at = [(g * group + i) * per for i in range(group)]
        mean = jnp.concatenate([got[a : a + rows, :] for a in at], 0).astype(bf16)
        table = got[at[0] + rows : at[0] + per, :]
        for i in range(1, group):
            table = jnp.where(part == i, got[at[i] + rows : at[i] + per, :], table)
        hot = []
        for k in range(topk):
            row = jnp.where(table[k : k + 1] == me, table[topk + k : topk + k + 1], -1.0)
            hot.append(jnp.where(to == row, 1.0, 0.0))
        hot = jnp.concatenate(hot, 0).astype(bf16)
        picked = picked + jnp.dot(hot, mean, preferred_element_type=f32)
    side = jnp.concatenate([picked[k * sea_rows : (k + 1) * sea_rows] for k in range(topk)], 1)
    first = side.astype(bf16).astype(f32)
    second = (side - first).astype(bf16).astype(f32)
    third = side - first - second
    parts = jnp.concatenate([first, second, third], 0).astype(bf16)
    y = jnp.dot(parts, shares[...], preferred_element_type=f32)
    heat = y[:sea_rows] + y[sea_rows : 2 * sea_rows] + y[2 * sea_rows :]
    heat = wet[...].astype(f32) * heat
    for l in range(sea_levels):
        after[l * sea_rows : (l + 1) * sea_rows, :] = (
            before[l * sea_rows : (l + 1) * sea_rows, :] + sea_first[l : l + 1, :] * heat
        )


def body(sky, forcing, curve, surface, rate, vmix, shares, owners, locals_, warmth, brine, wet, sea_mix):
    levels, rows, width = sky.shape
    steps = forcing.shape[0]
    sea_levels, sea_rows, _ = warmth.shape
    topk = owners.shape[1]
    stride = up_to(levels + steps + 3, 8)
    sea_stride = up_to(sea_levels, 16)
    sizes = (levels, rows, steps, sea_levels, sea_rows, stride, sea_stride)
    sky2, forcing2 = sky.reshape(-1, width), forcing.reshape(-1, width)
    warmth2, brine2 = warmth.reshape(-1, width), brine.reshape(-1, width)
    flat = lambda n, kind=f32: jax.ShapeDtypeStruct((n, width), kind)

    space = lambda *shape: pltpu.VMEM(shape, f32)
    length = HALO * stride + 2 * sea_stride + 8
    up, down = call(
        functools.partial(pack_kernel, sizes), [flat(length)] * 2,
        sky, forcing, surface, rate, warmth2, brine2, wet, moved=4 << 20, in_specs=[HBM] * 7,
        scratch=[
            space(2, levels, 8, width), space(steps, rows, width), space(2, sea_levels * sea_rows, width),
            space(2, rows, width), pltpu.VMEM(wet.shape, wet.dtype), pltpu.SemaphoreType.DMA((8,)),
        ],
    )
    count = lax.axis_size(("tile", "comp"))
    above = lax.ppermute(down, ("tile", "comp"), [(i, i + 1) for i in range(count - 1)])
    below = lax.ppermute(up, ("tile", "comp"), [(i + 1, i) for i in range(count - 1)])

    depth = up_to(levels + 2 * steps, 16)
    inner = rows - 2 * HALO
    mix_rows = up_to(levels, 16)
    sea_flat = flat(sea_levels * sea_rows)
    kept = [
        jax.ShapeDtypeStruct((mix_rows, 2 * width), bf16), flat(mix_rows, bf16),
        jax.ShapeDtypeStruct((sea_stride, 2 * width), bf16), flat(sea_stride), flat(inner * levels),
        sea_flat, sea_flat, flat(4 * sea_stride),
    ]
    found = [pltpu.VMEM(k.shape, k.dtype) for k in kept]
    (rows_of_mix, source_rows, own, weights, source_weights, sea_weights, sea_first, middle, warm, salt, sea_ends) = call(
        functools.partial(local_kernel, sizes),
        [flat((steps - 1) * levels), flat(8), flat((steps - 1) * rows)] + kept,
        vmix, curve[None], sea_mix, sky2, warmth2, brine2, wet,
        out_specs=[VMEM] * 3 + [HBM] * 8,
        scratch=found + [
            space(inner * depth, width), space(2, sea_rows * sea_stride, width), pltpu.SemaphoreType.DMA((8,)),
        ],
        flops=4 << 30, moved=8 << 20,
    )

    per = rows + 2 * topk
    tiles = lax.axis_size("tile")
    reach = 2 * steps * (rows + 2 * HALO)
    sent, fluxes = call(
        functools.partial(flux_kernel, sizes), [flat(tiles * per), flat(reach)],
        sky[-1], forcing2, surface, rate, rows_of_mix, source_rows, own, owners.T, locals_.T, below, above,
        scratch=[space(reach, width), space(2 * HALO * stride, width), pltpu.SemaphoreType.DMA],
        out_specs=[VMEM, HBM], moved=2 << 20,
    )
    got = lax.all_to_all(sent.reshape(tiles, per, width), "tile", split_axis=0, concat_axis=0, tiled=True)
    got = got.reshape(-1, width)

    sky_out, salt, warm = call(
        functools.partial(rest_kernel, sizes),
        [jax.ShapeDtypeStruct((levels, rows // 8, 8, width), f32), sea_flat, sea_flat],
        sky, fluxes, weights, source_weights, sea_weights, middle, warm, salt, sea_ends, wet, below, above,
        in_specs=[HBM] * 9 + [VMEM] * 3, out_specs=[HBM, HBM, VMEM],
        scratch=[
            space(2, levels, 8, width), space(reach, width), found[0], found[1], found[2], found[4], found[6], found[7],
            space(2 * HALO * depth, width), space(rows * 16, width), space(rows // 8, levels, 8, width),
            pltpu.SemaphoreType.DMA((11 + rows // 8,)),
        ],
        flops=2 << 30, moved=8 << 20,
    )
    mine = lax.axis_index("tile").astype(jnp.int32)[None]
    warm = call(
        functools.partial(heat_kernel, sizes, topk), flat(sea_levels * sea_rows),
        got, mine, shares.reshape(-1, width), wet, sea_first, warm,
        in_specs=[VMEM, pl.BlockSpec(memory_space=pltpu.SMEM)] + [VMEM] * 4, moved=2 << 20,
    )
    return sky_out.reshape(sky.shape), warm.reshape(warmth.shape), salt.reshape(brine.shape)


def solution(mesh):
    both = P(None, ("member", "tile", "comp"), None)
    one = P(("tile", "comp"), None)
    return jax.shard_map(
        body,
        mesh=mesh,
        in_specs=(
            both, both, P(), P(("member", "tile", "comp"), None), one, P(), P(), one, one, both, both, one, P(),
        ),
        out_specs=(both, both, both),
        check_vma=False,
    )
```

```python
import functools

import jax
import jax.numpy as jnp
from jax import lax
from jax.experimental import pallas as pl
from jax.experimental.pallas import tpu as pltpu
from jax.sharding import PartitionSpec as P

atm_diffusion = 0.2
ocean_diffusion = 0.2
HALO = 4
FULL = 64
EXACT = lax.Precision.HIGHEST
VMEM = pl.BlockSpec(memory_space=pltpu.VMEM)
HBM = pl.BlockSpec(memory_space=pltpu.HBM)
f32, bf16 = jnp.float32, jnp.bfloat16


def up_to(n, m):
    return -(-n // m) * m


def call(kernel, out_shape, *args, scratch=(), in_specs=None, out_specs=None, flops=0, moved=0, grant=24):
    return pl.pallas_call(
        kernel,
        out_shape=out_shape,
        in_specs=in_specs or [VMEM] * len(args),
        out_specs=out_specs or jax.tree.map(lambda _: VMEM, out_shape),
        scratch_shapes=list(scratch),
        compiler_params=pltpu.CompilerParams(vmem_limit_bytes=grant * 2**20),
        cost_estimate=pl.CostEstimate(flops=flops, bytes_accessed=moved, transcendentals=0),
    )(*args)


def copies(pairs, done):
    return [pltpu.make_async_copy(src, dst, done.at[i]) for i, (src, dst) in enumerate(pairs)]


def pack_kernel(
    sizes, sky, forcing, surface, rate, warmth, brine, wet, up, down,
    ends, force, sea, flat, marks, done
):
    levels, rows, steps, sea_levels, sea_rows, stride, sea_stride = sizes
    width = sky.shape[2]
    low = rows - 8
    moves = copies(
        [
            (sky.at[:, 0:8, :], ends.at[0]), (sky.at[:, low:rows, :], ends.at[1]), (forcing, force),
            (surface, flat.at[0]), (rate, flat.at[1]), (warmth, sea.at[0]), (brine, sea.at[1]), (wet, marks),
        ],
        done,
    )
    for move in moves:
        move.start()
    for move in moves:
        move.wait()
    m = marks[...].astype(f32)
    for which, out, first, sea_row in ((0, up, 0, 0), (1, down, rows - HALO, sea_rows - 1)):
        end = ends.at[which].reshape(levels * 8, width)
        for j in range(HALO):
            row = first + j
            out[j * stride : j * stride + levels, :] = end[pl.ds(row - which * low, levels, stride=8), :]
            base = j * stride + levels
            tail = [force[s, row : row + 1, :] for s in range(steps)]
            tail += [flat[0, row : row + 1, :], flat[1, row : row + 1, :], jnp.ones((1, width), f32)]
            tail += [jnp.zeros((stride - levels - len(tail), width), f32)]
            out[base : (j + 1) * stride, :] = jnp.concatenate(tail, 0)
        base = HALO * stride
        edge = m[sea_row : sea_row + 1]
        for f in range(2):
            out[base : base + sea_levels, :] = sea[f, pl.ds(sea_row, sea_levels, stride=sea_rows), :] * edge
            base += sea_stride
        out[base : base + 8, :] = jnp.concatenate([edge, jnp.zeros((7, width), f32)], 0)


def split(x):
    high = x.astype(bf16)
    return high, (x - high.astype(f32)).astype(bf16)


def three_terms(w, depth):
    high = w.astype(bf16).astype(f32)
    low = w - high
    return (high + pltpu.roll(high, depth, 1) + pltpu.roll(low, 2 * depth, 1)).astype(bf16)


def row_of(ref, first, count, step, size):
    x = ref[pl.ds(first, count, stride=step), :]
    if count < size:
        x = jnp.concatenate([x, jnp.zeros((size - count, x.shape[1]), f32)], 0)
    return x


def beside(x):
    return pltpu.roll(x, 1, 1) + pltpu.roll(x, x.shape[1] - 1, 1)


def stencil(x):
    return [x[i - 1] + x[i] + x[i + 1] + beside(x[i]) for i in range(1, len(x) - 1)]


def product(weights, x):
    high, low = split(x)
    return jnp.dot(weights, jnp.concatenate([high, low, high], 0), preferred_element_type=f32)


def local_kernel(
    sizes, vmix_in, curve_in, sea_mix_in, sky_in, warmth_in, brine_in, wet_in,
    rows_of_mix, source_rows, own, *others
):
    kept, found, held, (spread, sea_spread, done, here) = others[:8], others[8:16], others[16:23], others[23:]
    vmix, curve, sea_mix, sky, warmth, brine, wet = held
    fetches = copies(
        list(zip((vmix_in, curve_in, sea_mix_in, sky_in, warmth_in, brine_in, wet_in), held)), here
    )
    for fetch in fetches:
        fetch.start()
    for fetch in fetches[:3]:
        fetch.wait()
    weights, source_weights, sea_weights, sea_first, middle, warm_out, brine_out, sea_ends = found
    moves = copies(list(zip(found, kept)), done)
    levels, rows, steps, sea_levels, sea_rows, stride, sea_stride = sizes
    width = sky.shape[1]
    depth = up_to(levels + 2 * steps, 16)
    v = vmix[...]
    dot = functools.partial(jnp.dot, precision=EXACT, preferred_element_type=f32)
    powers = [v]
    for _ in range(steps - 1):
        powers.append(dot(v, powers[-1]))
    last = (lax.broadcasted_iota(jnp.int32, (levels, width), 0) == levels - 1).astype(f32)
    for s in range(1, steps):
        rows_of_mix[(s - 1) * levels : s * levels, :] = lax.dot_general(
            powers[s - 1], last, (((0,), (0,)), ((), ())), precision=EXACT, preferred_element_type=f32
        )
    by_curve = jnp.broadcast_to(curve[...], (width, levels))
    of_curve = [
        lax.dot_general(p, by_curve, (((1,), (1,)), ((), ())), precision=EXACT, preferred_element_type=f32)
        for p in powers
    ]
    of_last = [jnp.broadcast_to(p[:, levels - 1 : levels], (levels, width)) for p in powers]
    found = [of_curve[i][levels - 1 :] for i in range(steps - 1)]
    found += [of_last[i][levels - 1 :] for i in range(steps - 1)]
    found += [jnp.zeros((8 - len(found), width), f32)]
    source_rows[...] = jnp.concatenate(found, 0)
    lane = lax.broadcasted_iota(jnp.int32, (levels, width), 1)
    wide = jnp.concatenate(
        [powers[-1] * atm_diffusion**steps, jnp.zeros((levels, width - levels), f32)], 1
    )
    sources = jnp.zeros((levels, width), f32)
    for j in range(steps):
        factor = atm_diffusion ** (steps - 1 - j)
        for at, value in ((j, of_curve[steps - 1 - j] * factor), (steps + j, of_last[steps - 1 - j] * -factor)):
            wide = jnp.where(lane == levels + at, value, wide)
            sources = jnp.where(lane == at, value, sources)
    more = jnp.zeros((weights.shape[0] - levels, width), f32)
    wide = jnp.concatenate([wide, more], 0)
    wide = jnp.concatenate([wide, jnp.zeros_like(wide)], 1)
    weights[...] = three_terms(wide, depth)
    source_weights[...] = three_terms(jnp.concatenate([sources, more], 0), 16)
    sea = sea_mix[...]
    sea = jnp.concatenate([sea, jnp.zeros((sea_levels, 2 * width - sea_levels), f32)], 1)
    sea = jnp.concatenate([sea, jnp.zeros((sea_stride - sea_levels, 2 * width), f32)], 0)
    sea_weights[...] = three_terms(sea, sea_stride)
    sea_first[...] = jnp.broadcast_to(sea[:, 0:1], sea_first.shape)
    for move in moves[:4]:
        move.start()
    fetches[3].wait()
    sums = [jnp.zeros((rows, width), f32) for _ in range(steps - 1)]
    for l in range(levels):
        x = sky[l * rows : (l + 1) * rows, :]
        for s in range(steps - 1):
            sums[s] = sums[s] + rows_of_mix[s * levels + l : s * levels + l + 1, :] * x
    for s in range(steps - 1):
        own[s * rows : (s + 1) * rows, :] = sums[s]

    inner = rows - 2 * HALO

    @pl.loop(0, levels // 8)
    def _(c):
        x = [sky[pl.ds(c * 8 * rows + r, 8, stride=rows), :] for r in range(rows)]
        for _ in range(steps):
            x = stencil(x)
        for r in range(inner):
            spread[pl.ds(pl.multiple_of(r * depth + c * 8, 8), 8), :] = x[r]

    if depth > levels:
        for r in range(inner):
            spread[r * depth + levels : (r + 1) * depth, :] = jnp.zeros((depth - levels, width), f32)
    w = weights[:, : 3 * depth]
    for r in range(0, inner, 2):
        x = jnp.concatenate([spread[(r + i) * depth : (r + i + 1) * depth, :] for i in range(2)], 1)
        y = product(w, x)
        for i in range(2):
            middle[(r + i) * levels : (r + i + 1) * levels, :] = y[:levels, i * width : (i + 1) * width]
    moves[4].start()

    for fetch in fetches[4:]:
        fetch.wait()
    m = wet[...].astype(f32)
    mark = [m[r : r + 1] for r in range(sea_rows)]
    edge = jnp.zeros((1, width), f32)

    def near(x):
        x = [jnp.zeros_like(x[0])] + x + [jnp.zeros_like(x[0])]
        return [x[i - 1] + x[i + 1] + beside(x[i]) for i in range(1, len(x) - 1)]

    around = (
        jnp.concatenate([edge, m[:-1]], 0) + jnp.concatenate([m[1:], edge], 0) + beside(m)
    ) * ocean_diffusion
    share = [around[r : r + 1] for r in range(sea_rows)]
    for f, field in enumerate((warmth, brine)):
        for c in range(sea_stride // 8):
            count = min(8, sea_levels - c * 8)
            x = [row_of(field, c * 8 * sea_rows + r, count, sea_rows, 8) for r in range(sea_rows)]
            y = near([mark[r] * x[r] for r in range(sea_rows)])
            for r in range(sea_rows):
                at = r * sea_stride + c * 8
                sea_spread[f, at : at + 8, :] = x[r] + mark[r] * (ocean_diffusion * y[r] - x[r] * share[r])
    w = sea_weights[:, : 3 * sea_stride]
    for r in range(sea_rows):
        x = jnp.concatenate([sea_spread[f, r * sea_stride : (r + 1) * sea_stride, :] for f in range(2)], 1)
        y = product(w, x)
        for f, (field, out) in enumerate(((warmth, warm_out), (brine, brine_out))):
            old = field[pl.ds(r, sea_levels, stride=sea_rows), :]
            new = y[:sea_levels, f * width : (f + 1) * width]
            out[pl.ds(r, sea_levels, stride=sea_rows), :] = mark[r] * new + (1.0 - mark[r]) * old
            if r in (0, sea_rows - 1):
                at = (2 * f + (r > 0)) * sea_stride
                sea_ends[at : at + sea_levels, :] = old
    for move in moves[5:]:
        move.start()
    for move in moves:
        move.wait()


def cross(x):
    n, w = x.shape
    return (
        x + pltpu.roll(x, 1, 0) + pltpu.roll(x, n - 1, 0) + pltpu.roll(x, 1, 1) + pltpu.roll(x, w - 1, 1)
    )


def masked(x, rows, inside):
    return jnp.concatenate([x[:rows], x[rows:] * inside], 0)


def flux_kernel(
    sizes, sky, forcing, surface, rate, rows_of_mix, source_rows, own, owners, locals_, below, above,
    sent, kept, fluxes, halo, done
):
    levels, rows, steps, sea_levels, sea_rows, stride, sea_stride = sizes
    width = sky.shape[1]
    halo[: HALO * stride, :] = below[: HALO * stride, :]
    halo[HALO * stride :, :] = above[: HALO * stride, :]

    def edge(l):
        return halo[pl.ds(l, 2 * HALO, stride=stride), :]

    inside = edge(levels + steps + 2)
    sums = [jnp.zeros((2 * HALO, width), f32) for _ in range(steps - 1)]
    for l in range(levels):
        x = edge(l)
        for s in range(steps - 1):
            sums[s] = sums[s] + rows_of_mix[s * levels + l : s * levels + l + 1, :] * x
    tops = [jnp.concatenate([sky[...], edge(levels - 1)], 0)]
    tops += [jnp.concatenate([own[s * rows : (s + 1) * rows, :], sums[s]], 0) for s in range(steps - 1)]
    surf = jnp.concatenate([surface[...], edge(levels + steps)], 0)
    coef = jnp.concatenate([rate[...], edge(levels + steps + 1)], 0)
    force = [
        jnp.concatenate([forcing[s * rows : (s + 1) * rows, :], edge(levels + s)], 0) for s in range(steps)
    ]

    flux = []
    for s in range(steps):
        state = tops[s]
        for i in range(s):
            m = s - 1 - i
            state = masked(cross(state) * atm_diffusion, rows, inside)
            state = state + source_rows[m : m + 1, :] * force[i]
            state = state - source_rows[steps - 1 + m : steps + m, :] * flux[i]
        flux.append(coef * (state - surf))
        reach = rows + 2 * HALO
        fluxes[pl.ds(s, reach, stride=2 * steps), :] = force[s]
        fluxes[pl.ds(steps + s, reach, stride=2 * steps), :] = flux[s]
    move = pltpu.make_async_copy(fluxes, kept, done)
    move.start()
    total = flux[0][:rows]
    for s in range(1, steps):
        total = total + flux[s][:rows]
    mean = (total / steps).astype(bf16).astype(f32)
    times = width // rows
    owner = owners[...].astype(f32)
    row = locals_[...].astype(f32)
    table = jnp.concatenate(
        [jnp.concatenate([owner] * times, 1), jnp.concatenate([row] * times, 1)], 0
    )
    per = mean.shape[0] + table.shape[0]
    for t in range(sent.shape[0] // per):
        sent[t * per : t * per + rows, :] = mean
        sent[t * per + rows : (t + 1) * per, :] = table
    move.wait()


def rest_kernel(
    sizes, sky, fluxes_in, weights_in, source_weights_in, sea_weights_in, middle_in, warm_in, salt_in, sea_ends_in,
    wet, below, above, out, brine_out, warm_out,
    ends, fluxes, weights, source_weights, sea_weights, middle, salt, sea_ends, spread, sources, result, done
):
    levels, rows, steps, sea_levels, sea_rows, stride, sea_stride = sizes
    width = sky.shape[2]
    depth = up_to(levels + 2 * steps, 16)
    moves = copies(
        [
            (fluxes_in, fluxes), (sky.at[:, 0:8, :], ends.at[0]), (sky.at[:, rows - 8 : rows, :], ends.at[1]),
            (sea_weights_in, sea_weights), (sea_ends_in, sea_ends), (salt_in, salt), (warm_in, warm_out),
            (weights_in, weights), (source_weights_in, source_weights), (middle_in, middle),
        ],
        done,
    )
    count = len(moves)
    for move in moves:
        move.start()
    flag = levels + steps + 2
    inside_above, inside_below = above[flag : flag + 1, :], below[flag : flag + 1, :]

    moves[0].wait()
    reach = rows + 2 * HALO
    x = [fluxes[(r % reach) * 2 * steps : (r % reach + 1) * 2 * steps, :] for r in range(1 - steps, rows + steps - 1)]
    field = lax.broadcasted_iota(jnp.int32, (2 * steps, width), 0) % steps
    for n in range(1, steps):
        y = stencil(x)
        x = [jnp.where(field < steps - n, y[i], x[i + 1]) for i in range(len(y))]
        for i in range(steps - 1 - n):
            x[i] = x[i] * inside_above
            x[-1 - i] = x[-1 - i] * inside_below
    for r in range(rows):
        sources[r * 16 : (r + 1) * 16, :] = jnp.concatenate([x[r], jnp.zeros((16 - 2 * steps, width), f32)], 0)

    for move in moves[3:7]:
        move.wait()
    m = wet[...].astype(f32)
    base = HALO * stride
    w = sea_weights[:, : 3 * sea_stride]
    for e, (r, other) in enumerate(((0, above), (sea_rows - 1, below))):
        mark = m[r : r + 1]
        far = other[base + 2 * sea_stride : base + 2 * sea_stride + 1, :]
        x = []
        for f in range(2):
            at = base + f * sea_stride
            mine = (2 * f + e) * sea_stride
            step = other[at : at + sea_levels, :] - sea_ends[mine : mine + sea_levels, :] * far
            step = ocean_diffusion * (mark * step)
            x.append(jnp.concatenate([step, jnp.zeros((sea_stride - sea_levels, width), f32)], 0))
        y = product(w, jnp.concatenate(x, 1))
        for f, to in enumerate((warm_out, salt)):
            rows_at = pl.ds(r, sea_levels, stride=sea_rows)
            to[rows_at, :] = to[rows_at, :] + mark * y[:sea_levels, f * width : (f + 1) * width]
    leave = [pltpu.make_async_copy(salt, brine_out, done.at[count])]
    leave[0].start()

    moves[1].wait()
    moves[2].wait()
    first, final = (ends.at[i].reshape(levels * 8, width) for i in range(2))

    @pl.loop(0, levels // 8)
    def _(c):
        def own(ref, r):
            return ref[pl.ds(c * 64 + r, 8, stride=8), :]

        def other(ref, j):
            return ref[pl.ds(pl.multiple_of(j * stride + c * 8, 8), 8), :]

        top = [other(above, j) for j in range(HALO)] + [own(first, r) for r in range(2 * HALO)]
        low = [own(final, r) for r in range(2 * HALO)] + [other(below, j) for j in range(HALO)]
        for n in range(steps):
            top, low = stencil(top), stencil(low)
            for i in range(steps - 1 - n):
                top[i] = top[i] * inside_above
                low[-1 - i] = low[-1 - i] * inside_below
        for i, value in enumerate(top + low):
            spread[pl.ds(pl.multiple_of(i * depth + c * 8, 8), 8), :] = value

    for move in moves[7:]:
        move.wait()
    w = weights[:, : 3 * depth]
    v = source_weights[:, :48]
    for g in range(rows // 8):
        to = result.at[g].reshape(levels * 8, width)
        for r in range(g * 8, g * 8 + 8, 2):
            x = [sources[(r + q) * 16 : (r + q + 1) * 16, :] for q in range(2)]
            if HALO <= r < rows - HALO:
                y = product(v, jnp.concatenate(x, 1))
                for q in range(2):
                    at = (r + q - HALO) * levels
                    to[pl.ds((r + q) % 8, levels, stride=8), :] = (
                        middle[at : at + levels, :] + y[:levels, q * width : (q + 1) * width]
                    )
            else:
                i = r if r < HALO else r - rows + 2 * HALO
                x = [
                    jnp.concatenate(
                        [spread[(i + q) * depth : (i + q) * depth + levels, :], x[q][: depth - levels]], 0
                    )
                    for q in range(2)
                ]
                y = product(w, jnp.concatenate(x, 1))
                for q in range(2):
                    to[pl.ds((r + q) % 8, levels, stride=8), :] = y[:levels, q * width : (q + 1) * width]
        leave.append(pltpu.make_async_copy(result.at[g], out.at[:, g], done.at[count + 1 + g]))
        leave[-1].start()
    for move in leave:
        move.wait()


def heat_kernel(sizes, topk, got, mine, shares, wet, sea_first, before, after):
    levels, rows, steps, sea_levels, sea_rows, stride, sea_stride = sizes
    width = before.shape[1]
    per = rows + 2 * topk
    group = width // rows
    me = mine[0].astype(f32)
    part = lax.broadcasted_iota(jnp.int32, (1, width), 1) // rows
    to = lax.broadcasted_iota(jnp.int32, (sea_rows, width), 0).astype(f32)
    picked = jnp.zeros((topk * sea_rows, width), f32)
    for g in range(got.shape[0] // (per * group)):
        at = [(g * group + i) * per for i in range(group)]
        mean = jnp.concatenate([got[a : a + rows, :] for a in at], 0).astype(bf16)
        table = got[at[0] + rows : at[0] + per, :]
        for i in range(1, group):
            table = jnp.where(part == i, got[at[i] + rows : at[i] + per, :], table)
        hot = []
        for k in range(topk):
            row = jnp.where(table[k : k + 1] == me, table[topk + k : topk + k + 1], -1.0)
            hot.append(jnp.where(to == row, 1.0, 0.0))
        hot = jnp.concatenate(hot, 0).astype(bf16)
        picked = picked + jnp.dot(hot, mean, preferred_element_type=f32)
    side = jnp.concatenate([picked[k * sea_rows : (k + 1) * sea_rows] for k in range(topk)], 1)
    first = side.astype(bf16).astype(f32)
    second = (side - first).astype(bf16).astype(f32)
    third = side - first - second
    parts = jnp.concatenate([first, second, third], 0).astype(bf16)
    y = jnp.dot(parts, shares[...], preferred_element_type=f32)
    heat = y[:sea_rows] + y[sea_rows : 2 * sea_rows] + y[2 * sea_rows :]
    heat = wet[...].astype(f32) * heat
    for l in range(sea_levels):
        after[l * sea_rows : (l + 1) * sea_rows, :] = (
            before[l * sea_rows : (l + 1) * sea_rows, :] + sea_first[l : l + 1, :] * heat
        )


def body(sky, forcing, curve, surface, rate, vmix, shares, owners, locals_, warmth, brine, wet, sea_mix):
    levels, rows, width = sky.shape
    steps = forcing.shape[0]
    sea_levels, sea_rows, _ = warmth.shape
    topk = owners.shape[1]
    stride = up_to(levels + steps + 3, 8)
    sea_stride = up_to(sea_levels, 16)
    sizes = (levels, rows, steps, sea_levels, sea_rows, stride, sea_stride)
    sky2, forcing2 = sky.reshape(-1, width), forcing.reshape(-1, width)
    warmth2, brine2 = warmth.reshape(-1, width), brine.reshape(-1, width)
    flat = lambda n, kind=f32: jax.ShapeDtypeStruct((n, width), kind)

    space = lambda *shape: pltpu.VMEM(shape, f32)
    length = HALO * stride + 2 * sea_stride + 8
    up, down = call(
        functools.partial(pack_kernel, sizes), [flat(length)] * 2,
        sky, forcing, surface, rate, warmth2, brine2, wet, moved=4 << 20, in_specs=[HBM] * 7, grant=FULL,
        scratch=[
            space(2, levels, 8, width), space(steps, rows, width), space(2, sea_levels * sea_rows, width),
            space(2, rows, width), pltpu.VMEM(wet.shape, wet.dtype), pltpu.SemaphoreType.DMA((8,)),
        ],
    )
    count = lax.axis_size(("tile", "comp"))
    above = lax.ppermute(down, ("tile", "comp"), [(i, i + 1) for i in range(count - 1)])
    below = lax.ppermute(up, ("tile", "comp"), [(i + 1, i) for i in range(count - 1)])

    depth = up_to(levels + 2 * steps, 16)
    inner = rows - 2 * HALO
    mix_rows = up_to(levels, 16)
    sea_flat = flat(sea_levels * sea_rows)
    kept = [
        jax.ShapeDtypeStruct((mix_rows, 2 * width), bf16), flat(mix_rows, bf16),
        jax.ShapeDtypeStruct((sea_stride, 2 * width), bf16), flat(sea_stride), flat(inner * levels),
        sea_flat, sea_flat, flat(4 * sea_stride),
    ]
    found = [pltpu.VMEM(k.shape, k.dtype) for k in kept]
    local_args = (vmix, curve[None], sea_mix, sky2, warmth2, brine2, wet)
    held = [pltpu.VMEM(x.shape, x.dtype) for x in local_args]
    (rows_of_mix, source_rows, own, weights, source_weights, sea_weights, sea_first, middle, warm, salt, sea_ends) = call(
        functools.partial(local_kernel, sizes),
        [flat((steps - 1) * levels), flat(8), flat((steps - 1) * rows)] + kept,
        *local_args,
        in_specs=[HBM] * 7, out_specs=[VMEM] * 3 + [HBM] * 8,
        scratch=found + held + [
            space(inner * depth, width), space(2, sea_rows * sea_stride, width), pltpu.SemaphoreType.DMA((8,)),
            pltpu.SemaphoreType.DMA((7,)),
        ],
        flops=4 << 30, moved=8 << 20, grant=FULL,
    )

    per = rows + 2 * topk
    tiles = lax.axis_size("tile")
    reach = 2 * steps * (rows + 2 * HALO)
    sent, fluxes = call(
        functools.partial(flux_kernel, sizes), [flat(tiles * per), flat(reach)],
        sky[-1], forcing2, surface, rate, rows_of_mix, source_rows, own, owners.T, locals_.T, below, above,
        scratch=[space(reach, width), space(2 * HALO * stride, width), pltpu.SemaphoreType.DMA],
        out_specs=[VMEM, HBM], moved=2 << 20,
    )
    got = lax.all_to_all(sent.reshape(tiles, per, width), "tile", split_axis=0, concat_axis=0, tiled=True)
    got = got.reshape(-1, width)

    sky_out, salt, warm = call(
        functools.partial(rest_kernel, sizes),
        [jax.ShapeDtypeStruct((levels, rows // 8, 8, width), f32), sea_flat, sea_flat],
        sky, fluxes, weights, source_weights, sea_weights, middle, warm, salt, sea_ends, wet, below, above,
        in_specs=[HBM] * 9 + [VMEM] * 3, out_specs=[HBM, HBM, VMEM],
        scratch=[
            space(2, levels, 8, width), space(reach, width), found[0], found[1], found[2], found[4], found[6], found[7],
            space(2 * HALO * depth, width), space(rows * 16, width), space(rows // 8, levels, 8, width),
            pltpu.SemaphoreType.DMA((11 + rows // 8,)),
        ],
        flops=2 << 30, moved=8 << 20, grant=FULL,
    )
    mine = lax.axis_index("tile").astype(jnp.int32)[None]
    warm = call(
        functools.partial(heat_kernel, sizes, topk), flat(sea_levels * sea_rows),
        got, mine, shares.reshape(-1, width), wet, sea_first, warm,
        in_specs=[VMEM, pl.BlockSpec(memory_space=pltpu.SMEM)] + [VMEM] * 4, moved=2 << 20,
    )
    return sky_out.reshape(sky.shape), warm.reshape(warmth.shape), salt.reshape(brine.shape)


def solution(mesh):
    both = P(None, ("member", "tile", "comp"), None)
    one = P(("tile", "comp"), None)
    return jax.shard_map(
        body,
        mesh=mesh,
        in_specs=(
            both, both, P(), P(("member", "tile", "comp"), None), one, P(), P(), one, one, both, both, one, P(),
        ),
        out_specs=(both, both, both),
        check_vma=False,
    )
```

```python
import functools

import jax
import jax.numpy as jnp
from jax import lax
from jax.experimental import pallas as pl
from jax.experimental.pallas import tpu as pltpu
from jax.sharding import PartitionSpec as P

atm_diffusion = 0.2
ocean_diffusion = 0.2
HALO = 4
FULL = 60
EXACT = lax.Precision.HIGHEST
VMEM = pl.BlockSpec(memory_space=pltpu.VMEM)
HBM = pl.BlockSpec(memory_space=pltpu.HBM)
f32, bf16 = jnp.float32, jnp.bfloat16


def up_to(n, m):
    return -(-n // m) * m


def call(kernel, out_shape, *args, scratch=(), in_specs=None, out_specs=None, flops=0, moved=0, grant=24):
    return pl.pallas_call(
        kernel,
        out_shape=out_shape,
        in_specs=in_specs or [VMEM] * len(args),
        out_specs=out_specs or jax.tree.map(lambda _: VMEM, out_shape),
        scratch_shapes=list(scratch),
        compiler_params=pltpu.CompilerParams(vmem_limit_bytes=grant * 2**20),
        cost_estimate=pl.CostEstimate(flops=flops, bytes_accessed=moved, transcendentals=0),
    )(*args)


def copies(pairs, done):
    return [pltpu.make_async_copy(src, dst, done.at[i]) for i, (src, dst) in enumerate(pairs)]


def pack_kernel(
    sizes, sky, forcing, surface, rate, warmth, brine, wet, up, down,
    ends, force, sea, flat, marks, done
):
    levels, rows, steps, sea_levels, sea_rows, stride, sea_stride = sizes
    width = sky.shape[2]
    low = rows - 8
    moves = copies(
        [
            (sky.at[:, 0:8, :], ends.at[0]), (sky.at[:, low:rows, :], ends.at[1]), (forcing, force),
            (surface, flat.at[0]), (rate, flat.at[1]), (warmth, sea.at[0]), (brine, sea.at[1]), (wet, marks),
        ],
        done,
    )
    for move in moves:
        move.start()
    for move in moves:
        move.wait()
    m = marks[...].astype(f32)
    for which, out, first, sea_row in ((0, up, 0, 0), (1, down, rows - HALO, sea_rows - 1)):
        end = ends.at[which].reshape(levels * 8, width)
        for j in range(HALO):
            row = first + j
            out[j * stride : j * stride + levels, :] = end[pl.ds(row - which * low, levels, stride=8), :]
            base = j * stride + levels
            tail = [force[s, row : row + 1, :] for s in range(steps)]
            tail += [flat[0, row : row + 1, :], flat[1, row : row + 1, :], jnp.ones((1, width), f32)]
            tail += [jnp.zeros((stride - levels - len(tail), width), f32)]
            out[base : (j + 1) * stride, :] = jnp.concatenate(tail, 0)
        base = HALO * stride
        edge = m[sea_row : sea_row + 1]
        for f in range(2):
            out[base : base + sea_levels, :] = sea[f, pl.ds(sea_row, sea_levels, stride=sea_rows), :] * edge
            base += sea_stride
        out[base : base + 8, :] = jnp.concatenate([edge, jnp.zeros((7, width), f32)], 0)


def split(x):
    high = x.astype(bf16)
    return high, (x - high.astype(f32)).astype(bf16)


def three_terms(w, depth):
    high = w.astype(bf16).astype(f32)
    low = w - high
    return (high + pltpu.roll(high, depth, 1) + pltpu.roll(low, 2 * depth, 1)).astype(bf16)


def row_of(ref, first, count, step, size):
    x = ref[pl.ds(first, count, stride=step), :]
    if count < size:
        x = jnp.concatenate([x, jnp.zeros((size - count, x.shape[1]), f32)], 0)
    return x


def beside(x):
    return pltpu.roll(x, 1, 1) + pltpu.roll(x, x.shape[1] - 1, 1)


def stencil(x):
    return [x[i - 1] + x[i] + x[i + 1] + beside(x[i]) for i in range(1, len(x) - 1)]


def product(weights, x):
    high, low = split(x)
    return jnp.dot(weights, jnp.concatenate([high, low, high], 0), preferred_element_type=f32)


def local_kernel(
    sizes, last_place, place, vmix, curve, sea_mix, sky, warmth, brine, wet,
    rows_of_mix, source_rows, own, weights, source_weights, sea_weights, sea_first, middle, warm_out, brine_out, sea_ends,
    spread, sea_spread,
):
    levels, rows, steps, sea_levels, sea_rows, stride, sea_stride = sizes
    width = sky.shape[1]
    depth = up_to(levels + 2 * steps, 16)
    v = vmix[...]
    dot = functools.partial(jnp.dot, precision=EXACT, preferred_element_type=f32)
    powers = [v]
    for _ in range(steps - 1):
        powers.append(dot(v, powers[-1]))
    last = (lax.broadcasted_iota(jnp.int32, (levels, width), 0) == levels - 1).astype(f32)
    for s in range(1, steps):
        rows_of_mix[(s - 1) * levels : s * levels, :] = lax.dot_general(
            powers[s - 1], last, (((0,), (0,)), ((), ())), precision=EXACT, preferred_element_type=f32
        )
    by_curve = jnp.broadcast_to(curve[...], (width, levels))
    of_curve = [
        lax.dot_general(p, by_curve, (((1,), (1,)), ((), ())), precision=EXACT, preferred_element_type=f32)
        for p in powers
    ]
    of_last = [jnp.broadcast_to(p[:, levels - 1 : levels], (levels, width)) for p in powers]
    found = [of_curve[i][levels - 1 :] for i in range(steps - 1)]
    found += [of_last[i][levels - 1 :] for i in range(steps - 1)]
    found += [jnp.zeros((8 - len(found), width), f32)]
    source_rows[...] = jnp.concatenate(found, 0)
    lane = lax.broadcasted_iota(jnp.int32, (levels, width), 1)
    wide = jnp.concatenate(
        [powers[-1] * atm_diffusion**steps, jnp.zeros((levels, width - levels), f32)], 1
    )
    sources = jnp.zeros((levels, width), f32)
    for j in range(steps):
        factor = atm_diffusion ** (steps - 1 - j)
        for at, value in ((j, of_curve[steps - 1 - j] * factor), (steps + j, of_last[steps - 1 - j] * -factor)):
            wide = jnp.where(lane == levels + at, value, wide)
            sources = jnp.where(lane == at, value, sources)
    more = jnp.zeros((weights.shape[0] - levels, width), f32)
    wide = jnp.concatenate([wide, more], 0)
    wide = jnp.concatenate([wide, jnp.zeros_like(wide)], 1)
    weights[...] = three_terms(wide, depth)
    source_weights[...] = three_terms(jnp.concatenate([sources, more], 0), 16)
    sea = sea_mix[...]
    sea = jnp.concatenate([sea, jnp.zeros((sea_levels, 2 * width - sea_levels), f32)], 1)
    sea = jnp.concatenate([sea, jnp.zeros((sea_stride - sea_levels, 2 * width), f32)], 0)
    sea_weights[...] = three_terms(sea, sea_stride)
    sea_first[...] = jnp.broadcast_to(sea[:, 0:1], sea_first.shape)
    sums = [jnp.zeros((rows, width), f32) for _ in range(steps - 1)]
    for l in range(levels):
        x = sky[l * rows : (l + 1) * rows, :]
        for s in range(steps - 1):
            sums[s] = sums[s] + rows_of_mix[s * levels + l : s * levels + l + 1, :] * x
    for s in range(steps - 1):
        own[s * rows : (s + 1) * rows, :] = sums[s]

    before = jnp.where(place[0] > 0, 1.0, 0.0)
    behind = jnp.where(place[0] < last_place, 1.0, 0.0)

    @pl.loop(0, levels // 8)
    def _(c):
        x = [sky[pl.ds(c * 8 * rows + r, 8, stride=rows), :] for r in range(rows)]
        none = jnp.zeros_like(x[0])
        beyond = 0
        for n in range(steps):
            if beyond < steps - 1 - n:
                x = [x[0]] + stencil([none] + x + [none]) + [x[-1]]
                beyond += 1
            else:
                x = stencil(x)
                beyond -= 1
            for i in range(beyond):
                x[i] = x[i] * before
                x[-1 - i] = x[-1 - i] * behind
        for r in range(rows):
            spread[pl.ds(pl.multiple_of(r * depth + c * 8, 8), 8), :] = x[r]

    if depth > levels:
        for r in range(rows):
            spread[r * depth + levels : (r + 1) * depth, :] = jnp.zeros((depth - levels, width), f32)
    w = weights[:, : 3 * depth]
    for r in range(0, rows, 2):
        x = jnp.concatenate([spread[(r + i) * depth : (r + i + 1) * depth, :] for i in range(2)], 1)
        y = product(w, x)
        for i in range(2):
            middle[(r + i) * levels : (r + i + 1) * levels, :] = y[:levels, i * width : (i + 1) * width]

    m = wet[...].astype(f32)
    mark = [m[r : r + 1] for r in range(sea_rows)]
    edge = jnp.zeros((1, width), f32)

    def near(x):
        x = [jnp.zeros_like(x[0])] + x + [jnp.zeros_like(x[0])]
        return [x[i - 1] + x[i + 1] + beside(x[i]) for i in range(1, len(x) - 1)]

    around = (
        jnp.concatenate([edge, m[:-1]], 0) + jnp.concatenate([m[1:], edge], 0) + beside(m)
    ) * ocean_diffusion
    share = [around[r : r + 1] for r in range(sea_rows)]
    for f, field in enumerate((warmth, brine)):
        for c in range(sea_stride // 8):
            count = min(8, sea_levels - c * 8)
            x = [row_of(field, c * 8 * sea_rows + r, count, sea_rows, 8) for r in range(sea_rows)]
            y = near([mark[r] * x[r] for r in range(sea_rows)])
            for r in range(sea_rows):
                at = r * sea_stride + c * 8
                sea_spread[f, at : at + 8, :] = x[r] + mark[r] * (ocean_diffusion * y[r] - x[r] * share[r])
    w = sea_weights[:, : 3 * sea_stride]
    for r in range(sea_rows):
        x = jnp.concatenate([sea_spread[f, r * sea_stride : (r + 1) * sea_stride, :] for f in range(2)], 1)
        y = product(w, x)
        for f, (field, out) in enumerate(((warmth, warm_out), (brine, brine_out))):
            old = field[pl.ds(r, sea_levels, stride=sea_rows), :]
            new = y[:sea_levels, f * width : (f + 1) * width]
            out[pl.ds(r, sea_levels, stride=sea_rows), :] = mark[r] * new + (1.0 - mark[r]) * old
            if r in (0, sea_rows - 1):
                at = (2 * f + (r > 0)) * sea_stride
                sea_ends[at : at + sea_levels, :] = old


def cross(x):
    n, w = x.shape
    return (
        x + pltpu.roll(x, 1, 0) + pltpu.roll(x, n - 1, 0) + pltpu.roll(x, 1, 1) + pltpu.roll(x, w - 1, 1)
    )


def masked(x, rows, inside):
    return jnp.concatenate([x[:rows], x[rows:] * inside], 0)


def flux_kernel(
    sizes, sky, forcing, surface, rate, rows_of_mix, source_rows, own, owners, locals_, below, above,
    sent, fluxes, halo
):
    levels, rows, steps, sea_levels, sea_rows, stride, sea_stride = sizes
    width = sky.shape[1]
    halo[: HALO * stride, :] = below[: HALO * stride, :]
    halo[HALO * stride :, :] = above[: HALO * stride, :]

    def edge(l):
        return halo[pl.ds(l, 2 * HALO, stride=stride), :]

    inside = edge(levels + steps + 2)
    sums = [jnp.zeros((2 * HALO, width), f32) for _ in range(steps - 1)]
    for l in range(levels):
        x = edge(l)
        for s in range(steps - 1):
            sums[s] = sums[s] + rows_of_mix[s * levels + l : s * levels + l + 1, :] * x
    tops = [jnp.concatenate([sky[...], edge(levels - 1)], 0)]
    tops += [jnp.concatenate([own[s * rows : (s + 1) * rows, :], sums[s]], 0) for s in range(steps - 1)]
    surf = jnp.concatenate([surface[...], edge(levels + steps)], 0)
    coef = jnp.concatenate([rate[...], edge(levels + steps + 1)], 0)
    force = [
        jnp.concatenate([forcing[s * rows : (s + 1) * rows, :], edge(levels + s)], 0) for s in range(steps)
    ]

    flux = []
    for s in range(steps):
        state = tops[s]
        for i in range(s):
            m = s - 1 - i
            state = masked(cross(state) * atm_diffusion, rows, inside)
            state = state + source_rows[m : m + 1, :] * force[i]
            state = state - source_rows[steps - 1 + m : steps + m, :] * flux[i]
        flux.append(coef * (state - surf))
        reach = rows + 2 * HALO
        fluxes[pl.ds(s, reach, stride=2 * steps), :] = force[s]
        fluxes[pl.ds(steps + s, reach, stride=2 * steps), :] = flux[s]
    total = flux[0][:rows]
    for s in range(1, steps):
        total = total + flux[s][:rows]
    mean = (total / steps).astype(bf16).astype(f32)
    times = width // rows
    owner = owners[...].astype(f32)
    row = locals_[...].astype(f32)
    table = jnp.concatenate(
        [jnp.concatenate([owner] * times, 1), jnp.concatenate([row] * times, 1)], 0
    )
    per = mean.shape[0] + table.shape[0]
    for t in range(sent.shape[0] // per):
        sent[t * per : t * per + rows, :] = mean
        sent[t * per + rows : (t + 1) * per, :] = table


def rest_kernel(
    sizes, fluxes, weights, source_weights, sea_weights, middle, warm, salt, sea_ends, wet, below, above,
    out, brine_out, warm_out, salt_held, spread, sources, result, done
):
    levels, rows, steps, sea_levels, sea_rows, stride, sea_stride = sizes
    width = above.shape[1]
    depth = up_to(levels + 2 * steps, 16)
    flag = levels + steps + 2
    inside_above, inside_below = above[flag : flag + 1, :], below[flag : flag + 1, :]

    reach = rows + 2 * HALO
    x = [fluxes[(r % reach) * 2 * steps : (r % reach + 1) * 2 * steps, :] for r in range(1 - steps, rows + steps - 1)]
    field = lax.broadcasted_iota(jnp.int32, (2 * steps, width), 0) % steps
    for n in range(1, steps):
        y = stencil(x)
        x = [jnp.where(field < steps - n, y[i], x[i + 1]) for i in range(len(y))]
        for i in range(steps - 1 - n):
            x[i] = x[i] * inside_above
            x[-1 - i] = x[-1 - i] * inside_below
    for r in range(rows):
        sources[r * 16 : (r + 1) * 16, :] = jnp.concatenate([x[r], jnp.zeros((16 - 2 * steps, width), f32)], 0)

    warm_out[...] = warm[...]
    salt_held[...] = salt[...]
    m = wet[...].astype(f32)
    base = HALO * stride
    w = sea_weights[:, : 3 * sea_stride]
    for e, (r, other) in enumerate(((0, above), (sea_rows - 1, below))):
        mark = m[r : r + 1]
        far = other[base + 2 * sea_stride : base + 2 * sea_stride + 1, :]
        x = []
        for f in range(2):
            at = base + f * sea_stride
            mine = (2 * f + e) * sea_stride
            step = other[at : at + sea_levels, :] - sea_ends[mine : mine + sea_levels, :] * far
            step = ocean_diffusion * (mark * step)
            x.append(jnp.concatenate([step, jnp.zeros((sea_stride - sea_levels, width), f32)], 0))
        y = product(w, jnp.concatenate(x, 1))
        for f, to in enumerate((warm_out, salt_held)):
            rows_at = pl.ds(r, sea_levels, stride=sea_rows)
            to[rows_at, :] = to[rows_at, :] + mark * y[:sea_levels, f * width : (f + 1) * width]
    leave = [pltpu.make_async_copy(salt_held, brine_out, done.at[0])]
    leave[0].start()

    @pl.loop(0, levels // 8)
    def _(c):
        def other(ref, j):
            return ref[pl.ds(pl.multiple_of(j * stride + c * 8, 8), 8), :]

        top, low = ([other(ref, j) for j in range(HALO)] for ref in (above, below))
        none = jnp.zeros_like(top[0])
        for n in range(steps):
            top = stencil(top + [none]) + [top[-1]]
            low = [low[0]] + stencil([none] + low)
        for i, value in enumerate(top + low):
            spread[pl.ds(pl.multiple_of(i * depth + c * 8, 8), 8), :] = value

    w = weights[:, : 3 * depth]
    v = source_weights[:, :48]
    for g in range(rows // 8):
        to = result.at[g].reshape(levels * 8, width)
        for r in range(g * 8, g * 8 + 8, 2):
            x = [sources[(r + q) * 16 : (r + q + 1) * 16, :] for q in range(2)]
            if HALO <= r < rows - HALO:
                y = product(v, jnp.concatenate(x, 1))
            else:
                i = r if r < HALO else r - rows + 2 * HALO
                x = [
                    jnp.concatenate(
                        [spread[(i + q) * depth : (i + q) * depth + levels, :], x[q][: depth - levels]], 0
                    )
                    for q in range(2)
                ]
                y = product(w, jnp.concatenate(x, 1))
            for q in range(2):
                to[pl.ds((r + q) % 8, levels, stride=8), :] = (
                    middle[(r + q) * levels : (r + q + 1) * levels, :] + y[:levels, q * width : (q + 1) * width]
                )
        leave.append(pltpu.make_async_copy(result.at[g], out.at[:, g], done.at[1 + g]))
        leave[-1].start()
    for move in leave:
        move.wait()


def heat_kernel(sizes, topk, got, mine, shares, wet, sea_first, before, after):
    levels, rows, steps, sea_levels, sea_rows, stride, sea_stride = sizes
    width = before.shape[1]
    per = rows + 2 * topk
    group = width // rows
    me = mine[0].astype(f32)
    part = lax.broadcasted_iota(jnp.int32, (1, width), 1) // rows
    to = lax.broadcasted_iota(jnp.int32, (sea_rows, width), 0).astype(f32)
    picked = jnp.zeros((topk * sea_rows, width), f32)
    for g in range(got.shape[0] // (per * group)):
        at = [(g * group + i) * per for i in range(group)]
        mean = jnp.concatenate([got[a : a + rows, :] for a in at], 0).astype(bf16)
        table = got[at[0] + rows : at[0] + per, :]
        for i in range(1, group):
            table = jnp.where(part == i, got[at[i] + rows : at[i] + per, :], table)
        hot = []
        for k in range(topk):
            row = jnp.where(table[k : k + 1] == me, table[topk + k : topk + k + 1], -1.0)
            hot.append(jnp.where(to == row, 1.0, 0.0))
        hot = jnp.concatenate(hot, 0).astype(bf16)
        picked = picked + jnp.dot(hot, mean, preferred_element_type=f32)
    side = jnp.concatenate([picked[k * sea_rows : (k + 1) * sea_rows] for k in range(topk)], 1)
    first = side.astype(bf16).astype(f32)
    second = (side - first).astype(bf16).astype(f32)
    third = side - first - second
    parts = jnp.concatenate([first, second, third], 0).astype(bf16)
    y = jnp.dot(parts, shares[...], preferred_element_type=f32)
    heat = y[:sea_rows] + y[sea_rows : 2 * sea_rows] + y[2 * sea_rows :]
    heat = wet[...].astype(f32) * heat
    for l in range(sea_levels):
        after[l * sea_rows : (l + 1) * sea_rows, :] = (
            before[l * sea_rows : (l + 1) * sea_rows, :] + sea_first[l : l + 1, :] * heat
        )


def body(sky, forcing, curve, surface, rate, vmix, shares, owners, locals_, warmth, brine, wet, sea_mix):
    levels, rows, width = sky.shape
    steps = forcing.shape[0]
    sea_levels, sea_rows, _ = warmth.shape
    topk = owners.shape[1]
    stride = up_to(levels + steps + 3, 8)
    sea_stride = up_to(sea_levels, 16)
    sizes = (levels, rows, steps, sea_levels, sea_rows, stride, sea_stride)
    sky2, forcing2 = sky.reshape(-1, width), forcing.reshape(-1, width)
    warmth2, brine2 = warmth.reshape(-1, width), brine.reshape(-1, width)
    flat = lambda n, kind=f32: jax.ShapeDtypeStruct((n, width), kind)

    space = lambda *shape: pltpu.VMEM(shape, f32)
    length = HALO * stride + 2 * sea_stride + 8
    up, down = call(
        functools.partial(pack_kernel, sizes), [flat(length)] * 2,
        sky, forcing, surface, rate, warmth2, brine2, wet, moved=4 << 20, in_specs=[HBM] * 7, grant=FULL,
        scratch=[
            space(2, levels, 8, width), space(steps, rows, width), space(2, sea_levels * sea_rows, width),
            space(2, rows, width), pltpu.VMEM(wet.shape, wet.dtype), pltpu.SemaphoreType.DMA((8,)),
        ],
    )
    count = lax.axis_size(("tile", "comp"))
    above = lax.ppermute(down, ("tile", "comp"), [(i, i + 1) for i in range(count - 1)])
    below = lax.ppermute(up, ("tile", "comp"), [(i + 1, i) for i in range(count - 1)])

    depth = up_to(levels + 2 * steps, 16)
    mix_rows = up_to(levels, 16)
    sea_flat = flat(sea_levels * sea_rows)
    at = lax.axis_index(("tile", "comp")).astype(jnp.int32)[None]
    (rows_of_mix, source_rows, own, weights, source_weights, sea_weights, sea_first, middle, warm, salt, sea_ends) = call(
        functools.partial(local_kernel, sizes, count - 1),
        [
            flat((steps - 1) * levels), flat(8), flat((steps - 1) * rows),
            jax.ShapeDtypeStruct((mix_rows, 2 * width), bf16), flat(mix_rows, bf16),
            jax.ShapeDtypeStruct((sea_stride, 2 * width), bf16), flat(sea_stride), flat(rows * levels),
            sea_flat, sea_flat, flat(4 * sea_stride),
        ],
        at, vmix, curve[None], sea_mix, sky2, warmth2, brine2, wet,
        in_specs=[pl.BlockSpec(memory_space=pltpu.SMEM)] + [VMEM] * 7,
        scratch=[space(rows * depth, width), space(2, sea_rows * sea_stride, width)],
        flops=4 << 30, moved=8 << 20,
    )

    per = rows + 2 * topk
    tiles = lax.axis_size("tile")
    sent, fluxes = call(
        functools.partial(flux_kernel, sizes), [flat(tiles * per), flat(2 * steps * (rows + 2 * HALO))],
        sky[-1], forcing2, surface, rate, rows_of_mix, source_rows, own, owners.T, locals_.T, below, above,
        scratch=[space(2 * HALO * stride, width)], moved=2 << 20,
    )
    got = lax.all_to_all(sent.reshape(tiles, per, width), "tile", split_axis=0, concat_axis=0, tiled=True)
    got = got.reshape(-1, width)

    sky_out, salt, warm = call(
        functools.partial(rest_kernel, sizes),
        [jax.ShapeDtypeStruct((levels, rows // 8, 8, width), f32), sea_flat, sea_flat],
        fluxes, weights, source_weights, sea_weights, middle, warm, salt, sea_ends, wet, below, above,
        out_specs=[HBM, HBM, VMEM],
        scratch=[
            space(sea_levels * sea_rows, width), space(2 * HALO * depth, width), space(rows * 16, width),
            space(rows // 8, levels, 8, width), pltpu.SemaphoreType.DMA((1 + rows // 8,)),
        ],
        flops=2 << 30, moved=8 << 20,
    )
    mine = lax.axis_index("tile").astype(jnp.int32)[None]
    warm = call(
        functools.partial(heat_kernel, sizes, topk), flat(sea_levels * sea_rows),
        got, mine, shares.reshape(-1, width), wet, sea_first, warm,
        in_specs=[VMEM, pl.BlockSpec(memory_space=pltpu.SMEM)] + [VMEM] * 4, moved=2 << 20,
    )
    return sky_out.reshape(sky.shape), warm.reshape(warmth.shape), salt.reshape(brine.shape)


def solution(mesh):
    both = P(None, ("member", "tile", "comp"), None)
    one = P(("tile", "comp"), None)
    return jax.shard_map(
        body,
        mesh=mesh,
        in_specs=(
            both, both, P(), P(("member", "tile", "comp"), None), one, P(), P(), one, one, both, both, one, P(),
        ),
        out_specs=(both, both, both),
        check_vma=False,
    )
```

```python
import functools

import jax
import jax.numpy as jnp
from jax import lax
from jax.experimental import pallas as pl
from jax.experimental.pallas import tpu as pltpu
from jax.sharding import PartitionSpec as P

atm_diffusion = 0.2
ocean_diffusion = 0.2
HALO = 4
FULL = 60
ROOM = 20
EXACT = lax.Precision.HIGHEST
VMEM = pl.BlockSpec(memory_space=pltpu.VMEM)
HBM = pl.BlockSpec(memory_space=pltpu.HBM)
f32, bf16 = jnp.float32, jnp.bfloat16


def up_to(n, m):
    return -(-n // m) * m


def call(kernel, out_shape, *args, scratch=(), in_specs=None, out_specs=None, flops=0, moved=0, grant=24):
    return pl.pallas_call(
        kernel,
        out_shape=out_shape,
        in_specs=in_specs or [VMEM] * len(args),
        out_specs=out_specs or jax.tree.map(lambda _: VMEM, out_shape),
        scratch_shapes=list(scratch),
        compiler_params=pltpu.CompilerParams(vmem_limit_bytes=grant * 2**20),
        cost_estimate=pl.CostEstimate(flops=flops, bytes_accessed=moved, transcendentals=0),
    )(*args)


def copies(pairs, done):
    return [pltpu.make_async_copy(src, dst, done.at[i]) for i, (src, dst) in enumerate(pairs)]


def pack_kernel(
    sizes, sky, forcing, surface, rate, warmth, brine, wet, up, down,
    ends, force, sea, flat, marks, done
):
    levels, rows, steps, sea_levels, sea_rows, stride, sea_stride = sizes
    width = sky.shape[2]
    low = rows - 8
    moves = copies(
        [
            (sky.at[:, 0:8, :], ends.at[0]), (sky.at[:, low:rows, :], ends.at[1]), (forcing, force),
            (surface, flat.at[0]), (rate, flat.at[1]), (warmth, sea.at[0]), (brine, sea.at[1]), (wet, marks),
        ],
        done,
    )
    for move in moves:
        move.start()
    for move in moves:
        move.wait()
    m = marks[...].astype(f32)
    for which, out, first, sea_row in ((0, up, 0, 0), (1, down, rows - HALO, sea_rows - 1)):
        end = ends.at[which].reshape(levels * 8, width)
        for j in range(HALO):
            row = first + j
            out[j * stride : j * stride + levels, :] = end[pl.ds(row - which * low, levels, stride=8), :]
            base = j * stride + levels
            tail = [force[s, row : row + 1, :] for s in range(steps)]
            tail += [flat[0, row : row + 1, :], flat[1, row : row + 1, :], jnp.ones((1, width), f32)]
            tail += [jnp.zeros((stride - levels - len(tail), width), f32)]
            out[base : (j + 1) * stride, :] = jnp.concatenate(tail, 0)
        base = HALO * stride
        edge = m[sea_row : sea_row + 1]
        for f in range(2):
            out[base : base + sea_levels, :] = sea[f, pl.ds(sea_row, sea_levels, stride=sea_rows), :] * edge
            base += sea_stride
        out[base : base + 8, :] = jnp.concatenate([edge, jnp.zeros((7, width), f32)], 0)


def split(x):
    high = x.astype(bf16)
    return high, (x - high.astype(f32)).astype(bf16)


def three_terms(w, depth):
    high = w.astype(bf16).astype(f32)
    low = w - high
    return (high + pltpu.roll(high, depth, 1) + pltpu.roll(low, 2 * depth, 1)).astype(bf16)


def row_of(ref, first, count, step, size):
    x = ref[pl.ds(first, count, stride=step), :]
    if count < size:
        x = jnp.concatenate([x, jnp.zeros((size - count, x.shape[1]), f32)], 0)
    return x


def beside(x):
    return pltpu.roll(x, 1, 1) + pltpu.roll(x, x.shape[1] - 1, 1)


def stencil(x):
    return [x[i - 1] + x[i] + x[i + 1] + beside(x[i]) for i in range(1, len(x) - 1)]


def product(weights, x):
    high, low = split(x)
    return jnp.dot(weights, jnp.concatenate([high, low, high], 0), preferred_element_type=f32)


def local_kernel(
    sizes, last_place, place, vmix, curve, sea_mix, sky, warmth, brine, wet,
    rows_of_mix, source_rows, own, weights, source_weights, sea_weights, sea_first, sea_ends, store,
    middle, warm_out, brine_out, spread, sea_spread, done,
):
    levels, rows, steps, sea_levels, sea_rows, stride, sea_stride = sizes
    width = sky.shape[1]
    depth = up_to(levels + 2 * steps, 16)
    v = vmix[...]
    dot = functools.partial(jnp.dot, precision=EXACT, preferred_element_type=f32)
    powers = [v]
    for _ in range(steps - 1):
        powers.append(dot(v, powers[-1]))
    last = (lax.broadcasted_iota(jnp.int32, (levels, width), 0) == levels - 1).astype(f32)
    for s in range(1, steps):
        rows_of_mix[(s - 1) * levels : s * levels, :] = lax.dot_general(
            powers[s - 1], last, (((0,), (0,)), ((), ())), precision=EXACT, preferred_element_type=f32
        )
    by_curve = jnp.broadcast_to(curve[...], (width, levels))
    of_curve = [
        lax.dot_general(p, by_curve, (((1,), (1,)), ((), ())), precision=EXACT, preferred_element_type=f32)
        for p in powers
    ]
    of_last = [jnp.broadcast_to(p[:, levels - 1 : levels], (levels, width)) for p in powers]
    found = [of_curve[i][levels - 1 :] for i in range(steps - 1)]
    found += [of_last[i][levels - 1 :] for i in range(steps - 1)]
    found += [jnp.zeros((8 - len(found), width), f32)]
    source_rows[...] = jnp.concatenate(found, 0)
    lane = lax.broadcasted_iota(jnp.int32, (levels, width), 1)
    wide = jnp.concatenate(
        [powers[-1] * atm_diffusion**steps, jnp.zeros((levels, width - levels), f32)], 1
    )
    sources = jnp.zeros((levels, width), f32)
    for j in range(steps):
        factor = atm_diffusion ** (steps - 1 - j)
        for at, value in ((j, of_curve[steps - 1 - j] * factor), (steps + j, of_last[steps - 1 - j] * -factor)):
            wide = jnp.where(lane == levels + at, value, wide)
            sources = jnp.where(lane == at, value, sources)
    more = jnp.zeros((weights.shape[0] - levels, width), f32)
    wide = jnp.concatenate([wide, more], 0)
    wide = jnp.concatenate([wide, jnp.zeros_like(wide)], 1)
    weights[...] = three_terms(wide, depth)
    source_weights[...] = three_terms(jnp.concatenate([sources, more], 0), 16)
    sea = sea_mix[...]
    sea = jnp.concatenate([sea, jnp.zeros((sea_levels, 2 * width - sea_levels), f32)], 1)
    sea = jnp.concatenate([sea, jnp.zeros((sea_stride - sea_levels, 2 * width), f32)], 0)
    sea_weights[...] = three_terms(sea, sea_stride)
    sea_first[...] = jnp.broadcast_to(sea[:, 0:1], sea_first.shape)
    sums = [jnp.zeros((rows, width), f32) for _ in range(steps - 1)]
    for l in range(levels):
        x = sky[l * rows : (l + 1) * rows, :]
        for s in range(steps - 1):
            sums[s] = sums[s] + rows_of_mix[s * levels + l : s * levels + l + 1, :] * x
    for s in range(steps - 1):
        own[s * rows : (s + 1) * rows, :] = sums[s]

    m = wet[...].astype(f32)
    mark = [m[r : r + 1] for r in range(sea_rows)]
    edge = jnp.zeros((1, width), f32)

    def near(x):
        x = [jnp.zeros_like(x[0])] + x + [jnp.zeros_like(x[0])]
        return [x[i - 1] + x[i + 1] + beside(x[i]) for i in range(1, len(x) - 1)]

    around = (
        jnp.concatenate([edge, m[:-1]], 0) + jnp.concatenate([m[1:], edge], 0) + beside(m)
    ) * ocean_diffusion
    share = [around[r : r + 1] for r in range(sea_rows)]
    for f, field in enumerate((warmth, brine)):
        for c in range(sea_stride // 8):
            count = min(8, sea_levels - c * 8)
            x = [row_of(field, c * 8 * sea_rows + r, count, sea_rows, 8) for r in range(sea_rows)]
            y = near([mark[r] * x[r] for r in range(sea_rows)])
            for r in range(sea_rows):
                at = r * sea_stride + c * 8
                sea_spread[f, at : at + 8, :] = x[r] + mark[r] * (ocean_diffusion * y[r] - x[r] * share[r])
    w = sea_weights[:, : 3 * sea_stride]
    for r in range(sea_rows):
        x = jnp.concatenate([sea_spread[f, r * sea_stride : (r + 1) * sea_stride, :] for f in range(2)], 1)
        y = product(w, x)
        for f, (field, out) in enumerate(((warmth, warm_out), (brine, brine_out))):
            old = field[pl.ds(r, sea_levels, stride=sea_rows), :]
            new = y[:sea_levels, f * width : (f + 1) * width]
            out[pl.ds(r, sea_levels, stride=sea_rows), :] = mark[r] * new + (1.0 - mark[r]) * old
            if r in (0, sea_rows - 1):
                at = (2 * f + (r > 0)) * sea_stride
                sea_ends[at : at + sea_levels, :] = old
    area = sea_levels * sea_rows
    leave = []
    for f, out in enumerate((warm_out, brine_out)):
        part = store.at[pl.ds(rows * levels + f * area, area)]
        leave.append(pltpu.make_async_copy(out, part, done.at[rows // 8 + f]))
        leave[-1].start()

    before = jnp.where(place[0] > 0, 1.0, 0.0)
    behind = jnp.where(place[0] < last_place, 1.0, 0.0)

    @pl.loop(0, levels // 8)
    def _(c):
        x = [sky[pl.ds(c * 8 * rows + r, 8, stride=rows), :] for r in range(rows)]
        none = jnp.zeros_like(x[0])
        beyond = 0
        for n in range(steps):
            if beyond < steps - 1 - n:
                x = [x[0]] + stencil([none] + x + [none]) + [x[-1]]
                beyond += 1
            else:
                x = stencil(x)
                beyond -= 1
            for i in range(beyond):
                x[i] = x[i] * before
                x[-1 - i] = x[-1 - i] * behind
        for r in range(rows):
            spread[pl.ds(pl.multiple_of(r * depth + c * 8, 8), 8), :] = x[r]

    if depth > levels:
        for r in range(rows):
            spread[r * depth + levels : (r + 1) * depth, :] = jnp.zeros((depth - levels, width), f32)
    w = weights[:, : 3 * depth]
    for r in range(0, rows, 2):
        x = jnp.concatenate([spread[(r + i) * depth : (r + i + 1) * depth, :] for i in range(2)], 1)
        y = product(w, x)
        for i in range(2):
            middle[(r + i) * levels : (r + i + 1) * levels, :] = y[:levels, i * width : (i + 1) * width]
        if (r + 2) % 8 == 0:
            part = pl.ds((r - 6) * levels, 8 * levels)
            leave.append(pltpu.make_async_copy(middle.at[part], store.at[part], done.at[r // 8]))
            leave[-1].start()
    for move in leave:
        move.wait()


def cross(x):
    n, w = x.shape
    return (
        x + pltpu.roll(x, 1, 0) + pltpu.roll(x, n - 1, 0) + pltpu.roll(x, 1, 1) + pltpu.roll(x, w - 1, 1)
    )


def masked(x, rows, inside):
    return jnp.concatenate([x[:rows], x[rows:] * inside], 0)


def flux_kernel(
    sizes, sky, forcing, surface, rate, rows_of_mix, source_rows, own, owners, locals_, shares, below, above,
    sent, fluxes, halo
):
    levels, rows, steps, sea_levels, sea_rows, stride, sea_stride = sizes
    width = sky.shape[1]
    halo[: HALO * stride, :] = below[: HALO * stride, :]
    halo[HALO * stride :, :] = above[: HALO * stride, :]

    def edge(l):
        return halo[pl.ds(l, 2 * HALO, stride=stride), :]

    inside = edge(levels + steps + 2)
    sums = [jnp.zeros((2 * HALO, width), f32) for _ in range(steps - 1)]
    for l in range(levels):
        x = edge(l)
        for s in range(steps - 1):
            sums[s] = sums[s] + rows_of_mix[s * levels + l : s * levels + l + 1, :] * x
    tops = [jnp.concatenate([sky[...], edge(levels - 1)], 0)]
    tops += [jnp.concatenate([own[s * rows : (s + 1) * rows, :], sums[s]], 0) for s in range(steps - 1)]
    surf = jnp.concatenate([surface[...], edge(levels + steps)], 0)
    coef = jnp.concatenate([rate[...], edge(levels + steps + 1)], 0)
    force = [
        jnp.concatenate([forcing[s * rows : (s + 1) * rows, :], edge(levels + s)], 0) for s in range(steps)
    ]

    flux = []
    for s in range(steps):
        state = tops[s]
        for i in range(s):
            m = s - 1 - i
            state = masked(cross(state) * atm_diffusion, rows, inside)
            state = state + source_rows[m : m + 1, :] * force[i]
            state = state - source_rows[steps - 1 + m : steps + m, :] * flux[i]
        flux.append(coef * (state - surf))
        reach = rows + 2 * HALO
        fluxes[pl.ds(s, reach, stride=2 * steps), :] = force[s]
        fluxes[pl.ds(steps + s, reach, stride=2 * steps), :] = flux[s]
    total = flux[0][:rows]
    for s in range(1, steps):
        total = total + flux[s][:rows]
    mean = (total / steps).astype(bf16)
    topk = owners.shape[0]
    target = owners[...] * sea_rows + locals_[...]
    target = jnp.concatenate([target[k : k + 1, :] for k in range(topk)], 1)
    rowed = jnp.concatenate(
        [jnp.dot(mean, shares[k * width : (k + 1) * width, :], preferred_element_type=f32) for k in range(topk)], 0
    )
    first = rowed.astype(bf16)
    left = rowed - first.astype(f32)
    second = left.astype(bf16)
    third = (left - second.astype(f32)).astype(bf16)
    hot = lax.broadcasted_iota(jnp.int32, (sent.shape[0], topk * rows), 0) == target
    hot = jnp.where(hot, 1.0, 0.0).astype(bf16)
    sent[...] = jnp.dot(
        jnp.concatenate([hot, hot, hot], 1), jnp.concatenate([first, second, third], 0), preferred_element_type=f32
    )


def rest_kernel(
    sizes, fluxes, weights, source_weights, sea_weights, sea_ends, wet, below, above, store,
    out, brine_out, warm_out, salt_held, middle, spread, sources, result, done
):
    levels, rows, steps, sea_levels, sea_rows, stride, sea_stride = sizes
    width = above.shape[1]
    depth = up_to(levels + 2 * steps, 16)
    area = sea_levels * sea_rows
    fetches = [
        pltpu.make_async_copy(store.at[pl.ds(first, to.shape[0])], to, done.at[i])
        for i, (first, to) in enumerate(
            ((rows * levels, warm_out), (rows * levels + area, salt_held), (0, middle))
        )
    ]
    for fetch in fetches:
        fetch.start()
    flag = levels + steps + 2
    inside_above, inside_below = above[flag : flag + 1, :], below[flag : flag + 1, :]

    reach = rows + 2 * HALO
    x = [fluxes[(r % reach) * 2 * steps : (r % reach + 1) * 2 * steps, :] for r in range(1 - steps, rows + steps - 1)]
    field = lax.broadcasted_iota(jnp.int32, (2 * steps, width), 0) % steps
    for n in range(1, steps):
        y = stencil(x)
        x = [jnp.where(field < steps - n, y[i], x[i + 1]) for i in range(len(y))]
        for i in range(steps - 1 - n):
            x[i] = x[i] * inside_above
            x[-1 - i] = x[-1 - i] * inside_below
    for r in range(rows):
        sources[r * 16 : (r + 1) * 16, :] = jnp.concatenate([x[r], jnp.zeros((16 - 2 * steps, width), f32)], 0)

    @pl.loop(0, levels // 8)
    def _(c):
        def other(ref, j):
            return ref[pl.ds(pl.multiple_of(j * stride + c * 8, 8), 8), :]

        top, low = ([other(ref, j) for j in range(HALO)] for ref in (above, below))
        none = jnp.zeros_like(top[0])
        for n in range(steps):
            top = stencil(top + [none]) + [top[-1]]
            low = [low[0]] + stencil([none] + low)
        for i, value in enumerate(top + low):
            spread[pl.ds(pl.multiple_of(i * depth + c * 8, 8), 8), :] = value

    for fetch in fetches[:2]:
        fetch.wait()
    m = wet[...].astype(f32)
    base = HALO * stride
    w = sea_weights[:, : 3 * sea_stride]
    for e, (r, other) in enumerate(((0, above), (sea_rows - 1, below))):
        mark = m[r : r + 1]
        far = other[base + 2 * sea_stride : base + 2 * sea_stride + 1, :]
        x = []
        for f in range(2):
            at = base + f * sea_stride
            mine = (2 * f + e) * sea_stride
            step = other[at : at + sea_levels, :] - sea_ends[mine : mine + sea_levels, :] * far
            step = ocean_diffusion * (mark * step)
            x.append(jnp.concatenate([step, jnp.zeros((sea_stride - sea_levels, width), f32)], 0))
        y = product(w, jnp.concatenate(x, 1))
        for f, to in enumerate((warm_out, salt_held)):
            rows_at = pl.ds(r, sea_levels, stride=sea_rows)
            to[rows_at, :] = to[rows_at, :] + mark * y[:sea_levels, f * width : (f + 1) * width]
    leave = [pltpu.make_async_copy(salt_held, brine_out, done.at[3])]
    leave[0].start()

    fetches[2].wait()
    w = weights[:, : 3 * depth]
    v = source_weights[:, :48]
    for g in range(rows // 8):
        to = result.at[g].reshape(levels * 8, width)
        for r in range(g * 8, g * 8 + 8, 2):
            x = [sources[(r + q) * 16 : (r + q + 1) * 16, :] for q in range(2)]
            if HALO <= r < rows - HALO:
                y = product(v, jnp.concatenate(x, 1))
            else:
                i = r if r < HALO else r - rows + 2 * HALO
                x = [
                    jnp.concatenate(
                        [spread[(i + q) * depth : (i + q) * depth + levels, :], x[q][: depth - levels]], 0
                    )
                    for q in range(2)
                ]
                y = product(w, jnp.concatenate(x, 1))
            for q in range(2):
                to[pl.ds((r + q) % 8, levels, stride=8), :] = (
                    middle[(r + q) * levels : (r + q + 1) * levels, :] + y[:levels, q * width : (q + 1) * width]
                )
        leave.append(pltpu.make_async_copy(result.at[g], out.at[:, g], done.at[4 + g]))
        leave[-1].start()
    for move in leave:
        move.wait()


def heat_kernel(sizes, got, wet, sea_first, before, after):
    levels, rows, steps, sea_levels, sea_rows, stride, sea_stride = sizes
    heat = got[:sea_rows, :]
    for t in range(1, got.shape[0] // sea_rows):
        heat = heat + got[t * sea_rows : (t + 1) * sea_rows, :]
    heat = wet[...].astype(f32) * heat
    for l in range(sea_levels):
        after[l * sea_rows : (l + 1) * sea_rows, :] = (
            before[l * sea_rows : (l + 1) * sea_rows, :] + sea_first[l : l + 1, :] * heat
        )


def body(sky, forcing, curve, surface, rate, vmix, shares, owners, locals_, warmth, brine, wet, sea_mix):
    levels, rows, width = sky.shape
    steps = forcing.shape[0]
    sea_levels, sea_rows, _ = warmth.shape
    topk = owners.shape[1]
    stride = up_to(levels + steps + 3, 8)
    sea_stride = up_to(sea_levels, 16)
    sizes = (levels, rows, steps, sea_levels, sea_rows, stride, sea_stride)
    sky2, forcing2 = sky.reshape(-1, width), forcing.reshape(-1, width)
    warmth2, brine2 = warmth.reshape(-1, width), brine.reshape(-1, width)
    flat = lambda n, kind=f32: jax.ShapeDtypeStruct((n, width), kind)

    space = lambda *shape: pltpu.VMEM(shape, f32)
    length = HALO * stride + 2 * sea_stride + 8
    up, down = call(
        functools.partial(pack_kernel, sizes), [flat(length)] * 2,
        sky, forcing, surface, rate, warmth2, brine2, wet, moved=4 << 20, in_specs=[HBM] * 7, grant=FULL,
        scratch=[
            space(2, levels, 8, width), space(steps, rows, width), space(2, sea_levels * sea_rows, width),
            space(2, rows, width), pltpu.VMEM(wet.shape, wet.dtype), pltpu.SemaphoreType.DMA((8,)),
        ],
    )
    count = lax.axis_size(("tile", "comp"))
    above = lax.ppermute(down, ("tile", "comp"), [(i, i + 1) for i in range(count - 1)])
    below = lax.ppermute(up, ("tile", "comp"), [(i + 1, i) for i in range(count - 1)])

    depth = up_to(levels + 2 * steps, 16)
    mix_rows = up_to(levels, 16)
    sea_flat = flat(sea_levels * sea_rows)
    at = lax.axis_index(("tile", "comp")).astype(jnp.int32)[None]
    area = sea_levels * sea_rows
    large = max(rows * levels + 2 * area, ROOM * 2**20 // (4 * width))
    (rows_of_mix, source_rows, own, weights, source_weights, sea_weights, sea_first, sea_ends, store) = call(
        functools.partial(local_kernel, sizes, count - 1),
        [
            flat((steps - 1) * levels), flat(8), flat((steps - 1) * rows),
            jax.ShapeDtypeStruct((mix_rows, 2 * width), bf16), flat(mix_rows, bf16),
            jax.ShapeDtypeStruct((sea_stride, 2 * width), bf16), flat(sea_stride), flat(4 * sea_stride),
            flat(large),
        ],
        at, vmix, curve[None], sea_mix, sky2, warmth2, brine2, wet,
        in_specs=[pl.BlockSpec(memory_space=pltpu.SMEM)] + [VMEM] * 7, out_specs=[VMEM] * 8 + [HBM],
        scratch=[
            space(rows * levels, width), space(area, width), space(area, width),
            space(rows * depth, width), space(2, sea_rows * sea_stride, width),
            pltpu.SemaphoreType.DMA((rows // 8 + 2,)),
        ],
        flops=4 << 30, moved=8 << 20, grant=48,
    )

    tiles = lax.axis_size("tile")
    sent, fluxes = call(
        functools.partial(flux_kernel, sizes), [flat(tiles * sea_rows), flat(2 * steps * (rows + 2 * HALO))],
        sky[-1], forcing2, surface, rate, rows_of_mix, source_rows, own, owners.T, locals_.T,
        shares.reshape(-1, width), below, above,
        scratch=[space(2 * HALO * stride, width)], moved=2 << 20,
    )
    got = lax.all_to_all(sent.reshape(tiles, sea_rows, width), "tile", split_axis=0, concat_axis=0, tiled=True)
    got = got.reshape(-1, width)

    sky_out, salt, warm = call(
        functools.partial(rest_kernel, sizes),
        [jax.ShapeDtypeStruct((levels, rows // 8, 8, width), f32), sea_flat, sea_flat],
        fluxes, weights, source_weights, sea_weights, sea_ends, wet, below, above, store,
        in_specs=[VMEM] * 8 + [HBM], out_specs=[HBM, HBM, VMEM],
        scratch=[
            space(area, width), space(rows * levels, width), space(2 * HALO * depth, width), space(rows * 16, width),
            space(rows // 8, levels, 8, width), pltpu.SemaphoreType.DMA((4 + rows // 8,)),
        ],
        flops=2 << 30, moved=8 << 20, grant=48,
    )
    warm = call(functools.partial(heat_kernel, sizes), sea_flat, got, wet, sea_first, warm, moved=2 << 20)
    return sky_out.reshape(sky.shape), warm.reshape(warmth.shape), salt.reshape(brine.shape)


def solution(mesh):
    both = P(None, ("member", "tile", "comp"), None)
    one = P(("tile", "comp"), None)
    return jax.shard_map(
        body,
        mesh=mesh,
        in_specs=(
            both, both, P(), P(("member", "tile", "comp"), None), one, P(), P(), one, one, both, both, one, P(),
        ),
        out_specs=(both, both, both),
        check_vma=False,
    )
```

```python
import functools

import jax
import jax.numpy as jnp
from jax import lax
from jax.experimental import pallas as pl
from jax.experimental.pallas import tpu as pltpu
from jax.sharding import PartitionSpec as P

atm_diffusion = 0.2
ocean_diffusion = 0.2
HALO = 4
FULL = 60
EXACT = lax.Precision.HIGHEST
VMEM = pl.BlockSpec(memory_space=pltpu.VMEM)
HBM = pl.BlockSpec(memory_space=pltpu.HBM)
SMEM = pl.BlockSpec(memory_space=pltpu.SMEM)
f32, bf16 = jnp.float32, jnp.bfloat16


def up_to(n, m):
    return -(-n // m) * m


def call(kernel, out_shape, *args, scratch=(), in_specs=None, out_specs=None, flops=0, moved=0, grant=24):
    return pl.pallas_call(
        kernel,
        out_shape=out_shape,
        in_specs=in_specs or [VMEM] * len(args),
        out_specs=out_specs or jax.tree.map(lambda _: VMEM, out_shape),
        scratch_shapes=list(scratch),
        compiler_params=pltpu.CompilerParams(vmem_limit_bytes=grant * 2**20),
        cost_estimate=pl.CostEstimate(flops=flops, bytes_accessed=moved, transcendentals=0),
    )(*args)


def copies(pairs, done):
    return [pltpu.make_async_copy(src, dst, done.at[i]) for i, (src, dst) in enumerate(pairs)]


def pack_kernel(
    sizes, core, sky, forcing, surface, rate, warmth, brine, wet, inner, outer,
    ends, force, sea, flat, marks, done
):
    levels, rows, steps, sea_levels, sea_rows, stride, sea_stride = sizes
    width = sky.shape[2]
    low = rows - 8
    moves = copies(
        [
            (sky.at[:, 0:8, :], ends.at[0]), (sky.at[:, low:rows, :], ends.at[1]), (forcing, force),
            (surface, flat.at[0]), (rate, flat.at[1]), (warmth, sea.at[0]), (brine, sea.at[1]), (wet, marks),
        ],
        done,
    )
    for move in moves:
        move.start()
    for move in moves:
        move.wait()
    end = ends.reshape(2 * levels * 8, width)
    for which, out in enumerate((inner, outer)):
        last = jnp.where(core[0] == 0, 1 - which, which)
        sea_row = last * (sea_rows - 1)
        for j in range(HALO):
            row = last * (rows - HALO) + j
            first = last * (levels * 8 + 8 - HALO) + j
            out[j * stride : j * stride + levels, :] = end[pl.ds(first, levels, stride=8), :]
            base = j * stride + levels
            tail = [force[s, pl.ds(row, 1), :] for s in range(steps)]
            tail += [flat[0, pl.ds(row, 1), :], flat[1, pl.ds(row, 1), :], jnp.ones((1, width), f32)]
            tail += [jnp.zeros((stride - levels - len(tail), width), f32)]
            out[base : (j + 1) * stride, :] = jnp.concatenate(tail, 0)
        base = HALO * stride
        edge = marks[pl.ds(sea_row, 1), :].astype(f32)
        for f in range(2):
            out[base : base + sea_levels, :] = sea[f, pl.ds(sea_row, sea_levels, stride=sea_rows), :] * edge
            base += sea_stride
        out[base : base + 8, :] = jnp.concatenate([edge, jnp.zeros((7, width), f32)], 0)


def split(x):
    high = x.astype(bf16)
    return high, (x - high.astype(f32)).astype(bf16)


def three_terms(w, depth):
    high = w.astype(bf16).astype(f32)
    low = w - high
    return (high + pltpu.roll(high, depth, 1) + pltpu.roll(low, 2 * depth, 1)).astype(bf16)


def row_of(ref, first, count, step, size):
    x = ref[pl.ds(first, count, stride=step), :]
    if count < size:
        x = jnp.concatenate([x, jnp.zeros((size - count, x.shape[1]), f32)], 0)
    return x


def beside(x):
    return pltpu.roll(x, 1, 1) + pltpu.roll(x, x.shape[1] - 1, 1)


def stencil(x):
    return [x[i - 1] + x[i] + x[i + 1] + beside(x[i]) for i in range(1, len(x) - 1)]


def product(weights, x):
    high, low = split(x)
    return jnp.dot(weights, jnp.concatenate([high, low, high], 0), preferred_element_type=f32)


def local_kernel(
    sizes, last_place, place, vmix, curve, sea_mix, sky, warmth, brine, wet,
    rows_of_mix, source_rows, own, weights, source_weights, sea_weights, sea_first, sea_ends,
    middle, warm_out, brine_out, spread, sea_spread,
):
    levels, rows, steps, sea_levels, sea_rows, stride, sea_stride = sizes
    width = sky.shape[1]
    depth = up_to(levels + 2 * steps, 16)
    v = vmix[...]
    dot = functools.partial(jnp.dot, precision=EXACT, preferred_element_type=f32)
    powers = [v]
    for _ in range(steps - 1):
        powers.append(dot(v, powers[-1]))
    last = (lax.broadcasted_iota(jnp.int32, (levels, width), 0) == levels - 1).astype(f32)
    for s in range(1, steps):
        rows_of_mix[(s - 1) * levels : s * levels, :] = lax.dot_general(
            powers[s - 1], last, (((0,), (0,)), ((), ())), precision=EXACT, preferred_element_type=f32
        )
    by_curve = jnp.broadcast_to(curve[...], (width, levels))
    of_curve = [
        lax.dot_general(p, by_curve, (((1,), (1,)), ((), ())), precision=EXACT, preferred_element_type=f32)
        for p in powers
    ]
    of_last = [jnp.broadcast_to(p[:, levels - 1 : levels], (levels, width)) for p in powers]
    found = [of_curve[i][levels - 1 :] for i in range(steps - 1)]
    found += [of_last[i][levels - 1 :] for i in range(steps - 1)]
    found += [jnp.zeros((8 - len(found), width), f32)]
    source_rows[...] = jnp.concatenate(found, 0)
    lane = lax.broadcasted_iota(jnp.int32, (levels, width), 1)
    wide = jnp.concatenate(
        [powers[-1] * atm_diffusion**steps, jnp.zeros((levels, width - levels), f32)], 1
    )
    sources = jnp.zeros((levels, width), f32)
    for j in range(steps):
        factor = atm_diffusion ** (steps - 1 - j)
        for at, value in ((j, of_curve[steps - 1 - j] * factor), (steps + j, of_last[steps - 1 - j] * -factor)):
            wide = jnp.where(lane == levels + at, value, wide)
            sources = jnp.where(lane == at, value, sources)
    more = jnp.zeros((weights.shape[0] - levels, width), f32)
    wide = jnp.concatenate([wide, more], 0)
    wide = jnp.concatenate([wide, jnp.zeros_like(wide)], 1)
    weights[...] = three_terms(wide, depth)
    source_weights[...] = three_terms(jnp.concatenate([sources, more], 0), 16)
    sea = sea_mix[...]
    sea = jnp.concatenate([sea, jnp.zeros((sea_levels, 2 * width - sea_levels), f32)], 1)
    sea = jnp.concatenate([sea, jnp.zeros((sea_stride - sea_levels, 2 * width), f32)], 0)
    sea_weights[...] = three_terms(sea, sea_stride)
    sea_first[...] = jnp.broadcast_to(sea[:, 0:1], sea_first.shape)
    sums = [jnp.zeros((rows, width), f32) for _ in range(steps - 1)]
    for l in range(levels):
        x = sky[l * rows : (l + 1) * rows, :]
        for s in range(steps - 1):
            sums[s] = sums[s] + rows_of_mix[s * levels + l : s * levels + l + 1, :] * x
    for s in range(steps - 1):
        own[s * rows : (s + 1) * rows, :] = sums[s]

    m = wet[...].astype(f32)
    mark = [m[r : r + 1] for r in range(sea_rows)]
    edge = jnp.zeros((1, width), f32)

    def near(x):
        x = [jnp.zeros_like(x[0])] + x + [jnp.zeros_like(x[0])]
        return [x[i - 1] + x[i + 1] + beside(x[i]) for i in range(1, len(x) - 1)]

    around = (
        jnp.concatenate([edge, m[:-1]], 0) + jnp.concatenate([m[1:], edge], 0) + beside(m)
    ) * ocean_diffusion
    share = [around[r : r + 1] for r in range(sea_rows)]
    for f, field in enumerate((warmth, brine)):
        for c in range(sea_stride // 8):
            count = min(8, sea_levels - c * 8)
            x = [row_of(field, c * 8 * sea_rows + r, count, sea_rows, 8) for r in range(sea_rows)]
            y = near([mark[r] * x[r] for r in range(sea_rows)])
            for r in range(sea_rows):
                at = r * sea_stride + c * 8
                sea_spread[f, at : at + 8, :] = x[r] + mark[r] * (ocean_diffusion * y[r] - x[r] * share[r])
    w = sea_weights[:, : 3 * sea_stride]
    for r in range(sea_rows):
        x = jnp.concatenate([sea_spread[f, r * sea_stride : (r + 1) * sea_stride, :] for f in range(2)], 1)
        y = product(w, x)
        for f, (field, out) in enumerate(((warmth, warm_out), (brine, brine_out))):
            old = field[pl.ds(r, sea_levels, stride=sea_rows), :]
            new = y[:sea_levels, f * width : (f + 1) * width]
            out[pl.ds(r, sea_levels, stride=sea_rows), :] = mark[r] * new + (1.0 - mark[r]) * old
            if r in (0, sea_rows - 1):
                at = (2 * f + (r > 0)) * sea_stride
                sea_ends[at : at + sea_levels, :] = old

    before = jnp.where(place[0] > 0, 1.0, 0.0)
    behind = jnp.where(place[0] < last_place, 1.0, 0.0)

    @pl.loop(0, levels // 8)
    def _(c):
        x = [sky[pl.ds(c * 8 * rows + r, 8, stride=rows), :] for r in range(rows)]
        none = jnp.zeros_like(x[0])
        beyond = 0
        for n in range(steps):
            if beyond < steps - 1 - n:
                x = [x[0]] + stencil([none] + x + [none]) + [x[-1]]
                beyond += 1
            else:
                x = stencil(x)
                beyond -= 1
            for i in range(beyond):
                x[i] = x[i] * before
                x[-1 - i] = x[-1 - i] * behind
        for r in range(rows):
            spread[pl.ds(pl.multiple_of(r * depth + c * 8, 8), 8), :] = x[r]

    if depth > levels:
        for r in range(rows):
            spread[r * depth + levels : (r + 1) * depth, :] = jnp.zeros((depth - levels, width), f32)
    w = weights[:, : 3 * depth]
    for r in range(0, rows, 2):
        x = jnp.concatenate([spread[(r + i) * depth : (r + i + 1) * depth, :] for i in range(2)], 1)
        y = product(w, x)
        for i in range(2):
            middle[(r + i) * levels : (r + i + 1) * levels, :] = y[:levels, i * width : (i + 1) * width]


def cross(x):
    n, w = x.shape
    return (
        x + pltpu.roll(x, 1, 0) + pltpu.roll(x, n - 1, 0) + pltpu.roll(x, 1, 1) + pltpu.roll(x, w - 1, 1)
    )


def masked(x, rows, inside):
    return jnp.concatenate([x[:rows], x[rows:] * inside], 0)


def flux_kernel(
    sizes, core, tile, sky, forcing, surface, rate, rows_of_mix, source_rows, own, owners, locals_, shares, inner, outer,
    keep, send, fluxes, above, below, halo
):
    levels, rows, steps, sea_levels, sea_rows, stride, sea_stride = sizes
    width = sky.shape[1]
    one, two = inner[...], outer[...]
    above[...] = jnp.where(core[0] == 0, two, one)
    below[...] = jnp.where(core[0] == 0, one, two)
    halo[: HALO * stride, :] = below[: HALO * stride, :]
    halo[HALO * stride :, :] = above[: HALO * stride, :]

    def edge(l):
        return halo[pl.ds(l, 2 * HALO, stride=stride), :]

    inside = edge(levels + steps + 2)
    sums = [jnp.zeros((2 * HALO, width), f32) for _ in range(steps - 1)]
    for l in range(levels):
        x = edge(l)
        for s in range(steps - 1):
            sums[s] = sums[s] + rows_of_mix[s * levels + l : s * levels + l + 1, :] * x
    tops = [jnp.concatenate([sky[...], edge(levels - 1)], 0)]
    tops += [jnp.concatenate([own[s * rows : (s + 1) * rows, :], sums[s]], 0) for s in range(steps - 1)]
    surf = jnp.concatenate([surface[...], edge(levels + steps)], 0)
    coef = jnp.concatenate([rate[...], edge(levels + steps + 1)], 0)
    force = [
        jnp.concatenate([forcing[s * rows : (s + 1) * rows, :], edge(levels + s)], 0) for s in range(steps)
    ]

    flux = []
    for s in range(steps):
        state = tops[s]
        for i in range(s):
            m = s - 1 - i
            state = masked(cross(state) * atm_diffusion, rows, inside)
            state = state + source_rows[m : m + 1, :] * force[i]
            state = state - source_rows[steps - 1 + m : steps + m, :] * flux[i]
        flux.append(coef * (state - surf))
        reach = rows + 2 * HALO
        fluxes[pl.ds(s, reach, stride=2 * steps), :] = force[s]
        fluxes[pl.ds(steps + s, reach, stride=2 * steps), :] = flux[s]
    total = flux[0][:rows]
    for s in range(1, steps):
        total = total + flux[s][:rows]
    mean = (total / steps).astype(bf16)
    topk = owners.shape[0]
    target = (owners[...] ^ tile[0]) * sea_rows + locals_[...]
    target = jnp.concatenate([target[k : k + 1, :] for k in range(topk)], 1)
    rowed = jnp.concatenate(
        [jnp.dot(mean, shares[k * width : (k + 1) * width, :], preferred_element_type=f32) for k in range(topk)], 0
    )
    first = rowed.astype(bf16)
    left = rowed - first.astype(f32)
    second = left.astype(bf16)
    third = (left - second.astype(f32)).astype(bf16)
    half = keep.shape[0]
    hot = lax.broadcasted_iota(jnp.int32, (2 * half, topk * rows), 0) == target
    hot = jnp.where(hot, 1.0, 0.0).astype(bf16)
    sums = jnp.dot(
        jnp.concatenate([hot, hot, hot], 1), jnp.concatenate([first, second, third], 0), preferred_element_type=f32
    )
    keep[...] = sums[:half]
    send[...] = sums[half:]


def rest_kernel(
    sizes, fluxes, weights, source_weights, sea_weights, sea_ends, wet, below, above, middle, warm, salt,
    out, brine_out, warm_out, salt_held, spread, sources, result, done
):
    levels, rows, steps, sea_levels, sea_rows, stride, sea_stride = sizes
    width = above.shape[1]
    depth = up_to(levels + 2 * steps, 16)
    flag = levels + steps + 2
    inside_above, inside_below = above[flag : flag + 1, :], below[flag : flag + 1, :]

    reach = rows + 2 * HALO
    x = [fluxes[(r % reach) * 2 * steps : (r % reach + 1) * 2 * steps, :] for r in range(1 - steps, rows + steps - 1)]
    field = lax.broadcasted_iota(jnp.int32, (2 * steps, width), 0) % steps
    for n in range(1, steps):
        y = stencil(x)
        x = [jnp.where(field < steps - n, y[i], x[i + 1]) for i in range(len(y))]
        for i in range(steps - 1 - n):
            x[i] = x[i] * inside_above
            x[-1 - i] = x[-1 - i] * inside_below
    for r in range(rows):
        sources[r * 16 : (r + 1) * 16, :] = jnp.concatenate([x[r], jnp.zeros((16 - 2 * steps, width), f32)], 0)

    @pl.loop(0, levels // 8)
    def _(c):
        def other(ref, j):
            return ref[pl.ds(pl.multiple_of(j * stride + c * 8, 8), 8), :]

        top, low = ([other(ref, j) for j in range(HALO)] for ref in (above, below))
        none = jnp.zeros_like(top[0])
        for n in range(steps):
            top = stencil(top + [none]) + [top[-1]]
            low = [low[0]] + stencil([none] + low)
        for i, value in enumerate(top + low):
            spread[pl.ds(pl.multiple_of(i * depth + c * 8, 8), 8), :] = value

    warm_out[...] = warm[...]
    salt_held[...] = salt[...]
    m = wet[...].astype(f32)
    base = HALO * stride
    w = sea_weights[:, : 3 * sea_stride]
    for e, (r, other) in enumerate(((0, above), (sea_rows - 1, below))):
        mark = m[r : r + 1]
        far = other[base + 2 * sea_stride : base + 2 * sea_stride + 1, :]
        x = []
        for f in range(2):
            at = base + f * sea_stride
            mine = (2 * f + e) * sea_stride
            step = other[at : at + sea_levels, :] - sea_ends[mine : mine + sea_levels, :] * far
            step = ocean_diffusion * (mark * step)
            x.append(jnp.concatenate([step, jnp.zeros((sea_stride - sea_levels, width), f32)], 0))
        y = product(w, jnp.concatenate(x, 1))
        for f, to in enumerate((warm_out, salt_held)):
            rows_at = pl.ds(r, sea_levels, stride=sea_rows)
            to[rows_at, :] = to[rows_at, :] + mark * y[:sea_levels, f * width : (f + 1) * width]
    leave = [pltpu.make_async_copy(salt_held, brine_out, done.at[0])]
    leave[0].start()

    w = weights[:, : 3 * depth]
    v = source_weights[:, :48]
    for g in range(rows // 8):
        to = result.at[g].reshape(levels * 8, width)
        for r in range(g * 8, g * 8 + 8, 2):
            x = [sources[(r + q) * 16 : (r + q + 1) * 16, :] for q in range(2)]
            if HALO <= r < rows - HALO:
                y = product(v, jnp.concatenate(x, 1))
            else:
                i = r if r < HALO else r - rows + 2 * HALO
                x = [
                    jnp.concatenate(
                        [spread[(i + q) * depth : (i + q) * depth + levels, :], x[q][: depth - levels]], 0
                    )
                    for q in range(2)
                ]
                y = product(w, jnp.concatenate(x, 1))
            for q in range(2):
                to[pl.ds((r + q) % 8, levels, stride=8), :] = (
                    middle[(r + q) * levels : (r + q + 1) * levels, :] + y[:levels, q * width : (q + 1) * width]
                )
        leave.append(pltpu.make_async_copy(result.at[g], out.at[:, g], done.at[1 + g]))
        leave[-1].start()
    for move in leave:
        move.wait()


def heat_kernel(sizes, kept, got, wet, sea_first, before, after):
    levels, rows, steps, sea_levels, sea_rows, stride, sea_stride = sizes
    heat = kept[...] + got[...]
    heat = wet[...].astype(f32) * heat
    for l in range(sea_levels):
        after[l * sea_rows : (l + 1) * sea_rows, :] = (
            before[l * sea_rows : (l + 1) * sea_rows, :] + sea_first[l : l + 1, :] * heat
        )


def body(sky, forcing, curve, surface, rate, vmix, shares, owners, locals_, warmth, brine, wet, sea_mix):
    levels, rows, width = sky.shape
    steps = forcing.shape[0]
    sea_levels, sea_rows, _ = warmth.shape
    topk = owners.shape[1]
    stride = up_to(levels + steps + 3, 8)
    sea_stride = up_to(sea_levels, 16)
    sizes = (levels, rows, steps, sea_levels, sea_rows, stride, sea_stride)
    sky2, forcing2 = sky.reshape(-1, width), forcing.reshape(-1, width)
    warmth2, brine2 = warmth.reshape(-1, width), brine.reshape(-1, width)
    flat = lambda n, kind=f32: jax.ShapeDtypeStruct((n, width), kind)

    space = lambda *shape: pltpu.VMEM(shape, f32)
    space = lambda *shape: pltpu.VMEM(shape, f32)
    length = HALO * stride + 2 * sea_stride + 8
    ring = ("tile", "comp")
    tiles, count = lax.axis_size("tile"), lax.axis_size(ring)
    at = lax.axis_index(ring).astype(jnp.int32)[None]
    core = lax.axis_index("comp").astype(jnp.int32)[None]
    tile = lax.axis_index("tile").astype(jnp.int32)[None]
    inner, outer = call(
        functools.partial(pack_kernel, sizes), [flat(length)] * 2,
        core, sky, forcing, surface, rate, warmth2, brine2, wet, moved=4 << 20, in_specs=[SMEM] + [HBM] * 7,
        scratch=[
            space(2, levels, 8, width), space(steps, rows, width), space(2, sea_levels * sea_rows, width),
            space(2, rows, width), pltpu.VMEM(wet.shape, wet.dtype), pltpu.SemaphoreType.DMA((8,)),
        ],
        grant=FULL,
    )
    swap = lambda first: [(i + a, i + 1 - a) for i in range(first, count - 1, 2) for a in range(2)]
    inner = lax.ppermute(inner, ring, swap(0))
    outer = lax.ppermute(outer, ring, swap(1))

    depth = up_to(levels + 2 * steps, 16)
    mix_rows = up_to(levels, 16)
    area = sea_levels * sea_rows
    (
        rows_of_mix, source_rows, own, weights, source_weights, sea_weights, sea_first, sea_ends, middle, warm, salt
    ) = call(
        functools.partial(local_kernel, sizes, count - 1),
        [
            flat((steps - 1) * levels), flat(8), flat((steps - 1) * rows),
            jax.ShapeDtypeStruct((mix_rows, 2 * width), bf16), flat(mix_rows, bf16),
            jax.ShapeDtypeStruct((sea_stride, 2 * width), bf16), flat(sea_stride), flat(4 * sea_stride),
            flat(rows * levels), flat(area), flat(area),
        ],
        at, vmix, curve[None], sea_mix, sky2, warmth2, brine2, wet, in_specs=[SMEM] + [VMEM] * 7,
        scratch=[space(rows * depth, width), space(2, sea_rows * sea_stride, width)],
        flops=4 << 30, moved=8 << 20,
    )

    half = tiles // 2 * sea_rows
    keep, send, fluxes, above, below = call(
        functools.partial(flux_kernel, sizes),
        [flat(half), flat(half), flat(2 * steps * (rows + 2 * HALO)), flat(length), flat(length)],
        core, tile, sky[-1], forcing2, surface, rate, rows_of_mix, source_rows, own, owners.T, locals_.T,
        shares.reshape(-1, width), inner, outer,
        in_specs=[SMEM] * 2 + [VMEM] * 12, scratch=[space(2 * HALO * stride, width)], moved=2 << 20,
    )
    bit = tiles // 2
    while True:
        got = lax.ppermute(send, "tile", [(i, i ^ bit) for i in range(tiles)])
        if bit == 1:
            break
        bit //= 2
        both = keep + got
        keep, send = both[: bit * sea_rows], both[bit * sea_rows :]

    sky_out, salt, warm = call(
        functools.partial(rest_kernel, sizes),
        [jax.ShapeDtypeStruct((levels, rows // 8, 8, width), f32), flat(area), flat(area)],
        fluxes, weights, source_weights, sea_weights, sea_ends, wet, below, above, middle, warm, salt,
        out_specs=[HBM, HBM, VMEM],
        scratch=[
            space(area, width), space(2 * HALO * depth, width), space(rows * 16, width),
            space(rows // 8, levels, 8, width), pltpu.SemaphoreType.DMA((1 + rows // 8,)),
        ],
        flops=2 << 30, moved=8 << 20,
    )
    warm = call(functools.partial(heat_kernel, sizes), flat(area), keep, got, wet, sea_first, warm, moved=2 << 20)
    return sky_out.reshape(sky.shape), warm.reshape(warmth.shape), salt.reshape(brine.shape)


def solution(mesh):
    both = P(None, ("member", "tile", "comp"), None)
    one = P(("tile", "comp"), None)
    return jax.shard_map(
        body,
        mesh=mesh,
        in_specs=(
            both, both, P(), P(("member", "tile", "comp"), None), one, P(), P(), one, one, both, both, one, P(),
        ),
        out_specs=(both, both, both),
        check_vma=False,
    )
```

```python
import functools

import jax
import jax.numpy as jnp
from jax import lax
from jax.experimental import pallas as pl
from jax.experimental.pallas import tpu as pltpu
from jax.sharding import PartitionSpec as P

atm_diffusion = 0.2
ocean_diffusion = 0.2
HALO = 4
FULL = 60
FIELDS = 16
EXACT = lax.Precision.HIGHEST
VMEM = pl.BlockSpec(memory_space=pltpu.VMEM)
HBM = pl.BlockSpec(memory_space=pltpu.HBM)
SMEM = pl.BlockSpec(memory_space=pltpu.SMEM)
ANY = pl.BlockSpec(memory_space=pl.ANY)
f32, bf16 = jnp.float32, jnp.bfloat16


def up_to(n, m):
    return -(-n // m) * m


def call(kernel, out_shape, *args, scratch=(), in_specs=None, out_specs=None, flops=0, moved=0, grant=24):
    return pl.pallas_call(
        kernel,
        out_shape=out_shape,
        in_specs=in_specs or [VMEM] * len(args),
        out_specs=out_specs or jax.tree.map(lambda _: VMEM, out_shape),
        scratch_shapes=list(scratch),
        compiler_params=pltpu.CompilerParams(vmem_limit_bytes=grant * 2**20),
        cost_estimate=pl.CostEstimate(flops=flops, bytes_accessed=moved, transcendentals=0),
    )(*args)


def copies(pairs, done):
    return [pltpu.make_async_copy(src, dst, done.at[i]) for i, (src, dst) in enumerate(pairs)]


def side_of(core, which):
    return jnp.where(core[0] == 0, 1 - which, which)


def first_kernel(sizes, core, vmix_in, sky_in, forcing, surface, rate, inner, outer, rows_of_mix, own,
                 vmix, sky, force, flat, done):
    levels, rows, steps, sea_levels, sea_rows, stride, sea_stride = sizes
    width = sky.shape[1]
    moves = copies(
        [(vmix_in, vmix), (sky_in, sky), (forcing, force), (surface, flat.at[0]), (rate, flat.at[1])], done
    )
    for move in moves:
        move.start()
    moves[0].wait()
    last = (lax.broadcasted_iota(jnp.int32, (levels, width), 0) == levels - 1).astype(f32)
    for s in range(steps - 1):
        last = lax.dot_general(
            vmix[...], last, (((0,), (0,)), ((), ())), precision=EXACT, preferred_element_type=f32
        )
        rows_of_mix[s * levels : (s + 1) * levels, :] = last
    for move in moves[1:]:
        move.wait()
    own[:rows, :] = sky[(levels - 1) * rows :, :]
    sums = [jnp.zeros((rows, width), f32) for _ in range(steps - 1)]
    for l in range(levels):
        x = sky[l * rows : (l + 1) * rows, :]
        for s in range(steps - 1):
            sums[s] = sums[s] + rows_of_mix[s * levels + l : s * levels + l + 1, :] * x
    for s in range(steps - 1):
        own[(s + 1) * rows : (s + 2) * rows, :] = sums[s]
    for which, out in enumerate((inner, outer)):
        at = side_of(core, which) * (rows - HALO)
        for j in range(HALO):
            lines = [own[pl.ds(s * rows + at + j, 1), :] for s in range(steps)]
            lines += [force[s, pl.ds(at + j, 1), :] for s in range(steps)]
            lines += [flat[i, pl.ds(at + j, 1), :] for i in range(2)] + [jnp.ones((1, width), f32)]
            lines += [jnp.zeros((FIELDS - len(lines), width), f32)]
            out[j * FIELDS : (j + 1) * FIELDS, :] = jnp.concatenate(lines, 0)


def pack_kernel(sizes, core, sky, warmth, brine, wet, after, inner, outer):
    levels, rows, steps, sea_levels, sea_rows, stride, sea_stride = sizes
    width = sky.shape[1]
    for which, out in enumerate((inner, outer)):
        last = side_of(core, which)
        sea_row = last * (sea_rows - 1)
        for j in range(HALO):
            out[j * stride : j * stride + levels, :] = sky[pl.ds(last * (rows - HALO) + j, levels, stride=rows), :]
        base = HALO * stride
        edge = wet[pl.ds(sea_row, 1), :].astype(f32)
        for field in (warmth, brine):
            out[base : base + sea_levels, :] = field[pl.ds(sea_row, sea_levels, stride=sea_rows), :] * edge
            base += sea_stride
        out[base : base + 8, :] = jnp.concatenate([edge, jnp.zeros((7, width), f32)], 0)


def split(x):
    high = x.astype(bf16)
    return high, (x - high.astype(f32)).astype(bf16)


def three_terms(w, depth):
    high = w.astype(bf16).astype(f32)
    low = w - high
    return (high + pltpu.roll(high, depth, 1) + pltpu.roll(low, 2 * depth, 1)).astype(bf16)


def row_of(ref, first, count, step, size):
    x = ref[pl.ds(first, count, stride=step), :]
    if count < size:
        x = jnp.concatenate([x, jnp.zeros((size - count, x.shape[1]), f32)], 0)
    return x


def beside(x):
    return pltpu.roll(x, 1, 1) + pltpu.roll(x, x.shape[1] - 1, 1)


def stencil(x):
    return [x[i - 1] + x[i] + x[i + 1] + beside(x[i]) for i in range(1, len(x) - 1)]


def product(weights, x):
    high, low = split(x)
    return jnp.dot(weights, jnp.concatenate([high, low, high], 0), preferred_element_type=f32)


def local_kernel(
    sizes, vmix, curve, sea_mix, warmth, brine, wet,
    weights, sea_weights, sea_first, sea_ends, warm_out, brine_out, sea_spread,
):
    levels, rows, steps, sea_levels, sea_rows, stride, sea_stride = sizes
    width = warmth.shape[1]
    depth = up_to(levels + 2 * steps, 16)
    v = vmix[...]
    dot = functools.partial(jnp.dot, precision=EXACT, preferred_element_type=f32)
    powers = [v]
    for _ in range(steps - 1):
        powers.append(dot(v, powers[-1]))
    by_curve = jnp.broadcast_to(curve[...], (width, levels))
    of_curve = [
        lax.dot_general(p, by_curve, (((1,), (1,)), ((), ())), precision=EXACT, preferred_element_type=f32)
        for p in powers
    ]
    of_last = [jnp.broadcast_to(p[:, levels - 1 : levels], (levels, width)) for p in powers]
    lane = lax.broadcasted_iota(jnp.int32, (levels, width), 1)
    wide = jnp.concatenate(
        [powers[-1] * atm_diffusion**steps, jnp.zeros((levels, width - levels), f32)], 1
    )
    for j in range(steps):
        factor = atm_diffusion ** (steps - 1 - j)
        for at, value in ((j, of_curve[steps - 1 - j] * factor), (steps + j, of_last[steps - 1 - j] * -factor)):
            wide = jnp.where(lane == levels + at, value, wide)
    more = jnp.zeros((weights.shape[0] - levels, width), f32)
    wide = jnp.concatenate([wide, more], 0)
    wide = jnp.concatenate([wide, jnp.zeros_like(wide)], 1)
    weights[...] = three_terms(wide, depth)
    sea = sea_mix[...]
    sea = jnp.concatenate([sea, jnp.zeros((sea_levels, 2 * width - sea_levels), f32)], 1)
    sea = jnp.concatenate([sea, jnp.zeros((sea_stride - sea_levels, 2 * width), f32)], 0)
    sea_weights[...] = three_terms(sea, sea_stride)
    sea_first[...] = jnp.broadcast_to(sea[:, 0:1], sea_first.shape)
    m = wet[...].astype(f32)
    mark = [m[r : r + 1] for r in range(sea_rows)]
    edge = jnp.zeros((1, width), f32)

    def near(x):
        x = [jnp.zeros_like(x[0])] + x + [jnp.zeros_like(x[0])]
        return [x[i - 1] + x[i + 1] + beside(x[i]) for i in range(1, len(x) - 1)]

    around = (
        jnp.concatenate([edge, m[:-1]], 0) + jnp.concatenate([m[1:], edge], 0) + beside(m)
    ) * ocean_diffusion
    share = [around[r : r + 1] for r in range(sea_rows)]
    for f, field in enumerate((warmth, brine)):
        for c in range(sea_stride // 8):
            count = min(8, sea_levels - c * 8)
            x = [row_of(field, c * 8 * sea_rows + r, count, sea_rows, 8) for r in range(sea_rows)]
            y = near([mark[r] * x[r] for r in range(sea_rows)])
            for r in range(sea_rows):
                at = r * sea_stride + c * 8
                sea_spread[f, at : at + 8, :] = x[r] + mark[r] * (ocean_diffusion * y[r] - x[r] * share[r])
    w = sea_weights[:, : 3 * sea_stride]
    for r in range(sea_rows):
        x = jnp.concatenate([sea_spread[f, r * sea_stride : (r + 1) * sea_stride, :] for f in range(2)], 1)
        y = product(w, x)
        for f, (field, out) in enumerate(((warmth, warm_out), (brine, brine_out))):
            old = field[pl.ds(r, sea_levels, stride=sea_rows), :]
            new = y[:sea_levels, f * width : (f + 1) * width]
            out[pl.ds(r, sea_levels, stride=sea_rows), :] = mark[r] * new + (1.0 - mark[r]) * old
            if r in (0, sea_rows - 1):
                at = (2 * f + (r > 0)) * sea_stride
                sea_ends[at : at + sea_levels, :] = old


def inside_of(place, last_place):
    return jnp.where(place[0] > 0, 1.0, 0.0), jnp.where(place[0] < last_place, 1.0, 0.0)


def own_kernel(sizes, last_place, place, sky, after, spread):
    levels, rows, steps, sea_levels, sea_rows, stride, sea_stride = sizes
    before, behind = inside_of(place, last_place)


    @pl.loop(0, levels // 8)
    def _(c):
        x = [sky[pl.ds(c * 8 * rows + r, 8, stride=rows), :] for r in range(rows)]
        none = jnp.zeros_like(x[0])
        beyond = 0
        for n in range(steps):
            if beyond < steps - 1 - n:
                x = [x[0]] + stencil([none] + x + [none]) + [x[-1]]
                beyond += 1
            else:
                x = stencil(x)
                beyond -= 1
            for i in range(beyond):
                x[i] = x[i] * before
                x[-1 - i] = x[-1 - i] * behind
        for r in range(rows):
            spread[pl.ds(pl.multiple_of(r * levels + c * 8, 8), 8), :] = x[r]


def cross(x):
    n, w = x.shape
    return (
        x + pltpu.roll(x, 1, 0) + pltpu.roll(x, n - 1, 0) + pltpu.roll(x, 1, 1) + pltpu.roll(x, w - 1, 1)
    )


def masked(x, rows, inside):
    return jnp.concatenate([x[:rows], x[rows:] * inside], 0)


def flux_kernel(
    sizes, core, tile, own, forcing, surface, rate, rows_of_mix, curve, owners, locals_, shares, inner, outer, after,
    keep, send, fluxes, halo
):
    levels, rows, steps, sea_levels, sea_rows, stride, sea_stride = sizes
    width = own.shape[1]
    one, two = inner[...], outer[...]
    halo[: HALO * FIELDS, :] = jnp.where(core[0] == 0, one, two)
    halo[HALO * FIELDS :, :] = jnp.where(core[0] == 0, two, one)

    def edge(l):
        return halo[pl.ds(l, 2 * HALO, stride=FIELDS), :]

    inside = edge(2 * steps + 2)
    by_curve = jnp.broadcast_to(curve[...], (8, levels))
    of_curve = [
        jnp.dot(by_curve, rows_of_mix[s * levels : (s + 1) * levels, :], precision=EXACT, preferred_element_type=f32)[:1]
        for s in range(steps - 1)
    ]
    of_last = [rows_of_mix[(s + 1) * levels - 1 : (s + 1) * levels, :] for s in range(steps - 1)]
    tops = [jnp.concatenate([own[s * rows : (s + 1) * rows, :], edge(s)], 0) for s in range(steps)]
    surf = jnp.concatenate([surface[...], edge(2 * steps)], 0)
    coef = jnp.concatenate([rate[...], edge(2 * steps + 1)], 0)
    force = [
        jnp.concatenate([forcing[s * rows : (s + 1) * rows, :], edge(steps + s)], 0) for s in range(steps)
    ]

    flux = []
    for s in range(steps):
        state = tops[s]
        for i in range(s):
            m = s - 1 - i
            state = masked(cross(state) * atm_diffusion, rows, inside)
            state = state + of_curve[m] * force[i] - of_last[m] * flux[i]
        flux.append(coef * (state - surf))
        reach = rows + 2 * HALO
        fluxes[pl.ds(s, reach, stride=2 * steps), :] = force[s]
        fluxes[pl.ds(steps + s, reach, stride=2 * steps), :] = flux[s]
    total = flux[0][:rows]
    for s in range(1, steps):
        total = total + flux[s][:rows]
    mean = (total / steps).astype(bf16)
    topk = owners.shape[0]
    target = (owners[...] ^ tile[0]) * sea_rows + locals_[...]
    target = jnp.concatenate([target[k : k + 1, :] for k in range(topk)], 1)
    rowed = jnp.concatenate(
        [jnp.dot(mean, shares[k * width : (k + 1) * width, :], preferred_element_type=f32) for k in range(topk)], 0
    )
    first = rowed.astype(bf16)
    left = rowed - first.astype(f32)
    second = left.astype(bf16)
    third = (left - second.astype(f32)).astype(bf16)
    half = keep.shape[0]
    hot = lax.broadcasted_iota(jnp.int32, (2 * half, topk * rows), 0) == target
    hot = jnp.where(hot, 1.0, 0.0).astype(bf16)
    sums = jnp.dot(
        jnp.concatenate([hot, hot, hot], 1), jnp.concatenate([first, second, third], 0), preferred_element_type=f32
    )
    keep[...] = sums[:half]
    send[...] = sums[half:]


def edge_kernel(
    sizes, last_place, core, place, fluxes, own, sea_weights, sea_ends, wet, warm, salt, inner, outer, after,
    spread, warm_out, brine_out, above, below, salt_held, done
):
    levels, rows, steps, sea_levels, sea_rows, stride, sea_stride = sizes
    width = own.shape[1]
    depth = up_to(levels + 2 * steps, 16)
    one, two = inner[...], outer[...]
    above[...] = jnp.where(core[0] == 0, two, one)
    below[...] = jnp.where(core[0] == 0, one, two)
    inside_above, inside_below = inside_of(place, last_place)

    reach = rows + 2 * HALO
    x = [fluxes[(r % reach) * 2 * steps : (r % reach + 1) * 2 * steps, :] for r in range(1 - steps, rows + steps - 1)]
    field = lax.broadcasted_iota(jnp.int32, (2 * steps, width), 0) % steps
    for n in range(1, steps):
        y = stencil(x)
        x = [jnp.where(field < steps - n, y[i], x[i + 1]) for i in range(len(y))]
        for i in range(steps - 1 - n):
            x[i] = x[i] * inside_above
            x[-1 - i] = x[-1 - i] * inside_below
    for r in range(rows):
        spread[r * depth + levels : (r + 1) * depth, :] = x[r]
        if HALO <= r < rows - HALO:
            spread[r * depth : r * depth + levels, :] = own[r * levels : (r + 1) * levels, :]

    warm_out[...] = warm[...]
    salt_held[...] = salt[...]
    m = wet[...].astype(f32)
    base = HALO * stride
    w = sea_weights[:, : 3 * sea_stride]
    for e, (r, other) in enumerate(((0, above), (sea_rows - 1, below))):
        mark = m[r : r + 1]
        far = other[base + 2 * sea_stride : base + 2 * sea_stride + 1, :]
        x = []
        for f in range(2):
            at = base + f * sea_stride
            mine = (2 * f + e) * sea_stride
            step = other[at : at + sea_levels, :] - sea_ends[mine : mine + sea_levels, :] * far
            step = ocean_diffusion * (mark * step)
            x.append(jnp.concatenate([step, jnp.zeros((sea_stride - sea_levels, width), f32)], 0))
        y = product(w, jnp.concatenate(x, 1))
        for f, to in enumerate((warm_out, salt_held)):
            rows_at = pl.ds(r, sea_levels, stride=sea_rows)
            to[rows_at, :] = to[rows_at, :] + mark * y[:sea_levels, f * width : (f + 1) * width]
    leave = [pltpu.make_async_copy(salt_held, brine_out, done.at[0])]
    leave[0].start()

    @pl.loop(0, levels // 8)
    def _(c):
        def other(ref, j):
            return ref[pl.ds(pl.multiple_of(j * stride + c * 8, 8), 8), :]

        top, low = ([other(ref, j) for j in range(HALO)] for ref in (above, below))
        none = jnp.zeros_like(top[0])
        for n in range(steps):
            top = stencil(top + [none]) + [top[-1]]
            low = [low[0]] + stencil([none] + low)
        for i, value in enumerate(top + low):
            r = i if i < HALO else rows - 2 * HALO + i
            value = value + own[pl.ds(pl.multiple_of(r * levels + c * 8, 8), 8), :]
            spread[pl.ds(pl.multiple_of(r * depth + c * 8, 8), 8), :] = value

    for move in leave:
        move.wait()


def mix_kernel(sizes, spread, weights, after, out, result, done):
    levels, rows, steps, sea_levels, sea_rows, stride, sea_stride = sizes
    width = spread.shape[1]
    depth = up_to(levels + 2 * steps, 16)
    w = weights[:, : 3 * depth]
    leave = []
    for g in range(rows // 8):
        to = result.at[g].reshape(levels * 8, width)
        for r in range(g * 8, g * 8 + 8, 2):
            y = product(
                w, jnp.concatenate([spread[(r + q) * depth : (r + q + 1) * depth, :] for q in range(2)], 1)
            )
            for q in range(2):
                to[pl.ds((r + q) % 8, levels, stride=8), :] = y[:levels, q * width : (q + 1) * width]
        leave.append(pltpu.make_async_copy(result.at[g], out.at[:, g], done.at[g]))
        leave[-1].start()
    for move in leave:
        move.wait()


def add_kernel(keep, got, after, kept, send):
    n = kept.shape[0]
    kept[...] = keep[:n] + got[:n]
    send[...] = keep[n:] + got[n:]


def heat_kernel(sizes, kept, got, wet, sea_first, before, after):
    levels, rows, steps, sea_levels, sea_rows, stride, sea_stride = sizes
    heat = kept[...] + got[...]
    heat = wet[...].astype(f32) * heat
    for l in range(sea_levels):
        after[l * sea_rows : (l + 1) * sea_rows, :] = (
            before[l * sea_rows : (l + 1) * sea_rows, :] + sea_first[l : l + 1, :] * heat
        )


def body(sky, forcing, curve, surface, rate, vmix, shares, owners, locals_, warmth, brine, wet, sea_mix):
    levels, rows, width = sky.shape
    steps = forcing.shape[0]
    sea_levels, sea_rows, _ = warmth.shape
    topk = owners.shape[1]
    stride = up_to(levels, 8)
    sea_stride = up_to(sea_levels, 16)
    sizes = (levels, rows, steps, sea_levels, sea_rows, stride, sea_stride)
    sky2, forcing2 = sky.reshape(-1, width), forcing.reshape(-1, width)
    warmth2, brine2 = warmth.reshape(-1, width), brine.reshape(-1, width)
    flat = lambda n, kind=f32: jax.ShapeDtypeStruct((n, width), kind)

    space = lambda *shape: pltpu.VMEM(shape, f32)
    space = lambda *shape: pltpu.VMEM(shape, f32)
    length = HALO * stride + 2 * sea_stride + 8
    ring = ("tile", "comp")
    tiles, count = lax.axis_size("tile"), lax.axis_size(ring)
    at = lax.axis_index(ring).astype(jnp.int32)[None]
    core = lax.axis_index("comp").astype(jnp.int32)[None]
    tile = lax.axis_index("tile").astype(jnp.int32)[None]
    area = sea_levels * sea_rows
    swap = lambda first: [(i + a, i + 1 - a) for i in range(first, count - 1, 2) for a in range(2)]
    inner, outer, rows_of_mix, own = call(
        functools.partial(first_kernel, sizes),
        [flat(HALO * FIELDS)] * 2 + [flat((steps - 1) * levels), flat(steps * rows)],
        core, vmix, sky2, forcing, surface, rate, moved=4 << 20, in_specs=[SMEM] + [HBM] * 5,
        scratch=[
            space(levels, levels), space(levels * rows, width), space(steps, rows, width), space(2, rows, width),
            pltpu.SemaphoreType.DMA((5,)),
        ],
        grant=FULL,
    )
    inner = lax.ppermute(inner, ring, swap(0))
    outer = lax.ppermute(outer, ring, swap(1))
    far_inner, far_outer = call(
        functools.partial(pack_kernel, sizes), [flat(length)] * 2,
        core, sky2, warmth2, brine2, wet, own, moved=4 << 20, in_specs=[SMEM] + [VMEM] * 4 + [ANY],
    )
    far_inner = lax.ppermute(far_inner, ring, swap(0))
    far_outer = lax.ppermute(far_outer, ring, swap(1))

    depth = up_to(levels + 2 * steps, 16)
    weights, sea_weights, sea_first, sea_ends, warm, salt = call(
        functools.partial(local_kernel, sizes),
        [
            jax.ShapeDtypeStruct((up_to(levels, 16), 2 * width), bf16),
            jax.ShapeDtypeStruct((sea_stride, 2 * width), bf16), flat(sea_stride), flat(4 * sea_stride),
            flat(area), flat(area),
        ],
        vmix, curve[None], sea_mix, warmth2, brine2, wet,
        scratch=[space(2, sea_rows * sea_stride, width)],
        flops=2 << 30, moved=4 << 20,
    )

    half = tiles // 2 * sea_rows
    keep, send, fluxes = call(
        functools.partial(flux_kernel, sizes), [flat(half), flat(half), flat(2 * steps * (rows + 2 * HALO))],
        core, tile, own, forcing2, surface, rate, rows_of_mix, curve[None], owners.T, locals_.T,
        shares.reshape(-1, width), inner, outer, weights,
        in_specs=[SMEM] * 2 + [VMEM] * 11 + [ANY], scratch=[space(2 * HALO * FIELDS, width)], moved=2 << 20,
    )
    def own_part(after):
        return call(
            functools.partial(own_kernel, sizes, count - 1), flat(rows * levels), at, sky2, after,
            in_specs=[SMEM, VMEM, ANY], flops=1 << 28, moved=2 << 20,
        )

    def edge_part(spread, after):
        return call(
            functools.partial(edge_kernel, sizes, count - 1), [flat(rows * depth), flat(area), flat(area)],
            core, at, fluxes, spread, sea_weights, sea_ends, wet, warm, salt, far_inner, far_outer, after,
            in_specs=[SMEM] * 2 + [VMEM] * 9 + [ANY], out_specs=[VMEM, VMEM, HBM],
            scratch=[space(length, width), space(length, width), space(area, width), pltpu.SemaphoreType.DMA((1,))],
            flops=1 << 28, moved=4 << 20,
        )

    bit, spread = tiles // 2, None
    while True:
        got = lax.ppermute(send, "tile", [(i, i ^ bit) for i in range(tiles)])
        if bit == 4:
            spread = own_part(keep)
        if bit <= 2 and spread is None:
            spread = own_part(keep)
        if bit == 2 or (bit == 1 and tiles == 2):
            spread, warm, salt = edge_part(spread, keep)
        if bit == 1:
            break
        keep, send = call(
            add_kernel, [flat(bit // 2 * sea_rows)] * 2, keep, got, keep if spread is None else spread,
            in_specs=[VMEM, VMEM, ANY],
        )
        bit //= 2
    sky_out = call(
        functools.partial(mix_kernel, sizes), jax.ShapeDtypeStruct((levels, rows // 8, 8, width), f32),
        spread, weights, keep, in_specs=[VMEM, VMEM, ANY], out_specs=HBM,
        scratch=[space(rows // 8, levels, 8, width), pltpu.SemaphoreType.DMA((rows // 8,))],
        flops=2 << 30, moved=4 << 20,
    )
    warm = call(functools.partial(heat_kernel, sizes), flat(area), keep, got, wet, sea_first, warm, moved=2 << 20)
    return sky_out.reshape(sky.shape), warm.reshape(warmth.shape), salt.reshape(brine.shape)


def solution(mesh):
    both = P(None, ("member", "tile", "comp"), None)
    one = P(("tile", "comp"), None)
    return jax.shard_map(
        body,
        mesh=mesh,
        in_specs=(
            both, both, P(), P(("member", "tile", "comp"), None), one, P(), P(), one, one, both, both, one, P(),
        ),
        out_specs=(both, both, both),
        check_vma=False,
    )
```

```python
import functools

import jax
import jax.numpy as jnp
from jax import lax
from jax.experimental import pallas as pl
from jax.experimental.pallas import tpu as pltpu
from jax.sharding import PartitionSpec as P

atm_diffusion = 0.2
ocean_diffusion = 0.2
HALO = 4
FULL = 60
EXACT = lax.Precision.HIGHEST
VMEM = pl.BlockSpec(memory_space=pltpu.VMEM)
HBM = pl.BlockSpec(memory_space=pltpu.HBM)
SMEM = pl.BlockSpec(memory_space=pltpu.SMEM)
ANY = pl.BlockSpec(memory_space=pl.ANY)
f32, bf16 = jnp.float32, jnp.bfloat16


def up_to(n, m):
    return -(-n // m) * m


def call(kernel, out_shape, *args, scratch=(), in_specs=None, out_specs=None, flops=0, moved=0, grant=24):
    return pl.pallas_call(
        kernel,
        out_shape=out_shape,
        in_specs=in_specs or [VMEM] * len(args),
        out_specs=out_specs or jax.tree.map(lambda _: VMEM, out_shape),
        scratch_shapes=list(scratch),
        compiler_params=pltpu.CompilerParams(vmem_limit_bytes=grant * 2**20),
        cost_estimate=pl.CostEstimate(flops=flops, bytes_accessed=moved, transcendentals=0),
    )(*args)


def copies(pairs, done):
    return [pltpu.make_async_copy(src, dst, done.at[i]) for i, (src, dst) in enumerate(pairs)]


def pack_kernel(
    sizes, core, sky, forcing, surface, rate, warmth, brine, wet, inner, outer,
    ends, force, sea, flat, marks, done
):
    levels, rows, steps, sea_levels, sea_rows, stride, sea_stride = sizes
    width = sky.shape[2]
    low = rows - 8
    moves = copies(
        [
            (sky.at[:, 0:8, :], ends.at[0]), (sky.at[:, low:rows, :], ends.at[1]), (forcing, force),
            (surface, flat.at[0]), (rate, flat.at[1]), (warmth, sea.at[0]), (brine, sea.at[1]), (wet, marks),
        ],
        done,
    )
    for move in moves:
        move.start()
    for move in moves:
        move.wait()
    end = ends.reshape(2 * levels * 8, width)
    for which, out in enumerate((inner, outer)):
        last = jnp.where(core[0] == 0, 1 - which, which)
        sea_row = last * (sea_rows - 1)
        for j in range(HALO):
            row = last * (rows - HALO) + j
            first = last * (levels * 8 + 8 - HALO) + j
            out[j * stride : j * stride + levels, :] = end[pl.ds(first, levels, stride=8), :]
            base = j * stride + levels
            tail = [force[s, pl.ds(row, 1), :] for s in range(steps)]
            tail += [flat[0, pl.ds(row, 1), :], flat[1, pl.ds(row, 1), :], jnp.ones((1, width), f32)]
            tail += [jnp.zeros((stride - levels - len(tail), width), f32)]
            out[base : (j + 1) * stride, :] = jnp.concatenate(tail, 0)
        base = HALO * stride
        edge = marks[pl.ds(sea_row, 1), :].astype(f32)
        for f in range(2):
            out[base : base + sea_levels, :] = sea[f, pl.ds(sea_row, sea_levels, stride=sea_rows), :] * edge
            base += sea_stride
        out[base : base + 8, :] = jnp.concatenate([edge, jnp.zeros((7, width), f32)], 0)


def split(x):
    high = x.astype(bf16)
    return high, (x - high.astype(f32)).astype(bf16)


def three_terms(w, depth):
    high = w.astype(bf16).astype(f32)
    low = w - high
    return (high + pltpu.roll(high, depth, 1) + pltpu.roll(low, 2 * depth, 1)).astype(bf16)


def row_of(ref, first, count, step, size):
    x = ref[pl.ds(first, count, stride=step), :]
    if count < size:
        x = jnp.concatenate([x, jnp.zeros((size - count, x.shape[1]), f32)], 0)
    return x


def beside(x):
    return pltpu.roll(x, 1, 1) + pltpu.roll(x, x.shape[1] - 1, 1)


def stencil(x):
    return [x[i - 1] + x[i] + x[i + 1] + beside(x[i]) for i in range(1, len(x) - 1)]


def product(weights, x):
    high, low = split(x)
    return jnp.dot(weights, jnp.concatenate([high, low, high], 0), preferred_element_type=f32)


def local_kernel(
    sizes, last_place, place, vmix, curve, sea_mix, sky, warmth, brine, wet,
    rows_of_mix, source_rows, own, weights, sea_weights, sea_first, sea_ends, spread, warm_out, brine_out, sea_spread,
):
    levels, rows, steps, sea_levels, sea_rows, stride, sea_stride = sizes
    width = sky.shape[1]
    depth = up_to(levels + 2 * steps, 16)
    v = vmix[...]
    dot = functools.partial(jnp.dot, precision=EXACT, preferred_element_type=f32)
    powers = [v]
    for _ in range(steps - 1):
        powers.append(dot(v, powers[-1]))
    last = (lax.broadcasted_iota(jnp.int32, (levels, width), 0) == levels - 1).astype(f32)
    for s in range(1, steps):
        rows_of_mix[(s - 1) * levels : s * levels, :] = lax.dot_general(
            powers[s - 1], last, (((0,), (0,)), ((), ())), precision=EXACT, preferred_element_type=f32
        )
    by_curve = jnp.broadcast_to(curve[...], (width, levels))
    of_curve = [
        lax.dot_general(p, by_curve, (((1,), (1,)), ((), ())), precision=EXACT, preferred_element_type=f32)
        for p in powers
    ]
    of_last = [jnp.broadcast_to(p[:, levels - 1 : levels], (levels, width)) for p in powers]
    found = [of_curve[i][levels - 1 :] for i in range(steps - 1)]
    found += [of_last[i][levels - 1 :] for i in range(steps - 1)]
    found += [jnp.zeros((8 - len(found), width), f32)]
    source_rows[...] = jnp.concatenate(found, 0)
    lane = lax.broadcasted_iota(jnp.int32, (levels, width), 1)
    wide = jnp.concatenate(
        [powers[-1] * atm_diffusion**steps, jnp.zeros((levels, width - levels), f32)], 1
    )
    for j in range(steps):
        factor = atm_diffusion ** (steps - 1 - j)
        for at, value in ((j, of_curve[steps - 1 - j] * factor), (steps + j, of_last[steps - 1 - j] * -factor)):
            wide = jnp.where(lane == levels + at, value, wide)
    more = jnp.zeros((weights.shape[0] - levels, width), f32)
    wide = jnp.concatenate([wide, more], 0)
    wide = jnp.concatenate([wide, jnp.zeros_like(wide)], 1)
    weights[...] = three_terms(wide, depth)
    sea = sea_mix[...]
    sea = jnp.concatenate([sea, jnp.zeros((sea_levels, 2 * width - sea_levels), f32)], 1)
    sea = jnp.concatenate([sea, jnp.zeros((sea_stride - sea_levels, 2 * width), f32)], 0)
    sea_weights[...] = three_terms(sea, sea_stride)
    sea_first[...] = jnp.broadcast_to(sea[:, 0:1], sea_first.shape)
    sums = [jnp.zeros((rows, width), f32) for _ in range(steps - 1)]
    for l in range(levels):
        x = sky[l * rows : (l + 1) * rows, :]
        for s in range(steps - 1):
            sums[s] = sums[s] + rows_of_mix[s * levels + l : s * levels + l + 1, :] * x
    for s in range(steps - 1):
        own[s * rows : (s + 1) * rows, :] = sums[s]

    m = wet[...].astype(f32)
    mark = [m[r : r + 1] for r in range(sea_rows)]
    edge = jnp.zeros((1, width), f32)

    def near(x):
        x = [jnp.zeros_like(x[0])] + x + [jnp.zeros_like(x[0])]
        return [x[i - 1] + x[i + 1] + beside(x[i]) for i in range(1, len(x) - 1)]

    around = (
        jnp.concatenate([edge, m[:-1]], 0) + jnp.concatenate([m[1:], edge], 0) + beside(m)
    ) * ocean_diffusion
    share = [around[r : r + 1] for r in range(sea_rows)]
    for f, field in enumerate((warmth, brine)):
        for c in range(sea_stride // 8):
            count = min(8, sea_levels - c * 8)
            x = [row_of(field, c * 8 * sea_rows + r, count, sea_rows, 8) for r in range(sea_rows)]
            y = near([mark[r] * x[r] for r in range(sea_rows)])
            for r in range(sea_rows):
                at = r * sea_stride + c * 8
                sea_spread[f, at : at + 8, :] = x[r] + mark[r] * (ocean_diffusion * y[r] - x[r] * share[r])
    w = sea_weights[:, : 3 * sea_stride]
    for r in range(sea_rows):
        x = jnp.concatenate([sea_spread[f, r * sea_stride : (r + 1) * sea_stride, :] for f in range(2)], 1)
        y = product(w, x)
        for f, (field, out) in enumerate(((warmth, warm_out), (brine, brine_out))):
            old = field[pl.ds(r, sea_levels, stride=sea_rows), :]
            new = y[:sea_levels, f * width : (f + 1) * width]
            out[pl.ds(r, sea_levels, stride=sea_rows), :] = mark[r] * new + (1.0 - mark[r]) * old
            if r in (0, sea_rows - 1):
                at = (2 * f + (r > 0)) * sea_stride
                sea_ends[at : at + sea_levels, :] = old

    before = jnp.where(place[0] > 0, 1.0, 0.0)
    behind = jnp.where(place[0] < last_place, 1.0, 0.0)

    @pl.loop(0, levels // 8)
    def _(c):
        x = [sky[pl.ds(c * 8 * rows + r, 8, stride=rows), :] for r in range(rows)]
        none = jnp.zeros_like(x[0])
        beyond = 0
        for n in range(steps):
            if beyond < steps - 1 - n:
                x = [x[0]] + stencil([none] + x + [none]) + [x[-1]]
                beyond += 1
            else:
                x = stencil(x)
                beyond -= 1
            for i in range(beyond):
                x[i] = x[i] * before
                x[-1 - i] = x[-1 - i] * behind
        for r in range(rows):
            spread[pl.ds(pl.multiple_of(r * levels + c * 8, 8), 8), :] = x[r]


def cross(x):
    n, w = x.shape
    return (
        x + pltpu.roll(x, 1, 0) + pltpu.roll(x, n - 1, 0) + pltpu.roll(x, 1, 1) + pltpu.roll(x, w - 1, 1)
    )


def masked(x, rows, inside):
    return jnp.concatenate([x[:rows], x[rows:] * inside], 0)


def flux_kernel(
    sizes, core, tile, sky, forcing, surface, rate, rows_of_mix, source_rows, own, owners, locals_, shares, inner, outer,
    keep, send, fluxes, above, below, halo
):
    levels, rows, steps, sea_levels, sea_rows, stride, sea_stride = sizes
    width = sky.shape[1]
    one, two = inner[...], outer[...]
    above[...] = jnp.where(core[0] == 0, two, one)
    below[...] = jnp.where(core[0] == 0, one, two)
    halo[: HALO * stride, :] = below[: HALO * stride, :]
    halo[HALO * stride :, :] = above[: HALO * stride, :]

    def edge(l):
        return halo[pl.ds(l, 2 * HALO, stride=stride), :]

    inside = edge(levels + steps + 2)
    sums = [jnp.zeros((2 * HALO, width), f32) for _ in range(steps - 1)]
    for l in range(levels):
        x = edge(l)
        for s in range(steps - 1):
            sums[s] = sums[s] + rows_of_mix[s * levels + l : s * levels + l + 1, :] * x
    tops = [jnp.concatenate([sky[...], edge(levels - 1)], 0)]
    tops += [jnp.concatenate([own[s * rows : (s + 1) * rows, :], sums[s]], 0) for s in range(steps - 1)]
    surf = jnp.concatenate([surface[...], edge(levels + steps)], 0)
    coef = jnp.concatenate([rate[...], edge(levels + steps + 1)], 0)
    force = [
        jnp.concatenate([forcing[s * rows : (s + 1) * rows, :], edge(levels + s)], 0) for s in range(steps)
    ]

    flux = []
    for s in range(steps):
        state = tops[s]
        for i in range(s):
            m = s - 1 - i
            state = masked(cross(state) * atm_diffusion, rows, inside)
            state = state + source_rows[m : m + 1, :] * force[i]
            state = state - source_rows[steps - 1 + m : steps + m, :] * flux[i]
        flux.append(coef * (state - surf))
        reach = rows + 2 * HALO
        fluxes[pl.ds(s, reach, stride=2 * steps), :] = force[s]
        fluxes[pl.ds(steps + s, reach, stride=2 * steps), :] = flux[s]
    total = flux[0][:rows]
    for s in range(1, steps):
        total = total + flux[s][:rows]
    mean = (total / steps).astype(bf16)
    topk = owners.shape[0]
    target = (owners[...] ^ tile[0]) * sea_rows + locals_[...]
    target = jnp.concatenate([target[k : k + 1, :] for k in range(topk)], 1)
    rowed = jnp.concatenate(
        [jnp.dot(mean, shares[k * width : (k + 1) * width, :], preferred_element_type=f32) for k in range(topk)], 0
    )
    first = rowed.astype(bf16)
    left = rowed - first.astype(f32)
    second = left.astype(bf16)
    third = (left - second.astype(f32)).astype(bf16)
    half = keep.shape[0]
    hot = lax.broadcasted_iota(jnp.int32, (2 * half, topk * rows), 0) == target
    hot = jnp.where(hot, 1.0, 0.0).astype(bf16)
    sums = jnp.dot(
        jnp.concatenate([hot, hot, hot], 1), jnp.concatenate([first, second, third], 0), preferred_element_type=f32
    )
    keep[...] = sums[:half]
    send[...] = sums[half:]


def edge_kernel(
    sizes, fluxes, own, sea_weights, sea_ends, wet, warm, salt, above, below, after,
    spread, warm_out, brine_out, salt_held, done
):
    levels, rows, steps, sea_levels, sea_rows, stride, sea_stride = sizes
    width = own.shape[1]
    depth = up_to(levels + 2 * steps, 16)
    flag = levels + steps + 2
    inside_above, inside_below = above[flag : flag + 1, :], below[flag : flag + 1, :]

    reach = rows + 2 * HALO
    x = [fluxes[(r % reach) * 2 * steps : (r % reach + 1) * 2 * steps, :] for r in range(1 - steps, rows + steps - 1)]
    field = lax.broadcasted_iota(jnp.int32, (2 * steps, width), 0) % steps
    for n in range(1, steps):
        y = stencil(x)
        x = [jnp.where(field < steps - n, y[i], x[i + 1]) for i in range(len(y))]
        for i in range(steps - 1 - n):
            x[i] = x[i] * inside_above
            x[-1 - i] = x[-1 - i] * inside_below
    for r in range(rows):
        spread[r * depth + levels : (r + 1) * depth, :] = x[r]
        if HALO <= r < rows - HALO:
            spread[r * depth : r * depth + levels, :] = own[r * levels : (r + 1) * levels, :]

    warm_out[...] = warm[...]
    salt_held[...] = salt[...]
    m = wet[...].astype(f32)
    base = HALO * stride
    w = sea_weights[:, : 3 * sea_stride]
    for e, (r, other) in enumerate(((0, above), (sea_rows - 1, below))):
        mark = m[r : r + 1]
        far = other[base + 2 * sea_stride : base + 2 * sea_stride + 1, :]
        x = []
        for f in range(2):
            at = base + f * sea_stride
            mine = (2 * f + e) * sea_stride
            step = other[at : at + sea_levels, :] - sea_ends[mine : mine + sea_levels, :] * far
            step = ocean_diffusion * (mark * step)
            x.append(jnp.concatenate([step, jnp.zeros((sea_stride - sea_levels, width), f32)], 0))
        y = product(w, jnp.concatenate(x, 1))
        for f, to in enumerate((warm_out, salt_held)):
            rows_at = pl.ds(r, sea_levels, stride=sea_rows)
            to[rows_at, :] = to[rows_at, :] + mark * y[:sea_levels, f * width : (f + 1) * width]
    leave = [pltpu.make_async_copy(salt_held, brine_out, done.at[0])]
    leave[0].start()

    @pl.loop(0, levels // 8)
    def _(c):
        def other(ref, j):
            return ref[pl.ds(pl.multiple_of(j * stride + c * 8, 8), 8), :]

        top, low = ([other(ref, j) for j in range(HALO)] for ref in (above, below))
        none = jnp.zeros_like(top[0])
        for n in range(steps):
            top = stencil(top + [none]) + [top[-1]]
            low = [low[0]] + stencil([none] + low)
        for i, value in enumerate(top + low):
            r = i if i < HALO else rows - 2 * HALO + i
            value = value + own[pl.ds(pl.multiple_of(r * levels + c * 8, 8), 8), :]
            spread[pl.ds(pl.multiple_of(r * depth + c * 8, 8), 8), :] = value

    for move in leave:
        move.wait()


def mix_kernel(sizes, spread, weights, after, out, result, done):
    levels, rows, steps, sea_levels, sea_rows, stride, sea_stride = sizes
    width = spread.shape[1]
    depth = up_to(levels + 2 * steps, 16)
    w = weights[:, : 3 * depth]
    leave = []
    for g in range(rows // 8):
        to = result.at[g].reshape(levels * 8, width)
        for r in range(g * 8, g * 8 + 8, 2):
            y = product(
                w, jnp.concatenate([spread[(r + q) * depth : (r + q + 1) * depth, :] for q in range(2)], 1)
            )
            for q in range(2):
                to[pl.ds((r + q) % 8, levels, stride=8), :] = y[:levels, q * width : (q + 1) * width]
        leave.append(pltpu.make_async_copy(result.at[g], out.at[:, g], done.at[g]))
        leave[-1].start()
    for move in leave:
        move.wait()


def add_kernel(keep, got, after, kept, send):
    n = kept.shape[0]
    kept[...] = keep[:n] + got[:n]
    send[...] = keep[n:] + got[n:]


def heat_kernel(sizes, kept, got, wet, sea_first, before, after):
    levels, rows, steps, sea_levels, sea_rows, stride, sea_stride = sizes
    heat = kept[...] + got[...]
    heat = wet[...].astype(f32) * heat
    for l in range(sea_levels):
        after[l * sea_rows : (l + 1) * sea_rows, :] = (
            before[l * sea_rows : (l + 1) * sea_rows, :] + sea_first[l : l + 1, :] * heat
        )


def body(sky, forcing, curve, surface, rate, vmix, shares, owners, locals_, warmth, brine, wet, sea_mix):
    levels, rows, width = sky.shape
    steps = forcing.shape[0]
    sea_levels, sea_rows, _ = warmth.shape
    topk = owners.shape[1]
    stride = up_to(levels + steps + 3, 8)
    sea_stride = up_to(sea_levels, 16)
    sizes = (levels, rows, steps, sea_levels, sea_rows, stride, sea_stride)
    sky2, forcing2 = sky.reshape(-1, width), forcing.reshape(-1, width)
    warmth2, brine2 = warmth.reshape(-1, width), brine.reshape(-1, width)
    flat = lambda n, kind=f32: jax.ShapeDtypeStruct((n, width), kind)

    space = lambda *shape: pltpu.VMEM(shape, f32)
    space = lambda *shape: pltpu.VMEM(shape, f32)
    length = HALO * stride + 2 * sea_stride + 8
    ring = ("tile", "comp")
    tiles, count = lax.axis_size("tile"), lax.axis_size(ring)
    at = lax.axis_index(ring).astype(jnp.int32)[None]
    core = lax.axis_index("comp").astype(jnp.int32)[None]
    tile = lax.axis_index("tile").astype(jnp.int32)[None]
    inner, outer = call(
        functools.partial(pack_kernel, sizes), [flat(length)] * 2,
        core, sky, forcing, surface, rate, warmth2, brine2, wet, moved=4 << 20, in_specs=[SMEM] + [HBM] * 7,
        scratch=[
            space(2, levels, 8, width), space(steps, rows, width), space(2, sea_levels * sea_rows, width),
            space(2, rows, width), pltpu.VMEM(wet.shape, wet.dtype), pltpu.SemaphoreType.DMA((8,)),
        ],
        grant=FULL,
    )
    swap = lambda first: [(i + a, i + 1 - a) for i in range(first, count - 1, 2) for a in range(2)]
    inner = lax.ppermute(inner, ring, swap(0))
    outer = lax.ppermute(outer, ring, swap(1))

    depth = up_to(levels + 2 * steps, 16)
    mix_rows = up_to(levels, 16)
    area = sea_levels * sea_rows
    rows_of_mix, source_rows, own, weights, sea_weights, sea_first, sea_ends, spread, warm, salt = call(
        functools.partial(local_kernel, sizes, count - 1),
        [
            flat((steps - 1) * levels), flat(8), flat((steps - 1) * rows),
            jax.ShapeDtypeStruct((mix_rows, 2 * width), bf16),
            jax.ShapeDtypeStruct((sea_stride, 2 * width), bf16), flat(sea_stride), flat(4 * sea_stride),
            flat(rows * levels), flat(area), flat(area),
        ],
        at, vmix, curve[None], sea_mix, sky2, warmth2, brine2, wet, in_specs=[SMEM] + [VMEM] * 7,
        scratch=[space(2, sea_rows * sea_stride, width)],
        flops=4 << 30, moved=8 << 20,
    )

    half = tiles // 2 * sea_rows
    keep, send, fluxes, above, below = call(
        functools.partial(flux_kernel, sizes),
        [flat(half), flat(half), flat(2 * steps * (rows + 2 * HALO)), flat(length), flat(length)],
        core, tile, sky[-1], forcing2, surface, rate, rows_of_mix, source_rows, own, owners.T, locals_.T,
        shares.reshape(-1, width), inner, outer,
        in_specs=[SMEM] * 2 + [VMEM] * 12, scratch=[space(2 * HALO * stride, width)], moved=2 << 20,
    )
    bit, ready = tiles // 2, None
    while True:
        got = lax.ppermute(send, "tile", [(i, i ^ bit) for i in range(tiles)])
        if bit <= 4 and ready is None:
            ready, warm, salt = call(
                functools.partial(edge_kernel, sizes), [flat(rows * depth), flat(area), flat(area)],
                fluxes, spread, sea_weights, sea_ends, wet, warm, salt, above, below, keep,
                in_specs=[VMEM] * 9 + [ANY], out_specs=[VMEM, VMEM, HBM],
                scratch=[space(area, width), pltpu.SemaphoreType.DMA((1,))],
                flops=1 << 28, moved=4 << 20,
            )
        if bit == 1:
            break
        keep, send = call(
            add_kernel, [flat(bit // 2 * sea_rows)] * 2, keep, got, keep if ready is None else ready,
            in_specs=[VMEM, VMEM, ANY],
        )
        bit //= 2
    sky_out = call(
        functools.partial(mix_kernel, sizes), jax.ShapeDtypeStruct((levels, rows // 8, 8, width), f32),
        ready, weights, keep, in_specs=[VMEM, VMEM, ANY], out_specs=HBM,
        scratch=[space(rows // 8, levels, 8, width), pltpu.SemaphoreType.DMA((rows // 8,))],
        flops=2 << 30, moved=4 << 20,
    )
    warm = call(functools.partial(heat_kernel, sizes), flat(area), keep, got, wet, sea_first, warm, moved=2 << 20)
    return sky_out.reshape(sky.shape), warm.reshape(warmth.shape), salt.reshape(brine.shape)


def solution(mesh):
    both = P(None, ("member", "tile", "comp"), None)
    one = P(("tile", "comp"), None)
    return jax.shard_map(
        body,
        mesh=mesh,
        in_specs=(
            both, both, P(), P(("member", "tile", "comp"), None), one, P(), P(), one, one, both, both, one, P(),
        ),
        out_specs=(both, both, both),
        check_vma=False,
    )
```

```python
import functools

import jax
import jax.numpy as jnp
from jax import lax
from jax.experimental import pallas as pl
from jax.experimental.pallas import tpu as pltpu
from jax.sharding import PartitionSpec as P

atm_diffusion = 0.2
ocean_diffusion = 0.2
HALO = 4
FULL = 60
EXACT = lax.Precision.HIGHEST
VMEM = pl.BlockSpec(memory_space=pltpu.VMEM)
HBM = pl.BlockSpec(memory_space=pltpu.HBM)
SMEM = pl.BlockSpec(memory_space=pltpu.SMEM)
ANY = pl.BlockSpec(memory_space=pl.ANY)
f32, bf16 = jnp.float32, jnp.bfloat16


def up_to(n, m):
    return -(-n // m) * m


def call(kernel, out_shape, *args, scratch=(), in_specs=None, out_specs=None, flops=0, moved=0, grant=24):
    return pl.pallas_call(
        kernel,
        out_shape=out_shape,
        in_specs=in_specs or [VMEM] * len(args),
        out_specs=out_specs or jax.tree.map(lambda _: VMEM, out_shape),
        scratch_shapes=list(scratch),
        compiler_params=pltpu.CompilerParams(vmem_limit_bytes=grant * 2**20),
        cost_estimate=pl.CostEstimate(flops=flops, bytes_accessed=moved, transcendentals=0),
    )(*args)


def copies(pairs, done):
    return [pltpu.make_async_copy(src, dst, done.at[i]) for i, (src, dst) in enumerate(pairs)]


def pack_kernel(
    sizes, core, sky, forcing, surface, rate, warmth, brine, wet, inner, outer,
    ends, force, sea, flat, marks, done
):
    levels, rows, steps, sea_levels, sea_rows, stride, sea_stride = sizes
    width = sky.shape[2]
    low = rows - 8
    moves = copies(
        [
            (sky.at[:, 0:8, :], ends.at[0]), (sky.at[:, low:rows, :], ends.at[1]), (forcing, force),
            (surface, flat.at[0]), (rate, flat.at[1]), (warmth, sea.at[0]), (brine, sea.at[1]), (wet, marks),
        ],
        done,
    )
    for move in moves:
        move.start()
    for move in moves:
        move.wait()
    end = ends.reshape(2 * levels * 8, width)
    for which, out in enumerate((inner, outer)):
        last = jnp.where(core[0] == 0, 1 - which, which)
        sea_row = last * (sea_rows - 1)
        for j in range(HALO):
            row = last * (rows - HALO) + j
            first = last * (levels * 8 + 8 - HALO) + j
            out[j * stride : j * stride + levels, :] = end[pl.ds(first, levels, stride=8), :]
            base = j * stride + levels
            tail = [force[s, pl.ds(row, 1), :] for s in range(steps)]
            tail += [flat[0, pl.ds(row, 1), :], flat[1, pl.ds(row, 1), :], jnp.ones((1, width), f32)]
            tail += [jnp.zeros((stride - levels - len(tail), width), f32)]
            out[base : (j + 1) * stride, :] = jnp.concatenate(tail, 0)
        base = HALO * stride
        edge = marks[pl.ds(sea_row, 1), :].astype(f32)
        for f in range(2):
            out[base : base + sea_levels, :] = sea[f, pl.ds(sea_row, sea_levels, stride=sea_rows), :] * edge
            base += sea_stride
        out[base : base + 8, :] = jnp.concatenate([edge, jnp.zeros((7, width), f32)], 0)


def split(x):
    high = x.astype(bf16)
    return high, (x - high.astype(f32)).astype(bf16)


def three_terms(w, depth):
    high = w.astype(bf16).astype(f32)
    low = w - high
    return (high + pltpu.roll(high, depth, 1) + pltpu.roll(low, 2 * depth, 1)).astype(bf16)


def row_of(ref, first, count, step, size):
    x = ref[pl.ds(first, count, stride=step), :]
    if count < size:
        x = jnp.concatenate([x, jnp.zeros((size - count, x.shape[1]), f32)], 0)
    return x


def beside(x):
    return pltpu.roll(x, 1, 1) + pltpu.roll(x, x.shape[1] - 1, 1)


def stencil(x):
    return [x[i - 1] + x[i] + x[i + 1] + beside(x[i]) for i in range(1, len(x) - 1)]


def product(weights, x):
    high, low = split(x)
    return jnp.dot(weights, jnp.concatenate([high, low, high], 0), preferred_element_type=f32)


def local_kernel(
    sizes, last_place, place, vmix, curve, sea_mix, sky, warmth, brine, wet,
    rows_of_mix, source_rows, own, weights, sea_weights, sea_first, sea_ends, spread, warm_out, brine_out, sea_spread,
):
    levels, rows, steps, sea_levels, sea_rows, stride, sea_stride = sizes
    width = sky.shape[1]
    depth = up_to(levels + 2 * steps, 16)
    v = vmix[...]
    dot = functools.partial(jnp.dot, precision=EXACT, preferred_element_type=f32)
    powers = [v]
    for _ in range(steps - 1):
        powers.append(dot(v, powers[-1]))
    last = (lax.broadcasted_iota(jnp.int32, (levels, width), 0) == levels - 1).astype(f32)
    for s in range(1, steps):
        rows_of_mix[(s - 1) * levels : s * levels, :] = lax.dot_general(
            powers[s - 1], last, (((0,), (0,)), ((), ())), precision=EXACT, preferred_element_type=f32
        )
    by_curve = jnp.broadcast_to(curve[...], (width, levels))
    of_curve = [
        lax.dot_general(p, by_curve, (((1,), (1,)), ((), ())), precision=EXACT, preferred_element_type=f32)
        for p in powers
    ]
    of_last = [jnp.broadcast_to(p[:, levels - 1 : levels], (levels, width)) for p in powers]
    found = [of_curve[i][levels - 1 :] for i in range(steps - 1)]
    found += [of_last[i][levels - 1 :] for i in range(steps - 1)]
    found += [jnp.zeros((8 - len(found), width), f32)]
    source_rows[...] = jnp.concatenate(found, 0)
    lane = lax.broadcasted_iota(jnp.int32, (levels, width), 1)
    wide = jnp.concatenate(
        [powers[-1] * atm_diffusion**steps, jnp.zeros((levels, width - levels), f32)], 1
    )
    for j in range(steps):
        factor = atm_diffusion ** (steps - 1 - j)
        for at, value in ((j, of_curve[steps - 1 - j] * factor), (steps + j, of_last[steps - 1 - j] * -factor)):
            wide = jnp.where(lane == levels + at, value, wide)
    more = jnp.zeros((weights.shape[0] - levels, width), f32)
    wide = jnp.concatenate([wide, more], 0)
    wide = jnp.concatenate([wide, jnp.zeros_like(wide)], 1)
    weights[...] = three_terms(wide, depth)
    sea = sea_mix[...]
    sea = jnp.concatenate([sea, jnp.zeros((sea_levels, 2 * width - sea_levels), f32)], 1)
    sea = jnp.concatenate([sea, jnp.zeros((sea_stride - sea_levels, 2 * width), f32)], 0)
    sea_weights[...] = three_terms(sea, sea_stride)
    sea_first[...] = jnp.broadcast_to(sea[:, 0:1], sea_first.shape)
    sums = [jnp.zeros((rows, width), f32) for _ in range(steps - 1)]
    for l in range(levels):
        x = sky[l * rows : (l + 1) * rows, :]
        for s in range(steps - 1):
            sums[s] = sums[s] + rows_of_mix[s * levels + l : s * levels + l + 1, :] * x
    for s in range(steps - 1):
        own[s * rows : (s + 1) * rows, :] = sums[s]

    m = wet[...].astype(f32)
    mark = [m[r : r + 1] for r in range(sea_rows)]
    edge = jnp.zeros((1, width), f32)

    def near(x):
        x = [jnp.zeros_like(x[0])] + x + [jnp.zeros_like(x[0])]
        return [x[i - 1] + x[i + 1] + beside(x[i]) for i in range(1, len(x) - 1)]

    around = (
        jnp.concatenate([edge, m[:-1]], 0) + jnp.concatenate([m[1:], edge], 0) + beside(m)
    ) * ocean_diffusion
    share = [around[r : r + 1] for r in range(sea_rows)]
    for f, field in enumerate((warmth, brine)):
        for c in range(sea_stride // 8):
            count = min(8, sea_levels - c * 8)
            x = [row_of(field, c * 8 * sea_rows + r, count, sea_rows, 8) for r in range(sea_rows)]
            y = near([mark[r] * x[r] for r in range(sea_rows)])
            for r in range(sea_rows):
                at = r * sea_stride + c * 8
                sea_spread[f, at : at + 8, :] = x[r] + mark[r] * (ocean_diffusion * y[r] - x[r] * share[r])
    w = sea_weights[:, : 3 * sea_stride]
    for r in range(sea_rows):
        x = jnp.concatenate([sea_spread[f, r * sea_stride : (r + 1) * sea_stride, :] for f in range(2)], 1)
        y = product(w, x)
        for f, (field, out) in enumerate(((warmth, warm_out), (brine, brine_out))):
            old = field[pl.ds(r, sea_levels, stride=sea_rows), :]
            new = y[:sea_levels, f * width : (f + 1) * width]
            out[pl.ds(r, sea_levels, stride=sea_rows), :] = mark[r] * new + (1.0 - mark[r]) * old
            if r in (0, sea_rows - 1):
                at = (2 * f + (r > 0)) * sea_stride
                sea_ends[at : at + sea_levels, :] = old

    before = jnp.where(place[0] > 0, 1.0, 0.0)
    behind = jnp.where(place[0] < last_place, 1.0, 0.0)

    @pl.loop(0, levels // 8)
    def _(c):
        x = [sky[pl.ds(c * 8 * rows + r, 8, stride=rows), :] for r in range(rows)]
        none = jnp.zeros_like(x[0])
        beyond = 0
        for n in range(steps):
            if beyond < steps - 1 - n:
                x = [x[0]] + stencil([none] + x + [none]) + [x[-1]]
                beyond += 1
            else:
                x = stencil(x)
                beyond -= 1
            for i in range(beyond):
                x[i] = x[i] * before
                x[-1 - i] = x[-1 - i] * behind
        for r in range(rows):
            spread[pl.ds(pl.multiple_of(r * levels + c * 8, 8), 8), :] = x[r]


def cross(x):
    n, w = x.shape
    return (
        x + pltpu.roll(x, 1, 0) + pltpu.roll(x, n - 1, 0) + pltpu.roll(x, 1, 1) + pltpu.roll(x, w - 1, 1)
    )


def masked(x, rows, inside):
    return jnp.concatenate([x[:rows], x[rows:] * inside], 0)


def flux_kernel(
    sizes, core, tile, sky, forcing, surface, rate, rows_of_mix, source_rows, own, owners, locals_, shares, outer, inner,
    keep, send, fluxes, above, below, halo
):
    levels, rows, steps, sea_levels, sea_rows, stride, sea_stride = sizes
    width = sky.shape[1]
    one, two = inner[...], outer[...]
    above[...] = jnp.where(core[0] == 0, two, one)
    below[...] = jnp.where(core[0] == 0, one, two)
    halo[: HALO * stride, :] = below[: HALO * stride, :]
    halo[HALO * stride :, :] = above[: HALO * stride, :]

    def edge(l):
        return halo[pl.ds(l, 2 * HALO, stride=stride), :]

    inside = edge(levels + steps + 2)
    sums = [jnp.zeros((2 * HALO, width), f32) for _ in range(steps - 1)]
    for l in range(levels):
        x = edge(l)
        for s in range(steps - 1):
            sums[s] = sums[s] + rows_of_mix[s * levels + l : s * levels + l + 1, :] * x
    tops = [jnp.concatenate([sky[...], edge(levels - 1)], 0)]
    tops += [jnp.concatenate([own[s * rows : (s + 1) * rows, :], sums[s]], 0) for s in range(steps - 1)]
    surf = jnp.concatenate([surface[...], edge(levels + steps)], 0)
    coef = jnp.concatenate([rate[...], edge(levels + steps + 1)], 0)
    force = [
        jnp.concatenate([forcing[s * rows : (s + 1) * rows, :], edge(levels + s)], 0) for s in range(steps)
    ]

    flux = []
    for s in range(steps):
        state = tops[s]
        for i in range(s):
            m = s - 1 - i
            state = masked(cross(state) * atm_diffusion, rows, inside)
            state = state + source_rows[m : m + 1, :] * force[i]
            state = state - source_rows[steps - 1 + m : steps + m, :] * flux[i]
        flux.append(coef * (state - surf))
        reach = rows + 2 * HALO
        fluxes[pl.ds(s, reach, stride=2 * steps), :] = force[s]
        fluxes[pl.ds(steps + s, reach, stride=2 * steps), :] = flux[s]
    total = flux[0][:rows]
    for s in range(1, steps):
        total = total + flux[s][:rows]
    mean = (total / steps).astype(bf16)
    topk = owners.shape[0]
    target = (owners[...] ^ tile[0]) * sea_rows + locals_[...]
    target = jnp.concatenate([target[k : k + 1, :] for k in range(topk)], 1)
    rowed = jnp.concatenate(
        [jnp.dot(mean, shares[k * width : (k + 1) * width, :], preferred_element_type=f32) for k in range(topk)], 0
    )
    first = rowed.astype(bf16)
    left = rowed - first.astype(f32)
    second = left.astype(bf16)
    third = (left - second.astype(f32)).astype(bf16)
    half = keep.shape[0]
    hot = lax.broadcasted_iota(jnp.int32, (2 * half, topk * rows), 0) == target
    hot = jnp.where(hot, 1.0, 0.0).astype(bf16)
    sums = jnp.dot(
        jnp.concatenate([hot, hot, hot], 1), jnp.concatenate([first, second, third], 0), preferred_element_type=f32
    )
    keep[...] = sums[:half]
    send[...] = sums[half:]


def edge_kernel(
    sizes, fluxes, own, above, below, after, spread
):
    levels, rows, steps, sea_levels, sea_rows, stride, sea_stride = sizes
    width = own.shape[1]
    depth = up_to(levels + 2 * steps, 16)
    flag = levels + steps + 2
    inside_above, inside_below = above[flag : flag + 1, :], below[flag : flag + 1, :]

    reach = rows + 2 * HALO
    x = [fluxes[(r % reach) * 2 * steps : (r % reach + 1) * 2 * steps, :] for r in range(1 - steps, rows + steps - 1)]
    field = lax.broadcasted_iota(jnp.int32, (2 * steps, width), 0) % steps
    for n in range(1, steps):
        y = stencil(x)
        x = [jnp.where(field < steps - n, y[i], x[i + 1]) for i in range(len(y))]
        for i in range(steps - 1 - n):
            x[i] = x[i] * inside_above
            x[-1 - i] = x[-1 - i] * inside_below
    for r in range(rows):
        spread[r * depth + levels : (r + 1) * depth, :] = x[r]
        if HALO <= r < rows - HALO:
            spread[r * depth : r * depth + levels, :] = own[r * levels : (r + 1) * levels, :]

    @pl.loop(0, levels // 8)
    def _(c):
        def other(ref, j):
            return ref[pl.ds(pl.multiple_of(j * stride + c * 8, 8), 8), :]

        top, low = ([other(ref, j) for j in range(HALO)] for ref in (above, below))
        none = jnp.zeros_like(top[0])
        for n in range(steps):
            top = stencil(top + [none]) + [top[-1]]
            low = [low[0]] + stencil([none] + low)
        for i, value in enumerate(top + low):
            r = i if i < HALO else rows - 2 * HALO + i
            value = value + own[pl.ds(pl.multiple_of(r * levels + c * 8, 8), 8), :]
            spread[pl.ds(pl.multiple_of(r * depth + c * 8, 8), 8), :] = value


def shore_kernel(
    sizes, sea_weights, sea_ends, wet, warm, salt, above, below, after, warm_out, brine_out, salt_held, done
):
    levels, rows, steps, sea_levels, sea_rows, stride, sea_stride = sizes
    width = warm.shape[1]
    warm_out[...] = warm[...]
    salt_held[...] = salt[...]
    m = wet[...].astype(f32)
    base = HALO * stride
    w = sea_weights[:, : 3 * sea_stride]
    for e, (r, other) in enumerate(((0, above), (sea_rows - 1, below))):
        mark = m[r : r + 1]
        far = other[base + 2 * sea_stride : base + 2 * sea_stride + 1, :]
        x = []
        for f in range(2):
            at = base + f * sea_stride
            mine = (2 * f + e) * sea_stride
            step = other[at : at + sea_levels, :] - sea_ends[mine : mine + sea_levels, :] * far
            step = ocean_diffusion * (mark * step)
            x.append(jnp.concatenate([step, jnp.zeros((sea_stride - sea_levels, width), f32)], 0))
        y = product(w, jnp.concatenate(x, 1))
        for f, to in enumerate((warm_out, salt_held)):
            rows_at = pl.ds(r, sea_levels, stride=sea_rows)
            to[rows_at, :] = to[rows_at, :] + mark * y[:sea_levels, f * width : (f + 1) * width]
    leave = [pltpu.make_async_copy(salt_held, brine_out, done.at[0])]
    leave[0].start()
    for move in leave:
        move.wait()


def mix_kernel(sizes, spread, weights, after, out, result, done):
    levels, rows, steps, sea_levels, sea_rows, stride, sea_stride = sizes
    width = spread.shape[1]
    depth = up_to(levels + 2 * steps, 16)
    w = weights[:, : 3 * depth]
    leave = []
    for g in range(rows // 8):
        to = result.at[g].reshape(levels * 8, width)
        for r in range(g * 8, g * 8 + 8, 2):
            y = product(
                w, jnp.concatenate([spread[(r + q) * depth : (r + q + 1) * depth, :] for q in range(2)], 1)
            )
            for q in range(2):
                to[pl.ds((r + q) % 8, levels, stride=8), :] = y[:levels, q * width : (q + 1) * width]
        leave.append(pltpu.make_async_copy(result.at[g], out.at[:, g], done.at[g]))
        leave[-1].start()
    for move in leave:
        move.wait()


def add_kernel(keep, got, after, kept, send):
    n = kept.shape[0]
    kept[...] = keep[:n] + got[:n]
    send[...] = keep[n:] + got[n:]


def heat_kernel(sizes, kept, got, wet, sea_first, before, after):
    levels, rows, steps, sea_levels, sea_rows, stride, sea_stride = sizes
    heat = kept[...] + got[...]
    heat = wet[...].astype(f32) * heat
    for l in range(sea_levels):
        after[l * sea_rows : (l + 1) * sea_rows, :] = (
            before[l * sea_rows : (l + 1) * sea_rows, :] + sea_first[l : l + 1, :] * heat
        )


def body(sky, forcing, curve, surface, rate, vmix, shares, owners, locals_, warmth, brine, wet, sea_mix):
    levels, rows, width = sky.shape
    steps = forcing.shape[0]
    sea_levels, sea_rows, _ = warmth.shape
    topk = owners.shape[1]
    stride = up_to(levels + steps + 3, 8)
    sea_stride = up_to(sea_levels, 16)
    sizes = (levels, rows, steps, sea_levels, sea_rows, stride, sea_stride)
    sky2, forcing2 = sky.reshape(-1, width), forcing.reshape(-1, width)
    warmth2, brine2 = warmth.reshape(-1, width), brine.reshape(-1, width)
    flat = lambda n, kind=f32: jax.ShapeDtypeStruct((n, width), kind)

    space = lambda *shape: pltpu.VMEM(shape, f32)
    space = lambda *shape: pltpu.VMEM(shape, f32)
    length = HALO * stride + 2 * sea_stride + 8
    ring = ("tile", "comp")
    tiles, count = lax.axis_size("tile"), lax.axis_size(ring)
    at = lax.axis_index(ring).astype(jnp.int32)[None]
    core = lax.axis_index("comp").astype(jnp.int32)[None]
    tile = lax.axis_index("tile").astype(jnp.int32)[None]
    inner, outer = call(
        functools.partial(pack_kernel, sizes), [flat(length)] * 2,
        core, sky, forcing, surface, rate, warmth2, brine2, wet, moved=4 << 20, in_specs=[SMEM] + [HBM] * 7,
        scratch=[
            space(2, levels, 8, width), space(steps, rows, width), space(2, sea_levels * sea_rows, width),
            space(2, rows, width), pltpu.VMEM(wet.shape, wet.dtype), pltpu.SemaphoreType.DMA((8,)),
        ],
        grant=FULL,
    )
    swap = lambda first: [(i + a, i + 1 - a) for i in range(first, count - 1, 2) for a in range(2)]
    outer = lax.ppermute(outer, ring, swap(1))
    inner = lax.ppermute(inner, ring, swap(0))

    depth = up_to(levels + 2 * steps, 16)
    mix_rows = up_to(levels, 16)
    area = sea_levels * sea_rows
    rows_of_mix, source_rows, own, weights, sea_weights, sea_first, sea_ends, spread, warm, salt = call(
        functools.partial(local_kernel, sizes, count - 1),
        [
            flat((steps - 1) * levels), flat(8), flat((steps - 1) * rows),
            jax.ShapeDtypeStruct((mix_rows, 2 * width), bf16),
            jax.ShapeDtypeStruct((sea_stride, 2 * width), bf16), flat(sea_stride), flat(4 * sea_stride),
            flat(rows * levels), flat(area), flat(area),
        ],
        at, vmix, curve[None], sea_mix, sky2, warmth2, brine2, wet, in_specs=[SMEM] + [VMEM] * 7,
        scratch=[space(2, sea_rows * sea_stride, width)],
        flops=4 << 30, moved=8 << 20,
    )

    half = tiles // 2 * sea_rows
    keep, send, fluxes, above, below = call(
        functools.partial(flux_kernel, sizes),
        [flat(half), flat(half), flat(2 * steps * (rows + 2 * HALO)), flat(length), flat(length)],
        core, tile, sky[-1], forcing2, surface, rate, rows_of_mix, source_rows, own, owners.T, locals_.T,
        shares.reshape(-1, width), outer, inner,
        in_specs=[SMEM] * 2 + [VMEM] * 12, scratch=[space(2 * HALO * stride, width)], moved=2 << 20,
    )
    def edge_part(after):
        return call(
            functools.partial(edge_kernel, sizes), flat(rows * depth), fluxes, spread, above, below, after,
            in_specs=[VMEM] * 4 + [ANY], flops=1 << 28, moved=4 << 20,
        )

    def shore_part(after):
        return call(
            functools.partial(shore_kernel, sizes), [flat(area), flat(area)],
            sea_weights, sea_ends, wet, warm, salt, above, below, after,
            in_specs=[VMEM] * 7 + [ANY], out_specs=[VMEM, HBM],
            scratch=[space(area, width), pltpu.SemaphoreType.DMA((1,))], flops=1 << 28, moved=4 << 20,
        )

    bit, ready, shore = tiles // 2, None, None
    while True:
        got = lax.ppermute(send, "tile", [(i, i ^ bit) for i in range(tiles)])
        if bit <= 4 and ready is None:
            ready = edge_part(keep)
            done = ready
        elif ready is not None and shore is None:
            shore = shore_part(keep)
            done = shore[0]
        else:
            done = keep
        if bit == 1:
            break
        keep, send = call(
            add_kernel, [flat(bit // 2 * sea_rows)] * 2, keep, got, done, in_specs=[VMEM, VMEM, ANY],
        )
        bit //= 2
    warm, salt = shore_part(keep) if shore is None else shore
    sky_out = call(
        functools.partial(mix_kernel, sizes), jax.ShapeDtypeStruct((levels, rows // 8, 8, width), f32),
        ready, weights, keep, in_specs=[VMEM, VMEM, ANY], out_specs=HBM,
        scratch=[space(rows // 8, levels, 8, width), pltpu.SemaphoreType.DMA((rows // 8,))],
        flops=2 << 30, moved=4 << 20,
    )
    warm = call(functools.partial(heat_kernel, sizes), flat(area), keep, got, wet, sea_first, warm, moved=2 << 20)
    return sky_out.reshape(sky.shape), warm.reshape(warmth.shape), salt.reshape(brine.shape)


def solution(mesh):
    both = P(None, ("member", "tile", "comp"), None)
    one = P(("tile", "comp"), None)
    return jax.shard_map(
        body,
        mesh=mesh,
        in_specs=(
            both, both, P(), P(("member", "tile", "comp"), None), one, P(), P(), one, one, both, both, one, P(),
        ),
        out_specs=(both, both, both),
        check_vma=False,
    )
```

```python
import functools

import jax
import jax.numpy as jnp
from jax import lax
from jax.experimental import pallas as pl
from jax.experimental.pallas import tpu as pltpu
from jax.sharding import PartitionSpec as P

atm_diffusion = 0.2
ocean_diffusion = 0.2
HALO = 4
FULL = 60
FIELDS = 8
EXACT = lax.Precision.HIGHEST
VMEM = pl.BlockSpec(memory_space=pltpu.VMEM)
HBM = pl.BlockSpec(memory_space=pltpu.HBM)
SMEM = pl.BlockSpec(memory_space=pltpu.SMEM)
ANY = pl.BlockSpec(memory_space=pl.ANY)
f32, bf16 = jnp.float32, jnp.bfloat16


def up_to(n, m):
    return -(-n // m) * m


def call(kernel, out_shape, *args, scratch=(), in_specs=None, out_specs=None, flops=0, moved=0, grant=24):
    return pl.pallas_call(
        kernel,
        out_shape=out_shape,
        in_specs=in_specs or [VMEM] * len(args),
        out_specs=out_specs or jax.tree.map(lambda _: VMEM, out_shape),
        scratch_shapes=list(scratch),
        compiler_params=pltpu.CompilerParams(vmem_limit_bytes=grant * 2**20),
        cost_estimate=pl.CostEstimate(flops=flops, bytes_accessed=moved, transcendentals=0),
    )(*args)


def copies(pairs, done):
    return [pltpu.make_async_copy(src, dst, done.at[i]) for i, (src, dst) in enumerate(pairs)]


def pack_kernel(
    sizes, core, sky, forcing, surface, rate, warmth, brine, wet, inner, outer, force, flat, marks, small, done
):
    levels, rows, steps, sea_levels, sea_rows, stride, sea_stride = sizes
    width = sky.shape[2]
    fetches = copies([(forcing, force), (surface, flat.at[0]), (rate, flat.at[1]), (wet, marks)], done)
    for fetch in fetches:
        fetch.start()

    def moves(mine):
        pairs = []
        for which, out in enumerate((inner, outer)):
            last = which == mine
            row = rows - HALO if last else 0
            pairs += [(sky.at[:, row + j], out.at[pl.ds(j * levels, levels)]) for j in range(HALO)]
            for f, field in enumerate((warmth, brine)):
                to = out.at[pl.ds(HALO * levels + f * sea_stride, sea_levels)]
                pairs.append((field.at[:, sea_rows - 1 if last else 0], to))
        return [pltpu.make_async_copy(src, dst, done.at[4 + i]) for i, (src, dst) in enumerate(pairs)]

    for mine in range(2):

        @pl.when(core[0] == mine)
        def _():
            for move in moves(mine):
                move.start()

    for fetch in fetches:
        fetch.wait()
    base = HALO * levels + 2 * sea_stride
    leave = []
    for which, out in enumerate((inner, outer)):
        last = jnp.where(core[0] == which, 1, 0)
        for j in range(HALO):
            row = last * (rows - HALO) + j
            lines = [force[s, pl.ds(row, 1), :] for s in range(steps)]
            lines += [flat[i, pl.ds(row, 1), :] for i in range(2)]
            lines += [marks[pl.ds(last * (sea_rows - 1), 1), :].astype(f32)]
            lines += [jnp.zeros((FIELDS - len(lines), width), f32)]
            small[which, j * FIELDS : (j + 1) * FIELDS, :] = jnp.concatenate(lines, 0)
        to = out.at[pl.ds(base, HALO * FIELDS)]
        leave.append(pltpu.make_async_copy(small.at[which], to, done.at[4 + 2 * (HALO + 2) + which]))
        leave[-1].start()
    for move in leave:
        move.wait()
    for mine in range(2):

        @pl.when(core[0] == mine)
        def _():
            for move in moves(mine):
                move.wait()


def split(x):
    high = x.astype(bf16)
    return high, (x - high.astype(f32)).astype(bf16)


def three_terms(w, depth):
    high = w.astype(bf16).astype(f32)
    low = w - high
    return (high + pltpu.roll(high, depth, 1) + pltpu.roll(low, 2 * depth, 1)).astype(bf16)


def inside_of(place, last_place):
    return jnp.where(place[0] > 0, 1.0, 0.0), jnp.where(place[0] < last_place, 1.0, 0.0)


def row_of(ref, first, count, step, size):
    x = ref[pl.ds(first, count, stride=step), :]
    if count < size:
        x = jnp.concatenate([x, jnp.zeros((size - count, x.shape[1]), f32)], 0)
    return x


def beside(x):
    return pltpu.roll(x, 1, 1) + pltpu.roll(x, x.shape[1] - 1, 1)


def stencil(x):
    return [x[i - 1] + x[i] + x[i + 1] + beside(x[i]) for i in range(1, len(x) - 1)]


def product(weights, x):
    high, low = split(x)
    return jnp.dot(weights, jnp.concatenate([high, low, high], 0), preferred_element_type=f32)


def local_kernel(
    sizes, last_place, place, vmix, curve, sea_mix, sky, warmth, brine, wet,
    rows_of_mix, source_rows, own, weights, sea_weights, sea_first, sea_ends, spread, warm_out, brine_out, sea_spread,
):
    levels, rows, steps, sea_levels, sea_rows, stride, sea_stride = sizes
    width = sky.shape[1]
    depth = up_to(levels + 2 * steps, 16)
    v = vmix[...]
    dot = functools.partial(jnp.dot, precision=EXACT, preferred_element_type=f32)
    powers = [v]
    for _ in range(steps - 1):
        powers.append(dot(v, powers[-1]))
    last = (lax.broadcasted_iota(jnp.int32, (levels, width), 0) == levels - 1).astype(f32)
    for s in range(1, steps):
        rows_of_mix[(s - 1) * levels : s * levels, :] = lax.dot_general(
            powers[s - 1], last, (((0,), (0,)), ((), ())), precision=EXACT, preferred_element_type=f32
        )
    by_curve = jnp.broadcast_to(curve[...], (width, levels))
    of_curve = [
        lax.dot_general(p, by_curve, (((1,), (1,)), ((), ())), precision=EXACT, preferred_element_type=f32)
        for p in powers
    ]
    of_last = [jnp.broadcast_to(p[:, levels - 1 : levels], (levels, width)) for p in powers]
    found = [of_curve[i][levels - 1 :] for i in range(steps - 1)]
    found += [of_last[i][levels - 1 :] for i in range(steps - 1)]
    found += [jnp.zeros((8 - len(found), width), f32)]
    source_rows[...] = jnp.concatenate(found, 0)
    lane = lax.broadcasted_iota(jnp.int32, (levels, width), 1)
    wide = jnp.concatenate(
        [powers[-1] * atm_diffusion**steps, jnp.zeros((levels, width - levels), f32)], 1
    )
    for j in range(steps):
        factor = atm_diffusion ** (steps - 1 - j)
        for at, value in ((j, of_curve[steps - 1 - j] * factor), (steps + j, of_last[steps - 1 - j] * -factor)):
            wide = jnp.where(lane == levels + at, value, wide)
    more = jnp.zeros((weights.shape[0] - levels, width), f32)
    wide = jnp.concatenate([wide, more], 0)
    wide = jnp.concatenate([wide, jnp.zeros_like(wide)], 1)
    weights[...] = three_terms(wide, depth)
    sea = sea_mix[...]
    sea = jnp.concatenate([sea, jnp.zeros((sea_levels, 2 * width - sea_levels), f32)], 1)
    sea = jnp.concatenate([sea, jnp.zeros((sea_stride - sea_levels, 2 * width), f32)], 0)
    sea_weights[...] = three_terms(sea, sea_stride)
    sea_first[...] = jnp.broadcast_to(sea[:, 0:1], sea_first.shape)
    sums = [jnp.zeros((rows, width), f32) for _ in range(steps - 1)]
    for l in range(levels):
        x = sky[l * rows : (l + 1) * rows, :]
        for s in range(steps - 1):
            sums[s] = sums[s] + rows_of_mix[s * levels + l : s * levels + l + 1, :] * x
    for s in range(steps - 1):
        own[s * rows : (s + 1) * rows, :] = sums[s]

    m = wet[...].astype(f32)
    mark = [m[r : r + 1] for r in range(sea_rows)]
    edge = jnp.zeros((1, width), f32)

    def near(x):
        x = [jnp.zeros_like(x[0])] + x + [jnp.zeros_like(x[0])]
        return [x[i - 1] + x[i + 1] + beside(x[i]) for i in range(1, len(x) - 1)]

    around = (
        jnp.concatenate([edge, m[:-1]], 0) + jnp.concatenate([m[1:], edge], 0) + beside(m)
    ) * ocean_diffusion
    share = [around[r : r + 1] for r in range(sea_rows)]
    for f, field in enumerate((warmth, brine)):
        for c in range(sea_stride // 8):
            count = min(8, sea_levels - c * 8)
            x = [row_of(field, c * 8 * sea_rows + r, count, sea_rows, 8) for r in range(sea_rows)]
            y = near([mark[r] * x[r] for r in range(sea_rows)])
            for r in range(sea_rows):
                at = r * sea_stride + c * 8
                sea_spread[f, at : at + 8, :] = x[r] + mark[r] * (ocean_diffusion * y[r] - x[r] * share[r])
    w = sea_weights[:, : 3 * sea_stride]
    for r in range(sea_rows):
        x = jnp.concatenate([sea_spread[f, r * sea_stride : (r + 1) * sea_stride, :] for f in range(2)], 1)
        y = product(w, x)
        for f, (field, out) in enumerate(((warmth, warm_out), (brine, brine_out))):
            old = field[pl.ds(r, sea_levels, stride=sea_rows), :]
            new = y[:sea_levels, f * width : (f + 1) * width]
            out[pl.ds(r, sea_levels, stride=sea_rows), :] = mark[r] * new + (1.0 - mark[r]) * old
            if r in (0, sea_rows - 1):
                at = (2 * f + (r > 0)) * sea_stride
                sea_ends[at : at + sea_levels, :] = old

    before, behind = inside_of(place, last_place)

    @pl.loop(0, levels // 8)
    def _(c):
        x = [sky[pl.ds(c * 8 * rows + r, 8, stride=rows), :] for r in range(rows)]
        none = jnp.zeros_like(x[0])
        beyond = 0
        for n in range(steps):
            if beyond < steps - 1 - n:
                x = [x[0]] + stencil([none] + x + [none]) + [x[-1]]
                beyond += 1
            else:
                x = stencil(x)
                beyond -= 1
            for i in range(beyond):
                x[i] = x[i] * before
                x[-1 - i] = x[-1 - i] * behind
        for r in range(rows):
            spread[pl.ds(pl.multiple_of(r * levels + c * 8, 8), 8), :] = x[r]


def cross(x):
    n, w = x.shape
    return (
        x + pltpu.roll(x, 1, 0) + pltpu.roll(x, n - 1, 0) + pltpu.roll(x, 1, 1) + pltpu.roll(x, w - 1, 1)
    )


def masked(x, rows, inside):
    return jnp.concatenate([x[:rows], x[rows:] * inside], 0)


def flux_kernel(
    sizes, last_place, bits, core, tile, place, sky, forcing, surface, rate, rows_of_mix, source_rows, own, owners,
    locals_, shares, outer, inner, keep, send, fluxes, above, below, halo, fields
):
    levels, rows, steps, sea_levels, sea_rows, stride, sea_stride = sizes
    width = sky.shape[1]
    one, two = inner[...], outer[...]
    above[...] = jnp.where(core[0] == 0, two, one)
    below[...] = jnp.where(core[0] == 0, one, two)
    base = HALO * levels + 2 * sea_stride
    for i, ref in enumerate((below, above)):
        halo[i * HALO * levels : (i + 1) * HALO * levels, :] = ref[: HALO * levels, :]
        fields[i * HALO * FIELDS : (i + 1) * HALO * FIELDS, :] = ref[base : base + HALO * FIELDS, :]

    def edge(l):
        return halo[pl.ds(l, 2 * HALO, stride=levels), :]

    def field(f):
        return fields[pl.ds(f, 2 * HALO, stride=FIELDS), :]

    before, behind = inside_of(place, last_place)
    inside = jnp.where(lax.broadcasted_iota(jnp.int32, (2 * HALO, width), 0) < HALO, behind, before)
    sums = [jnp.zeros((2 * HALO, width), f32) for _ in range(steps - 1)]
    for l in range(levels):
        x = edge(l)
        for s in range(steps - 1):
            sums[s] = sums[s] + rows_of_mix[s * levels + l : s * levels + l + 1, :] * x
    tops = [jnp.concatenate([sky[...], edge(levels - 1)], 0)]
    tops += [jnp.concatenate([own[s * rows : (s + 1) * rows, :], sums[s]], 0) for s in range(steps - 1)]
    surf = jnp.concatenate([surface[...], field(steps)], 0)
    coef = jnp.concatenate([rate[...], field(steps + 1)], 0)
    force = [
        jnp.concatenate([forcing[s * rows : (s + 1) * rows, :], field(s)], 0) for s in range(steps)
    ]

    flux = []
    for s in range(steps):
        state = tops[s]
        for i in range(s):
            m = s - 1 - i
            state = masked(cross(state) * atm_diffusion, rows, inside)
            state = state + source_rows[m : m + 1, :] * force[i]
            state = state - source_rows[steps - 1 + m : steps + m, :] * flux[i]
        flux.append(coef * (state - surf))
        reach = rows + 2 * HALO
        fluxes[pl.ds(s, reach, stride=2 * steps), :] = force[s]
        fluxes[pl.ds(steps + s, reach, stride=2 * steps), :] = flux[s]
    total = flux[0][:rows]
    for s in range(1, steps):
        total = total + flux[s][:rows]
    mean = (total / steps).astype(bf16)
    topk = owners.shape[0]
    other = owners[...] ^ tile[0]
    target = locals_[...]
    for i in range(bits):
        target = target + ((other >> i) & 1) * (sea_rows << (bits - 1 - i))
    target = jnp.concatenate([target[k : k + 1, :] for k in range(topk)], 1)
    rowed = jnp.concatenate(
        [jnp.dot(mean, shares[k * width : (k + 1) * width, :], preferred_element_type=f32) for k in range(topk)], 0
    )
    first = rowed.astype(bf16)
    left = rowed - first.astype(f32)
    second = left.astype(bf16)
    third = (left - second.astype(f32)).astype(bf16)
    half = keep.shape[0]
    hot = lax.broadcasted_iota(jnp.int32, (2 * half, topk * rows), 0) == target
    hot = jnp.where(hot, 1.0, 0.0).astype(bf16)
    sums = jnp.dot(
        jnp.concatenate([hot, hot, hot], 1), jnp.concatenate([first, second, third], 0), preferred_element_type=f32
    )
    keep[...] = sums[:half]
    send[...] = sums[half:]


def edge_kernel(
    sizes, last_place, place, fluxes, own, above, below, after, spread
):
    levels, rows, steps, sea_levels, sea_rows, stride, sea_stride = sizes
    width = own.shape[1]
    depth = up_to(levels + 2 * steps, 16)
    inside_above, inside_below = inside_of(place, last_place)

    reach = rows + 2 * HALO
    x = [fluxes[(r % reach) * 2 * steps : (r % reach + 1) * 2 * steps, :] for r in range(1 - steps, rows + steps - 1)]
    field = lax.broadcasted_iota(jnp.int32, (2 * steps, width), 0) % steps
    for n in range(1, steps):
        y = stencil(x)
        x = [jnp.where(field < steps - n, y[i], x[i + 1]) for i in range(len(y))]
        for i in range(steps - 1 - n):
            x[i] = x[i] * inside_above
            x[-1 - i] = x[-1 - i] * inside_below
    for r in range(rows):
        spread[r * depth + levels : (r + 1) * depth, :] = x[r]
        if HALO <= r < rows - HALO:
            spread[r * depth : r * depth + levels, :] = own[r * levels : (r + 1) * levels, :]

    @pl.loop(0, levels // 8)
    def _(c):
        def other(ref, j):
            return ref[pl.ds(pl.multiple_of(j * stride + c * 8, 8), 8), :]

        top, low = ([other(ref, j) for j in range(HALO)] for ref in (above, below))
        none = jnp.zeros_like(top[0])
        for n in range(steps):
            top = stencil(top + [none]) + [top[-1]]
            low = [low[0]] + stencil([none] + low)
        for i, value in enumerate(top + low):
            r = i if i < HALO else rows - 2 * HALO + i
            value = value + own[pl.ds(pl.multiple_of(r * levels + c * 8, 8), 8), :]
            spread[pl.ds(pl.multiple_of(r * depth + c * 8, 8), 8), :] = value


def shore_kernel(
    sizes, sea_weights, sea_ends, wet, warm, salt, above, below, after, warm_out, brine_out, salt_held, done
):
    levels, rows, steps, sea_levels, sea_rows, stride, sea_stride = sizes
    width = warm.shape[1]
    warm_out[...] = warm[...]
    salt_held[...] = salt[...]
    m = wet[...].astype(f32)
    base = HALO * stride
    w = sea_weights[:, : 3 * sea_stride]
    for e, (r, other) in enumerate(((0, above), (sea_rows - 1, below))):
        mark = m[r : r + 1]
        wet_at = base + 2 * sea_stride + steps + 2
        far = other[wet_at : wet_at + 1, :]
        x = []
        for f in range(2):
            at = base + f * sea_stride
            mine = (2 * f + e) * sea_stride
            step = (other[at : at + sea_levels, :] - sea_ends[mine : mine + sea_levels, :]) * far
            step = ocean_diffusion * (mark * step)
            x.append(jnp.concatenate([step, jnp.zeros((sea_stride - sea_levels, width), f32)], 0))
        y = product(w, jnp.concatenate(x, 1))
        for f, to in enumerate((warm_out, salt_held)):
            rows_at = pl.ds(r, sea_levels, stride=sea_rows)
            to[rows_at, :] = to[rows_at, :] + mark * y[:sea_levels, f * width : (f + 1) * width]
    leave = [pltpu.make_async_copy(salt_held, brine_out, done.at[0])]
    leave[0].start()
    for move in leave:
        move.wait()


def mix_kernel(sizes, spread, weights, after, out, result, done):
    levels, rows, steps, sea_levels, sea_rows, stride, sea_stride = sizes
    width = spread.shape[1]
    depth = up_to(levels + 2 * steps, 16)
    w = weights[:, : 3 * depth]
    leave = []
    for g in range(rows // 8):
        to = result.at[g].reshape(levels * 8, width)
        for r in range(g * 8, g * 8 + 8, 2):
            y = product(
                w, jnp.concatenate([spread[(r + q) * depth : (r + q + 1) * depth, :] for q in range(2)], 1)
            )
            for q in range(2):
                to[pl.ds((r + q) % 8, levels, stride=8), :] = y[:levels, q * width : (q + 1) * width]
        leave.append(pltpu.make_async_copy(result.at[g], out.at[:, g], done.at[g]))
        leave[-1].start()
    for move in leave:
        move.wait()


def add_kernel(keep, got, after, kept, send):
    n = kept.shape[0]
    kept[...] = keep[:n] + got[:n]
    send[...] = keep[n:] + got[n:]


def heat_kernel(sizes, kept, got, wet, sea_first, before, after):
    levels, rows, steps, sea_levels, sea_rows, stride, sea_stride = sizes
    heat = kept[...] + got[...]
    heat = wet[...].astype(f32) * heat
    for l in range(sea_levels):
        after[l * sea_rows : (l + 1) * sea_rows, :] = (
            before[l * sea_rows : (l + 1) * sea_rows, :] + sea_first[l : l + 1, :] * heat
        )


def body(sky, forcing, curve, surface, rate, vmix, shares, owners, locals_, warmth, brine, wet, sea_mix):
    levels, rows, width = sky.shape
    steps = forcing.shape[0]
    sea_levels, sea_rows, _ = warmth.shape
    topk = owners.shape[1]
    stride = levels
    sea_stride = up_to(sea_levels, 16)
    sizes = (levels, rows, steps, sea_levels, sea_rows, stride, sea_stride)
    sky2, forcing2 = sky.reshape(-1, width), forcing.reshape(-1, width)
    warmth2, brine2 = warmth.reshape(-1, width), brine.reshape(-1, width)
    flat = lambda n, kind=f32: jax.ShapeDtypeStruct((n, width), kind)

    space = lambda *shape: pltpu.VMEM(shape, f32)
    space = lambda *shape: pltpu.VMEM(shape, f32)
    length = HALO * stride + 2 * sea_stride + HALO * FIELDS
    ring = ("tile", "comp")
    tiles, count = lax.axis_size("tile"), lax.axis_size(ring)
    at = lax.axis_index(ring).astype(jnp.int32)[None]
    core = lax.axis_index("comp").astype(jnp.int32)[None]
    tile = lax.axis_index("tile").astype(jnp.int32)[None]
    inner, outer = call(
        functools.partial(pack_kernel, sizes), [flat(length)] * 2,
        core, sky, forcing, surface, rate, warmth, brine, wet, moved=4 << 20,
        in_specs=[SMEM] + [HBM] * 7, out_specs=[HBM] * 2,
        scratch=[
            space(steps, rows, width), space(2, rows, width), pltpu.VMEM(wet.shape, wet.dtype),
            space(2, HALO * FIELDS, width), pltpu.SemaphoreType.DMA((4 + 2 * (HALO + 2) + 2,)),
        ],
        grant=FULL,
    )
    swap = lambda first: [(i + a, i + 1 - a) for i in range(first, count - 1, 2) for a in range(2)]
    outer = lax.ppermute(outer, ring, swap(1))
    inner = lax.ppermute(inner, ring, swap(0))

    depth = up_to(levels + 2 * steps, 16)
    mix_rows = up_to(levels, 16)
    area = sea_levels * sea_rows
    rows_of_mix, source_rows, own, weights, sea_weights, sea_first, sea_ends, spread, warm, salt = call(
        functools.partial(local_kernel, sizes, count - 1),
        [
            flat((steps - 1) * levels), flat(8), flat((steps - 1) * rows),
            jax.ShapeDtypeStruct((mix_rows, 2 * width), bf16),
            jax.ShapeDtypeStruct((sea_stride, 2 * width), bf16), flat(sea_stride), flat(4 * sea_stride),
            flat(rows * levels), flat(area), flat(area),
        ],
        at, vmix, curve[None], sea_mix, sky2, warmth2, brine2, wet, in_specs=[SMEM] + [VMEM] * 7,
        scratch=[space(2, sea_rows * sea_stride, width)],
        flops=4 << 30, moved=8 << 20,
    )

    half = tiles // 2 * sea_rows
    keep, send, fluxes, above, below = call(
        functools.partial(flux_kernel, sizes, count - 1, tiles.bit_length() - 1),
        [flat(half), flat(half), flat(2 * steps * (rows + 2 * HALO)), flat(length), flat(length)],
        core, tile, at, sky[-1], forcing2, surface, rate, rows_of_mix, source_rows, own, owners.T, locals_.T,
        shares.reshape(-1, width), outer, inner,
        in_specs=[SMEM] * 3 + [VMEM] * 12,
        scratch=[space(2 * HALO * levels, width), space(2 * HALO * FIELDS, width)], moved=2 << 20,
    )
    def edge_part(after):
        return call(
            functools.partial(edge_kernel, sizes, count - 1), flat(rows * depth),
            at, fluxes, spread, above, below, after, in_specs=[SMEM] + [VMEM] * 4 + [ANY], flops=1 << 28, moved=4 << 20,
        )

    def shore_part(after):
        return call(
            functools.partial(shore_kernel, sizes), [flat(area), flat(area)],
            sea_weights, sea_ends, wet, warm, salt, above, below, after,
            in_specs=[VMEM] * 7 + [ANY], out_specs=[VMEM, HBM],
            scratch=[space(area, width), pltpu.SemaphoreType.DMA((1,))], flops=1 << 28, moved=4 << 20,
        )

    bit, ready, shore = tiles // 2, None, None
    while True:
        got = lax.ppermute(send, "tile", [(i, i ^ (tiles // 2 // bit)) for i in range(tiles)])
        if bit <= 4 and ready is None:
            ready = edge_part(keep)
            done = ready
        elif ready is not None and shore is None:
            shore = shore_part(keep)
            done = shore[0]
        else:
            done = keep
        if bit == 1:
            break
        keep, send = call(
            add_kernel, [flat(bit // 2 * sea_rows)] * 2, keep, got, done, in_specs=[VMEM, VMEM, ANY],
        )
        bit //= 2
    warm, salt = shore_part(keep) if shore is None else shore
    sky_out = call(
        functools.partial(mix_kernel, sizes), jax.ShapeDtypeStruct((levels, rows // 8, 8, width), f32),
        ready, weights, keep, in_specs=[VMEM, VMEM, ANY], out_specs=HBM,
        scratch=[space(rows // 8, levels, 8, width), pltpu.SemaphoreType.DMA((rows // 8,))],
        flops=2 << 30, moved=4 << 20,
    )
    warm = call(functools.partial(heat_kernel, sizes), flat(area), keep, got, wet, sea_first, warm, moved=2 << 20)
    return sky_out.reshape(sky.shape), warm.reshape(warmth.shape), salt.reshape(brine.shape)


def solution(mesh):
    both = P(None, ("member", "tile", "comp"), None)
    one = P(("tile", "comp"), None)
    return jax.shard_map(
        body,
        mesh=mesh,
        in_specs=(
            both, both, P(), P(("member", "tile", "comp"), None), one, P(), P(), one, one, both, both, one, P(),
        ),
        out_specs=(both, both, both),
        check_vma=False,
    )
```

```python
import functools

import jax
import jax.numpy as jnp
from jax import lax
from jax.experimental import pallas as pl
from jax.experimental.pallas import tpu as pltpu
from jax.sharding import PartitionSpec as P

atm_diffusion = 0.2
ocean_diffusion = 0.2
HALO = 4
FULL = 60
EXACT = lax.Precision.HIGHEST
VMEM = pl.BlockSpec(memory_space=pltpu.VMEM)
HBM = pl.BlockSpec(memory_space=pltpu.HBM)
SMEM = pl.BlockSpec(memory_space=pltpu.SMEM)
ANY = pl.BlockSpec(memory_space=pl.ANY)
f32, bf16 = jnp.float32, jnp.bfloat16


def up_to(n, m):
    return -(-n // m) * m


def call(kernel, out_shape, *args, scratch=(), in_specs=None, out_specs=None, flops=0, moved=0, grant=24):
    return pl.pallas_call(
        kernel,
        out_shape=out_shape,
        in_specs=in_specs or [VMEM] * len(args),
        out_specs=out_specs or jax.tree.map(lambda _: VMEM, out_shape),
        scratch_shapes=list(scratch),
        compiler_params=pltpu.CompilerParams(vmem_limit_bytes=grant * 2**20),
        cost_estimate=pl.CostEstimate(flops=flops, bytes_accessed=moved, transcendentals=0),
    )(*args)


def copies(pairs, done):
    return [pltpu.make_async_copy(src, dst, done.at[i]) for i, (src, dst) in enumerate(pairs)]


def pack_kernel(
    sizes, core, sky, forcing, surface, rate, warmth, brine, wet, inner, outer,
    ends, force, sea, flat, marks, done
):
    levels, rows, steps, sea_levels, sea_rows, stride, sea_stride = sizes
    width = sky.shape[2]
    low = rows - 8
    moves = copies(
        [
            (sky.at[:, 0:8, :], ends.at[0]), (sky.at[:, low:rows, :], ends.at[1]), (forcing, force),
            (surface, flat.at[0]), (rate, flat.at[1]), (warmth, sea.at[0]), (brine, sea.at[1]), (wet, marks),
        ],
        done,
    )
    for move in moves:
        move.start()
    for move in moves:
        move.wait()
    end = ends.reshape(2 * levels * 8, width)
    for which, out in enumerate((inner, outer)):
        last = jnp.where(core[0] == 0, 1 - which, which)
        sea_row = last * (sea_rows - 1)
        for j in range(HALO):
            row = last * (rows - HALO) + j
            first = last * (levels * 8 + 8 - HALO) + j
            out[j * stride : j * stride + levels, :] = end[pl.ds(first, levels, stride=8), :]
            base = j * stride + levels
            tail = [force[s, pl.ds(row, 1), :] for s in range(steps)]
            tail += [flat[0, pl.ds(row, 1), :], flat[1, pl.ds(row, 1), :], jnp.ones((1, width), f32)]
            tail += [jnp.zeros((stride - levels - len(tail), width), f32)]
            out[base : (j + 1) * stride, :] = jnp.concatenate(tail, 0)
        base = HALO * stride
        edge = marks[pl.ds(sea_row, 1), :].astype(f32)
        for f in range(2):
            out[base : base + sea_levels, :] = sea[f, pl.ds(sea_row, sea_levels, stride=sea_rows), :] * edge
            base += sea_stride
        out[base : base + 8, :] = jnp.concatenate([edge, jnp.zeros((7, width), f32)], 0)


def split(x):
    high = x.astype(bf16)
    return high, (x - high.astype(f32)).astype(bf16)


def three_terms(w, depth):
    high = w.astype(bf16).astype(f32)
    low = w - high
    return (high + pltpu.roll(high, depth, 1) + pltpu.roll(low, 2 * depth, 1)).astype(bf16)


def row_of(ref, first, count, step, size):
    x = ref[pl.ds(first, count, stride=step), :]
    if count < size:
        x = jnp.concatenate([x, jnp.zeros((size - count, x.shape[1]), f32)], 0)
    return x


def beside(x):
    return pltpu.roll(x, 1, 1) + pltpu.roll(x, x.shape[1] - 1, 1)


def stencil(x):
    return [x[i - 1] + x[i] + x[i + 1] + beside(x[i]) for i in range(1, len(x) - 1)]


def product(weights, x):
    high, low = split(x)
    return jnp.dot(weights, jnp.concatenate([high, low, high], 0), preferred_element_type=f32)


def local_kernel(
    sizes, last_place, place, vmix, curve, sea_mix, sky, warmth, brine, wet,
    rows_of_mix, source_rows, own, weights, sea_weights, sea_first, sea_ends, spread, warm_out, brine_out, sea_spread,
):
    levels, rows, steps, sea_levels, sea_rows, stride, sea_stride = sizes
    width = sky.shape[1]
    depth = up_to(levels + 2 * steps, 16)
    v = vmix[...]
    dot = functools.partial(jnp.dot, precision=EXACT, preferred_element_type=f32)
    powers = [v]
    for _ in range(steps - 1):
        powers.append(dot(v, powers[-1]))
    last = (lax.broadcasted_iota(jnp.int32, (levels, width), 0) == levels - 1).astype(f32)
    for s in range(1, steps):
        rows_of_mix[(s - 1) * levels : s * levels, :] = lax.dot_general(
            powers[s - 1], last, (((0,), (0,)), ((), ())), precision=EXACT, preferred_element_type=f32
        )
    by_curve = jnp.broadcast_to(curve[...], (width, levels))
    of_curve = [
        lax.dot_general(p, by_curve, (((1,), (1,)), ((), ())), precision=EXACT, preferred_element_type=f32)
        for p in powers
    ]
    of_last = [jnp.broadcast_to(p[:, levels - 1 : levels], (levels, width)) for p in powers]
    found = [of_curve[i][levels - 1 :] for i in range(steps - 1)]
    found += [of_last[i][levels - 1 :] for i in range(steps - 1)]
    found += [jnp.zeros((8 - len(found), width), f32)]
    source_rows[...] = jnp.concatenate(found, 0)
    lane = lax.broadcasted_iota(jnp.int32, (levels, width), 1)
    wide = jnp.concatenate(
        [powers[-1] * atm_diffusion**steps, jnp.zeros((levels, width - levels), f32)], 1
    )
    for j in range(steps):
        factor = atm_diffusion ** (steps - 1 - j)
        for at, value in ((j, of_curve[steps - 1 - j] * factor), (steps + j, of_last[steps - 1 - j] * -factor)):
            wide = jnp.where(lane == levels + at, value, wide)
    more = jnp.zeros((weights.shape[0] - levels, width), f32)
    wide = jnp.concatenate([wide, more], 0)
    wide = jnp.concatenate([wide, jnp.zeros_like(wide)], 1)
    weights[...] = three_terms(wide, depth)
    sea = sea_mix[...]
    sea = jnp.concatenate([sea, jnp.zeros((sea_levels, 2 * width - sea_levels), f32)], 1)
    sea = jnp.concatenate([sea, jnp.zeros((sea_stride - sea_levels, 2 * width), f32)], 0)
    sea_weights[...] = three_terms(sea, sea_stride)
    sea_first[...] = jnp.broadcast_to(sea[:, 0:1], sea_first.shape)
    sums = [jnp.zeros((rows, width), f32) for _ in range(steps - 1)]
    for l in range(levels):
        x = sky[l * rows : (l + 1) * rows, :]
        for s in range(steps - 1):
            sums[s] = sums[s] + rows_of_mix[s * levels + l : s * levels + l + 1, :] * x
    for s in range(steps - 1):
        own[s * rows : (s + 1) * rows, :] = sums[s]

    m = wet[...].astype(f32)
    mark = [m[r : r + 1] for r in range(sea_rows)]
    edge = jnp.zeros((1, width), f32)

    def near(x):
        x = [jnp.zeros_like(x[0])] + x + [jnp.zeros_like(x[0])]
        return [x[i - 1] + x[i + 1] + beside(x[i]) for i in range(1, len(x) - 1)]

    around = (
        jnp.concatenate([edge, m[:-1]], 0) + jnp.concatenate([m[1:], edge], 0) + beside(m)
    ) * ocean_diffusion
    share = [around[r : r + 1] for r in range(sea_rows)]
    for f, field in enumerate((warmth, brine)):
        for c in range(sea_stride // 8):
            count = min(8, sea_levels - c * 8)
            x = [row_of(field, c * 8 * sea_rows + r, count, sea_rows, 8) for r in range(sea_rows)]
            y = near([mark[r] * x[r] for r in range(sea_rows)])
            for r in range(sea_rows):
                at = r * sea_stride + c * 8
                sea_spread[f, at : at + 8, :] = x[r] + mark[r] * (ocean_diffusion * y[r] - x[r] * share[r])
    w = sea_weights[:, : 3 * sea_stride]
    for r in range(sea_rows):
        x = jnp.concatenate([sea_spread[f, r * sea_stride : (r + 1) * sea_stride, :] for f in range(2)], 1)
        y = product(w, x)
        for f, (field, out) in enumerate(((warmth, warm_out), (brine, brine_out))):
            old = field[pl.ds(r, sea_levels, stride=sea_rows), :]
            new = y[:sea_levels, f * width : (f + 1) * width]
            out[pl.ds(r, sea_levels, stride=sea_rows), :] = mark[r] * new + (1.0 - mark[r]) * old
            if r in (0, sea_rows - 1):
                at = (2 * f + (r > 0)) * sea_stride
                sea_ends[at : at + sea_levels, :] = old

    before = jnp.where(place[0] > 0, 1.0, 0.0)
    behind = jnp.where(place[0] < last_place, 1.0, 0.0)

    @pl.loop(0, levels // 8)
    def _(c):
        x = [sky[pl.ds(c * 8 * rows + r, 8, stride=rows), :] for r in range(rows)]
        none = jnp.zeros_like(x[0])
        beyond = 0
        for n in range(steps):
            if beyond < steps - 1 - n:
                x = [x[0]] + stencil([none] + x + [none]) + [x[-1]]
                beyond += 1
            else:
                x = stencil(x)
                beyond -= 1
            for i in range(beyond):
                x[i] = x[i] * before
                x[-1 - i] = x[-1 - i] * behind
        for r in range(rows):
            spread[pl.ds(pl.multiple_of(r * levels + c * 8, 8), 8), :] = x[r]


def cross(x):
    n, w = x.shape
    return (
        x + pltpu.roll(x, 1, 0) + pltpu.roll(x, n - 1, 0) + pltpu.roll(x, 1, 1) + pltpu.roll(x, w - 1, 1)
    )


def masked(x, rows, inside):
    return jnp.concatenate([x[:rows], x[rows:] * inside], 0)


def flux_kernel(
    sizes, core, tile, sky, forcing, surface, rate, rows_of_mix, source_rows, own, owners, locals_, shares, outer, inner,
    keep, send_1, send_2, send_3, fluxes, above, below, halo
):
    levels, rows, steps, sea_levels, sea_rows, stride, sea_stride = sizes
    width = sky.shape[1]
    one, two = inner[...], outer[...]
    above[...] = jnp.where(core[0] == 0, two, one)
    below[...] = jnp.where(core[0] == 0, one, two)
    halo[: HALO * stride, :] = below[: HALO * stride, :]
    halo[HALO * stride :, :] = above[: HALO * stride, :]

    def edge(l):
        return halo[pl.ds(l, 2 * HALO, stride=stride), :]

    inside = edge(levels + steps + 2)
    sums = [jnp.zeros((2 * HALO, width), f32) for _ in range(steps - 1)]
    for l in range(levels):
        x = edge(l)
        for s in range(steps - 1):
            sums[s] = sums[s] + rows_of_mix[s * levels + l : s * levels + l + 1, :] * x
    tops = [jnp.concatenate([sky[...], edge(levels - 1)], 0)]
    tops += [jnp.concatenate([own[s * rows : (s + 1) * rows, :], sums[s]], 0) for s in range(steps - 1)]
    surf = jnp.concatenate([surface[...], edge(levels + steps)], 0)
    coef = jnp.concatenate([rate[...], edge(levels + steps + 1)], 0)
    force = [
        jnp.concatenate([forcing[s * rows : (s + 1) * rows, :], edge(levels + s)], 0) for s in range(steps)
    ]

    flux = []
    for s in range(steps):
        state = tops[s]
        for i in range(s):
            m = s - 1 - i
            state = masked(cross(state) * atm_diffusion, rows, inside)
            state = state + source_rows[m : m + 1, :] * force[i]
            state = state - source_rows[steps - 1 + m : steps + m, :] * flux[i]
        flux.append(coef * (state - surf))
        reach = rows + 2 * HALO
        fluxes[pl.ds(s, reach, stride=2 * steps), :] = force[s]
        fluxes[pl.ds(steps + s, reach, stride=2 * steps), :] = flux[s]
    total = flux[0][:rows]
    for s in range(1, steps):
        total = total + flux[s][:rows]
    mean = (total / steps).astype(bf16)
    topk = owners.shape[0]
    target = (owners[...] ^ tile[0]) * sea_rows + locals_[...]
    target = jnp.concatenate([target[k : k + 1, :] for k in range(topk)], 1)
    rowed = jnp.concatenate(
        [jnp.dot(mean, shares[k * width : (k + 1) * width, :], preferred_element_type=f32) for k in range(topk)], 0
    )
    first = rowed.astype(bf16)
    left = rowed - first.astype(f32)
    second = left.astype(bf16)
    third = (left - second.astype(f32)).astype(bf16)
    part = keep.shape[0]
    hot = lax.broadcasted_iota(jnp.int32, (4 * part, topk * rows), 0) == target
    hot = jnp.where(hot, 1.0, 0.0).astype(bf16)
    sums = jnp.dot(
        jnp.concatenate([hot, hot, hot], 1), jnp.concatenate([first, second, third], 0), preferred_element_type=f32
    )
    for q, to in enumerate((keep, send_1, send_2, send_3)):
        to[...] = sums[q * part : (q + 1) * part]


def edge_kernel(
    sizes, fluxes, own, above, below, after, spread
):
    levels, rows, steps, sea_levels, sea_rows, stride, sea_stride = sizes
    width = own.shape[1]
    depth = up_to(levels + 2 * steps, 16)
    flag = levels + steps + 2
    inside_above, inside_below = above[flag : flag + 1, :], below[flag : flag + 1, :]

    reach = rows + 2 * HALO
    x = [fluxes[(r % reach) * 2 * steps : (r % reach + 1) * 2 * steps, :] for r in range(1 - steps, rows + steps - 1)]
    field = lax.broadcasted_iota(jnp.int32, (2 * steps, width), 0) % steps
    for n in range(1, steps):
        y = stencil(x)
        x = [jnp.where(field < steps - n, y[i], x[i + 1]) for i in range(len(y))]
        for i in range(steps - 1 - n):
            x[i] = x[i] * inside_above
            x[-1 - i] = x[-1 - i] * inside_below
    for r in range(rows):
        spread[r * depth + levels : (r + 1) * depth, :] = x[r]
        if HALO <= r < rows - HALO:
            spread[r * depth : r * depth + levels, :] = own[r * levels : (r + 1) * levels, :]

    @pl.loop(0, levels // 8)
    def _(c):
        def other(ref, j):
            return ref[pl.ds(pl.multiple_of(j * stride + c * 8, 8), 8), :]

        top, low = ([other(ref, j) for j in range(HALO)] for ref in (above, below))
        none = jnp.zeros_like(top[0])
        for n in range(steps):
            top = stencil(top + [none]) + [top[-1]]
            low = [low[0]] + stencil([none] + low)
        for i, value in enumerate(top + low):
            r = i if i < HALO else rows - 2 * HALO + i
            value = value + own[pl.ds(pl.multiple_of(r * levels + c * 8, 8), 8), :]
            spread[pl.ds(pl.multiple_of(r * depth + c * 8, 8), 8), :] = value


def shore_kernel(
    sizes, sea_weights, sea_ends, wet, warm, salt, above, below, after, warm_out, brine_out, salt_held, done
):
    levels, rows, steps, sea_levels, sea_rows, stride, sea_stride = sizes
    width = warm.shape[1]
    warm_out[...] = warm[...]
    salt_held[...] = salt[...]
    m = wet[...].astype(f32)
    base = HALO * stride
    w = sea_weights[:, : 3 * sea_stride]
    for e, (r, other) in enumerate(((0, above), (sea_rows - 1, below))):
        mark = m[r : r + 1]
        far = other[base + 2 * sea_stride : base + 2 * sea_stride + 1, :]
        x = []
        for f in range(2):
            at = base + f * sea_stride
            mine = (2 * f + e) * sea_stride
            step = other[at : at + sea_levels, :] - sea_ends[mine : mine + sea_levels, :] * far
            step = ocean_diffusion * (mark * step)
            x.append(jnp.concatenate([step, jnp.zeros((sea_stride - sea_levels, width), f32)], 0))
        y = product(w, jnp.concatenate(x, 1))
        for f, to in enumerate((warm_out, salt_held)):
            rows_at = pl.ds(r, sea_levels, stride=sea_rows)
            to[rows_at, :] = to[rows_at, :] + mark * y[:sea_levels, f * width : (f + 1) * width]
    leave = [pltpu.make_async_copy(salt_held, brine_out, done.at[0])]
    leave[0].start()
    for move in leave:
        move.wait()


def mix_kernel(sizes, spread, weights, after, out, result, done):
    levels, rows, steps, sea_levels, sea_rows, stride, sea_stride = sizes
    width = spread.shape[1]
    depth = up_to(levels + 2 * steps, 16)
    w = weights[:, : 3 * depth]
    leave = []
    for g in range(rows // 8):
        to = result.at[g].reshape(levels * 8, width)
        for r in range(g * 8, g * 8 + 8, 2):
            y = product(
                w, jnp.concatenate([spread[(r + q) * depth : (r + q + 1) * depth, :] for q in range(2)], 1)
            )
            for q in range(2):
                to[pl.ds((r + q) % 8, levels, stride=8), :] = y[:levels, q * width : (q + 1) * width]
        leave.append(pltpu.make_async_copy(result.at[g], out.at[:, g], done.at[g]))
        leave[-1].start()
    for move in leave:
        move.wait()


def add_kernel(keep, *others):
    gots, (after, kept, send) = others[:-3], others[-3:]
    total = keep[...]
    for got in gots:
        total = total + got[...]
    n = kept.shape[0]
    kept[...] = total[:n]
    send[...] = total[n:]


def heat_kernel(sizes, kept, got, wet, sea_first, before, after):
    levels, rows, steps, sea_levels, sea_rows, stride, sea_stride = sizes
    heat = kept[...] + got[...]
    heat = wet[...].astype(f32) * heat
    for l in range(sea_levels):
        after[l * sea_rows : (l + 1) * sea_rows, :] = (
            before[l * sea_rows : (l + 1) * sea_rows, :] + sea_first[l : l + 1, :] * heat
        )


def body(sky, forcing, curve, surface, rate, vmix, shares, owners, locals_, warmth, brine, wet, sea_mix):
    levels, rows, width = sky.shape
    steps = forcing.shape[0]
    sea_levels, sea_rows, _ = warmth.shape
    topk = owners.shape[1]
    stride = up_to(levels + steps + 3, 8)
    sea_stride = up_to(sea_levels, 16)
    sizes = (levels, rows, steps, sea_levels, sea_rows, stride, sea_stride)
    sky2, forcing2 = sky.reshape(-1, width), forcing.reshape(-1, width)
    warmth2, brine2 = warmth.reshape(-1, width), brine.reshape(-1, width)
    flat = lambda n, kind=f32: jax.ShapeDtypeStruct((n, width), kind)

    space = lambda *shape: pltpu.VMEM(shape, f32)
    space = lambda *shape: pltpu.VMEM(shape, f32)
    length = HALO * stride + 2 * sea_stride + 8
    ring = ("tile", "comp")
    tiles, count = lax.axis_size("tile"), lax.axis_size(ring)
    at = lax.axis_index(ring).astype(jnp.int32)[None]
    core = lax.axis_index("comp").astype(jnp.int32)[None]
    tile = lax.axis_index("tile").astype(jnp.int32)[None]
    inner, outer = call(
        functools.partial(pack_kernel, sizes), [flat(length)] * 2,
        core, sky, forcing, surface, rate, warmth2, brine2, wet, moved=4 << 20, in_specs=[SMEM] + [HBM] * 7,
        scratch=[
            space(2, levels, 8, width), space(steps, rows, width), space(2, sea_levels * sea_rows, width),
            space(2, rows, width), pltpu.VMEM(wet.shape, wet.dtype), pltpu.SemaphoreType.DMA((8,)),
        ],
        grant=FULL,
    )
    swap = lambda first: [(i + a, i + 1 - a) for i in range(first, count - 1, 2) for a in range(2)]
    outer = lax.ppermute(outer, ring, swap(1))
    inner = lax.ppermute(inner, ring, swap(0))

    depth = up_to(levels + 2 * steps, 16)
    mix_rows = up_to(levels, 16)
    area = sea_levels * sea_rows
    rows_of_mix, source_rows, own, weights, sea_weights, sea_first, sea_ends, spread, warm, salt = call(
        functools.partial(local_kernel, sizes, count - 1),
        [
            flat((steps - 1) * levels), flat(8), flat((steps - 1) * rows),
            jax.ShapeDtypeStruct((mix_rows, 2 * width), bf16),
            jax.ShapeDtypeStruct((sea_stride, 2 * width), bf16), flat(sea_stride), flat(4 * sea_stride),
            flat(rows * levels), flat(area), flat(area),
        ],
        at, vmix, curve[None], sea_mix, sky2, warmth2, brine2, wet, in_specs=[SMEM] + [VMEM] * 7,
        scratch=[space(2, sea_rows * sea_stride, width)],
        flops=4 << 30, moved=8 << 20,
    )

    part = tiles // 4 * sea_rows
    keep, send_1, send_2, send_3, fluxes, above, below = call(
        functools.partial(flux_kernel, sizes),
        [flat(part)] * 4 + [flat(2 * steps * (rows + 2 * HALO)), flat(length), flat(length)],
        core, tile, sky[-1], forcing2, surface, rate, rows_of_mix, source_rows, own, owners.T, locals_.T,
        shares.reshape(-1, width), outer, inner,
        in_specs=[SMEM] * 2 + [VMEM] * 12, scratch=[space(2 * HALO * stride, width)], moved=2 << 20,
    )
    def edge_part(after):
        return call(
            functools.partial(edge_kernel, sizes), flat(rows * depth), fluxes, spread, above, below, after,
            in_specs=[VMEM] * 4 + [ANY], flops=1 << 28, moved=4 << 20,
        )

    def shore_part(after):
        return call(
            functools.partial(shore_kernel, sizes), [flat(area), flat(area)],
            sea_weights, sea_ends, wet, warm, salt, above, below, after,
            in_specs=[VMEM] * 7 + [ANY], out_specs=[VMEM, HBM],
            scratch=[space(area, width), pltpu.SemaphoreType.DMA((1,))], flops=1 << 28, moved=4 << 20,
        )

    bit = tiles // 4
    gots = [
        lax.ppermute(x, "tile", [(i, i ^ (q * bit)) for i in range(tiles)])
        for q, x in ((1, send_1), (2, send_2), (3, send_3))
    ]
    ready = edge_part(keep)
    while bit > 1:
        bit //= 2
        keep, send = call(
            add_kernel, [flat(bit * sea_rows)] * 2, keep, *gots, ready, in_specs=[VMEM] * (1 + len(gots)) + [ANY],
        )
        gots = [lax.ppermute(send, "tile", [(i, i ^ bit) for i in range(tiles)])]
    got = gots[0]
    warm, salt = shore_part(keep)
    sky_out = call(
        functools.partial(mix_kernel, sizes), jax.ShapeDtypeStruct((levels, rows // 8, 8, width), f32),
        ready, weights, keep, in_specs=[VMEM, VMEM, ANY], out_specs=HBM,
        scratch=[space(rows // 8, levels, 8, width), pltpu.SemaphoreType.DMA((rows // 8,))],
        flops=2 << 30, moved=4 << 20,
    )
    warm = call(functools.partial(heat_kernel, sizes), flat(area), keep, got, wet, sea_first, warm, moved=2 << 20)
    return sky_out.reshape(sky.shape), warm.reshape(warmth.shape), salt.reshape(brine.shape)


def solution(mesh):
    both = P(None, ("member", "tile", "comp"), None)
    one = P(("tile", "comp"), None)
    return jax.shard_map(
        body,
        mesh=mesh,
        in_specs=(
            both, both, P(), P(("member", "tile", "comp"), None), one, P(), P(), one, one, both, both, one, P(),
        ),
        out_specs=(both, both, both),
        check_vma=False,
    )
```

```python
import functools

import jax
import jax.numpy as jnp
from jax import lax
from jax.experimental import pallas as pl
from jax.experimental.pallas import tpu as pltpu
from jax.sharding import PartitionSpec as P

atm_diffusion = 0.2
ocean_diffusion = 0.2
HALO = 4
FULL = 60
EXACT = lax.Precision.HIGHEST
VMEM = pl.BlockSpec(memory_space=pltpu.VMEM)
HBM = pl.BlockSpec(memory_space=pltpu.HBM)
SMEM = pl.BlockSpec(memory_space=pltpu.SMEM)
ANY = pl.BlockSpec(memory_space=pl.ANY)
f32, bf16 = jnp.float32, jnp.bfloat16


def up_to(n, m):
    return -(-n // m) * m


def call(kernel, out_shape, *args, scratch=(), in_specs=None, out_specs=None, flops=0, moved=0, grant=24):
    return pl.pallas_call(
        kernel,
        out_shape=out_shape,
        in_specs=in_specs or [VMEM] * len(args),
        out_specs=out_specs or jax.tree.map(lambda _: VMEM, out_shape),
        scratch_shapes=list(scratch),
        compiler_params=pltpu.CompilerParams(vmem_limit_bytes=grant * 2**20),
        cost_estimate=pl.CostEstimate(flops=flops, bytes_accessed=moved, transcendentals=0),
    )(*args)


def copies(pairs, done):
    return [pltpu.make_async_copy(src, dst, done.at[i]) for i, (src, dst) in enumerate(pairs)]


def pack_kernel(
    sizes, core, sky, forcing, surface, rate, warmth, brine, wet, inner, outer,
    ends, force, sea, flat, marks, done
):
    levels, rows, steps, sea_levels, sea_rows, stride, sea_stride = sizes
    width = sky.shape[2]
    low = rows - 8
    moves = copies(
        [
            (sky.at[:, 0:8, :], ends.at[0]), (sky.at[:, low:rows, :], ends.at[1]), (forcing, force),
            (surface, flat.at[0]), (rate, flat.at[1]), (warmth, sea.at[0]), (brine, sea.at[1]), (wet, marks),
        ],
        done,
    )
    for move in moves:
        move.start()
    for move in moves:
        move.wait()
    end = ends.reshape(2 * levels * 8, width)
    for which, out in enumerate((inner, outer)):
        last = jnp.where(core[0] == 0, 1 - which, which)
        sea_row = last * (sea_rows - 1)
        for j in range(HALO):
            row = last * (rows - HALO) + j
            first = last * (levels * 8 + 8 - HALO) + j
            out[j * stride : j * stride + levels, :] = end[pl.ds(first, levels, stride=8), :]
            base = j * stride + levels
            tail = [force[s, pl.ds(row, 1), :] for s in range(steps)]
            tail += [flat[0, pl.ds(row, 1), :], flat[1, pl.ds(row, 1), :], jnp.ones((1, width), f32)]
            tail += [jnp.zeros((stride - levels - len(tail), width), f32)]
            out[base : (j + 1) * stride, :] = jnp.concatenate(tail, 0)
        base = HALO * stride
        edge = marks[pl.ds(sea_row, 1), :].astype(f32)
        for f in range(2):
            out[base : base + sea_levels, :] = sea[f, pl.ds(sea_row, sea_levels, stride=sea_rows), :] * edge
            base += sea_stride
        out[base : base + 8, :] = jnp.concatenate([edge, jnp.zeros((7, width), f32)], 0)


def split(x):
    high = x.astype(bf16)
    return high, (x - high.astype(f32)).astype(bf16)


def three_terms(w, depth):
    high = w.astype(bf16).astype(f32)
    low = w - high
    return (high + pltpu.roll(high, depth, 1) + pltpu.roll(low, 2 * depth, 1)).astype(bf16)


def row_of(ref, first, count, step, size):
    x = ref[pl.ds(first, count, stride=step), :]
    if count < size:
        x = jnp.concatenate([x, jnp.zeros((size - count, x.shape[1]), f32)], 0)
    return x


def beside(x):
    return pltpu.roll(x, 1, 1) + pltpu.roll(x, x.shape[1] - 1, 1)


def stencil(x):
    return [x[i - 1] + x[i] + x[i + 1] + beside(x[i]) for i in range(1, len(x) - 1)]


def product(weights, x):
    high, low = split(x)
    return jnp.dot(weights, jnp.concatenate([high, low, high], 0), preferred_element_type=f32)


def local_kernel(
    sizes, last_place, place, vmix, curve, sea_mix, sky, warmth, brine, wet,
    rows_of_mix, source_rows, own, weights, sea_weights, sea_first, sea_ends, spread, warm_out, brine_out, sea_spread,
):
    levels, rows, steps, sea_levels, sea_rows, stride, sea_stride = sizes
    width = sky.shape[1]
    depth = up_to(levels + 2 * steps, 16)
    v = vmix[...]
    dot = functools.partial(jnp.dot, precision=EXACT, preferred_element_type=f32)
    powers = [v]
    for _ in range(steps - 1):
        powers.append(dot(v, powers[-1]))
    last = (lax.broadcasted_iota(jnp.int32, (levels, width), 0) == levels - 1).astype(f32)
    for s in range(1, steps):
        rows_of_mix[(s - 1) * levels : s * levels, :] = lax.dot_general(
            powers[s - 1], last, (((0,), (0,)), ((), ())), precision=EXACT, preferred_element_type=f32
        )
    by_curve = jnp.broadcast_to(curve[...], (width, levels))
    of_curve = [
        lax.dot_general(p, by_curve, (((1,), (1,)), ((), ())), precision=EXACT, preferred_element_type=f32)
        for p in powers
    ]
    of_last = [jnp.broadcast_to(p[:, levels - 1 : levels], (levels, width)) for p in powers]
    found = [of_curve[i][levels - 1 :] for i in range(steps - 1)]
    found += [of_last[i][levels - 1 :] for i in range(steps - 1)]
    found += [jnp.zeros((8 - len(found), width), f32)]
    source_rows[...] = jnp.concatenate(found, 0)
    lane = lax.broadcasted_iota(jnp.int32, (levels, width), 1)
    wide = jnp.concatenate(
        [powers[-1] * atm_diffusion**steps, jnp.zeros((levels, width - levels), f32)], 1
    )
    for j in range(steps):
        factor = atm_diffusion ** (steps - 1 - j)
        for at, value in ((j, of_curve[steps - 1 - j] * factor), (steps + j, of_last[steps - 1 - j] * -factor)):
            wide = jnp.where(lane == levels + at, value, wide)
    more = jnp.zeros((weights.shape[0] - levels, width), f32)
    wide = jnp.concatenate([wide, more], 0)
    wide = jnp.concatenate([wide, jnp.zeros_like(wide)], 1)
    weights[...] = three_terms(wide, depth)
    sea = sea_mix[...]
    sea = jnp.concatenate([sea, jnp.zeros((sea_levels, 2 * width - sea_levels), f32)], 1)
    sea = jnp.concatenate([sea, jnp.zeros((sea_stride - sea_levels, 2 * width), f32)], 0)
    sea_weights[...] = three_terms(sea, sea_stride)
    sea_first[...] = jnp.broadcast_to(sea[:, 0:1], sea_first.shape)
    sums = [jnp.zeros((rows, width), f32) for _ in range(steps - 1)]
    for l in range(levels):
        x = sky[l * rows : (l + 1) * rows, :]
        for s in range(steps - 1):
            sums[s] = sums[s] + rows_of_mix[s * levels + l : s * levels + l + 1, :] * x
    for s in range(steps - 1):
        own[s * rows : (s + 1) * rows, :] = sums[s]

    m = wet[...].astype(f32)
    mark = [m[r : r + 1] for r in range(sea_rows)]
    edge = jnp.zeros((1, width), f32)

    def near(x):
        x = [jnp.zeros_like(x[0])] + x + [jnp.zeros_like(x[0])]
        return [x[i - 1] + x[i + 1] + beside(x[i]) for i in range(1, len(x) - 1)]

    around = (
        jnp.concatenate([edge, m[:-1]], 0) + jnp.concatenate([m[1:], edge], 0) + beside(m)
    ) * ocean_diffusion
    share = [around[r : r + 1] for r in range(sea_rows)]
    for f, field in enumerate((warmth, brine)):
        for c in range(sea_stride // 8):
            count = min(8, sea_levels - c * 8)
            x = [row_of(field, c * 8 * sea_rows + r, count, sea_rows, 8) for r in range(sea_rows)]
            y = near([mark[r] * x[r] for r in range(sea_rows)])
            for r in range(sea_rows):
                at = r * sea_stride + c * 8
                sea_spread[f, at : at + 8, :] = x[r] + mark[r] * (ocean_diffusion * y[r] - x[r] * share[r])
    w = sea_weights[:, : 3 * sea_stride]
    for r in range(sea_rows):
        x = jnp.concatenate([sea_spread[f, r * sea_stride : (r + 1) * sea_stride, :] for f in range(2)], 1)
        y = product(w, x)
        for f, (field, out) in enumerate(((warmth, warm_out), (brine, brine_out))):
            old = field[pl.ds(r, sea_levels, stride=sea_rows), :]
            new = y[:sea_levels, f * width : (f + 1) * width]
            out[pl.ds(r, sea_levels, stride=sea_rows), :] = mark[r] * new + (1.0 - mark[r]) * old
            if r in (0, sea_rows - 1):
                at = (2 * f + (r > 0)) * sea_stride
                sea_ends[at : at + sea_levels, :] = old

    before = jnp.where(place[0] > 0, 1.0, 0.0)
    behind = jnp.where(place[0] < last_place, 1.0, 0.0)

    @pl.loop(0, levels // 8)
    def _(c):
        x = [sky[pl.ds(c * 8 * rows + r, 8, stride=rows), :] for r in range(rows)]
        none = jnp.zeros_like(x[0])
        beyond = 0
        for n in range(steps):
            if beyond < steps - 1 - n:
                x = [x[0]] + stencil([none] + x + [none]) + [x[-1]]
                beyond += 1
            else:
                x = stencil(x)
                beyond -= 1
            for i in range(beyond):
                x[i] = x[i] * before
                x[-1 - i] = x[-1 - i] * behind
        for r in range(rows):
            spread[pl.ds(pl.multiple_of(r * levels + c * 8, 8), 8), :] = x[r]


def cross(x):
    n, w = x.shape
    return (
        x + pltpu.roll(x, 1, 0) + pltpu.roll(x, n - 1, 0) + pltpu.roll(x, 1, 1) + pltpu.roll(x, w - 1, 1)
    )


def masked(x, rows, inside):
    return jnp.concatenate([x[:rows], x[rows:] * inside], 0)


def flux_kernel(
    sizes, core, tile, sky, forcing, surface, rate, rows_of_mix, source_rows, own, owners, locals_, shares, outer, inner,
    keep, send_1, send_2, send_3, fluxes, above, below, halo
):
    levels, rows, steps, sea_levels, sea_rows, stride, sea_stride = sizes
    width = sky.shape[1]
    one, two = inner[...], outer[...]
    above[...] = jnp.where(core[0] == 0, two, one)
    below[...] = jnp.where(core[0] == 0, one, two)
    halo[: HALO * stride, :] = below[: HALO * stride, :]
    halo[HALO * stride :, :] = above[: HALO * stride, :]

    def edge(l):
        return halo[pl.ds(l, 2 * HALO, stride=stride), :]

    inside = edge(levels + steps + 2)
    sums = [jnp.zeros((2 * HALO, width), f32) for _ in range(steps - 1)]
    for l in range(levels):
        x = edge(l)
        for s in range(steps - 1):
            sums[s] = sums[s] + rows_of_mix[s * levels + l : s * levels + l + 1, :] * x
    tops = [jnp.concatenate([sky[...], edge(levels - 1)], 0)]
    tops += [jnp.concatenate([own[s * rows : (s + 1) * rows, :], sums[s]], 0) for s in range(steps - 1)]
    surf = jnp.concatenate([surface[...], edge(levels + steps)], 0)
    coef = jnp.concatenate([rate[...], edge(levels + steps + 1)], 0)
    force = [
        jnp.concatenate([forcing[s * rows : (s + 1) * rows, :], edge(levels + s)], 0) for s in range(steps)
    ]

    flux = []
    for s in range(steps):
        state = tops[s]
        for i in range(s):
            m = s - 1 - i
            state = masked(cross(state) * atm_diffusion, rows, inside)
            state = state + source_rows[m : m + 1, :] * force[i]
            state = state - source_rows[steps - 1 + m : steps + m, :] * flux[i]
        flux.append(coef * (state - surf))
        reach = rows + 2 * HALO
        fluxes[pl.ds(s, reach, stride=2 * steps), :] = force[s]
        fluxes[pl.ds(steps + s, reach, stride=2 * steps), :] = flux[s]
    total = flux[0][:rows]
    for s in range(1, steps):
        total = total + flux[s][:rows]
    mean = (total / steps).astype(bf16)
    topk = owners.shape[0]
    target = (owners[...] ^ tile[0]) * sea_rows + locals_[...]
    target = jnp.concatenate([target[k : k + 1, :] for k in range(topk)], 1)
    rowed = jnp.concatenate(
        [jnp.dot(mean, shares[k * width : (k + 1) * width, :], preferred_element_type=f32) for k in range(topk)], 0
    )
    first = rowed.astype(bf16)
    left = rowed - first.astype(f32)
    second = left.astype(bf16)
    third = (left - second.astype(f32)).astype(bf16)
    part = keep.shape[0]
    hot = lax.broadcasted_iota(jnp.int32, (4 * part, topk * rows), 0) == target
    hot = jnp.where(hot, 1.0, 0.0).astype(bf16)
    sums = jnp.dot(
        jnp.concatenate([hot, hot, hot], 1), jnp.concatenate([first, second, third], 0), preferred_element_type=f32
    )
    for q, to in enumerate((keep, send_1, send_2, send_3)):
        to[...] = sums[q * part : (q + 1) * part]


def edge_kernel(
    sizes, fluxes, own, above, below, after, spread
):
    levels, rows, steps, sea_levels, sea_rows, stride, sea_stride = sizes
    width = own.shape[1]
    depth = up_to(levels + 2 * steps, 16)
    flag = levels + steps + 2
    inside_above, inside_below = above[flag : flag + 1, :], below[flag : flag + 1, :]

    reach = rows + 2 * HALO
    x = [fluxes[(r % reach) * 2 * steps : (r % reach + 1) * 2 * steps, :] for r in range(1 - steps, rows + steps - 1)]
    field = lax.broadcasted_iota(jnp.int32, (2 * steps, width), 0) % steps
    for n in range(1, steps):
        y = stencil(x)
        x = [jnp.where(field < steps - n, y[i], x[i + 1]) for i in range(len(y))]
        for i in range(steps - 1 - n):
            x[i] = x[i] * inside_above
            x[-1 - i] = x[-1 - i] * inside_below
    for r in range(rows):
        spread[r * depth + levels : (r + 1) * depth, :] = x[r]
        if HALO <= r < rows - HALO:
            spread[r * depth : r * depth + levels, :] = own[r * levels : (r + 1) * levels, :]

    @pl.loop(0, levels // 8)
    def _(c):
        def other(ref, j):
            return ref[pl.ds(pl.multiple_of(j * stride + c * 8, 8), 8), :]

        top, low = ([other(ref, j) for j in range(HALO)] for ref in (above, below))
        none = jnp.zeros_like(top[0])
        for n in range(steps):
            top = stencil(top + [none]) + [top[-1]]
            low = [low[0]] + stencil([none] + low)
        for i, value in enumerate(top + low):
            r = i if i < HALO else rows - 2 * HALO + i
            value = value + own[pl.ds(pl.multiple_of(r * levels + c * 8, 8), 8), :]
            spread[pl.ds(pl.multiple_of(r * depth + c * 8, 8), 8), :] = value


def shore_kernel(
    sizes, sea_weights, sea_ends, wet, warm, salt, above, below, after, warm_out, brine_out, salt_held, done
):
    levels, rows, steps, sea_levels, sea_rows, stride, sea_stride = sizes
    width = warm.shape[1]
    warm_out[...] = warm[...]
    salt_held[...] = salt[...]
    m = wet[...].astype(f32)
    base = HALO * stride
    w = sea_weights[:, : 3 * sea_stride]
    for e, (r, other) in enumerate(((0, above), (sea_rows - 1, below))):
        mark = m[r : r + 1]
        far = other[base + 2 * sea_stride : base + 2 * sea_stride + 1, :]
        x = []
        for f in range(2):
            at = base + f * sea_stride
            mine = (2 * f + e) * sea_stride
            step = other[at : at + sea_levels, :] - sea_ends[mine : mine + sea_levels, :] * far
            step = ocean_diffusion * (mark * step)
            x.append(jnp.concatenate([step, jnp.zeros((sea_stride - sea_levels, width), f32)], 0))
        y = product(w, jnp.concatenate(x, 1))
        for f, to in enumerate((warm_out, salt_held)):
            rows_at = pl.ds(r, sea_levels, stride=sea_rows)
            to[rows_at, :] = to[rows_at, :] + mark * y[:sea_levels, f * width : (f + 1) * width]
    leave = [pltpu.make_async_copy(salt_held, brine_out, done.at[0])]
    leave[0].start()
    for move in leave:
        move.wait()


def mix_kernel(sizes, spread, weights, after, out, result, done):
    levels, rows, steps, sea_levels, sea_rows, stride, sea_stride = sizes
    width = spread.shape[1]
    depth = up_to(levels + 2 * steps, 16)
    w = weights[:, : 3 * depth]
    leave = []
    for g in range(rows // 8):
        to = result.at[g].reshape(levels * 8, width)
        for r in range(g * 8, g * 8 + 8, 2):
            y = product(
                w, jnp.concatenate([spread[(r + q) * depth : (r + q + 1) * depth, :] for q in range(2)], 1)
            )
            for q in range(2):
                to[pl.ds((r + q) % 8, levels, stride=8), :] = y[:levels, q * width : (q + 1) * width]
        leave.append(pltpu.make_async_copy(result.at[g], out.at[:, g], done.at[g]))
        leave[-1].start()
    for move in leave:
        move.wait()


def add_kernel(keep, *others):
    gots, (after, kept, send) = others[:-3], others[-3:]
    total = keep[...]
    for got in gots:
        total = total + got[...]
    n = kept.shape[0]
    kept[...] = total[:n]
    send[...] = total[n:]


def heat_kernel(sizes, kept, got, wet, sea_first, before, after):
    levels, rows, steps, sea_levels, sea_rows, stride, sea_stride = sizes
    heat = kept[...] + got[...]
    heat = wet[...].astype(f32) * heat
    for l in range(sea_levels):
        after[l * sea_rows : (l + 1) * sea_rows, :] = (
            before[l * sea_rows : (l + 1) * sea_rows, :] + sea_first[l : l + 1, :] * heat
        )


def body(sky, forcing, curve, surface, rate, vmix, shares, owners, locals_, warmth, brine, wet, sea_mix):
    levels, rows, width = sky.shape
    steps = forcing.shape[0]
    sea_levels, sea_rows, _ = warmth.shape
    topk = owners.shape[1]
    stride = up_to(levels + steps + 3, 8)
    sea_stride = up_to(sea_levels, 16)
    sizes = (levels, rows, steps, sea_levels, sea_rows, stride, sea_stride)
    sky2, forcing2 = sky.reshape(-1, width), forcing.reshape(-1, width)
    warmth2, brine2 = warmth.reshape(-1, width), brine.reshape(-1, width)
    flat = lambda n, kind=f32: jax.ShapeDtypeStruct((n, width), kind)

    space = lambda *shape: pltpu.VMEM(shape, f32)
    space = lambda *shape: pltpu.VMEM(shape, f32)
    length = HALO * stride + 2 * sea_stride + 8
    ring = ("tile", "comp")
    tiles, count = lax.axis_size("tile"), lax.axis_size(ring)
    at = lax.axis_index(ring).astype(jnp.int32)[None]
    core = lax.axis_index("comp").astype(jnp.int32)[None]
    tile = lax.axis_index("tile").astype(jnp.int32)[None]
    inner, outer = call(
        functools.partial(pack_kernel, sizes), [flat(length)] * 2,
        core, sky, forcing, surface, rate, warmth2, brine2, wet, moved=4 << 20, in_specs=[SMEM] + [HBM] * 7,
        scratch=[
            space(2, levels, 8, width), space(steps, rows, width), space(2, sea_levels * sea_rows, width),
            space(2, rows, width), pltpu.VMEM(wet.shape, wet.dtype), pltpu.SemaphoreType.DMA((8,)),
        ],
        grant=FULL,
    )
    swap = lambda first: [(i + a, i + 1 - a) for i in range(first, count - 1, 2) for a in range(2)]
    outer = lax.ppermute(outer, ring, swap(1))
    inner = lax.ppermute(inner, ring, swap(0))

    depth = up_to(levels + 2 * steps, 16)
    mix_rows = up_to(levels, 16)
    area = sea_levels * sea_rows
    rows_of_mix, source_rows, own, weights, sea_weights, sea_first, sea_ends, spread, warm, salt = call(
        functools.partial(local_kernel, sizes, count - 1),
        [
            flat((steps - 1) * levels), flat(8), flat((steps - 1) * rows),
            jax.ShapeDtypeStruct((mix_rows, 2 * width), bf16),
            jax.ShapeDtypeStruct((sea_stride, 2 * width), bf16), flat(sea_stride), flat(4 * sea_stride),
            flat(rows * levels), flat(area), flat(area),
        ],
        at, vmix, curve[None], sea_mix, sky2, warmth2, brine2, wet, in_specs=[SMEM] + [VMEM] * 7,
        scratch=[space(2, sea_rows * sea_stride, width)],
        flops=4 << 30, moved=8 << 20,
    )

    part = tiles // 4 * sea_rows
    keep, send_1, send_2, send_3, fluxes, above, below = call(
        functools.partial(flux_kernel, sizes),
        [flat(part)] * 4 + [flat(2 * steps * (rows + 2 * HALO)), flat(length), flat(length)],
        core, tile, sky[-1], forcing2, surface, rate, rows_of_mix, source_rows, own, owners.T, locals_.T,
        shares.reshape(-1, width), outer, inner,
        in_specs=[SMEM] * 2 + [VMEM] * 12, scratch=[space(2 * HALO * stride, width)], moved=2 << 20,
    )
    def edge_part(after):
        return call(
            functools.partial(edge_kernel, sizes), flat(rows * depth), fluxes, spread, above, below, after,
            in_specs=[VMEM] * 4 + [ANY], flops=1 << 28, moved=4 << 20,
        )

    def shore_part(after):
        return call(
            functools.partial(shore_kernel, sizes), [flat(area), flat(area)],
            sea_weights, sea_ends, wet, warm, salt, above, below, after,
            in_specs=[VMEM] * 7 + [ANY], out_specs=[VMEM, HBM],
            scratch=[space(area, width), pltpu.SemaphoreType.DMA((1,))], flops=1 << 28, moved=4 << 20,
        )

    bit = tiles // 4
    gots = [
        lax.ppermute(x, "tile", [(i, i ^ (q * bit)) for i in range(tiles)])
        for q, x in ((3, send_3), (2, send_2), (1, send_1))
    ]
    ready = edge_part(keep)
    while bit > 1:
        bit //= 2
        keep, send = call(
            add_kernel, [flat(bit * sea_rows)] * 2, keep, *gots, ready, in_specs=[VMEM] * (1 + len(gots)) + [ANY],
        )
        gots = [lax.ppermute(send, "tile", [(i, i ^ bit) for i in range(tiles)])]
    got = gots[0]
    warm, salt = shore_part(keep)
    sky_out = call(
        functools.partial(mix_kernel, sizes), jax.ShapeDtypeStruct((levels, rows // 8, 8, width), f32),
        ready, weights, keep, in_specs=[VMEM, VMEM, ANY], out_specs=HBM,
        scratch=[space(rows // 8, levels, 8, width), pltpu.SemaphoreType.DMA((rows // 8,))],
        flops=2 << 30, moved=4 << 20,
    )
    warm = call(functools.partial(heat_kernel, sizes), flat(area), keep, got, wet, sea_first, warm, moved=2 << 20)
    return sky_out.reshape(sky.shape), warm.reshape(warmth.shape), salt.reshape(brine.shape)


def solution(mesh):
    both = P(None, ("member", "tile", "comp"), None)
    one = P(("tile", "comp"), None)
    return jax.shard_map(
        body,
        mesh=mesh,
        in_specs=(
            both, both, P(), P(("member", "tile", "comp"), None), one, P(), P(), one, one, both, both, one, P(),
        ),
        out_specs=(both, both, both),
        check_vma=False,
    )
```

```python
import functools

import jax
import jax.numpy as jnp
from jax import lax
from jax.experimental import pallas as pl
from jax.experimental.pallas import tpu as pltpu
from jax.sharding import PartitionSpec as P

atm_diffusion = 0.2
ocean_diffusion = 0.2
HALO = 4
FULL = 60
EXACT = lax.Precision.HIGHEST
VMEM = pl.BlockSpec(memory_space=pltpu.VMEM)
HBM = pl.BlockSpec(memory_space=pltpu.HBM)
SMEM = pl.BlockSpec(memory_space=pltpu.SMEM)
ANY = pl.BlockSpec(memory_space=pl.ANY)
f32, bf16 = jnp.float32, jnp.bfloat16


def up_to(n, m):
    return -(-n // m) * m


def call(kernel, out_shape, *args, scratch=(), in_specs=None, out_specs=None, flops=0, moved=0, grant=24):
    return pl.pallas_call(
        kernel,
        out_shape=out_shape,
        in_specs=in_specs or [VMEM] * len(args),
        out_specs=out_specs or jax.tree.map(lambda _: VMEM, out_shape),
        scratch_shapes=list(scratch),
        compiler_params=pltpu.CompilerParams(vmem_limit_bytes=grant * 2**20),
        cost_estimate=pl.CostEstimate(flops=flops, bytes_accessed=moved, transcendentals=0),
    )(*args)


def copies(pairs, done):
    return [pltpu.make_async_copy(src, dst, done.at[i]) for i, (src, dst) in enumerate(pairs)]


def pack_kernel(
    sizes, core, sky, forcing, surface, rate, warmth, brine, wet, inner, outer,
    ends, force, sea, flat, marks, done
):
    levels, rows, steps, sea_levels, sea_rows, stride, sea_stride = sizes
    width = sky.shape[2]
    low = rows - 8
    moves = copies(
        [
            (sky.at[:, 0:8, :], ends.at[0]), (sky.at[:, low:rows, :], ends.at[1]), (forcing, force),
            (surface, flat.at[0]), (rate, flat.at[1]), (warmth, sea.at[0]), (brine, sea.at[1]), (wet, marks),
        ],
        done,
    )
    for move in moves:
        move.start()
    for move in moves:
        move.wait()
    end = ends.reshape(2 * levels * 8, width)
    for which, out in enumerate((inner, outer)):
        last = jnp.where(core[0] == 0, 1 - which, which)
        sea_row = last * (sea_rows - 1)
        for j in range(HALO):
            row = last * (rows - HALO) + j
            first = last * (levels * 8 + 8 - HALO) + j
            out[j * stride : j * stride + levels, :] = end[pl.ds(first, levels, stride=8), :]
            base = j * stride + levels
            tail = [force[s, pl.ds(row, 1), :] for s in range(steps)]
            tail += [flat[0, pl.ds(row, 1), :], flat[1, pl.ds(row, 1), :], jnp.ones((1, width), f32)]
            tail += [jnp.zeros((stride - levels - len(tail), width), f32)]
            out[base : (j + 1) * stride, :] = jnp.concatenate(tail, 0)
        base = HALO * stride
        edge = marks[pl.ds(sea_row, 1), :].astype(f32)
        for f in range(2):
            out[base : base + sea_levels, :] = sea[f, pl.ds(sea_row, sea_levels, stride=sea_rows), :] * edge
            base += sea_stride
        out[base : base + 8, :] = jnp.concatenate([edge, jnp.zeros((7, width), f32)], 0)


def split(x):
    high = x.astype(bf16)
    return high, (x - high.astype(f32)).astype(bf16)


def three_terms(w, depth):
    high = w.astype(bf16).astype(f32)
    low = w - high
    return (high + pltpu.roll(high, depth, 1) + pltpu.roll(low, 2 * depth, 1)).astype(bf16)


def row_of(ref, first, count, step, size):
    x = ref[pl.ds(first, count, stride=step), :]
    if count < size:
        x = jnp.concatenate([x, jnp.zeros((size - count, x.shape[1]), f32)], 0)
    return x


def beside(x):
    return pltpu.roll(x, 1, 1) + pltpu.roll(x, x.shape[1] - 1, 1)


def stencil(x):
    return [x[i - 1] + x[i] + x[i + 1] + beside(x[i]) for i in range(1, len(x) - 1)]


def product(weights, x):
    high, low = split(x)
    return jnp.dot(weights, jnp.concatenate([high, low, high], 0), preferred_element_type=f32)


def local_kernel(
    sizes, last_place, place, vmix, curve, sea_mix, sky, warmth, brine, wet,
    rows_of_mix, source_rows, own, weights, sea_weights, sea_first, sea_ends, spread, warm_out, brine_out, sea_spread,
):
    levels, rows, steps, sea_levels, sea_rows, stride, sea_stride = sizes
    width = sky.shape[1]
    depth = up_to(levels + 2 * steps, 16)
    v = vmix[...]
    dot = functools.partial(jnp.dot, precision=EXACT, preferred_element_type=f32)
    powers = [v]
    for _ in range(steps - 1):
        powers.append(dot(v, powers[-1]))
    last = (lax.broadcasted_iota(jnp.int32, (levels, width), 0) == levels - 1).astype(f32)
    for s in range(1, steps):
        rows_of_mix[(s - 1) * levels : s * levels, :] = lax.dot_general(
            powers[s - 1], last, (((0,), (0,)), ((), ())), precision=EXACT, preferred_element_type=f32
        )
    by_curve = jnp.broadcast_to(curve[...], (width, levels))
    of_curve = [
        lax.dot_general(p, by_curve, (((1,), (1,)), ((), ())), precision=EXACT, preferred_element_type=f32)
        for p in powers
    ]
    of_last = [jnp.broadcast_to(p[:, levels - 1 : levels], (levels, width)) for p in powers]
    found = [of_curve[i][levels - 1 :] for i in range(steps - 1)]
    found += [of_last[i][levels - 1 :] for i in range(steps - 1)]
    found += [jnp.zeros((8 - len(found), width), f32)]
    source_rows[...] = jnp.concatenate(found, 0)
    lane = lax.broadcasted_iota(jnp.int32, (levels, width), 1)
    wide = jnp.concatenate(
        [powers[-1] * atm_diffusion**steps, jnp.zeros((levels, width - levels), f32)], 1
    )
    for j in range(steps):
        factor = atm_diffusion ** (steps - 1 - j)
        for at, value in ((j, of_curve[steps - 1 - j] * factor), (steps + j, of_last[steps - 1 - j] * -factor)):
            wide = jnp.where(lane == levels + at, value, wide)
    more = jnp.zeros((weights.shape[0] - levels, width), f32)
    wide = jnp.concatenate([wide, more], 0)
    wide = jnp.concatenate([wide, jnp.zeros_like(wide)], 1)
    weights[...] = three_terms(wide, depth)
    sea = sea_mix[...]
    sea = jnp.concatenate([sea, jnp.zeros((sea_levels, 2 * width - sea_levels), f32)], 1)
    sea = jnp.concatenate([sea, jnp.zeros((sea_stride - sea_levels, 2 * width), f32)], 0)
    sea_weights[...] = three_terms(sea, sea_stride)
    sea_first[...] = jnp.broadcast_to(sea[:, 0:1], sea_first.shape)
    sums = [jnp.zeros((rows, width), f32) for _ in range(steps - 1)]
    for l in range(levels):
        x = sky[l * rows : (l + 1) * rows, :]
        for s in range(steps - 1):
            sums[s] = sums[s] + rows_of_mix[s * levels + l : s * levels + l + 1, :] * x
    for s in range(steps - 1):
        own[s * rows : (s + 1) * rows, :] = sums[s]

    m = wet[...].astype(f32)
    mark = [m[r : r + 1] for r in range(sea_rows)]
    edge = jnp.zeros((1, width), f32)

    def near(x):
        x = [jnp.zeros_like(x[0])] + x + [jnp.zeros_like(x[0])]
        return [x[i - 1] + x[i + 1] + beside(x[i]) for i in range(1, len(x) - 1)]

    around = (
        jnp.concatenate([edge, m[:-1]], 0) + jnp.concatenate([m[1:], edge], 0) + beside(m)
    ) * ocean_diffusion
    share = [around[r : r + 1] for r in range(sea_rows)]
    for f, field in enumerate((warmth, brine)):
        for c in range(sea_stride // 8):
            count = min(8, sea_levels - c * 8)
            x = [row_of(field, c * 8 * sea_rows + r, count, sea_rows, 8) for r in range(sea_rows)]
            y = near([mark[r] * x[r] for r in range(sea_rows)])
            for r in range(sea_rows):
                at = r * sea_stride + c * 8
                sea_spread[f, at : at + 8, :] = x[r] + mark[r] * (ocean_diffusion * y[r] - x[r] * share[r])
    w = sea_weights[:, : 3 * sea_stride]
    for r in range(sea_rows):
        x = jnp.concatenate([sea_spread[f, r * sea_stride : (r + 1) * sea_stride, :] for f in range(2)], 1)
        y = product(w, x)
        for f, (field, out) in enumerate(((warmth, warm_out), (brine, brine_out))):
            old = field[pl.ds(r, sea_levels, stride=sea_rows), :]
            new = y[:sea_levels, f * width : (f + 1) * width]
            out[pl.ds(r, sea_levels, stride=sea_rows), :] = mark[r] * new + (1.0 - mark[r]) * old
            if r in (0, sea_rows - 1):
                at = (2 * f + (r > 0)) * sea_stride
                sea_ends[at : at + sea_levels, :] = old

    before = jnp.where(place[0] > 0, 1.0, 0.0)
    behind = jnp.where(place[0] < last_place, 1.0, 0.0)

    @pl.loop(0, levels // 8)
    def _(c):
        x = [sky[pl.ds(c * 8 * rows + r, 8, stride=rows), :] for r in range(rows)]
        none = jnp.zeros_like(x[0])
        beyond = 0
        for n in range(steps):
            if beyond < steps - 1 - n:
                x = [x[0]] + stencil([none] + x + [none]) + [x[-1]]
                beyond += 1
            else:
                x = stencil(x)
                beyond -= 1
            for i in range(beyond):
                x[i] = x[i] * before
                x[-1 - i] = x[-1 - i] * behind
        for r in range(rows):
            spread[pl.ds(pl.multiple_of(r * levels + c * 8, 8), 8), :] = x[r]


def cross(x):
    n, w = x.shape
    return (
        x + pltpu.roll(x, 1, 0) + pltpu.roll(x, n - 1, 0) + pltpu.roll(x, 1, 1) + pltpu.roll(x, w - 1, 1)
    )


def masked(x, rows, inside):
    return jnp.concatenate([x[:rows], x[rows:] * inside], 0)


def flux_kernel(
    sizes, core, tile, sky, forcing, surface, rate, rows_of_mix, source_rows, own, owners, locals_, shares, outer, inner,
    keep, send_1, send_2, send_3, fluxes, above, below, halo
):
    levels, rows, steps, sea_levels, sea_rows, stride, sea_stride = sizes
    width = sky.shape[1]
    one, two = inner[...], outer[...]
    above[...] = jnp.where(core[0] == 0, two, one)
    below[...] = jnp.where(core[0] == 0, one, two)
    halo[: HALO * stride, :] = below[: HALO * stride, :]
    halo[HALO * stride :, :] = above[: HALO * stride, :]

    def edge(l):
        return halo[pl.ds(l, 2 * HALO, stride=stride), :]

    inside = edge(levels + steps + 2)
    sums = [jnp.zeros((2 * HALO, width), f32) for _ in range(steps - 1)]
    for l in range(levels):
        x = edge(l)
        for s in range(steps - 1):
            sums[s] = sums[s] + rows_of_mix[s * levels + l : s * levels + l + 1, :] * x
    tops = [jnp.concatenate([sky[...], edge(levels - 1)], 0)]
    tops += [jnp.concatenate([own[s * rows : (s + 1) * rows, :], sums[s]], 0) for s in range(steps - 1)]
    surf = jnp.concatenate([surface[...], edge(levels + steps)], 0)
    coef = jnp.concatenate([rate[...], edge(levels + steps + 1)], 0)
    force = [
        jnp.concatenate([forcing[s * rows : (s + 1) * rows, :], edge(levels + s)], 0) for s in range(steps)
    ]

    flux = []
    for s in range(steps):
        state = tops[s]
        for i in range(s):
            m = s - 1 - i
            state = masked(cross(state) * atm_diffusion, rows, inside)
            state = state + source_rows[m : m + 1, :] * force[i]
            state = state - source_rows[steps - 1 + m : steps + m, :] * flux[i]
        flux.append(coef * (state - surf))
        reach = rows + 2 * HALO
        fluxes[pl.ds(s, reach, stride=2 * steps), :] = force[s]
        fluxes[pl.ds(steps + s, reach, stride=2 * steps), :] = flux[s]
    total = flux[0][:rows]
    for s in range(1, steps):
        total = total + flux[s][:rows]
    mean = (total / steps).astype(bf16)
    topk = owners.shape[0]
    target = (owners[...] ^ tile[0]) * sea_rows + locals_[...]
    target = jnp.concatenate([target[k : k + 1, :] for k in range(topk)], 1)
    rowed = jnp.concatenate(
        [jnp.dot(mean, shares[k * width : (k + 1) * width, :], preferred_element_type=f32) for k in range(topk)], 0
    )
    first = rowed.astype(bf16)
    left = rowed - first.astype(f32)
    second = left.astype(bf16)
    third = (left - second.astype(f32)).astype(bf16)
    part = keep.shape[0]
    hot = lax.broadcasted_iota(jnp.int32, (4 * part, topk * rows), 0) == target
    hot = jnp.where(hot, 1.0, 0.0).astype(bf16)
    sums = jnp.dot(
        jnp.concatenate([hot, hot, hot], 1), jnp.concatenate([first, second, third], 0), preferred_element_type=f32
    )
    for q, to in enumerate((keep, send_1, send_2, send_3)):
        to[...] = sums[q * part : (q + 1) * part]


def edge_kernel(
    sizes, fluxes, own, above, below, after, spread
):
    levels, rows, steps, sea_levels, sea_rows, stride, sea_stride = sizes
    width = own.shape[1]
    depth = up_to(levels + 2 * steps, 16)
    flag = levels + steps + 2
    inside_above, inside_below = above[flag : flag + 1, :], below[flag : flag + 1, :]

    reach = rows + 2 * HALO
    x = [fluxes[(r % reach) * 2 * steps : (r % reach + 1) * 2 * steps, :] for r in range(1 - steps, rows + steps - 1)]
    field = lax.broadcasted_iota(jnp.int32, (2 * steps, width), 0) % steps
    for n in range(1, steps):
        y = stencil(x)
        x = [jnp.where(field < steps - n, y[i], x[i + 1]) for i in range(len(y))]
        for i in range(steps - 1 - n):
            x[i] = x[i] * inside_above
            x[-1 - i] = x[-1 - i] * inside_below
    for r in range(rows):
        spread[r * depth + levels : (r + 1) * depth, :] = x[r]
        if HALO <= r < rows - HALO:
            spread[r * depth : r * depth + levels, :] = own[r * levels : (r + 1) * levels, :]

    @pl.loop(0, levels // 8)
    def _(c):
        def other(ref, j):
            return ref[pl.ds(pl.multiple_of(j * stride + c * 8, 8), 8), :]

        top, low = ([other(ref, j) for j in range(HALO)] for ref in (above, below))
        none = jnp.zeros_like(top[0])
        for n in range(steps):
            top = stencil(top + [none]) + [top[-1]]
            low = [low[0]] + stencil([none] + low)
        for i, value in enumerate(top + low):
            r = i if i < HALO else rows - 2 * HALO + i
            value = value + own[pl.ds(pl.multiple_of(r * levels + c * 8, 8), 8), :]
            spread[pl.ds(pl.multiple_of(r * depth + c * 8, 8), 8), :] = value


def shore_kernel(
    sizes, sea_weights, sea_ends, wet, warm, salt, above, below, after, warm_out, brine_out, salt_held, done
):
    levels, rows, steps, sea_levels, sea_rows, stride, sea_stride = sizes
    width = warm.shape[1]
    warm_out[...] = warm[...]
    salt_held[...] = salt[...]
    m = wet[...].astype(f32)
    base = HALO * stride
    w = sea_weights[:, : 3 * sea_stride]
    for e, (r, other) in enumerate(((0, above), (sea_rows - 1, below))):
        mark = m[r : r + 1]
        far = other[base + 2 * sea_stride : base + 2 * sea_stride + 1, :]
        x = []
        for f in range(2):
            at = base + f * sea_stride
            mine = (2 * f + e) * sea_stride
            step = other[at : at + sea_levels, :] - sea_ends[mine : mine + sea_levels, :] * far
            step = ocean_diffusion * (mark * step)
            x.append(jnp.concatenate([step, jnp.zeros((sea_stride - sea_levels, width), f32)], 0))
        y = product(w, jnp.concatenate(x, 1))
        for f, to in enumerate((warm_out, salt_held)):
            rows_at = pl.ds(r, sea_levels, stride=sea_rows)
            to[rows_at, :] = to[rows_at, :] + mark * y[:sea_levels, f * width : (f + 1) * width]
    leave = [pltpu.make_async_copy(salt_held, brine_out, done.at[0])]
    leave[0].start()
    for move in leave:
        move.wait()


def mix_kernel(sizes, spread, weights, after, out, result, done):
    levels, rows, steps, sea_levels, sea_rows, stride, sea_stride = sizes
    width = spread.shape[1]
    depth = up_to(levels + 2 * steps, 16)
    w = weights[:, : 3 * depth]
    leave = []
    for g in range(rows // 8):
        to = result.at[g].reshape(levels * 8, width)
        for r in range(g * 8, g * 8 + 8, 2):
            y = product(
                w, jnp.concatenate([spread[(r + q) * depth : (r + q + 1) * depth, :] for q in range(2)], 1)
            )
            for q in range(2):
                to[pl.ds((r + q) % 8, levels, stride=8), :] = y[:levels, q * width : (q + 1) * width]
        leave.append(pltpu.make_async_copy(result.at[g], out.at[:, g], done.at[g]))
        leave[-1].start()
    for move in leave:
        move.wait()


def add_kernel(keep, *others):
    gots, (after, kept, send) = others[:-3], others[-3:]
    total = keep[...]
    for got in gots:
        total = total + got[...]
    n = kept.shape[0]
    kept[...] = total[:n]
    send[...] = total[n:]


def heat_kernel(sizes, kept, got, wet, sea_first, before, after):
    levels, rows, steps, sea_levels, sea_rows, stride, sea_stride = sizes
    heat = kept[...] + got[...]
    heat = wet[...].astype(f32) * heat
    for l in range(sea_levels):
        after[l * sea_rows : (l + 1) * sea_rows, :] = (
            before[l * sea_rows : (l + 1) * sea_rows, :] + sea_first[l : l + 1, :] * heat
        )


def body(sky, forcing, curve, surface, rate, vmix, shares, owners, locals_, warmth, brine, wet, sea_mix):
    levels, rows, width = sky.shape
    steps = forcing.shape[0]
    sea_levels, sea_rows, _ = warmth.shape
    topk = owners.shape[1]
    stride = up_to(levels + steps + 3, 8)
    sea_stride = up_to(sea_levels, 16)
    sizes = (levels, rows, steps, sea_levels, sea_rows, stride, sea_stride)
    sky2, forcing2 = sky.reshape(-1, width), forcing.reshape(-1, width)
    warmth2, brine2 = warmth.reshape(-1, width), brine.reshape(-1, width)
    flat = lambda n, kind=f32: jax.ShapeDtypeStruct((n, width), kind)

    space = lambda *shape: pltpu.VMEM(shape, f32)
    space = lambda *shape: pltpu.VMEM(shape, f32)
    length = HALO * stride + 2 * sea_stride + 8
    ring = ("tile", "comp")
    tiles, count = lax.axis_size("tile"), lax.axis_size(ring)
    at = lax.axis_index(ring).astype(jnp.int32)[None]
    core = lax.axis_index("comp").astype(jnp.int32)[None]
    tile = lax.axis_index("tile").astype(jnp.int32)[None]
    inner, outer = call(
        functools.partial(pack_kernel, sizes), [flat(length)] * 2,
        core, sky, forcing, surface, rate, warmth2, brine2, wet, moved=4 << 20, in_specs=[SMEM] + [HBM] * 7,
        scratch=[
            space(2, levels, 8, width), space(steps, rows, width), space(2, sea_levels * sea_rows, width),
            space(2, rows, width), pltpu.VMEM(wet.shape, wet.dtype), pltpu.SemaphoreType.DMA((8,)),
        ],
        grant=FULL,
    )
    swap = lambda first: [(i + a, i + 1 - a) for i in range(first, count - 1, 2) for a in range(2)]
    outer = lax.ppermute(outer, ring, swap(1))
    inner = lax.ppermute(inner, ring, swap(0))

    depth = up_to(levels + 2 * steps, 16)
    mix_rows = up_to(levels, 16)
    area = sea_levels * sea_rows
    rows_of_mix, source_rows, own, weights, sea_weights, sea_first, sea_ends, spread, warm, salt = call(
        functools.partial(local_kernel, sizes, count - 1),
        [
            flat((steps - 1) * levels), flat(8), flat((steps - 1) * rows),
            jax.ShapeDtypeStruct((mix_rows, 2 * width), bf16),
            jax.ShapeDtypeStruct((sea_stride, 2 * width), bf16), flat(sea_stride), flat(4 * sea_stride),
            flat(rows * levels), flat(area), flat(area),
        ],
        at, vmix, curve[None], sea_mix, sky2, warmth2, brine2, wet, in_specs=[SMEM] + [VMEM] * 7,
        scratch=[space(2, sea_rows * sea_stride, width)],
        flops=4 << 30, moved=8 << 20,
    )

    part = tiles // 4 * sea_rows
    keep, send_1, send_2, send_3, fluxes, above, below = call(
        functools.partial(flux_kernel, sizes),
        [flat(part)] * 4 + [flat(2 * steps * (rows + 2 * HALO)), flat(length), flat(length)],
        core, tile, sky[-1], forcing2, surface, rate, rows_of_mix, source_rows, own, owners.T, locals_.T,
        shares.reshape(-1, width), outer, inner,
        in_specs=[SMEM] * 2 + [VMEM] * 12, scratch=[space(2 * HALO * stride, width)], moved=2 << 20,
    )
    def edge_part(after):
        return call(
            functools.partial(edge_kernel, sizes), flat(rows * depth), fluxes, spread, above, below, after,
            in_specs=[VMEM] * 4 + [ANY], flops=1 << 28, moved=4 << 20,
        )

    def shore_part(after):
        return call(
            functools.partial(shore_kernel, sizes), [flat(area), flat(area)],
            sea_weights, sea_ends, wet, warm, salt, above, below, after,
            in_specs=[VMEM] * 7 + [ANY], out_specs=[VMEM, HBM],
            scratch=[space(area, width), pltpu.SemaphoreType.DMA((1,))], flops=1 << 28, moved=4 << 20,
        )

    bit = tiles // 4
    gots = [
        lax.ppermute(x, "tile", [(i, i ^ (q * bit)) for i in range(tiles)])
        for q, x in ((2, send_2), (3, send_3), (1, send_1))
    ]
    ready = edge_part(keep)
    while bit > 1:
        bit //= 2
        keep, send = call(
            add_kernel, [flat(bit * sea_rows)] * 2, keep, *gots, ready, in_specs=[VMEM] * (1 + len(gots)) + [ANY],
        )
        gots = [lax.ppermute(send, "tile", [(i, i ^ bit) for i in range(tiles)])]
    got = gots[0]
    warm, salt = shore_part(keep)
    sky_out = call(
        functools.partial(mix_kernel, sizes), jax.ShapeDtypeStruct((levels, rows // 8, 8, width), f32),
        ready, weights, keep, in_specs=[VMEM, VMEM, ANY], out_specs=HBM,
        scratch=[space(rows // 8, levels, 8, width), pltpu.SemaphoreType.DMA((rows // 8,))],
        flops=2 << 30, moved=4 << 20,
    )
    warm = call(functools.partial(heat_kernel, sizes), flat(area), keep, got, wet, sea_first, warm, moved=2 << 20)
    return sky_out.reshape(sky.shape), warm.reshape(warmth.shape), salt.reshape(brine.shape)


def solution(mesh):
    both = P(None, ("member", "tile", "comp"), None)
    one = P(("tile", "comp"), None)
    return jax.shard_map(
        body,
        mesh=mesh,
        in_specs=(
            both, both, P(), P(("member", "tile", "comp"), None), one, P(), P(), one, one, both, both, one, P(),
        ),
        out_specs=(both, both, both),
        check_vma=False,
    )
```

```python
import functools

import jax
import jax.numpy as jnp
from jax import lax
from jax.experimental import pallas as pl
from jax.experimental.pallas import tpu as pltpu
from jax.sharding import PartitionSpec as P

atm_diffusion = 0.2
ocean_diffusion = 0.2
HALO = 4
FULL = 60
EXACT = lax.Precision.HIGHEST
VMEM = pl.BlockSpec(memory_space=pltpu.VMEM)
HBM = pl.BlockSpec(memory_space=pltpu.HBM)
SMEM = pl.BlockSpec(memory_space=pltpu.SMEM)
ANY = pl.BlockSpec(memory_space=pl.ANY)
f32, bf16 = jnp.float32, jnp.bfloat16


def up_to(n, m):
    return -(-n // m) * m


def call(kernel, out_shape, *args, scratch=(), in_specs=None, out_specs=None, flops=0, moved=0, grant=24):
    return pl.pallas_call(
        kernel,
        out_shape=out_shape,
        in_specs=in_specs or [VMEM] * len(args),
        out_specs=out_specs or jax.tree.map(lambda _: VMEM, out_shape),
        scratch_shapes=list(scratch),
        compiler_params=pltpu.CompilerParams(vmem_limit_bytes=grant * 2**20),
        cost_estimate=pl.CostEstimate(flops=flops, bytes_accessed=moved, transcendentals=0),
    )(*args)


def copies(pairs, done):
    return [pltpu.make_async_copy(src, dst, done.at[i]) for i, (src, dst) in enumerate(pairs)]


def pack_kernel(
    sizes, core, sky, forcing, surface, rate, warmth, brine, wet, inner, outer,
    ends, force, sea, flat, marks, done
):
    levels, rows, steps, sea_levels, sea_rows, stride, sea_stride = sizes
    width = sky.shape[2]
    low = rows - 8
    moves = copies(
        [
            (sky.at[:, 0:8, :], ends.at[0]), (sky.at[:, low:rows, :], ends.at[1]), (forcing, force),
            (surface, flat.at[0]), (rate, flat.at[1]), (warmth, sea.at[0]), (brine, sea.at[1]), (wet, marks),
        ],
        done,
    )
    for move in moves:
        move.start()
    for move in moves:
        move.wait()
    end = ends.reshape(2 * levels * 8, width)
    for which, out in enumerate((inner, outer)):
        last = jnp.where(core[0] == 0, 1 - which, which)
        sea_row = last * (sea_rows - 1)
        for j in range(HALO):
            row = last * (rows - HALO) + j
            first = last * (levels * 8 + 8 - HALO) + j
            out[j * stride : j * stride + levels, :] = end[pl.ds(first, levels, stride=8), :]
            base = j * stride + levels
            tail = [force[s, pl.ds(row, 1), :] for s in range(steps)]
            tail += [flat[0, pl.ds(row, 1), :], flat[1, pl.ds(row, 1), :], jnp.ones((1, width), f32)]
            tail += [jnp.zeros((stride - levels - len(tail), width), f32)]
            out[base : (j + 1) * stride, :] = jnp.concatenate(tail, 0)
        base = HALO * stride
        edge = marks[pl.ds(sea_row, 1), :].astype(f32)
        for f in range(2):
            out[base : base + sea_levels, :] = sea[f, pl.ds(sea_row, sea_levels, stride=sea_rows), :] * edge
            base += sea_stride
        out[base : base + 8, :] = jnp.concatenate([edge, jnp.zeros((7, width), f32)], 0)


def split(x):
    high = x.astype(bf16)
    return high, (x - high.astype(f32)).astype(bf16)


def three_terms(w, depth):
    high = w.astype(bf16).astype(f32)
    low = w - high
    return (high + pltpu.roll(high, depth, 1) + pltpu.roll(low, 2 * depth, 1)).astype(bf16)


def row_of(ref, first, count, step, size):
    x = ref[pl.ds(first, count, stride=step), :]
    if count < size:
        x = jnp.concatenate([x, jnp.zeros((size - count, x.shape[1]), f32)], 0)
    return x


def beside(x):
    return pltpu.roll(x, 1, 1) + pltpu.roll(x, x.shape[1] - 1, 1)


def stencil(x):
    return [x[i - 1] + x[i] + x[i + 1] + beside(x[i]) for i in range(1, len(x) - 1)]


def product(weights, x):
    high, low = split(x)
    return jnp.dot(weights, jnp.concatenate([high, low, high], 0), preferred_element_type=f32)


def local_kernel(
    sizes, last_place, place, vmix, curve, sea_mix, sky, warmth, brine, wet,
    rows_of_mix, source_rows, own, weights, sea_weights, sea_first, sea_ends, spread, warm_out, brine_out, sea_spread,
):
    levels, rows, steps, sea_levels, sea_rows, stride, sea_stride = sizes
    width = sky.shape[1]
    depth = up_to(levels + 2 * steps, 16)
    v = vmix[...]
    dot = functools.partial(jnp.dot, precision=EXACT, preferred_element_type=f32)
    powers = [v]
    for _ in range(steps - 1):
        powers.append(dot(v, powers[-1]))
    last = (lax.broadcasted_iota(jnp.int32, (levels, width), 0) == levels - 1).astype(f32)
    for s in range(1, steps):
        rows_of_mix[(s - 1) * levels : s * levels, :] = lax.dot_general(
            powers[s - 1], last, (((0,), (0,)), ((), ())), precision=EXACT, preferred_element_type=f32
        )
    by_curve = jnp.broadcast_to(curve[...], (width, levels))
    of_curve = [
        lax.dot_general(p, by_curve, (((1,), (1,)), ((), ())), precision=EXACT, preferred_element_type=f32)
        for p in powers
    ]
    of_last = [jnp.broadcast_to(p[:, levels - 1 : levels], (levels, width)) for p in powers]
    found = [of_curve[i][levels - 1 :] for i in range(steps - 1)]
    found += [of_last[i][levels - 1 :] for i in range(steps - 1)]
    found += [jnp.zeros((8 - len(found), width), f32)]
    source_rows[...] = jnp.concatenate(found, 0)
    lane = lax.broadcasted_iota(jnp.int32, (levels, width), 1)
    wide = jnp.concatenate(
        [powers[-1] * atm_diffusion**steps, jnp.zeros((levels, width - levels), f32)], 1
    )
    for j in range(steps):
        factor = atm_diffusion ** (steps - 1 - j)
        for at, value in ((j, of_curve[steps - 1 - j] * factor), (steps + j, of_last[steps - 1 - j] * -factor)):
            wide = jnp.where(lane == levels + at, value, wide)
    more = jnp.zeros((weights.shape[0] - levels, width), f32)
    wide = jnp.concatenate([wide, more], 0)
    wide = jnp.concatenate([wide, jnp.zeros_like(wide)], 1)
    weights[...] = three_terms(wide, depth)
    sea = sea_mix[...]
    sea = jnp.concatenate([sea, jnp.zeros((sea_levels, 2 * width - sea_levels), f32)], 1)
    sea = jnp.concatenate([sea, jnp.zeros((sea_stride - sea_levels, 2 * width), f32)], 0)
    sea_weights[...] = three_terms(sea, sea_stride)
    sea_first[...] = jnp.broadcast_to(sea[:, 0:1], sea_first.shape)
    sums = [jnp.zeros((rows, width), f32) for _ in range(steps - 1)]
    for l in range(levels):
        x = sky[l * rows : (l + 1) * rows, :]
        for s in range(steps - 1):
            sums[s] = sums[s] + rows_of_mix[s * levels + l : s * levels + l + 1, :] * x
    for s in range(steps - 1):
        own[s * rows : (s + 1) * rows, :] = sums[s]

    m = wet[...].astype(f32)
    mark = [m[r : r + 1] for r in range(sea_rows)]
    edge = jnp.zeros((1, width), f32)

    def near(x):
        x = [jnp.zeros_like(x[0])] + x + [jnp.zeros_like(x[0])]
        return [x[i - 1] + x[i + 1] + beside(x[i]) for i in range(1, len(x) - 1)]

    around = (
        jnp.concatenate([edge, m[:-1]], 0) + jnp.concatenate([m[1:], edge], 0) + beside(m)
    ) * ocean_diffusion
    share = [around[r : r + 1] for r in range(sea_rows)]
    for f, field in enumerate((warmth, brine)):
        for c in range(sea_stride // 8):
            count = min(8, sea_levels - c * 8)
            x = [row_of(field, c * 8 * sea_rows + r, count, sea_rows, 8) for r in range(sea_rows)]
            y = near([mark[r] * x[r] for r in range(sea_rows)])
            for r in range(sea_rows):
                at = r * sea_stride + c * 8
                sea_spread[f, at : at + 8, :] = x[r] + mark[r] * (ocean_diffusion * y[r] - x[r] * share[r])
    w = sea_weights[:, : 3 * sea_stride]
    for r in range(sea_rows):
        x = jnp.concatenate([sea_spread[f, r * sea_stride : (r + 1) * sea_stride, :] for f in range(2)], 1)
        y = product(w, x)
        for f, (field, out) in enumerate(((warmth, warm_out), (brine, brine_out))):
            old = field[pl.ds(r, sea_levels, stride=sea_rows), :]
            new = y[:sea_levels, f * width : (f + 1) * width]
            out[pl.ds(r, sea_levels, stride=sea_rows), :] = mark[r] * new + (1.0 - mark[r]) * old
            if r in (0, sea_rows - 1):
                at = (2 * f + (r > 0)) * sea_stride
                sea_ends[at : at + sea_levels, :] = old

    before = jnp.where(place[0] > 0, 1.0, 0.0)
    behind = jnp.where(place[0] < last_place, 1.0, 0.0)

    @pl.loop(0, levels // 8)
    def _(c):
        x = [sky[pl.ds(c * 8 * rows + r, 8, stride=rows), :] for r in range(rows)]
        none = jnp.zeros_like(x[0])
        beyond = 0
        for n in range(steps):
            if beyond < steps - 1 - n:
                x = [x[0]] + stencil([none] + x + [none]) + [x[-1]]
                beyond += 1
            else:
                x = stencil(x)
                beyond -= 1
            for i in range(beyond):
                x[i] = x[i] * before
                x[-1 - i] = x[-1 - i] * behind
        for r in range(rows):
            spread[pl.ds(pl.multiple_of(r * levels + c * 8, 8), 8), :] = x[r]


def cross(x):
    n, w = x.shape
    return (
        x + pltpu.roll(x, 1, 0) + pltpu.roll(x, n - 1, 0) + pltpu.roll(x, 1, 1) + pltpu.roll(x, w - 1, 1)
    )


def masked(x, rows, inside):
    return jnp.concatenate([x[:rows], x[rows:] * inside], 0)


def flux_kernel(
    sizes, core, tile, sky, forcing, surface, rate, rows_of_mix, source_rows, own, owners, locals_, shares, outer, inner,
    keep, send, fluxes, above, below, halo
):
    levels, rows, steps, sea_levels, sea_rows, stride, sea_stride = sizes
    width = sky.shape[1]
    one, two = inner[...], outer[...]
    above[...] = jnp.where(core[0] == 0, two, one)
    below[...] = jnp.where(core[0] == 0, one, two)
    halo[: HALO * stride, :] = below[: HALO * stride, :]
    halo[HALO * stride :, :] = above[: HALO * stride, :]

    def edge(l):
        return halo[pl.ds(l, 2 * HALO, stride=stride), :]

    inside = edge(levels + steps + 2)
    sums = [jnp.zeros((2 * HALO, width), f32) for _ in range(steps - 1)]
    for l in range(levels):
        x = edge(l)
        for s in range(steps - 1):
            sums[s] = sums[s] + rows_of_mix[s * levels + l : s * levels + l + 1, :] * x
    tops = [jnp.concatenate([sky[...], edge(levels - 1)], 0)]
    tops += [jnp.concatenate([own[s * rows : (s + 1) * rows, :], sums[s]], 0) for s in range(steps - 1)]
    surf = jnp.concatenate([surface[...], edge(levels + steps)], 0)
    coef = jnp.concatenate([rate[...], edge(levels + steps + 1)], 0)
    force = [
        jnp.concatenate([forcing[s * rows : (s + 1) * rows, :], edge(levels + s)], 0) for s in range(steps)
    ]

    flux = []
    for s in range(steps):
        state = tops[s]
        for i in range(s):
            m = s - 1 - i
            state = masked(cross(state) * atm_diffusion, rows, inside)
            state = state + source_rows[m : m + 1, :] * force[i]
            state = state - source_rows[steps - 1 + m : steps + m, :] * flux[i]
        flux.append(coef * (state - surf))
        reach = rows + 2 * HALO
        fluxes[pl.ds(s, reach, stride=2 * steps), :] = force[s]
        fluxes[pl.ds(steps + s, reach, stride=2 * steps), :] = flux[s]
    total = flux[0][:rows]
    for s in range(1, steps):
        total = total + flux[s][:rows]
    mean = (total / steps).astype(bf16)
    topk = owners.shape[0]
    other = owners[...] ^ tile[0]
    target = (other & 1) * keep.shape[0] + (other >> 1) * sea_rows + locals_[...]
    target = jnp.concatenate([target[k : k + 1, :] for k in range(topk)], 1)
    rowed = jnp.concatenate(
        [jnp.dot(mean, shares[k * width : (k + 1) * width, :], preferred_element_type=f32) for k in range(topk)], 0
    )
    first = rowed.astype(bf16)
    left = rowed - first.astype(f32)
    second = left.astype(bf16)
    third = (left - second.astype(f32)).astype(bf16)
    half = keep.shape[0]
    hot = lax.broadcasted_iota(jnp.int32, (2 * half, topk * rows), 0) == target
    hot = jnp.where(hot, 1.0, 0.0).astype(bf16)
    sums = jnp.dot(
        jnp.concatenate([hot, hot, hot], 1), jnp.concatenate([first, second, third], 0), preferred_element_type=f32
    )
    keep[...] = sums[:half]
    send[...] = sums[half:]


def edge_kernel(
    sizes, fluxes, own, above, below, after, spread
):
    levels, rows, steps, sea_levels, sea_rows, stride, sea_stride = sizes
    width = own.shape[1]
    depth = up_to(levels + 2 * steps, 16)
    flag = levels + steps + 2
    inside_above, inside_below = above[flag : flag + 1, :], below[flag : flag + 1, :]

    reach = rows + 2 * HALO
    x = [fluxes[(r % reach) * 2 * steps : (r % reach + 1) * 2 * steps, :] for r in range(1 - steps, rows + steps - 1)]
    field = lax.broadcasted_iota(jnp.int32, (2 * steps, width), 0) % steps
    for n in range(1, steps):
        y = stencil(x)
        x = [jnp.where(field < steps - n, y[i], x[i + 1]) for i in range(len(y))]
        for i in range(steps - 1 - n):
            x[i] = x[i] * inside_above
            x[-1 - i] = x[-1 - i] * inside_below
    for r in range(rows):
        spread[r * depth + levels : (r + 1) * depth, :] = x[r]
        if HALO <= r < rows - HALO:
            spread[r * depth : r * depth + levels, :] = own[r * levels : (r + 1) * levels, :]

    @pl.loop(0, levels // 8)
    def _(c):
        def other(ref, j):
            return ref[pl.ds(pl.multiple_of(j * stride + c * 8, 8), 8), :]

        top, low = ([other(ref, j) for j in range(HALO)] for ref in (above, below))
        none = jnp.zeros_like(top[0])
        for n in range(steps):
            top = stencil(top + [none]) + [top[-1]]
            low = [low[0]] + stencil([none] + low)
        for i, value in enumerate(top + low):
            r = i if i < HALO else rows - 2 * HALO + i
            value = value + own[pl.ds(pl.multiple_of(r * levels + c * 8, 8), 8), :]
            spread[pl.ds(pl.multiple_of(r * depth + c * 8, 8), 8), :] = value


def shore_kernel(
    sizes, sea_weights, sea_ends, wet, warm, salt, above, below, after, warm_out, brine_out, salt_held, done
):
    levels, rows, steps, sea_levels, sea_rows, stride, sea_stride = sizes
    width = warm.shape[1]
    warm_out[...] = warm[...]
    salt_held[...] = salt[...]
    m = wet[...].astype(f32)
    base = HALO * stride
    w = sea_weights[:, : 3 * sea_stride]
    for e, (r, other) in enumerate(((0, above), (sea_rows - 1, below))):
        mark = m[r : r + 1]
        far = other[base + 2 * sea_stride : base + 2 * sea_stride + 1, :]
        x = []
        for f in range(2):
            at = base + f * sea_stride
            mine = (2 * f + e) * sea_stride
            step = other[at : at + sea_levels, :] - sea_ends[mine : mine + sea_levels, :] * far
            step = ocean_diffusion * (mark * step)
            x.append(jnp.concatenate([step, jnp.zeros((sea_stride - sea_levels, width), f32)], 0))
        y = product(w, jnp.concatenate(x, 1))
        for f, to in enumerate((warm_out, salt_held)):
            rows_at = pl.ds(r, sea_levels, stride=sea_rows)
            to[rows_at, :] = to[rows_at, :] + mark * y[:sea_levels, f * width : (f + 1) * width]
    leave = [pltpu.make_async_copy(salt_held, brine_out, done.at[0])]
    leave[0].start()
    for move in leave:
        move.wait()


def mix_kernel(sizes, spread, weights, after, out, result, done):
    levels, rows, steps, sea_levels, sea_rows, stride, sea_stride = sizes
    width = spread.shape[1]
    depth = up_to(levels + 2 * steps, 16)
    w = weights[:, : 3 * depth]
    leave = []
    for g in range(rows // 8):
        to = result.at[g].reshape(levels * 8, width)
        for r in range(g * 8, g * 8 + 8, 2):
            y = product(
                w, jnp.concatenate([spread[(r + q) * depth : (r + q + 1) * depth, :] for q in range(2)], 1)
            )
            for q in range(2):
                to[pl.ds((r + q) % 8, levels, stride=8), :] = y[:levels, q * width : (q + 1) * width]
        leave.append(pltpu.make_async_copy(result.at[g], out.at[:, g], done.at[g]))
        leave[-1].start()
    for move in leave:
        move.wait()


def add_kernel(keep, got, after, *parts):
    total = keep[...] + got[...]
    n = parts[0].shape[0]
    for q, part in enumerate(parts):
        part[...] = total[q * n : (q + 1) * n]


def heat_kernel(sizes, kept, got_1, got_2, got_3, wet, sea_first, before, after):
    levels, rows, steps, sea_levels, sea_rows, stride, sea_stride = sizes
    heat = kept[...] + got_1[...] + got_2[...] + got_3[...]
    heat = wet[...].astype(f32) * heat
    for l in range(sea_levels):
        after[l * sea_rows : (l + 1) * sea_rows, :] = (
            before[l * sea_rows : (l + 1) * sea_rows, :] + sea_first[l : l + 1, :] * heat
        )


def body(sky, forcing, curve, surface, rate, vmix, shares, owners, locals_, warmth, brine, wet, sea_mix):
    levels, rows, width = sky.shape
    steps = forcing.shape[0]
    sea_levels, sea_rows, _ = warmth.shape
    topk = owners.shape[1]
    stride = up_to(levels + steps + 3, 8)
    sea_stride = up_to(sea_levels, 16)
    sizes = (levels, rows, steps, sea_levels, sea_rows, stride, sea_stride)
    sky2, forcing2 = sky.reshape(-1, width), forcing.reshape(-1, width)
    warmth2, brine2 = warmth.reshape(-1, width), brine.reshape(-1, width)
    flat = lambda n, kind=f32: jax.ShapeDtypeStruct((n, width), kind)

    space = lambda *shape: pltpu.VMEM(shape, f32)
    space = lambda *shape: pltpu.VMEM(shape, f32)
    length = HALO * stride + 2 * sea_stride + 8
    ring = ("tile", "comp")
    tiles, count = lax.axis_size("tile"), lax.axis_size(ring)
    at = lax.axis_index(ring).astype(jnp.int32)[None]
    core = lax.axis_index("comp").astype(jnp.int32)[None]
    tile = lax.axis_index("tile").astype(jnp.int32)[None]
    inner, outer = call(
        functools.partial(pack_kernel, sizes), [flat(length)] * 2,
        core, sky, forcing, surface, rate, warmth2, brine2, wet, moved=4 << 20, in_specs=[SMEM] + [HBM] * 7,
        scratch=[
            space(2, levels, 8, width), space(steps, rows, width), space(2, sea_levels * sea_rows, width),
            space(2, rows, width), pltpu.VMEM(wet.shape, wet.dtype), pltpu.SemaphoreType.DMA((8,)),
        ],
        grant=FULL,
    )
    swap = lambda first: [(i + a, i + 1 - a) for i in range(first, count - 1, 2) for a in range(2)]
    outer = lax.ppermute(outer, ring, swap(1))
    inner = lax.ppermute(inner, ring, swap(0))

    depth = up_to(levels + 2 * steps, 16)
    mix_rows = up_to(levels, 16)
    area = sea_levels * sea_rows
    rows_of_mix, source_rows, own, weights, sea_weights, sea_first, sea_ends, spread, warm, salt = call(
        functools.partial(local_kernel, sizes, count - 1),
        [
            flat((steps - 1) * levels), flat(8), flat((steps - 1) * rows),
            jax.ShapeDtypeStruct((mix_rows, 2 * width), bf16),
            jax.ShapeDtypeStruct((sea_stride, 2 * width), bf16), flat(sea_stride), flat(4 * sea_stride),
            flat(rows * levels), flat(area), flat(area),
        ],
        at, vmix, curve[None], sea_mix, sky2, warmth2, brine2, wet, in_specs=[SMEM] + [VMEM] * 7,
        scratch=[space(2, sea_rows * sea_stride, width)],
        flops=4 << 30, moved=8 << 20,
    )

    half = tiles // 2 * sea_rows
    keep, send, fluxes, above, below = call(
        functools.partial(flux_kernel, sizes),
        [flat(half)] * 2 + [flat(2 * steps * (rows + 2 * HALO)), flat(length), flat(length)],
        core, tile, sky[-1], forcing2, surface, rate, rows_of_mix, source_rows, own, owners.T, locals_.T,
        shares.reshape(-1, width), outer, inner,
        in_specs=[SMEM] * 2 + [VMEM] * 12, scratch=[space(2 * HALO * stride, width)], moved=2 << 20,
    )
    def edge_part(after):
        return call(
            functools.partial(edge_kernel, sizes), flat(rows * depth), fluxes, spread, above, below, after,
            in_specs=[VMEM] * 4 + [ANY], flops=1 << 28, moved=4 << 20,
        )

    def shore_part(after):
        return call(
            functools.partial(shore_kernel, sizes), [flat(area), flat(area)],
            sea_weights, sea_ends, wet, warm, salt, above, below, after,
            in_specs=[VMEM] * 7 + [ANY], out_specs=[VMEM, HBM],
            scratch=[space(area, width), pltpu.SemaphoreType.DMA((1,))], flops=1 << 28, moved=4 << 20,
        )

    swapped = lambda x, bits: lax.ppermute(x, "tile", [(i, i ^ bits) for i in range(tiles)])
    got = swapped(send, 1)
    ready = edge_part(keep)
    size = tiles // 2
    while size > 4:
        keep, send = call(add_kernel, [flat(size // 2 * sea_rows)] * 2, keep, got, ready, in_specs=[VMEM] * 2 + [ANY])
        got = swapped(send, size)
        size //= 2
    keep, *sends = call(add_kernel, [flat(sea_rows)] * 4, keep, got, ready, in_specs=[VMEM] * 2 + [ANY])
    gots = [swapped(sends[q - 1], 2 * q) for q in (3, 2, 1)]
    warm, salt = shore_part(keep)
    sky_out = call(
        functools.partial(mix_kernel, sizes), jax.ShapeDtypeStruct((levels, rows // 8, 8, width), f32),
        ready, weights, keep, in_specs=[VMEM, VMEM, ANY], out_specs=HBM,
        scratch=[space(rows // 8, levels, 8, width), pltpu.SemaphoreType.DMA((rows // 8,))],
        flops=2 << 30, moved=4 << 20,
    )
    warm = call(functools.partial(heat_kernel, sizes), flat(area), keep, *gots, wet, sea_first, warm, moved=2 << 20)
    return sky_out.reshape(sky.shape), warm.reshape(warmth.shape), salt.reshape(brine.shape)


def solution(mesh):
    both = P(None, ("member", "tile", "comp"), None)
    one = P(("tile", "comp"), None)
    return jax.shard_map(
        body,
        mesh=mesh,
        in_specs=(
            both, both, P(), P(("member", "tile", "comp"), None), one, P(), P(), one, one, both, both, one, P(),
        ),
        out_specs=(both, both, both),
        check_vma=False,
    )
```

```python
import functools

import jax
import jax.numpy as jnp
from jax import lax
from jax.experimental import pallas as pl
from jax.experimental.pallas import tpu as pltpu
from jax.sharding import PartitionSpec as P

atm_diffusion = 0.2
ocean_diffusion = 0.2
HALO = 4
FULL = 60
EXACT = lax.Precision.HIGHEST
VMEM = pl.BlockSpec(memory_space=pltpu.VMEM)
HBM = pl.BlockSpec(memory_space=pltpu.HBM)
SMEM = pl.BlockSpec(memory_space=pltpu.SMEM)
ANY = pl.BlockSpec(memory_space=pl.ANY)
f32, bf16 = jnp.float32, jnp.bfloat16


def up_to(n, m):
    return -(-n // m) * m


def call(kernel, out_shape, *args, scratch=(), in_specs=None, out_specs=None, flops=0, moved=0, grant=24):
    return pl.pallas_call(
        kernel,
        out_shape=out_shape,
        in_specs=in_specs or [VMEM] * len(args),
        out_specs=out_specs or jax.tree.map(lambda _: VMEM, out_shape),
        scratch_shapes=list(scratch),
        compiler_params=pltpu.CompilerParams(vmem_limit_bytes=grant * 2**20),
        cost_estimate=pl.CostEstimate(flops=flops, bytes_accessed=moved, transcendentals=0),
    )(*args)


def copies(pairs, done):
    return [pltpu.make_async_copy(src, dst, done.at[i]) for i, (src, dst) in enumerate(pairs)]


def pack_kernel(
    sizes, core, sky, forcing, surface, rate, warmth, brine, wet, inner, outer,
    ends, force, sea, flat, marks, done
):
    levels, rows, steps, sea_levels, sea_rows, stride, sea_stride = sizes
    width = sky.shape[2]
    low = rows - 8
    moves = copies(
        [
            (sky.at[:, 0:8, :], ends.at[0]), (sky.at[:, low:rows, :], ends.at[1]), (forcing, force),
            (surface, flat.at[0]), (rate, flat.at[1]), (warmth, sea.at[0]), (brine, sea.at[1]), (wet, marks),
        ],
        done,
    )
    for move in moves:
        move.start()
    for move in moves:
        move.wait()
    end = ends.reshape(2 * levels * 8, width)
    for which, out in enumerate((inner, outer)):
        last = jnp.where(core[0] == 0, 1 - which, which)
        sea_row = last * (sea_rows - 1)
        for j in range(HALO):
            row = last * (rows - HALO) + j
            first = last * (levels * 8 + 8 - HALO) + j
            out[j * stride : j * stride + levels, :] = end[pl.ds(first, levels, stride=8), :]
            base = j * stride + levels
            tail = [force[s, pl.ds(row, 1), :] for s in range(steps)]
            tail += [flat[0, pl.ds(row, 1), :], flat[1, pl.ds(row, 1), :], jnp.ones((1, width), f32)]
            tail += [jnp.zeros((stride - levels - len(tail), width), f32)]
            out[base : (j + 1) * stride, :] = jnp.concatenate(tail, 0)
        base = HALO * stride
        edge = marks[pl.ds(sea_row, 1), :].astype(f32)
        for f in range(2):
            out[base : base + sea_levels, :] = sea[f, pl.ds(sea_row, sea_levels, stride=sea_rows), :] * edge
            base += sea_stride
        out[base : base + 8, :] = jnp.concatenate([edge, jnp.zeros((7, width), f32)], 0)


def split(x):
    high = x.astype(bf16)
    return high, (x - high.astype(f32)).astype(bf16)


def three_terms(w, depth):
    high = w.astype(bf16).astype(f32)
    low = w - high
    return (high + pltpu.roll(high, depth, 1) + pltpu.roll(low, 2 * depth, 1)).astype(bf16)


def row_of(ref, first, count, step, size):
    x = ref[pl.ds(first, count, stride=step), :]
    if count < size:
        x = jnp.concatenate([x, jnp.zeros((size - count, x.shape[1]), f32)], 0)
    return x


def beside(x):
    return pltpu.roll(x, 1, 1) + pltpu.roll(x, x.shape[1] - 1, 1)


def stencil(x):
    return [x[i - 1] + x[i] + x[i + 1] + beside(x[i]) for i in range(1, len(x) - 1)]


def product(weights, x):
    high, low = split(x)
    return jnp.dot(weights, jnp.concatenate([high, low, high], 0), preferred_element_type=f32)


def local_kernel(
    sizes, last_place, place, vmix, curve, sea_mix, sky, warmth, brine, wet,
    rows_of_mix, source_rows, own, weights, sea_weights, sea_first, sea_ends, spread, warm_out, brine_out, sea_spread,
):
    levels, rows, steps, sea_levels, sea_rows, stride, sea_stride = sizes
    width = sky.shape[1]
    depth = up_to(levels + 2 * steps, 16)
    v = vmix[...]
    dot = functools.partial(jnp.dot, precision=EXACT, preferred_element_type=f32)
    powers = [v]
    for _ in range(steps - 1):
        powers.append(dot(v, powers[-1]))
    last = (lax.broadcasted_iota(jnp.int32, (levels, width), 0) == levels - 1).astype(f32)
    for s in range(1, steps):
        rows_of_mix[(s - 1) * levels : s * levels, :] = lax.dot_general(
            powers[s - 1], last, (((0,), (0,)), ((), ())), precision=EXACT, preferred_element_type=f32
        )
    by_curve = jnp.broadcast_to(curve[...], (width, levels))
    of_curve = [
        lax.dot_general(p, by_curve, (((1,), (1,)), ((), ())), precision=EXACT, preferred_element_type=f32)
        for p in powers
    ]
    of_last = [jnp.broadcast_to(p[:, levels - 1 : levels], (levels, width)) for p in powers]
    found = [of_curve[i][levels - 1 :] for i in range(steps - 1)]
    found += [of_last[i][levels - 1 :] for i in range(steps - 1)]
    found += [jnp.zeros((8 - len(found), width), f32)]
    source_rows[...] = jnp.concatenate(found, 0)
    lane = lax.broadcasted_iota(jnp.int32, (levels, width), 1)
    wide = jnp.concatenate(
        [powers[-1] * atm_diffusion**steps, jnp.zeros((levels, width - levels), f32)], 1
    )
    for j in range(steps):
        factor = atm_diffusion ** (steps - 1 - j)
        for at, value in ((j, of_curve[steps - 1 - j] * factor), (steps + j, of_last[steps - 1 - j] * -factor)):
            wide = jnp.where(lane == levels + at, value, wide)
    more = jnp.zeros((weights.shape[0] - levels, width), f32)
    wide = jnp.concatenate([wide, more], 0)
    wide = jnp.concatenate([wide, jnp.zeros_like(wide)], 1)
    weights[...] = three_terms(wide, depth)
    sea = sea_mix[...]
    sea = jnp.concatenate([sea, jnp.zeros((sea_levels, 2 * width - sea_levels), f32)], 1)
    sea = jnp.concatenate([sea, jnp.zeros((sea_stride - sea_levels, 2 * width), f32)], 0)
    sea_weights[...] = three_terms(sea, sea_stride)
    sea_first[...] = jnp.broadcast_to(sea[:, 0:1], sea_first.shape)
    sums = [jnp.zeros((rows, width), f32) for _ in range(steps - 1)]
    for l in range(levels):
        x = sky[l * rows : (l + 1) * rows, :]
        for s in range(steps - 1):
            sums[s] = sums[s] + rows_of_mix[s * levels + l : s * levels + l + 1, :] * x
    for s in range(steps - 1):
        own[s * rows : (s + 1) * rows, :] = sums[s]

    m = wet[...].astype(f32)
    mark = [m[r : r + 1] for r in range(sea_rows)]
    edge = jnp.zeros((1, width), f32)

    def near(x):
        x = [jnp.zeros_like(x[0])] + x + [jnp.zeros_like(x[0])]
        return [x[i - 1] + x[i + 1] + beside(x[i]) for i in range(1, len(x) - 1)]

    around = (
        jnp.concatenate([edge, m[:-1]], 0) + jnp.concatenate([m[1:], edge], 0) + beside(m)
    ) * ocean_diffusion
    share = [around[r : r + 1] for r in range(sea_rows)]
    for f, field in enumerate((warmth, brine)):
        for c in range(sea_stride // 8):
            count = min(8, sea_levels - c * 8)
            x = [row_of(field, c * 8 * sea_rows + r, count, sea_rows, 8) for r in range(sea_rows)]
            y = near([mark[r] * x[r] for r in range(sea_rows)])
            for r in range(sea_rows):
                at = r * sea_stride + c * 8
                sea_spread[f, at : at + 8, :] = x[r] + mark[r] * (ocean_diffusion * y[r] - x[r] * share[r])
    w = sea_weights[:, : 3 * sea_stride]
    for r in range(sea_rows):
        x = jnp.concatenate([sea_spread[f, r * sea_stride : (r + 1) * sea_stride, :] for f in range(2)], 1)
        y = product(w, x)
        for f, (field, out) in enumerate(((warmth, warm_out), (brine, brine_out))):
            old = field[pl.ds(r, sea_levels, stride=sea_rows), :]
            new = y[:sea_levels, f * width : (f + 1) * width]
            out[pl.ds(r, sea_levels, stride=sea_rows), :] = mark[r] * new + (1.0 - mark[r]) * old
            if r in (0, sea_rows - 1):
                at = (2 * f + (r > 0)) * sea_stride
                sea_ends[at : at + sea_levels, :] = old

    before = jnp.where(place[0] > 0, 1.0, 0.0)
    behind = jnp.where(place[0] < last_place, 1.0, 0.0)

    @pl.loop(0, levels // 8)
    def _(c):
        x = [sky[pl.ds(c * 8 * rows + r, 8, stride=rows), :] for r in range(rows)]
        none = jnp.zeros_like(x[0])
        beyond = 0
        for n in range(steps):
            if beyond < steps - 1 - n:
                x = [x[0]] + stencil([none] + x + [none]) + [x[-1]]
                beyond += 1
            else:
                x = stencil(x)
                beyond -= 1
            for i in range(beyond):
                x[i] = x[i] * before
                x[-1 - i] = x[-1 - i] * behind
        for r in range(rows):
            spread[pl.ds(pl.multiple_of(r * levels + c * 8, 8), 8), :] = x[r]


def cross(x):
    n, w = x.shape
    return (
        x + pltpu.roll(x, 1, 0) + pltpu.roll(x, n - 1, 0) + pltpu.roll(x, 1, 1) + pltpu.roll(x, w - 1, 1)
    )


def masked(x, rows, inside):
    return jnp.concatenate([x[:rows], x[rows:] * inside], 0)


def flux_kernel(
    sizes, core, tile, sky, forcing, surface, rate, rows_of_mix, source_rows, own, owners, locals_, shares, outer, inner,
    keep, send_1, send_2, send_3, fluxes, above, below, halo
):
    levels, rows, steps, sea_levels, sea_rows, stride, sea_stride = sizes
    width = sky.shape[1]
    one, two = inner[...], outer[...]
    above[...] = jnp.where(core[0] == 0, two, one)
    below[...] = jnp.where(core[0] == 0, one, two)
    halo[: HALO * stride, :] = below[: HALO * stride, :]
    halo[HALO * stride :, :] = above[: HALO * stride, :]

    def edge(l):
        return halo[pl.ds(l, 2 * HALO, stride=stride), :]

    inside = edge(levels + steps + 2)
    sums = [jnp.zeros((2 * HALO, width), f32) for _ in range(steps - 1)]
    for l in range(levels):
        x = edge(l)
        for s in range(steps - 1):
            sums[s] = sums[s] + rows_of_mix[s * levels + l : s * levels + l + 1, :] * x
    tops = [jnp.concatenate([sky[...], edge(levels - 1)], 0)]
    tops += [jnp.concatenate([own[s * rows : (s + 1) * rows, :], sums[s]], 0) for s in range(steps - 1)]
    surf = jnp.concatenate([surface[...], edge(levels + steps)], 0)
    coef = jnp.concatenate([rate[...], edge(levels + steps + 1)], 0)
    force = [
        jnp.concatenate([forcing[s * rows : (s + 1) * rows, :], edge(levels + s)], 0) for s in range(steps)
    ]

    flux = []
    for s in range(steps):
        state = tops[s]
        for i in range(s):
            m = s - 1 - i
            state = masked(cross(state) * atm_diffusion, rows, inside)
            state = state + source_rows[m : m + 1, :] * force[i]
            state = state - source_rows[steps - 1 + m : steps + m, :] * flux[i]
        flux.append(coef * (state - surf))
        reach = rows + 2 * HALO
        fluxes[pl.ds(s, reach, stride=2 * steps), :] = force[s]
        fluxes[pl.ds(steps + s, reach, stride=2 * steps), :] = flux[s]
    total = flux[0][:rows]
    for s in range(1, steps):
        total = total + flux[s][:rows]
    mean = (total / steps).astype(bf16)
    topk = owners.shape[0]
    target = (owners[...] ^ tile[0]) * sea_rows + locals_[...]
    target = jnp.concatenate([target[k : k + 1, :] for k in range(topk)], 1)
    rowed = jnp.concatenate(
        [jnp.dot(mean, shares[k * width : (k + 1) * width, :], preferred_element_type=f32) for k in range(topk)], 0
    )
    first = rowed.astype(bf16)
    left = rowed - first.astype(f32)
    second = left.astype(bf16)
    third = (left - second.astype(f32)).astype(bf16)
    part = keep.shape[0]
    hot = lax.broadcasted_iota(jnp.int32, (4 * part, topk * rows), 0) == target
    hot = jnp.where(hot, 1.0, 0.0).astype(bf16)
    sums = jnp.dot(
        jnp.concatenate([hot, hot, hot], 1), jnp.concatenate([first, second, third], 0), preferred_element_type=f32
    )
    for q, to in enumerate((keep, send_1, send_2, send_3)):
        to[...] = sums[q * part : (q + 1) * part]


def edge_kernel(
    sizes, fluxes, own, above, below, after, spread
):
    levels, rows, steps, sea_levels, sea_rows, stride, sea_stride = sizes
    width = own.shape[1]
    depth = up_to(levels + 2 * steps, 16)
    flag = levels + steps + 2
    inside_above, inside_below = above[flag : flag + 1, :], below[flag : flag + 1, :]

    reach = rows + 2 * HALO
    x = [fluxes[(r % reach) * 2 * steps : (r % reach + 1) * 2 * steps, :] for r in range(1 - steps, rows + steps - 1)]
    field = lax.broadcasted_iota(jnp.int32, (2 * steps, width), 0) % steps
    for n in range(1, steps):
        y = stencil(x)
        x = [jnp.where(field < steps - n, y[i], x[i + 1]) for i in range(len(y))]
        for i in range(steps - 1 - n):
            x[i] = x[i] * inside_above
            x[-1 - i] = x[-1 - i] * inside_below
    for r in range(rows):
        spread[r * depth + levels : (r + 1) * depth, :] = x[r]
        if HALO <= r < rows - HALO:
            spread[r * depth : r * depth + levels, :] = own[r * levels : (r + 1) * levels, :]

    @pl.loop(0, levels // 8)
    def _(c):
        def other(ref, j):
            return ref[pl.ds(pl.multiple_of(j * stride + c * 8, 8), 8), :]

        top, low = ([other(ref, j) for j in range(HALO)] for ref in (above, below))
        none = jnp.zeros_like(top[0])
        for n in range(steps):
            top = stencil(top + [none]) + [top[-1]]
            low = [low[0]] + stencil([none] + low)
        for i, value in enumerate(top + low):
            r = i if i < HALO else rows - 2 * HALO + i
            value = value + own[pl.ds(pl.multiple_of(r * levels + c * 8, 8), 8), :]
            spread[pl.ds(pl.multiple_of(r * depth + c * 8, 8), 8), :] = value


def shore_kernel(
    sizes, sea_weights, sea_ends, wet, warm, salt, above, below, after, warm_out, brine_out, salt_held, done
):
    levels, rows, steps, sea_levels, sea_rows, stride, sea_stride = sizes
    width = warm.shape[1]
    warm_out[...] = warm[...]
    salt_held[...] = salt[...]
    m = wet[...].astype(f32)
    base = HALO * stride
    w = sea_weights[:, : 3 * sea_stride]
    for e, (r, other) in enumerate(((0, above), (sea_rows - 1, below))):
        mark = m[r : r + 1]
        far = other[base + 2 * sea_stride : base + 2 * sea_stride + 1, :]
        x = []
        for f in range(2):
            at = base + f * sea_stride
            mine = (2 * f + e) * sea_stride
            step = other[at : at + sea_levels, :] - sea_ends[mine : mine + sea_levels, :] * far
            step = ocean_diffusion * (mark * step)
            x.append(jnp.concatenate([step, jnp.zeros((sea_stride - sea_levels, width), f32)], 0))
        y = product(w, jnp.concatenate(x, 1))
        for f, to in enumerate((warm_out, salt_held)):
            rows_at = pl.ds(r, sea_levels, stride=sea_rows)
            to[rows_at, :] = to[rows_at, :] + mark * y[:sea_levels, f * width : (f + 1) * width]
    leave = [pltpu.make_async_copy(salt_held, brine_out, done.at[0])]
    leave[0].start()
    for move in leave:
        move.wait()


def mix_kernel(sizes, spread, weights, after, out, result, done):
    levels, rows, steps, sea_levels, sea_rows, stride, sea_stride = sizes
    width = spread.shape[1]
    depth = up_to(levels + 2 * steps, 16)
    w = weights[:, : 3 * depth]
    leave = []
    for g in range(rows // 8):
        to = result.at[g].reshape(levels * 8, width)
        for r in range(g * 8, g * 8 + 8, 2):
            y = product(
                w, jnp.concatenate([spread[(r + q) * depth : (r + q + 1) * depth, :] for q in range(2)], 1)
            )
            for q in range(2):
                to[pl.ds((r + q) % 8, levels, stride=8), :] = y[:levels, q * width : (q + 1) * width]
        leave.append(pltpu.make_async_copy(result.at[g], out.at[:, g], done.at[g]))
        leave[-1].start()
    for move in leave:
        move.wait()


def add_kernel(keep, *others):
    gots, (after, kept, send) = others[:-3], others[-3:]
    total = keep[...]
    for got in gots:
        total = total + got[...]
    n = kept.shape[0]
    kept[...] = total[:n]
    send[...] = total[n:]


def heat_kernel(sizes, kept, got, wet, sea_first, before, after):
    levels, rows, steps, sea_levels, sea_rows, stride, sea_stride = sizes
    heat = kept[...] + got[...]
    heat = wet[...].astype(f32) * heat
    for l in range(sea_levels):
        after[l * sea_rows : (l + 1) * sea_rows, :] = (
            before[l * sea_rows : (l + 1) * sea_rows, :] + sea_first[l : l + 1, :] * heat
        )


def body(sky, forcing, curve, surface, rate, vmix, shares, owners, locals_, warmth, brine, wet, sea_mix):
    levels, rows, width = sky.shape
    steps = forcing.shape[0]
    sea_levels, sea_rows, _ = warmth.shape
    topk = owners.shape[1]
    stride = up_to(levels + steps + 3, 8)
    sea_stride = up_to(sea_levels, 16)
    sizes = (levels, rows, steps, sea_levels, sea_rows, stride, sea_stride)
    sky2, forcing2 = sky.reshape(-1, width), forcing.reshape(-1, width)
    warmth2, brine2 = warmth.reshape(-1, width), brine.reshape(-1, width)
    flat = lambda n, kind=f32: jax.ShapeDtypeStruct((n, width), kind)

    space = lambda *shape: pltpu.VMEM(shape, f32)
    space = lambda *shape: pltpu.VMEM(shape, f32)
    length = HALO * stride + 2 * sea_stride + 8
    ring = ("tile", "comp")
    tiles, count = lax.axis_size("tile"), lax.axis_size(ring)
    at = lax.axis_index(ring).astype(jnp.int32)[None]
    core = lax.axis_index("comp").astype(jnp.int32)[None]
    tile = lax.axis_index("tile").astype(jnp.int32)[None]
    inner, outer = call(
        functools.partial(pack_kernel, sizes), [flat(length)] * 2,
        core, sky, forcing, surface, rate, warmth2, brine2, wet, moved=4 << 20, in_specs=[SMEM] + [HBM] * 7,
        scratch=[
            space(2, levels, 8, width), space(steps, rows, width), space(2, sea_levels * sea_rows, width),
            space(2, rows, width), pltpu.VMEM(wet.shape, wet.dtype), pltpu.SemaphoreType.DMA((8,)),
        ],
        grant=FULL,
    )
    swap = lambda first: [(i + a, i + 1 - a) for i in range(first, count - 1, 2) for a in range(2)]
    outer = lax.ppermute(outer, ring, swap(1))
    inner = lax.ppermute(inner, ring, swap(0))

    depth = up_to(levels + 2 * steps, 16)
    mix_rows = up_to(levels, 16)
    area = sea_levels * sea_rows
    rows_of_mix, source_rows, own, weights, sea_weights, sea_first, sea_ends, spread, warm, salt = call(
        functools.partial(local_kernel, sizes, count - 1),
        [
            flat((steps - 1) * levels), flat(8), flat((steps - 1) * rows),
            jax.ShapeDtypeStruct((mix_rows, 2 * width), bf16),
            jax.ShapeDtypeStruct((sea_stride, 2 * width), bf16), flat(sea_stride), flat(4 * sea_stride),
            flat(rows * levels), flat(area), flat(area),
        ],
        at, vmix, curve[None], sea_mix, sky2, warmth2, brine2, wet, in_specs=[SMEM] + [VMEM] * 7,
        scratch=[space(2, sea_rows * sea_stride, width)],
        flops=4 << 30, moved=8 << 20,
    )

    part = tiles // 4 * sea_rows
    keep, send_1, send_2, send_3, fluxes, above, below = call(
        functools.partial(flux_kernel, sizes),
        [flat(part)] * 4 + [flat(2 * steps * (rows + 2 * HALO)), flat(length), flat(length)],
        core, tile, sky[-1], forcing2, surface, rate, rows_of_mix, source_rows, own, owners.T, locals_.T,
        shares.reshape(-1, width), outer, inner,
        in_specs=[SMEM] * 2 + [VMEM] * 12, scratch=[space(2 * HALO * stride, width)], moved=2 << 20,
    )
    def edge_part(after):
        return call(
            functools.partial(edge_kernel, sizes), flat(rows * depth), fluxes, spread, above, below, after,
            in_specs=[VMEM] * 4 + [ANY], flops=1 << 28, moved=4 << 20,
        )

    def shore_part(after):
        return call(
            functools.partial(shore_kernel, sizes), [flat(area), flat(area)],
            sea_weights, sea_ends, wet, warm, salt, above, below, after,
            in_specs=[VMEM] * 7 + [ANY], out_specs=[VMEM, HBM],
            scratch=[space(area, width), pltpu.SemaphoreType.DMA((1,))], flops=1 << 28, moved=4 << 20,
        )

    bit = tiles // 4
    gots = [
        lax.ppermute(x, "tile", [(i, i ^ (q * bit)) for i in range(tiles)])
        for q, x in ((3, send_3), (2, send_2), (1, send_1))
    ]
    ready = edge_part(keep)
    warm, salt = shore_part(keep)
    while bit > 1:
        bit //= 2
        keep, send = call(
            add_kernel, [flat(bit * sea_rows)] * 2, keep, *gots, ready, in_specs=[VMEM] * (1 + len(gots)) + [ANY],
        )
        gots = [lax.ppermute(send, "tile", [(i, i ^ bit) for i in range(tiles)])]
    got = gots[0]
    sky_out = call(
        functools.partial(mix_kernel, sizes), jax.ShapeDtypeStruct((levels, rows // 8, 8, width), f32),
        ready, weights, keep, in_specs=[VMEM, VMEM, ANY], out_specs=HBM,
        scratch=[space(rows // 8, levels, 8, width), pltpu.SemaphoreType.DMA((rows // 8,))],
        flops=2 << 30, moved=4 << 20,
    )
    warm = call(functools.partial(heat_kernel, sizes), flat(area), keep, got, wet, sea_first, warm, moved=2 << 20)
    return sky_out.reshape(sky.shape), warm.reshape(warmth.shape), salt.reshape(brine.shape)


def solution(mesh):
    both = P(None, ("member", "tile", "comp"), None)
    one = P(("tile", "comp"), None)
    return jax.shard_map(
        body,
        mesh=mesh,
        in_specs=(
            both, both, P(), P(("member", "tile", "comp"), None), one, P(), P(), one, one, both, both, one, P(),
        ),
        out_specs=(both, both, both),
        check_vma=False,
    )
```
